32 devices in a mesh: section: 4 (over y, x), dp: 8 (over z, core).
Axes of the slice: x: 2, y: 2, z: 4, core: 2. Of those that a mesh axis runs over, the one named last changes fastest.
Arguments:
- layer_input: bfloat16 [2, 8, 512, 640], P(None, 'dp'), may hold values from -6 to 6
- out_cotangent: bfloat16 [2, 8, 512, 640], P(None, 'dp'), may hold values from -6 to 6
- lengths: int32 [2, 8], P(None, 'dp'), may hold values from 20 to 512, as said below
- qkv_weight: float32 [4, 640, 960], P('section', 'dp'), may hold values from -0.3125 to 0.3125
- qv_bias: float32 [4, 640], P('section', 'dp'), may hold values from -1.8 to 1.8
- out_weight: float32 [4, 320, 640], P('section', 'dp'), may hold values from -0.5 to 0.5
- up_weight: float32 [4, 640, 2560], P('section', 'dp'), may hold values from -0.25 to 0.25
- up_bias: float32 [4, 2560], P('section', 'dp'), may hold values from -3 to 3
- down_weight: float32 [4, 2560, 640], P('section', 'dp'), may hold values from -0.078125 to 0.078125
- norm_vectors: float32 [4, 3, 640], P('section', None, 'dp'), may hold values from -0.9 to 1.4
Outputs:
- layer_output: bfloat16 [2, 8, 512, 640], P(None, 'dp', 'section')
- input_grad: bfloat16 [2, 8, 512, 640], P(None, 'dp', 'section')
- qkv_grad: float32 [4, 640, 960], P('section', 'dp')
- qv_bias_grad: float32 [4, 640], P('section', 'dp')
- out_grad: float32 [4, 320, 640], P('section', 'dp')
- up_grad: float32 [4, 640, 2560], P('section', 'dp')
- up_bias_grad: float32 [4, 2560], P('section', 'dp')
- down_grad: float32 [4, 2560, 640], P('section', 'dp')
- norm_grad: float32 [4, 3, 640], P('section', None, 'dp')
- stream_rms: float32 [2, 8, 4, 2], P(None, 'dp', 'section')
The draws below stay inside these ranges and needn't reach their ends.
Inputs may be any that keep to these rules, and one draw needn't show every extreme that they name: `lengths`: in every micro-batch one sequence has exactly 512 nucleotides and another exactly 20.
All inputs are finite; a program needn't handle non-finite values.
Results may differ from the reference program's by a relative error of at most 0.025.
The reference program's roundings to bfloat16 on the way count: a program that leaves them out, or rounds other values in their place, can miss the bound.
Values may be sent and summed in bfloat16 or wider, within the bound.
A program may use at most 640 MiB of HBM per device.

```python
import jax
import jax.numpy as jnp
from jax import lax

D = 640
HEAD_DIM = 32
FF = 5120
LEN = 512
MIN_LEN = 20
MICRO = 2
SEQS = 8
N_SECTION = 4


def draw_lengths(key, part):
    key = jax.random.fold_in(key, 11)
    subkeys = jax.random.split(key, 2)
    drawn = jax.random.randint(subkeys[0], (MICRO, SEQS), MIN_LEN, LEN + 1)
    order_keys = jax.random.split(subkeys[1], MICRO)
    orders = jax.vmap(lambda order_key: jax.random.permutation(order_key, SEQS))(order_keys)
    column = jnp.arange(SEQS)[None, :]
    drawn = jnp.where(column == orders[:, :1], LEN, drawn)
    drawn = jnp.where(column == orders[:, 1:2], MIN_LEN, drawn)
    return drawn.astype(jnp.int32)


def draw_norm_vectors(key, part):
    key = jax.random.fold_in(key, 7)
    subkeys = jax.random.split(key, 2)
    gain_rows = 1.0 + 0.25 * jnp.tanh(jax.random.normal(subkeys[0], (N_SECTION, 1, D), jnp.float32))
    bias_rows = 0.3 * jnp.clip(jax.random.normal(subkeys[1], (N_SECTION, 2, D), jnp.float32), -3.0, 3.0)
    return jnp.concatenate([gain_rows, bias_rows], axis=1)


def shard_levels(key, dims, shards, least, top_value):
    level = 1.0
    for position, shards_of in shards:
        draws = jax.random.uniform(jax.random.fold_in(jax.random.fold_in(key, 6), position), (shards_of,), jnp.float32, least / len(shards), top_value / len(shards))
        level = level * jnp.repeat(jnp.exp(draws), dims[position] // shards_of).reshape((-1,) + (1,) * (len(dims) - 1 - position))
    return level


def noise(rng, dims, deviation, most, shards=(), kind=jnp.bfloat16):
    loudness = shard_levels(rng, dims, shards, -0.22, 0.18) if shards else 1.0
    entries = jax.random.normal(rng, dims, jnp.float32) * deviation * loudness
    return jnp.minimum(jnp.maximum(entries, -most), most).astype(kind)


def setup_inputs(seed: int = 0) -> dict:
    keys = jax.random.split(jax.random.key(seed), 11)
    layer_input = noise(keys[0], (MICRO, SEQS, LEN, D), 1.0, 6.0, ((1, 8),))
    out_cotangent = noise(keys[1], (MICRO, SEQS, LEN, D), 1.0, 6.0, ((1, 8),))
    lengths = draw_lengths(jax.random.fold_in(keys[10], 71), 0)
    qkv_weight = noise(keys[3], (N_SECTION, D, 3 * (D // 2)), (D // 2) ** -0.5, 0.3125, ((0, 4), (1, 8)), jnp.float32)
    qv_bias = noise(keys[4], (N_SECTION, D), 0.3, 1.8, ((0, 4), (1, 8)), jnp.float32)
    out_weight = noise(keys[5], (N_SECTION, D // 2, D), (D // 4) ** -0.5, 0.5, ((0, 4), (1, 8)), jnp.float32)
    up_weight = noise(keys[6], (N_SECTION, D, FF // 2), D ** -0.5, 0.25, ((0, 4), (1, 8)), jnp.float32)
    up_bias = noise(keys[7], (N_SECTION, FF // 2), 0.5, 3.0, ((0, 4), (1, 8)), jnp.float32)
    down_weight = noise(keys[8], (N_SECTION, FF // 2, D), FF ** -0.5, 0.078125, ((0, 4), (1, 8)), jnp.float32)
    norm_vectors = draw_norm_vectors(jax.random.fold_in(keys[10], 71), 0)
    return {"layer_input": layer_input, "out_cotangent": out_cotangent, "lengths": lengths, "qkv_weight": qkv_weight, "qv_bias": qv_bias, "out_weight": out_weight, "up_weight": up_weight, "up_bias": up_bias, "down_weight": down_weight, "norm_vectors": norm_vectors}


@jax.custom_vjp
def low(v):
    return lax.optimization_barrier(v.astype(jnp.bfloat16)).astype(jnp.float32)

@jax.custom_vjp
def low_back(v):
    return v

def low_keep(v):
    return (low(v), None)

def low_pass(kept, grad):
    return (grad,)

def back_keep(v):
    return (v, None)

def back_low(kept, grad):
    return (low(grad),)
low.defvjp(low_keep, low_pass)
low_back.defvjp(back_keep, back_low)
EPSILON = 1e-05
MASKED = -1e+30

def round_both(value_in):
    return low_back(low(value_in))

def layer_norm(stream, gain_row, shift_row):
    row_mean = lax.optimization_barrier(jnp.mean(stream, axis=-1, keepdims=True))
    centred = stream - row_mean
    spread = lax.optimization_barrier(jnp.mean(centred * centred, axis=-1, keepdims=True))
    return centred * lax.rsqrt(spread + EPSILON) * gain_row + shift_row

def matmul_high(left, right):
    return jnp.dot(left, right, precision=lax.Precision.HIGHEST)

def attend_half(rescaled_token_vectors, query_key_value_portion, bias_half, length):
    features = query_key_value_portion.shape[1] // 3
    head_count = features // HEAD_DIM
    block_rows = min(512, LEN)
    linear_rows = matmul_high(rescaled_token_vectors, query_key_value_portion)
    query_rows = round_both(linear_rows[:, :features] + bias_half[:features])
    key_rows = round_both(linear_rows[:, features:2 * features])
    value_rows = round_both(linear_rows[:, 2 * features:] + bias_half[features:])
    query_rows = query_rows.reshape(LEN // block_rows, block_rows, head_count, HEAD_DIM)
    key_rows = key_rows.reshape(LEN, head_count, HEAD_DIM)
    value_rows = value_rows.reshape(LEN, head_count, HEAD_DIM)
    live_keys = lax.iota(jnp.int32, LEN) < length

    def per_block(query_block):
        raw_scores = jnp.einsum('qhd,khd->hqk', query_block, key_rows, precision=lax.Precision.HIGHEST)
        scores = jnp.where(live_keys[None, None, :], low_back(raw_scores) * HEAD_DIM ** (-0.5), MASKED)
        probabilities = round_both(jax.nn.softmax(scores, axis=-1))
        return jnp.einsum('hqk,khd->qhd', probabilities, value_rows, precision=lax.Precision.HIGHEST)
    attention_result = lax.map(jax.checkpoint(per_block), query_rows)
    return round_both(attention_result.reshape(LEN, features))

def feed_half(rescaled_token_vectors, up_weight_portion, bias_half, down_weight_portion):
    pre_act = low_back(matmul_high(rescaled_token_vectors, up_weight_portion) + bias_half)
    hidden_rows = low(jax.nn.gelu(pre_act, approximate=False))
    return matmul_high(hidden_rows, down_weight_portion)

def run_sequence(sequence, length, rounded):
    qkv_weight, qv_bias, out_weight, up_weight, up_bias, down_weight, norm_vectors = rounded
    valid_rows = (lax.iota(jnp.int32, LEN) < length).astype(sequence.dtype)[:, None]
    stream = sequence
    squares = []
    for section_pos in range(N_SECTION):
        first_entry = section_pos - section_pos % 2
        vectors = norm_vectors[section_pos]
        rescaled_token_vectors = low(layer_norm(stream, vectors[0], vectors[1]))
        mixture = jnp.zeros_like(stream)
        for entry_index in (first_entry, first_entry + 1):
            if section_pos % 2 == 0:
                attention_result = attend_half(rescaled_token_vectors, qkv_weight[entry_index], qv_bias[entry_index], length)
                mixture = mixture + matmul_high(attention_result, out_weight[entry_index])
            else:
                mixture = mixture + feed_half(rescaled_token_vectors, up_weight[entry_index], up_bias[entry_index], down_weight[entry_index])
        branch = low_back(mixture + vectors[2])
        squares.append(jnp.stack([jnp.sum(stream * stream * valid_rows), jnp.sum(branch * branch * valid_rows)]))
        stream = round_both(stream + branch)
    return (stream, jnp.stack(squares))

def reference(layer_input, out_cotangent, lengths, qkv_weight, qv_bias, out_weight, up_weight, up_bias, down_weight, norm_vectors):
    params = (qkv_weight, qv_bias, out_weight, up_weight, up_bias, down_weight, norm_vectors)
    sequences = layer_input.astype(jnp.float32).reshape(MICRO * SEQS, LEN, D)
    flat_lengths = lengths.reshape(MICRO * SEQS)

    def forward(sequences, params):
        rounded = tuple((low(weights) for weights in params))

        def per_sequence(record):
            return run_sequence(record[0], record[1], rounded)
        streams, squares = lax.map(jax.checkpoint(per_sequence), (sequences, flat_lengths))
        return (streams, squares)
    streams, pullback, squares = jax.vjp(forward, sequences, params, has_aux=True)
    cotangent = out_cotangent.astype(jnp.float32).reshape(MICRO * SEQS, LEN, D)
    d_sequences, d_params = pullback(cotangent)
    counts = flat_lengths.astype(jnp.float32)[:, None, None] * D
    stream_rms = jnp.sqrt(squares / counts).reshape(MICRO, SEQS, N_SECTION, 2)
    shape_out = (MICRO, SEQS, LEN, D)
    return (streams.reshape(shape_out).astype(jnp.bfloat16), d_sequences.reshape(shape_out).astype(jnp.bfloat16), d_params[0], d_params[1], d_params[2], d_params[3], d_params[4], d_params[5], d_params[6], stream_rms)
```

```python
import types

import jax
import jax.numpy as jnp
from jax import lax
from jax.experimental import pallas as pl
from jax.experimental.pallas import tpu as pltpu
from jax.sharding import PartitionSpec as P

F32, BF16 = jnp.float32, jnp.bfloat16
MESH = pl.DeviceIdType.MESH
HEAD_DIM = 32
EPSILON = 1e-05
MASKED = -1e30
SCALE = HEAD_DIM**-0.5
SECTIONS = 4
NN = (((1,), (0,)), ((), ()))
NT = (((1,), (1,)), ((), ()))
TN = (((0,), (0,)), ((), ()))


def mm(left, right, dims=NN):
    return lax.dot_general(left, right, dims, preferred_element_type=F32)


def aligned(start, size):
    return pl.ds(pl.multiple_of(start, size), size)


def head_rows(h, heads):
    full = heads // 8 * 8
    low, rest = full * HEAD_DIM, (heads - full) * HEAD_DIM
    high = h // full if rest else 0
    q = h * HEAD_DIM + high * 2 * low
    k = low + h * HEAD_DIM + high * (low + rest)
    v = 2 * low + h * HEAD_DIM + high * 2 * rest
    return tuple(pl.multiple_of(row, HEAD_DIM) for row in (q, k, v))


def split_columns(half, heads):
    low = heads // 8 * 8 * HEAD_DIM
    lows = [(i * half, i * half + low) for i in range(3)]
    rests = [(i * half + low, (i + 1) * half) for i in range(3)]
    return lows + rests


def to_packed(rows, heads, width):
    half = rows.shape[-1] // 3
    parts = [rows[..., a:b] for a, b in split_columns(half, heads)]
    packed = jnp.concatenate(parts, axis=-1)
    return jnp.pad(packed, [(0, 0)] * (rows.ndim - 1) + [(0, width - packed.shape[-1])])


def from_packed(rows, half, heads):
    low = heads // 8 * 8 * HEAD_DIM
    rest = half - low
    out = []
    for i in range(3):
        out.append(rows[..., i * low : (i + 1) * low])
        out.append(rows[..., 3 * low + i * rest : 3 * low + (i + 1) * rest])
    return jnp.concatenate(out, axis=-1)


def normed_rows(h, gain, shift):
    mean = jnp.mean(h, axis=-1, keepdims=True)
    centred = h - mean
    spread = jnp.mean(centred * centred, axis=-1, keepdims=True)
    inverse = lax.rsqrt(spread + EPSILON)
    return centred * inverse, inverse, centred * inverse * gain + shift


def make_kernel(cfg, names):
    c_ = cfg
    D, L, U, F, W = c_.width, c_.length, c_.units, c_.features, c_.packed
    Q = L // SECTIONS
    NO, n, inner, heads = c_.outer, c_.outer // 2, c_.inner, c_.heads
    ru, rd, ro, rop = c_.up_rows, c_.down_rows, c_.out_rows, c_.out_padded
    piece_rows = (ru, rop, ru, rd)

    def kernel(*refs):
        R = types.SimpleNamespace(**dict(zip(names, refs)))
        s = lax.axis_index("section")
        y, x = s // 2, s % 2
        dp = lax.axis_index("dp")
        o, i = dp // inner, dp % inner
        zz, c = o // 2, o % 2
        other_x, other_y = s + 1 - 2 * x, s + 2 - 4 * y
        mate = o + 1 - 2 * c

        def remote(src, dst, send, recv, section, outer):
            return pltpu.make_async_remote_copy(
                src_ref=src,
                dst_ref=dst,
                send_sem=send,
                recv_sem=recv,
                device_id=(section, outer * inner + i),
                device_id_type=MESH,
            )

        def loop(count, body, first=0):
            def step(k, carry):
                body(k)
                return carry

            lax.fori_loop(first, count, step, 0)

        barrier = pltpu.get_barrier_semaphore()

        def greet(section, outer):
            pl.semaphore_signal(
                barrier, inc=1, device_id=(section, outer * inner + i), device_id_type=MESH
            )

        loop(SECTIONS, lambda k: greet((s + k) % SECTIONS, o), 1)
        loop(NO, lambda k: greet(s, (o + k) % NO), 1)
        pl.semaphore_wait(barrier, SECTIONS - 1 + NO - 1)

        def small_out(k):
            peer = (o + k) % NO
            return remote(
                R.small_in, R.small_a.at[o], R.sma_send.at[k], R.sma_recv.at[o], s, peer
            )

        loop(NO, lambda k: small_out(k).start(), 1)
        R.small_a[o] = R.small_in[...]

        def piece(kind, layer, outer):
            rows = piece_rows[kind]
            buf = (R.wqkv, R.wout_raw, R.wup, R.wdown)[kind]
            return buf.at[layer, aligned(outer * rows, rows)]

        def shard(kind, half):
            if kind == 0:
                return R.qkv_in
            if kind == 1:
                return R.out_in
            return (R.up_in if kind == 2 else R.down_in).at[half]

        def y_copy(kind):
            return remote(
                shard(kind, 1 - y),
                piece(kind, y, o),
                R.y_send.at[kind],
                R.y_recv.at[kind],
                other_y,
                o,
            )

        def own_copy(kind):
            return pltpu.make_async_copy(shard(kind, y), piece(kind, y, o), R.own_sem.at[kind])

        stream_copy = pltpu.make_async_copy(R.stream_in.at[y], R.seq_rows, R.load_sem.at[0])
        stream_copy.start()
        load_copies = []
        for m in range(2):
            mine = pl.ds(m * Q, Q)
            load_copies.append(
                pltpu.make_async_copy(
                    R.stream_in.at[m, aligned(s * Q, Q)], R.hid_rows.at[0, mine], R.load_sem.at[1 + m]
                )
            )
            load_copies.append(
                pltpu.make_async_copy(
                    R.cot_in.at[m, aligned(s * Q, Q)], R.grad_rows.at[mine], R.load_sem.at[3 + m]
                )
            )
            load_copies.append(
                pltpu.make_async_copy(
                    R.cot_in.at[m], R.grad_ff.at[0, pl.ds(m * L, L)], R.load_sem.at[5 + m]
                )
            )
        for kind in range(4):
            own_copy(kind).start()
            y_copy(kind).start()
        for copy in load_copies:
            copy.start()

        def acquire(layer, kind):
            @pl.when(y == layer)
            def _():
                own_copy(kind).wait()

            @pl.when(y != layer)
            def _():
                remote(
                    shard(kind, 0),
                    piece(kind, layer, o),
                    R.y_send.at[kind],
                    R.y_recv.at[kind],
                    other_y,
                    o,
                ).wait_recv()

        def z_copy(layer, kind, q):
            item = layer * 4 + kind
            part = piece(kind, layer, o)
            return remote(
                part, part, R.z_send.at[item, q], R.z_recv.at[item, zz], s, 2 * q + c
            )

        def z_arrival(layer, kind, q):
            item = layer * 4 + kind
            part = piece(kind, layer, 2 * q + c)
            return remote(part, part, R.z_send.at[item, q], R.z_recv.at[item, q], s, 2 * q + c)

        def mate_copy(layer, kind, q):
            item = layer * 4 + kind
            part = piece(kind, layer, 2 * q + c)
            return remote(part, part, R.p_send.at[item, q], R.p_recv.at[item, q], s, mate)

        def mate_arrival(layer, kind, q):
            item = layer * 4 + kind
            part = piece(kind, layer, 2 * q + 1 - c)
            return remote(part, part, R.p_send.at[item, q], R.p_recv.at[item, q], s, mate)

        def spread(layer, group):
            for kind in group:
                acquire(layer, kind)
                loop(n, lambda k, kind=kind: z_copy(layer, kind, (zz + k) % n).start(), 1)
                mate_copy(layer, kind, zz).start()

        def collect(layer, group):
            for kind in group:

                def onward(k, kind=kind):
                    q = (zz + k) % n
                    z_arrival(layer, kind, q).wait_recv()
                    mate_copy(layer, kind, q).start()

                loop(n, onward, 1)
            for kind in group:
                loop(n, lambda q, kind=kind: mate_arrival(layer, kind, q).wait_recv())

        ATT, FEED = (0, 1), (2, 3)
        spread(0, ATT)

        loop(
            NO,
            lambda k: remote(
                R.small_in,
                R.small_a.at[(o + k) % NO],
                R.sma_send.at[k],
                R.sma_recv.at[(o + k) % NO],
                s,
                (o + k) % NO,
            ).wait_recv(),
            1,
        )
        wide = R.small_b.shape[-1]
        row_index = lax.broadcasted_iota(jnp.int32, (16, wide), 0)
        lane = lax.broadcasted_iota(jnp.int32, (16, wide), 1)
        table = jnp.zeros((16, wide), F32)
        for k in range(NO):
            part = R.small_a[k].astype(F32)
            part = jnp.concatenate([part, jnp.zeros((16, wide - part.shape[1]), F32)], axis=1)
            narrow = pltpu.roll(part, ru * k, 1) if k else part
            broad = pltpu.roll(part, rd * k, 1) if k else part
            table = table + jnp.where(row_index < 4, narrow, broad)
        low = heads // 8 * 8 * HEAD_DIM
        rest = F - low
        moved = jnp.where(lane < low, table, 0.0)
        moved += pltpu.roll(jnp.where((lane >= low) & (lane < F), table, 0.0), 2 * low, 1)
        moved += pltpu.roll(
            jnp.where((lane >= F) & (lane < F + low), table, 0.0), 2 * low - F, 1
        )
        moved += pltpu.roll(
            jnp.where((lane >= F + low) & (lane < 2 * F), table, 0.0), 2 * low + 2 * rest - F, 1
        )
        table = jnp.where(row_index == 3, moved, table)
        R.small_own[...] = table[:8]
        R.small_b[s] = table[:8]

        def small_b_copy(k, of):
            return remote(
                R.small_own,
                R.small_b.at[of],
                R.smb_send.at[k],
                R.smb_recv.at[of],
                (s + k) % SECTIONS,
                o,
            )

        loop(SECTIONS, lambda k: small_b_copy(k, s).start(), 1)
        loop(SECTIONS, lambda k: small_b_copy(k, (s + k) % SECTIONS).wait_recv(), 1)

        R.small_grad[...] = jnp.zeros_like(R.small_grad)
        row8 = lax.broadcasted_iota(jnp.int32, (8, wide), 0)
        lane8 = lax.broadcasted_iota(jnp.int32, (8, wide), 1)

        def widened(row):
            if row.shape[1] == wide:
                return row
            return jnp.concatenate([row, jnp.zeros((1, wide - row.shape[1]), F32)], axis=1)

        def note_rows(block, index, row):
            R.small_grad[block] += jnp.where(row8 == index, widened(row), 0.0)

        stream_copy.wait()
        gain0 = R.small_b[0, 0:1, :D]
        shift0 = R.small_b[0, 1:2, :D]

        def first_norm(k):
            rows = aligned(k * Q, Q)
            _, _, out = normed_rows(R.seq_rows[rows, :].astype(F32), gain0, shift0)
            R.norm_at[0, rows, :] = out.astype(BF16)

        loop(L // Q, first_norm)
        for copy in load_copies:
            copy.wait()

        def rows_copy(phase, m, src, dst, slot, to):
            return remote(
                src, dst, R.ag_send.at[phase, m, slot], R.ag_recv.at[phase, m, s], to, o
            )

        def share_all(phase, m, buf):
            part = buf.at[aligned(m * L + s * Q, Q)]
            return lambda k: rows_copy(phase, m, part, part, k, (s + k) % SECTIONS)

        def share_pair(phase, m, buf):
            part = buf.at[aligned(s * Q, Q)]
            stage = R.stage.at[m]
            return lambda t: rows_copy(phase, m, stage, part, t, 2 * m + t)

        def arrival(phase, m, buf, base, k):
            src = (s + k) % SECTIONS
            part = buf.at[aligned(base + src * Q, Q)]
            return remote(
                part, part, R.ag_send.at[phase, m, k], R.ag_recv.at[phase, m, src], src, o
            )

        def send_rows(phase, attention, m, buf, value):
            if attention:
                R.stage[m] = value
                copies = share_pair(phase, m, buf)

                @pl.when(y == m)
                def _():
                    buf[aligned(s * Q, Q), :] = value
                    copies(1 - x).start()

                @pl.when(y != m)
                def _():
                    copies(0).start()
                    copies(1).start()
            else:
                buf[aligned(m * L + s * Q, Q), :] = value
                copies = share_all(phase, m, buf)
                loop(SECTIONS, lambda k: copies(k).start(), 1)

        def finish_send_rows(phase, attention, m, buf):
            if attention:
                copies = share_pair(phase, m, buf)

                @pl.when(y == m)
                def _():
                    copies(1 - x).wait_send()

                @pl.when(y != m)
                def _():
                    copies(0).wait_send()
                    copies(1).wait_send()
            else:
                copies = share_all(phase, m, buf)
                loop(SECTIONS, lambda k: copies(k).wait_send(), 1)

        def await_rows(phase, attention, m, buf):
            if attention:

                @pl.when(y == 0)
                def _():
                    loop(SECTIONS, lambda k: arrival(phase, 0, buf, 0, k).wait_recv(), 1)

                @pl.when(y == 1)
                def _():
                    loop(SECTIONS, lambda k: arrival(phase, 1, buf, 0, k).wait_recv(), 1)
            else:
                loop(SECTIONS, lambda k: arrival(phase, m, buf, m * L, k).wait_recv(), 1)

        def sum_slot(phase):
            return 0 if phase < 4 else 1

        def part_copy(phase, m, base, k):
            to = (s + k) % SECTIONS
            return remote(
                R.parts.at[aligned(base + to * Q, Q)],
                R.sums.at[sum_slot(phase), s, m],
                R.rs_send.at[phase, m, k],
                R.rs_recv.at[phase, m, s],
                to,
                o,
            )

        def send_parts(phase, attention, m):
            slot = sum_slot(phase)
            if attention:
                for mm_ in range(2):

                    @pl.when(y == mm_)
                    def _(mm_=mm_):
                        loop(SECTIONS, lambda k: part_copy(phase, mm_, 0, k).start(), 1)
                        R.sums[slot, s, mm_] = R.parts[aligned(s * Q, Q), :]
            else:
                loop(SECTIONS, lambda k: part_copy(phase, m, m * L, k).start(), 1)
                R.sums[slot, s, m] = R.parts[aligned(m * L + s * Q, Q), :]

        def finish_send_parts(phase, attention):
            for m in range(2):
                if attention:

                    @pl.when(y == m)
                    def _(m=m):
                        loop(SECTIONS, lambda k: part_copy(phase, m, 0, k).wait_send(), 1)
                else:
                    loop(SECTIONS, lambda k: part_copy(phase, m, m * L, k).wait_send(), 1)

        def part_arrival(phase, m, src):
            return remote(
                R.parts.at[pl.ds(0, Q)],
                R.sums.at[sum_slot(phase), src, m],
                R.rs_send.at[phase, m, 0],
                R.rs_recv.at[phase, m, src],
                src,
                o,
            )

        def await_parts(phase, attention, m):
            slot = sum_slot(phase)
            if attention:

                @pl.when(y == m)
                def _():
                    part_arrival(phase, m, other_x).wait_recv()

                @pl.when(y != m)
                def _():
                    part_arrival(phase, m, 2 * m).wait_recv()
                    part_arrival(phase, m, 2 * m + 1).wait_recv()

                sources = (2 * m, 2 * m + 1)
            else:
                loop(
                    SECTIONS,
                    lambda k: part_arrival(phase, m, (s + k) % SECTIONS).wait_recv(),
                    1,
                )
                sources = range(SECTIONS)
            total = None
            for src in sources:
                part = R.sums[slot, src, m].astype(F32)
                total = part if total is None else total + part
            return total

        def close_forward(phase, m):
            e = phase
            attention = e % 2 == 0
            branch = await_parts(phase, attention, m) + R.small_b[e, 2:3, :D]
            mine = pl.ds(m * Q, Q)
            h = R.hid_rows[e, mine, :].astype(F32)
            position = s * Q + lax.broadcasted_iota(jnp.int32, (Q, 1), 0)
            valid = (position < R.lens[m]).astype(F32)
            square_h = jnp.sum(jnp.sum(h * h * valid, axis=1, keepdims=True), axis=0, keepdims=True)
            square_b = jnp.sum(
                jnp.sum(branch * branch * valid, axis=1, keepdims=True), axis=0, keepdims=True
            )
            R.small_grad[e] += jnp.where((row8 == 6) & (lane8 == 2 * m), square_h, 0.0)
            R.small_grad[e] += jnp.where((row8 == 6) & (lane8 == 2 * m + 1), square_b, 0.0)
            fresh = (h + branch).astype(BF16)
            if e == 3:
                R.out_stream[mine, :] = fresh
                return
            R.hid_rows[e + 1, mine, :] = fresh
            _, _, out = normed_rows(
                fresh.astype(F32), R.small_b[e + 1, 0:1, :D], R.small_b[e + 1, 1:2, :D]
            )
            to_attention = (e + 1) % 2 == 0
            buf = (R.norm_at if to_attention else R.norm_ff).at[(e + 1) // 2]
            send_rows(phase + 1, to_attention, m, buf, out.astype(BF16))

        def close_backward(phase, m):
            e = 7 - phase
            attention = e % 2 == 0
            d_norm = await_parts(phase, attention, m)
            mine = pl.ds(m * Q, Q)
            unit, inverse, _ = normed_rows(R.hid_rows[e, mine, :].astype(F32), 1.0, 0.0)
            flow = R.grad_rows[mine, :].astype(F32)
            note_rows(e, 0, jnp.sum(d_norm * unit, axis=0, keepdims=True))
            note_rows(e, 1, jnp.sum(d_norm, axis=0, keepdims=True))
            note_rows(e, 2, jnp.sum(flow, axis=0, keepdims=True))
            a = d_norm * R.small_b[e, 0:1, :D]
            mean_a = jnp.mean(a, axis=-1, keepdims=True)
            mean_ax = jnp.mean(a * unit, axis=-1, keepdims=True)
            fresh = (flow + (a - mean_a - unit * mean_ax) * inverse).astype(BF16)
            if e == 0:
                R.out_grad_rows[mine, :] = fresh
                return
            R.grad_rows[mine, :] = fresh
            to_attention = (e - 1) % 2 == 0
            buf = R.grad_at if to_attention else R.grad_ff.at[1]
            send_rows(phase + 1, to_attention, m, buf, fresh)

        def out_weights(layer):
            for k in range(NO):
                block = R.wout_raw[layer, pl.ds(k * rop, rop), :].astype(F32)
                R.wide_rows[pl.ds(k * ro, ro), :] = block[:ro]
            R.wout[layer] = R.wide_rows[pl.ds(0, F), :].astype(BF16)

        length_here = R.lens[y]

        def attention_forward(layer):
            bias = R.small_b[2 * layer + x, 3:4, :W]
            xs = R.norm_at.at[layer]
            for t in range(0, W, 256):
                cols = pl.ds(t, 256)
                lin = mm(xs[...], R.wqkv[layer, :, cols]) + bias[:, t : t + 256]
                R.lin_t[layer, cols, :] = lin.T.astype(BF16)

            def head(h):
                q0, k0, v0 = head_rows(h, heads)
                score = mm(
                    R.lin_t[layer, pl.ds(k0, HEAD_DIM), :],
                    R.lin_t[layer, pl.ds(q0, HEAD_DIM), :],
                    TN,
                )
                live = lax.broadcasted_iota(jnp.int32, score.shape, 0) < length_here
                score = jnp.where(live, score * SCALE, MASKED)
                top = jnp.max(score, axis=0, keepdims=True)
                powers = jnp.exp(score - top)
                total = jnp.sum(powers, axis=0, keepdims=True)
                probs = (powers * (1.0 / total)).astype(BF16)
                R.log_total[layer, h] = top + jnp.log(total)
                mixed = mm(R.lin_t[layer, pl.ds(v0, HEAD_DIM), :], probs)
                R.att_t[layer, aligned(h * HEAD_DIM, HEAD_DIM), :] = mixed.astype(BF16)

            loop(heads, head)
            out_weights(layer)
            R.parts[pl.ds(0, L), :] = mm(R.att_t[layer], R.wout[layer], TN).astype(BF16)

        def attention_backward(layer):
            xs, g = R.norm_at.at[layer], R.grad_at
            R.wide_rows[pl.ds(0, F), :] = mm(R.att_t[layer], g[...])
            for k in range(NO):
                block = R.wide_rows[pl.ds(k * ro, rop), :].astype(BF16)
                R.sb_out[k % 2, pl.ds(k // 2 * rop, rop), :] = block
            R.d_att_t[...] = mm(R.wout[layer], g[...], NT).astype(BF16)

            def head(h):
                q0, k0, v0 = head_rows(h, heads)
                q_t = R.lin_t[layer, pl.ds(q0, HEAD_DIM), :]
                k_t = R.lin_t[layer, pl.ds(k0, HEAD_DIM), :]
                v_t = R.lin_t[layer, pl.ds(v0, HEAD_DIM), :]
                d_a = R.d_att_t[aligned(h * HEAD_DIM, HEAD_DIM), :]
                score = mm(k_t, q_t, TN)
                live = lax.broadcasted_iota(jnp.int32, score.shape, 0) < length_here
                probs = jnp.where(live, jnp.exp(score * SCALE - R.log_total[layer, h]), 0.0)
                d_probs = mm(v_t, d_a, TN)
                product = probs * d_probs
                inner_sum = jnp.sum(product, axis=0, keepdims=True)
                d_score = ((product - probs * inner_sum) * SCALE).astype(BF16)
                R.d_lin_t[pl.ds(q0, HEAD_DIM), :] = mm(k_t, d_score).astype(BF16)
                R.d_lin_t[pl.ds(k0, HEAD_DIM), :] = mm(q_t, d_score, NT).astype(BF16)
                R.d_lin_t[pl.ds(v0, HEAD_DIM), :] = mm(d_a, probs.astype(BF16), NT).astype(BF16)

            loop(heads, head)
            sums = []
            for t in range(0, W, 256):
                cols = pl.ds(t, 256)
                d_lin = R.d_lin_t[cols, :].T
                sums.append(jnp.sum(d_lin.astype(F32), axis=0, keepdims=True))
                d_w = mm(xs[...], d_lin, TN).astype(BF16)
                for k in range(NO):
                    R.sb_qkv[k % 2, pl.ds(k // 2 * ru, ru), cols] = d_w[k * ru : (k + 1) * ru]
                part = mm(d_lin, R.wqkv[layer, :, cols], NT)
                if t == 0:
                    R.acc[...] = part
                else:
                    R.acc[...] += part
            R.parts[pl.ds(0, L), :] = R.acc[...].astype(BF16)
            note_rows(2 * layer + x, 3, jnp.concatenate(sums, axis=1))

        def feed_bias(layer):
            block = R.small_b[2 * layer + x]
            return jnp.where(y == 0, block[4:5], block[5:6])[:, :U]

        def feed_forward(layer, m):
            bias = feed_bias(layer)

            def rows_step(r):
                rows = aligned(m * L + r * Q, Q)
                pre = mm(R.norm_ff[layer, rows, :], R.wup[layer]) + bias
                cdf = 0.5 + 0.5 * lax.erf(pre * 0.7071067811865476)
                density = jnp.exp(pre * pre * -0.5) * 0.3989422804014327
                hidden = (pre * cdf).astype(BF16)
                R.hidden[layer, rows, :] = hidden
                R.slope[layer, rows, :] = (cdf + pre * density).astype(BF16)
                R.parts[rows, :] = mm(hidden, R.wdown[layer]).astype(BF16)

            loop(SECTIONS, rows_step)

        def feed_backward(layer, m):
            rows = pl.ds(m * L, L)
            xs = R.norm_ff.at[layer, rows]
            g = R.grad_ff.at[0 if layer == 1 else 1, rows]
            tile = U // 2
            owners = tile // rd
            for j in range(2):
                cols = pl.ds(j * tile, tile)
                d_hidden = mm(g[...], R.wdown[layer, cols, :], NT)
                d_pre = (d_hidden * R.slope[layer, rows, cols].astype(F32)).astype(BF16)
                d_down = mm(R.hidden[layer, rows, cols], g[...], TN)
                d_up = mm(xs[...], d_pre, TN)
                for k in range(owners):
                    owner = j * owners + k
                    place = (owner % 2, pl.ds(owner // 2 * rd, rd), slice(None))
                    block = d_down[k * rd : (k + 1) * rd]
                    if m:
                        block = block + R.sb_down[place].astype(F32)
                    R.sb_down[place] = block.astype(BF16)
                for k in range(NO):
                    place = (k % 2, pl.ds(k // 2 * ru, ru), cols)
                    block = d_up[k * ru : (k + 1) * ru]
                    if m:
                        block = block + R.sb_up[place].astype(F32)
                    R.sb_up[place] = block.astype(BF16)
                total = jnp.sum(d_pre.astype(F32), axis=0, keepdims=True)
                blank = jnp.zeros((1, tile), F32)
                row = jnp.concatenate([total, blank] if j == 0 else [blank, total], axis=1)
                note_rows(2 * layer + x, 4 + y, row)
                part = mm(d_pre, R.wup[layer, :, cols], NT)
                if j == 0:
                    R.acc[...] = part
                else:
                    R.parts[rows, :] = (R.acc[...] + part).astype(BF16)

        FEED_GRADS = (
            (0, R.sb_up, R.rb_up, R.mb_up, R.zb_up, R.yb_up, R.yr_up, ru),
            (1, R.sb_down, R.rb_down, R.mb_down, R.zb_down, R.yb_down, R.yr_down, rd),
        )
        ATT_GRADS = (
            (0, R.sb_qkv, R.rb_qkv, R.mb_qkv, R.zb_qkv, R.yb_qkv, R.yr_qkv, ru),
            (1, R.sb_out, R.rb_out, R.mb_out, R.zb_out, R.yb_out, R.yr_out, rop),
        )

        def mate_grads(stage, kind):
            return [
                remote(sb.at[1 - c], rb, R.r1_send.at[stage, a], R.r1_recv.at[stage, a], s, mate)
                for a, sb, rb, *_ in kind
            ]

        def z_grads(stage, kind, k):
            q = (zz + k) % n
            return [
                remote(
                    mb.at[aligned(q * rows, rows)],
                    zb.at[zz],
                    R.r2_send.at[stage, a, q],
                    R.r2_recv.at[stage, a, zz],
                    s,
                    2 * q + c,
                )
                for a, sb, rb, mb, zb, yb, yr, rows in kind
            ]

        def grads_to_mate(stage, kind):
            for copy in mate_grads(stage, kind):
                copy.start()

        def grads_along_z(stage, kind):
            for copy in mate_grads(stage, kind):
                copy.wait()
            if stage >= 2:
                loop(n, lambda k: [copy.wait_send() for copy in z_grads(stage - 2, kind, k)], 1)
            for a, sb, rb, mb, zb, yb, yr, rows in kind:

                def add(q, sb=sb, rb=rb, mb=mb, rows=rows):
                    part = aligned(q * rows, rows)
                    both = sb[c, part, :].astype(F32) + rb[part, :].astype(F32)
                    mb[part, :] = both.astype(BF16)

                loop(n, add)
            loop(n, lambda k: [copy.start() for copy in z_grads(stage, kind, k)], 1)

        def y_grad(a, yb, yr):
            return remote(yb, yr, R.r4_send.at[a], R.r4_recv.at[a], other_y, o)

        def grads_owned(stage, kind):
            layer = 1 - stage // 2
            for a, sb, rb, mb, zb, yb, yr, rows in kind:

                def landed(k, a=a, zb=zb, mb=mb, rows=rows):
                    q = (zz + k) % n
                    remote(
                        mb.at[pl.ds(0, rows)],
                        zb.at[q],
                        R.r2_send.at[stage, a, q],
                        R.r2_recv.at[stage, a, q],
                        s,
                        2 * q + c,
                    ).wait_recv()

                loop(n, landed, 1)
                total = mb[aligned(zz * rows, rows), :].astype(F32)
                for k in range(1, n):
                    total = total + zb[(zz + k) % n].astype(F32)
                place = a + (0 if kind is FEED_GRADS else 2)

                @pl.when(y == layer)
                def _(a=a, total=total):
                    if kind is FEED_GRADS:
                        (R.o_up if a == 0 else R.o_down)[y] = total
                    else:
                        (R.o_qkv if a == 0 else R.o_out)[...] = total

                @pl.when(y != layer)
                def _(yb=yb, yr=yr, total=total, place=place):
                    yb[...] = total.astype(BF16)
                    y_grad(place, yb, yr).start()

        def grads_home(kind):
            for a, sb, rb, mb, zb, yb, yr, rows in kind:
                place = a + (0 if kind is FEED_GRADS else 2)
                y_grad(place, yb, yr).wait()
                if kind is FEED_GRADS:
                    (R.o_up if a == 0 else R.o_down)[1 - y] = yr[...].astype(F32)
                else:
                    (R.o_qkv if a == 0 else R.o_out)[...] += yr[...].astype(F32)

        collect(0, ATT)
        spread(0, FEED)
        attention_forward(0)
        send_parts(0, True, None)
        spread(1, ATT)
        for m in range(2):
            close_forward(0, m)
        collect(0, FEED)
        spread(1, FEED)
        finish_send_parts(0, True)
        for m in range(2):
            await_rows(1, False, m, R.norm_ff.at[0])
            feed_forward(0, m)
            send_parts(1, False, m)
        for m in range(2):
            close_forward(1, m)
        collect(1, ATT)
        finish_send_parts(1, False)
        await_rows(2, True, None, R.norm_at.at[1])
        attention_forward(1)
        send_parts(2, True, None)
        for m in range(2):
            finish_send_rows(2, True, m, R.norm_at.at[1])
        for m in range(2):
            close_forward(2, m)
        collect(1, FEED)
        finish_send_parts(2, True)
        for m in range(2):
            await_rows(3, False, m, R.norm_ff.at[1])
            feed_forward(1, m)
            send_parts(3, False, m)
        finish_send_parts(3, False)

        for m in range(2):
            feed_backward(1, m)
            send_parts(4, False, m)
        grads_to_mate(0, FEED_GRADS)
        for m in range(2):
            close_forward(3, m)
        for m in range(2):
            close_backward(4, m)
        grads_along_z(0, FEED_GRADS)
        finish_send_parts(4, False)
        await_rows(5, True, None, R.grad_at)
        attention_backward(1)
        send_parts(5, True, None)
        grads_to_mate(1, ATT_GRADS)
        for m in range(2):
            finish_send_rows(5, True, m, R.grad_at)
        for m in range(2):
            close_backward(5, m)
        finish_send_parts(5, True)
        await_rows(6, False, 0, R.grad_ff.at[1])
        feed_backward(0, 0)
        send_parts(6, False, 0)
        grads_owned(0, FEED_GRADS)
        grads_along_z(1, ATT_GRADS)
        await_rows(6, False, 1, R.grad_ff.at[1])
        feed_backward(0, 1)
        send_parts(6, False, 1)
        grads_to_mate(2, FEED_GRADS)
        for m in range(2):
            close_backward(6, m)
        grads_owned(1, ATT_GRADS)
        grads_along_z(2, FEED_GRADS)
        finish_send_parts(6, False)
        await_rows(7, True, None, R.grad_at)
        attention_backward(0)
        send_parts(7, True, None)
        grads_to_mate(3, ATT_GRADS)
        for m in range(2):
            finish_send_rows(7, True, m, R.grad_at)
        for m in range(2):
            close_backward(7, m)

        def small_grad_copy(k, of):
            to = (s + k) % SECTIONS
            return remote(
                R.small_grad.at[to],
                R.small_sum.at[of],
                R.sga_send.at[k],
                R.sga_recv.at[of],
                to,
                o,
            )

        loop(SECTIONS, lambda k: small_grad_copy(k, s).start(), 1)
        R.small_sum[s] = R.small_grad[s]
        grads_owned(2, FEED_GRADS)
        grads_along_z(3, ATT_GRADS)
        loop(SECTIONS, lambda k: small_grad_copy(k, (s + k) % SECTIONS).wait_recv(), 1)
        total = R.small_sum[0]
        for k in range(1, SECTIONS):
            total = total + R.small_sum[k]
        R.small_line[...] = total
        R.o_stat[...] = total[:, :128]

        def small_line_copy(k, of):
            peer = (o + k) % NO
            return remote(
                R.small_line, R.small_all.at[of], R.sgb_send.at[k], R.sgb_recv.at[of], s, peer
            )

        loop(NO, lambda k: small_line_copy(k, o).start(), 1)
        R.small_all[o] = total
        grads_owned(3, ATT_GRADS)
        loop(NO, lambda k: small_line_copy(k, (o + k) % NO).wait_recv(), 1)
        total = R.small_all[0]
        for k in range(1, NO):
            total = total + R.small_all[k]
        R.o_small[...] = total
        grads_home(FEED_GRADS)
        grads_home(ATT_GRADS)

        loop(NO, lambda k: small_out(k).wait_send(), 1)
        loop(SECTIONS, lambda k: small_b_copy(k, s).wait_send(), 1)
        loop(SECTIONS, lambda k: small_grad_copy(k, s).wait_send(), 1)
        loop(NO, lambda k: small_line_copy(k, o).wait_send(), 1)
        for kind in range(4):
            y_copy(kind).wait_send()
        for layer in range(2):
            for kind in range(4):
                loop(
                    n,
                    lambda k, kind=kind, layer=layer: z_copy(
                        layer, kind, (zz + k) % n
                    ).wait_send(),
                    1,
                )
                loop(n, lambda q, kind=kind, layer=layer: mate_copy(layer, kind, q).wait_send())
        for m in range(2):
            finish_send_rows(1, False, m, R.norm_ff.at[0])
            finish_send_rows(3, False, m, R.norm_ff.at[1])
            finish_send_rows(6, False, m, R.grad_ff.at[1])
        finish_send_parts(7, True)
        for stage, kind in ((2, FEED_GRADS), (3, ATT_GRADS)):
            loop(
                n,
                lambda k, stage=stage, kind=kind: [
                    copy.wait_send() for copy in z_grads(stage, kind, k)
                ],
                1,
            )

    return kernel


def one_step(cfg, lens, small, qkv, out, up, down, stream, cotangent):
    D, L, U, F, W = cfg.width, cfg.length, cfg.units, cfg.features, cfg.packed
    Q = L // SECTIONS
    NO, n = cfg.outer, cfg.outer // 2
    ru, rd, rop = cfg.up_rows, cfg.down_rows, cfg.out_padded
    wide = max(U, W)
    dma = pltpu.SemaphoreType.DMA
    inputs = dict(
        lens=lens,
        small_in=small,
        qkv_in=qkv,
        out_in=out,
        up_in=up,
        down_in=down,
        stream_in=stream,
        cot_in=cotangent,
    )
    outputs = dict(
        out_stream=((2 * Q, D), BF16),
        out_grad_rows=((2 * Q, D), BF16),
        o_qkv=((ru, W), F32),
        o_out=((rop, D), F32),
        o_up=((2, ru, U), F32),
        o_down=((2, rd, D), F32),
        o_small=((8, wide), F32),
        o_stat=((8, 128), F32),
    )
    scratch = dict(
        small_a=((NO, 16, small.shape[1]), BF16),
        small_own=((8, wide), F32),
        small_b=((SECTIONS, 8, wide), F32),
        small_grad=((SECTIONS, 8, wide), F32),
        small_sum=((SECTIONS, 8, wide), F32),
        small_line=((8, wide), F32),
        small_all=((NO, 8, wide), F32),
        wqkv=((2, D, W), BF16),
        wout_raw=((2, NO * rop, D), BF16),
        wout=((2, F, D), BF16),
        wup=((2, D, U), BF16),
        wdown=((2, U, D), BF16),
        seq_rows=((L, D), BF16),
        hid_rows=((SECTIONS, 2 * Q, D), BF16),
        grad_rows=((2 * Q, D), BF16),
        norm_at=((2, L, D), BF16),
        norm_ff=((2, 2 * L, D), BF16),
        stage=((2, Q, D), BF16),
        lin_t=((2, W, L), BF16),
        att_t=((2, F, L), BF16),
        log_total=((2, cfg.heads, 1, L), F32),
        hidden=((2, 2 * L, U), BF16),
        slope=((2, 2 * L, U), BF16),
        grad_ff=((2, 2 * L, D), BF16),
        grad_at=((L, D), BF16),
        parts=((2 * L, D), BF16),
        sums=((2, SECTIONS, 2, Q, D), BF16),
        acc=((L, D), F32),
        wide_rows=((F + 64, D), F32),
        d_att_t=((F, L), BF16),
        d_lin_t=((W, L), BF16),
        sb_up=((2, n * ru, U), BF16),
        rb_up=((n * ru, U), BF16),
        mb_up=((n * ru, U), BF16),
        zb_up=((n, ru, U), BF16),
        yb_up=((ru, U), BF16),
        yr_up=((ru, U), BF16),
        sb_down=((2, n * rd, D), BF16),
        rb_down=((n * rd, D), BF16),
        mb_down=((n * rd, D), BF16),
        zb_down=((n, rd, D), BF16),
        yb_down=((rd, D), BF16),
        yr_down=((rd, D), BF16),
        sb_qkv=((2, n * ru, W), BF16),
        rb_qkv=((n * ru, W), BF16),
        mb_qkv=((n * ru, W), BF16),
        zb_qkv=((n, ru, W), BF16),
        yb_qkv=((ru, W), BF16),
        yr_qkv=((ru, W), BF16),
        sb_out=((2, n * rop, D), BF16),
        rb_out=((n * rop, D), BF16),
        mb_out=((n * rop, D), BF16),
        zb_out=((n, rop, D), BF16),
        yb_out=((rop, D), BF16),
        yr_out=((rop, D), BF16),
    )
    semaphores = dict(
        load_sem=(7,),
        own_sem=(4,),
        sma_send=(NO,),
        sma_recv=(NO,),
        smb_send=(SECTIONS,),
        smb_recv=(SECTIONS,),
        y_send=(4,),
        y_recv=(4,),
        z_send=(8, n),
        z_recv=(8, n),
        p_send=(8, n),
        p_recv=(8, n),
        ag_send=(8, 2, SECTIONS),
        ag_recv=(8, 2, SECTIONS),
        rs_send=(8, 2, SECTIONS),
        rs_recv=(8, 2, SECTIONS),
        r1_send=(4, 2),
        r1_recv=(4, 2),
        r2_send=(4, 2, n),
        r2_recv=(4, 2, n),
        r4_send=(4,),
        r4_recv=(4,),
        sga_send=(SECTIONS,),
        sga_recv=(SECTIONS,),
        sgb_send=(NO,),
        sgb_recv=(NO,),
    )
    names = [*inputs, *outputs, *scratch, *semaphores]
    vmem = pl.BlockSpec(memory_space=pltpu.VMEM)
    hbm = pl.BlockSpec(memory_space=pl.ANY)
    return pl.pallas_call(
        make_kernel(cfg, names),
        out_shape=[jax.ShapeDtypeStruct(*spec) for spec in outputs.values()],
        in_specs=[pl.BlockSpec(memory_space=pltpu.SMEM), vmem, hbm, hbm, hbm, hbm, hbm, hbm],
        out_specs=[vmem] * len(outputs),
        scratch_shapes=[pltpu.VMEM(*spec) for spec in scratch.values()]
        + [dma(shape) for shape in semaphores.values()],
        compiler_params=pltpu.CompilerParams(
            collective_id=0, has_side_effects=True, vmem_limit_bytes=62 * 2**20
        ),
        name="layers",
    )(*inputs.values())


def shards(
    layer_input,
    out_cotangent,
    lengths,
    qkv_weight,
    qv_bias,
    out_weight,
    up_weight,
    up_bias,
    down_weight,
    norm_vectors,
):
    section_count = lax.axis_size("section")
    dp_count = lax.axis_size("dp")
    section = lax.axis_index("section")
    dp = lax.axis_index("dp")
    L, D = layer_input.shape[2:]
    sequences = layer_input.shape[0] * layer_input.shape[1]
    assert section_count == SECTIONS and sequences == 2
    F = out_weight.shape[1] * dp_count
    U2 = up_weight.shape[2]
    heads = F // HEAD_DIM
    outer = max(
        k
        for k in range(2, dp_count + 1, 2)
        if dp_count % k == 0 and D % (16 * k) == 0 and U2 % (32 * k) == 0 and F % (8 * k) == 0
    )
    inner = dp_count // outer
    groups = [[g * inner + k for k in range(inner)] for g in range(outer)]

    def joined(block, axis=0):
        if inner == 1:
            return block
        return lax.all_gather(block, "dp", axis=axis, tiled=True, axis_index_groups=groups)

    def own_share(block, axis=0):
        if inner == 1:
            return block
        return lax.psum_scatter(
            block, "dp", scatter_dimension=axis, tiled=True, axis_index_groups=groups
        )

    cfg = types.SimpleNamespace(
        width=D,
        length=L,
        units=U2 // 2,
        features=F,
        packed=-(-3 * F // 256) * 256,
        outer=outer,
        inner=inner,
        heads=heads,
        up_rows=D // outer,
        down_rows=U2 // outer // 2,
        out_rows=F // outer,
        out_padded=-(-(F // outer) // 16) * 16,
    )
    ru, rd = cfg.up_rows, cfg.down_rows

    qkv = joined(to_packed(qkv_weight[0].astype(BF16), heads, cfg.packed))
    out = joined(out_weight[0].astype(BF16))
    out = jnp.pad(out, ((0, cfg.out_padded - cfg.out_rows), (0, 0)))
    up = joined(up_weight[0].astype(BF16))
    up = up.reshape(ru, outer, 2, rd).transpose(2, 0, 1, 3).reshape(2, ru, outer * rd)
    down = joined(down_weight[0].astype(BF16)).reshape(2, rd, D)
    norm = joined(norm_vectors[0].astype(BF16), 1)
    projection_bias = joined(qv_bias[0].astype(BF16))
    hidden_bias = joined(up_bias[0].astype(BF16)).reshape(2, rd)
    lanes = -(-rd // 128) * 128
    small = jnp.concatenate(
        [
            jnp.pad(norm, ((0, 0), (0, lanes - norm.shape[1]))),
            jnp.pad(projection_bias[None], ((0, 0), (0, lanes - projection_bias.shape[0]))),
            jnp.pad(hidden_bias, ((0, 10), (0, lanes - rd))),
        ]
    )
    stream = layer_input.reshape(2, L, D)
    cotangent = out_cotangent.reshape(2, L, D)
    out_stream, grad_rows, g_qkv, g_out, g_up, g_down, g_small, stat = one_step(
        cfg, lengths.reshape(2), small, qkv, out, up, down, stream, cotangent
    )
    rows_shape = layer_input.shape[:2] + (L // SECTIONS, D)
    g_qkv = own_share(from_packed(g_qkv, F, heads))
    g_out = own_share(g_out[: cfg.out_rows])
    g_up = g_up.reshape(2, ru, outer, rd).transpose(1, 2, 0, 3).reshape(ru, U2)
    g_up = own_share(g_up)
    g_down = own_share(g_down.reshape(2 * rd, D))
    if inner > 1:
        g_small = lax.psum(g_small, "dp", axis_index_groups=groups)
    d_rows, b_rows, u_rows = D // dp_count, 2 * F // dp_count, U2 // dp_count
    g_norm = lax.dynamic_slice(g_small[:3, :D], (0, dp * d_rows), (3, d_rows))
    packed_bias = from_packed(g_small[3, : cfg.packed], F, heads)
    packed_bias = jnp.concatenate([packed_bias[:F], packed_bias[2 * F :]])
    g_bias = lax.dynamic_slice(packed_bias, (dp * b_rows,), (b_rows,))
    g_hidden = g_small[4:6, : cfg.units].reshape(2, outer, rd).transpose(1, 0, 2).reshape(U2)
    g_hidden = lax.dynamic_slice(g_hidden, (dp * u_rows,), (u_rows,))
    counts = lengths.astype(F32)[:, :, None] * D
    squares = stat[6, :4].reshape(layer_input.shape[:2] + (2,))
    stream_rms = jnp.sqrt(squares / counts)[:, :, None, :]
    return (
        out_stream.reshape(rows_shape),
        grad_rows.reshape(rows_shape),
        g_qkv[None],
        g_bias[None],
        g_out[None],
        g_up[None],
        g_hidden[None],
        g_down[None],
        g_norm[None],
        stream_rms,
    )


def solution(mesh):
    placed = (
        P(None, "dp", None, None),
        P(None, "dp", None, None),
        P(None, "dp"),
        P("section", "dp", None),
        P("section", "dp"),
        P("section", "dp", None),
        P("section", "dp", None),
        P("section", "dp"),
        P("section", "dp", None),
        P("section", None, "dp"),
    )
    return jax.shard_map(
        shards,
        mesh=mesh,
        in_specs=placed,
        out_specs=(
            P(None, "dp", "section", None),
            P(None, "dp", "section", None),
            P("section", "dp", None),
            P("section", "dp"),
            P("section", "dp", None),
            P("section", "dp", None),
            P("section", "dp"),
            P("section", "dp", None),
            P("section", None, "dp"),
            P(None, "dp", "section", None),
        ),
        check_vma=False,
    )
```

```python
import types

import jax
import jax.numpy as jnp
from jax import lax
from jax.experimental import pallas as pl
from jax.experimental.pallas import tpu as pltpu
from jax.sharding import PartitionSpec as P

F32, BF16 = jnp.float32, jnp.bfloat16
MESH = pl.DeviceIdType.MESH
HEAD_DIM = 32
EPSILON = 1e-05
MASKED = -1e30
SCALE = HEAD_DIM**-0.5
SECTIONS = 4
NN = (((1,), (0,)), ((), ()))
NT = (((1,), (1,)), ((), ()))
TN = (((0,), (0,)), ((), ()))


def mm(left, right, dims=NN):
    return lax.dot_general(left, right, dims, preferred_element_type=F32)


def aligned(start, size):
    return pl.ds(pl.multiple_of(start, size), size)


def head_rows(h, heads):
    full = heads // 8 * 8
    low, rest = full * HEAD_DIM, (heads - full) * HEAD_DIM
    high = h // full if rest else 0
    q = h * HEAD_DIM + high * 2 * low
    k = low + h * HEAD_DIM + high * (low + rest)
    v = 2 * low + h * HEAD_DIM + high * 2 * rest
    return tuple(pl.multiple_of(row, HEAD_DIM) for row in (q, k, v))


def to_packed(rows, heads):
    half = rows.shape[-1] // 3
    low = heads // 8 * 8 * HEAD_DIM
    parts = [rows[:, i * half : i * half + low] for i in range(3)]
    parts += [rows[:, i * half + low : (i + 1) * half] for i in range(3)]
    return jnp.concatenate(parts, axis=1)


def from_packed(rows, half, heads):
    low = heads // 8 * 8 * HEAD_DIM
    rest = half - low
    parts = []
    for i in range(3):
        parts.append(rows[:, i * low : (i + 1) * low])
        parts.append(rows[:, 3 * low + i * rest : 3 * low + (i + 1) * rest])
    return jnp.concatenate(parts, axis=1)


def lanes_to(rows, width):
    if rows.shape[1] == width:
        return rows
    return jnp.concatenate([rows, jnp.zeros((rows.shape[0], width - rows.shape[1]), F32)], axis=1)


def normed_rows(h, gain, shift):
    mean = jnp.mean(h, axis=-1, keepdims=True)
    centred = h - mean
    spread = jnp.mean(centred * centred, axis=-1, keepdims=True)
    inverse = lax.rsqrt(spread + EPSILON)
    return centred * inverse, inverse, centred * inverse * gain + shift


def make_kernel(cfg, names):
    c_ = cfg
    D, L, U, F, W = c_.width, c_.length, c_.units, c_.features, c_.packed
    Q = L // SECTIONS
    NO, n, inner, heads = c_.outer, c_.outer // 2, c_.inner, c_.heads
    ru, rd, ro = c_.up_rows, c_.down_rows, c_.out_rows
    ra, rp = c_.att_rows, c_.att_rows // SECTIONS
    wide = max(U, W)
    low = heads // 8 * 8 * HEAD_DIM
    rest = F - low

    def kernel(*refs):
        R = types.SimpleNamespace(**dict(zip(names, refs)))
        s = lax.axis_index("section")
        y, x = s // 2, s % 2
        dp = lax.axis_index("dp")
        o, i = dp // inner, dp % inner
        zz, c = o // 2, o % 2
        other_y = s + 2 - 4 * y
        mate = o + 1 - 2 * c

        def remote(src, dst, send, recv, section, outer):
            return pltpu.make_async_remote_copy(
                src_ref=src,
                dst_ref=dst,
                send_sem=send,
                recv_sem=recv,
                device_id=(section, outer * inner + i),
                device_id_type=MESH,
            )

        def loop(count, body, first=0):
            def step(k, carry):
                body(k)
                return carry

            lax.fori_loop(first, count, step, 0)

        raw = (R.qkv_w, R.out_w, R.up_w, R.down_w)
        raw_home = (R.o_qkv, R.o_out, R.o_up, R.o_down)
        raw_copies = [
            pltpu.make_async_copy(a, b, R.raw_sem.at[k])
            for k, (a, b) in enumerate(zip(raw, raw_home))
        ]
        for copy in raw_copies:
            copy.start()

        barrier = pltpu.get_barrier_semaphore()

        def greet(section, outer):
            pl.semaphore_signal(
                barrier, inc=1, device_id=(section, outer * inner + i), device_id_type=MESH
            )

        loop(SECTIONS, lambda k: greet((s + k) % SECTIONS, o), 1)
        loop(SECTIONS, lambda k: greet((s + k) % SECTIONS, mate), 1)
        loop(NO, lambda k: greet(s, (o + k) % NO), 1)

        row8 = lax.broadcasted_iota(jnp.int32, (8, wide), 0)
        lane8 = lax.broadcasted_iota(jnp.int32, (8, wide), 1)
        here = row8[:, : R.small_in.shape[1]], lane8[:, : R.small_in.shape[1]]

        def rounded(v):
            return v.astype(BF16).astype(F32)

        R.small_in[...] = jnp.zeros_like(R.small_in)
        for k in range(3):
            R.small_in[k : k + 1, 0:ru] = rounded(R.norm_v[k])
        R.small_in[3:4, 0:ru] = rounded(R.qv_b[...])
        R.small_in[4:5, 0:rd] = rounded(R.up_b[:, 0:rd])
        R.small_in[5:6, 0:rd] = rounded(R.up_b[:, rd : 2 * rd])
        R.len_own[...] = jnp.where(here[1] == 0, R.lens[0, 0], R.lens[0, 1])[:, :128].astype(F32)
        pl.semaphore_wait(barrier, 2 * (SECTIONS - 1) + NO - 1)

        def small_out(k):
            peer = (o + k) % NO
            return remote(
                R.small_in, R.small_a.at[o], R.sma_send.at[k], R.sma_recv.at[o], s, peer
            )

        loop(NO, lambda k: small_out(k).start(), 1)
        R.small_a[o] = R.small_in[...]
        len_copy = remote(R.len_own, R.len_mate, R.len_send.at[0], R.len_recv.at[0], s, mate)
        len_copy.start()

        raw_copies[0].wait()
        raw_copies[1].wait()
        packed = lanes_to(to_packed(R.o_qkv[...], heads), W).astype(BF16)
        R.att_own[pl.ds(0, ru), :] = packed
        bottom = jnp.concatenate([R.o_out[...], jnp.zeros((ra - ru - ro, D), F32)], axis=0)
        R.att_own[pl.ds(ru, ra - ru), :] = lanes_to(bottom, W).astype(BF16)

        def quarter_copy(p):
            return remote(
                R.att_own.at[pl.ds(p * rp, rp)],
                R.watt.at[y, p, aligned(o * rp, rp)],
                R.a1_send.at[p],
                R.a1_recv.at[y, c],
                p,
                2 * zz + x,
            )

        def each_quarter(act, own):
            for p in range(SECTIONS):
                stays = (s == p) & (x == c)

                @pl.when(stays)
                def _(p=p):
                    if own:
                        R.watt[y, p, aligned(o * rp, rp), :] = R.att_own[pl.ds(p * rp, rp), :]

                @pl.when(jnp.logical_not(stays))
                def _(p=p):
                    act(quarter_copy(p))

        each_quarter(lambda copy: copy.start(), True)

        def seq_copy(local):
            if local:
                return pltpu.make_async_copy(R.stream_in.at[y], R.seq_rows, R.load_sem.at[0])
            return remote(
                R.stream_in.at[y], R.seq_rows, R.seq_send.at[0], R.seq_recv.at[0], s, mate
            )

        @pl.when(x == c)
        def _():
            seq_copy(True).start()
            seq_copy(False).start()

        def cot_copy(m, j, local):
            half = c if local else 1 - c
            src = R.cot_in.at[m, aligned((2 * half + j) * Q, Q)]
            dst = R.grad_ff.at[0, aligned(j * L + (2 * m + c) * Q, Q)]
            if local:
                return pltpu.make_async_copy(src, dst, R.load_sem.at[1 + 2 * m + j])
            return remote(src, dst, R.cot_send.at[m, j], R.cot_recv.at[m, j], s, mate)

        for m in range(2):
            for j in range(2):
                cot_copy(m, j, True).start()
                cot_copy(m, j, False).start()

        raw_copies[2].wait()
        raw_copies[3].wait()
        halves = [
            jnp.concatenate(
                [R.o_up[:, (2 * k + h) * rd : (2 * k + h + 1) * rd] for k in range(NO)], axis=1
            ).astype(BF16)
            for h in range(2)
        ]
        R.wup[y, aligned(o * ru, ru), :] = jnp.where(y == 0, halves[0], halves[1])
        R.yb_up[...] = jnp.where(y == 0, halves[1], halves[0])
        R.wdown[y, aligned(o * rd, rd), :] = R.o_down[aligned(y * rd, rd), :].astype(BF16)
        R.yb_down[...] = R.o_down[aligned((1 - y) * rd, rd), :].astype(BF16)

        def piece(kind, layer, outer):
            rows = rd if kind else ru
            return (R.wdown if kind else R.wup).at[layer, aligned(outer * rows, rows)]

        def y_copy(kind):
            return remote(
                R.yb_down if kind else R.yb_up,
                piece(kind, y, o),
                R.y_send.at[kind],
                R.y_recv.at[kind],
                other_y,
                o,
            )

        for kind in range(2):
            y_copy(kind).start()

        def chips_at(distances, body):
            for distance in distances:
                for sign in (1, -1):
                    q = zz + sign * distance

                    @pl.when((q >= 0) & (q < n))
                    def _(q=q, sign=sign, distance=distance):
                        body(q, sign, distance)

        def relays(distance, sign, body):
            if distance >= 2:
                after = zz - sign

                @pl.when((after >= 0) & (after < n))
                def _():
                    body(after)

        NEAR, FAR = tuple(range(min(2, n - 1), 0, -1)), range(3, n)

        def z_copy(layer, kind, origin, to):
            item = layer * 2 + kind
            part = piece(kind, layer, 2 * origin + c)
            send = R.z_send.at[item, origin, to]
            return remote(part, part, send, R.z_recv.at[item, origin], s, 2 * to + c)

        def mate_copy(layer, kind, q):
            item = layer * 2 + kind
            part = piece(kind, layer, 2 * q + c)
            return remote(part, part, R.p_send.at[item, q], R.p_recv.at[item, q], s, mate)

        def mate_arrival(layer, kind, q):
            item = layer * 2 + kind
            part = piece(kind, layer, 2 * q + 1 - c)
            return remote(part, part, R.p_send.at[item, q], R.p_recv.at[item, q], s, mate)

        def feed_spread(layer):
            for kind in range(2):

                @pl.when(y != layer)
                def _(kind=kind):
                    src = R.yb_down if kind else R.yb_up
                    remote(
                        src,
                        piece(kind, layer, o),
                        R.y_send.at[kind],
                        R.y_recv.at[kind],
                        other_y,
                        o,
                    ).wait_recv()

                chips_at(NEAR, lambda q, *_: z_copy(layer, kind, zz, q).start())
                mate_copy(layer, kind, zz).start()

        def feed_arrivals(layer, distances):
            for kind in range(2):

                def landed(q, sign, distance):
                    z_copy(layer, kind, q, zz).wait_recv()
                    relays(
                        distance, sign, lambda after: z_copy(layer, kind, q, after).start()
                    )
                    mate_copy(layer, kind, q).start()

                chips_at(distances, landed)

        def feed_collect(layer):
            feed_arrivals(layer, FAR)
            for kind in range(2):
                loop(n, lambda q, kind=kind: mate_arrival(layer, kind, q).wait_recv())

        def feed_sent(layer):
            for kind in range(2):
                chips_at(NEAR, lambda q, *_: z_copy(layer, kind, zz, q).wait_send())
                for distances in (NEAR, FAR):
                    chips_at(
                        distances,
                        lambda q, sign, distance: relays(
                            distance,
                            sign,
                            lambda after: z_copy(layer, kind, q, after).wait_send(),
                        ),
                    )
                loop(n, lambda q, kind=kind: mate_copy(layer, kind, q).wait_send())

        def att_block(layer, p, q):
            return R.watt.at[layer, p, aligned(q * 2 * rp, 2 * rp)]

        def att_z_copy(layer, origin, to):
            part = att_block(layer, s, origin)
            send = R.a2_send.at[layer, origin, to]
            return remote(part, part, send, R.a2_recv.at[layer, origin], s, 2 * to + c)

        def att_plane_copy(layer, q, k):
            part = att_block(layer, s, q)
            to = (s + k) % SECTIONS
            return remote(
                part, part, R.a3_send.at[layer, q, k], R.a3_recv.at[layer, q, s], to, o
            )

        def att_spread(layer):
            for core in range(2):
                mine = (s == 2 * layer + c) & (c == core)

                @pl.when(jnp.logical_not(mine))
                def _(core=core):
                    remote(
                        R.att_own.at[pl.ds(0, rp)],
                        R.watt.at[layer, s, aligned((2 * zz + core) * rp, rp)],
                        R.a1_send.at[0],
                        R.a1_recv.at[layer, core],
                        2 * layer + c,
                        2 * zz + core,
                    ).wait_recv()

            chips_at(reach(layer), lambda q, *_: att_z_copy(layer, zz, q).start())
            loop(SECTIONS, lambda k: att_plane_copy(layer, zz, k).start(), 1)

        def reach(layer):
            return NEAR if layer else tuple(range(1, n))

        def att_onward(layer, distances):
            def landed(q, sign, distance):
                att_z_copy(layer, q, zz).wait_recv()
                if layer:
                    relays(distance, sign, lambda after: att_z_copy(layer, q, after).start())
                loop(SECTIONS, lambda j: att_plane_copy(layer, q, j).start(), 1)

            chips_at(distances, landed)

        def att_sent(layer):
            chips_at(reach(layer), lambda q, *_: att_z_copy(layer, zz, q).wait_send())
            if layer:
                for distances in (NEAR, FAR):
                    chips_at(
                        distances,
                        lambda q, sign, distance: relays(
                            distance,
                            sign,
                            lambda after: att_z_copy(layer, q, after).wait_send(),
                        ),
                    )
            loop(
                n,
                lambda q: loop(
                    SECTIONS, lambda k: att_plane_copy(layer, q, k).wait_send(), 1
                ),
            )

        def att_collect(layer):
            def from_section(k):
                src = (s + k) % SECTIONS

                def block(q):
                    part = att_block(layer, src, q)
                    remote(
                        part, part, R.a3_send.at[layer, q, k], R.a3_recv.at[layer, q, src], src, o
                    ).wait_recv()

                loop(n, block)

            loop(SECTIONS, from_section, 1)

            def unpack(k):
                for r in range(0, ru, 16):
                    R.wqkv[layer, aligned(k * ru + r, 16), :] = R.watt[
                        layer, r // rp, aligned(k * rp + r % rp, 16), :
                    ]
                for r in range(0, ro, 16):
                    rows = min(16, ro - r)
                    p, off = (ru + r) // rp, (ru + r) % rp
                    block = R.watt[layer, p, aligned(k * rp + off, 16), :][:, :D].astype(F32)
                    R.wide_rows[aligned(k * ro + r, 8), :] = block[:rows][:8]
                    if rows > 8:
                        R.wide_rows[aligned(k * ro + r + 8, 8), :] = block[8:rows]

            loop(NO, unpack)
            R.wout[layer] = R.wide_rows[pl.ds(0, F), :].astype(BF16)

        att_spread(0)

        loop(
            NO,
            lambda k: remote(
                R.small_in,
                R.small_a.at[(o + k) % NO],
                R.sma_send.at[k],
                R.sma_recv.at[(o + k) % NO],
                s,
                (o + k) % NO,
            ).wait_recv(),
            1,
        )
        table = jnp.zeros((8, wide), F32)
        for k in range(NO):
            part = lanes_to(R.small_a[k], wide)
            narrow = pltpu.roll(part, ru * k, 1) if k else part
            broad = pltpu.roll(part, rd * k, 1) if k else part
            table = table + jnp.where(row8 < 4, narrow, broad)
        moved = jnp.where(lane8 < low, table, 0.0)
        moved += pltpu.roll(jnp.where((lane8 >= low) & (lane8 < F), table, 0.0), 2 * low, 1)
        moved += pltpu.roll(
            jnp.where((lane8 >= F) & (lane8 < F + low), table, 0.0), 2 * low - F, 1
        )
        moved += pltpu.roll(
            jnp.where((lane8 >= F + low) & (lane8 < 2 * F), table, 0.0), 2 * low + 2 * rest - F, 1
        )
        table = jnp.where(row8 == 3, moved, table)
        R.small_own[...] = table
        R.small_b[s] = table

        def small_b_copy(k, of):
            return remote(
                R.small_own,
                R.small_b.at[of],
                R.smb_send.at[k],
                R.smb_recv.at[of],
                (s + k) % SECTIONS,
                o,
            )

        loop(SECTIONS, lambda k: small_b_copy(k, s).start(), 1)
        loop(SECTIONS, lambda k: small_b_copy(k, (s + k) % SECTIONS).wait_recv(), 1)

        R.small_grad[...] = jnp.zeros_like(R.small_grad)
        def note_rows(block, index, row):
            R.small_grad[block] += jnp.where(row8 == index, lanes_to(row, wide), 0.0)

        att_spread(1)
        feed_spread(0)

        @pl.when(x == c)
        def _():
            seq_copy(True).wait()

        @pl.when(x != c)
        def _():
            seq_copy(False).wait_recv()

        gain0 = R.small_b[0, 0:1, :D]
        shift0 = R.small_b[0, 1:2, :D]

        def first_norm(k):
            rows = aligned(k * Q, Q)
            _, _, out = normed_rows(R.seq_rows[rows, :].astype(F32), gain0, shift0)
            R.norm_at[0, rows, :] = out.astype(BF16)

        loop(L // Q, first_norm)
        R.hid_rows[0] = R.seq_rows[aligned(c * 2 * Q, 2 * Q), :]
        len_copy.wait_recv()
        tile = jnp.where(x == c, R.len_own[...], R.len_mate[...])
        tile = jnp.where((row8[:, :128] == 0) & (lane8[:, :128] == y), tile, 0.0)
        length_here = jnp.sum(jnp.sum(tile, axis=1, keepdims=True), axis=0, keepdims=True)
        length_here = length_here.astype(jnp.int32)
        att_onward(0, reach(0))

        def rows_copy(phase, m, src, dst, slot, to):
            return remote(
                src, dst, R.ag_send.at[phase, m, slot], R.ag_recv.at[phase, m, s], to, o
            )

        def share_all(phase, m, buf):
            part = buf.at[aligned(m * L + s * Q, Q)]
            return lambda k: rows_copy(phase, m, part, part, k, (s + k) % SECTIONS)

        def share_mate(phase, m, buf):
            part = buf.at[aligned((2 * c + m) * Q, Q)]
            return remote(
                part, part, R.ag_send.at[phase, m, 0], R.ag_recv.at[phase, m, c], s, mate
            )

        def arrival(phase, m, buf, base, k):
            src = (s + k) % SECTIONS
            part = buf.at[aligned(base + src * Q, Q)]
            return remote(
                part, part, R.ag_send.at[phase, m, k], R.ag_recv.at[phase, m, src], src, o
            )

        def send_rows(phase, attention, m, buf, value):
            if attention:
                buf[aligned((2 * c + m) * Q, Q), :] = value
                share_mate(phase, m, buf).start()
            else:
                buf[aligned(m * L + s * Q, Q), :] = value
                copies = share_all(phase, m, buf)
                loop(SECTIONS, lambda k: copies(k).start(), 1)

        def finish_send_rows(phase, attention, m, buf):
            if attention:
                share_mate(phase, m, buf).wait_send()
            else:
                copies = share_all(phase, m, buf)
                loop(SECTIONS, lambda k: copies(k).wait_send(), 1)

        def await_rows(phase, attention, m, buf):
            if attention:
                for j in range(2):
                    part = buf.at[aligned((2 * (1 - c) + j) * Q, Q)]
                    remote(
                        part, part, R.ag_send.at[phase, j, 0], R.ag_recv.at[phase, j, 1 - c], s, mate
                    ).wait_recv()
            else:
                loop(SECTIONS, lambda k: arrival(phase, m, buf, m * L, k).wait_recv(), 1)

        def sum_slot(phase):
            return 0 if phase < 4 else 1

        def part_copy(phase, m, base, k):
            to = (s + k) % SECTIONS
            return remote(
                R.parts.at[aligned(base + to * Q, Q)],
                R.sums.at[sum_slot(phase), s, m],
                R.rs_send.at[phase, m, k],
                R.rs_recv.at[phase, m, s],
                to,
                o,
            )

        def mate_part(phase, j):
            return remote(
                R.parts.at[aligned((2 * (1 - c) + j) * Q, Q)],
                R.sums.at[sum_slot(phase), c, j],
                R.rs_send.at[phase, j, 0],
                R.rs_recv.at[phase, j, c],
                s,
                mate,
            )

        def send_parts(phase, attention, m):
            slot = sum_slot(phase)
            if attention:
                for j in range(2):
                    mate_part(phase, j).start()
                    R.sums[slot, c, j] = R.parts[aligned((2 * c + j) * Q, Q), :]
            else:
                loop(SECTIONS, lambda k: part_copy(phase, m, m * L, k).start(), 1)
                R.sums[slot, s, m] = R.parts[aligned(m * L + s * Q, Q), :]

        def finish_send_parts(phase, attention):
            for m in range(2):
                if attention:
                    mate_part(phase, m).wait_send()
                else:
                    loop(SECTIONS, lambda k: part_copy(phase, m, m * L, k).wait_send(), 1)

        def part_arrival(phase, m, src):
            return remote(
                R.parts.at[pl.ds(0, Q)],
                R.sums.at[sum_slot(phase), src, m],
                R.rs_send.at[phase, m, 0],
                R.rs_recv.at[phase, m, src],
                s,
                mate,
            )

        def await_parts(phase, attention, m):
            slot = sum_slot(phase)
            if attention:
                part_arrival(phase, m, 1 - c).wait_recv()
                sources = range(2)
            else:
                loop(
                    SECTIONS,
                    lambda k: part_arrival(phase, m, (s + k) % SECTIONS).wait_recv(),
                    1,
                )
                sources = range(SECTIONS)
            total = None
            for src in sources:
                part = R.sums[slot, src, m].astype(F32)
                total = part if total is None else total + part
            return total

        def place_copy(which, j):
            return remote(
                R.finished.at[which, j],
                (R.out_grad_rows if which else R.out_stream).at[aligned(y * Q, Q)],
                R.fo_send.at[which, j],
                R.fo_recv.at[which, y],
                2 * c + j,
                2 * zz + x,
            )

        def place_rows(which, j, value):
            stays = (s == 2 * c + j) & (x == c)
            R.finished[which, j] = value

            @pl.when(stays)
            def _():
                (R.out_grad_rows if which else R.out_stream)[aligned(y * Q, Q), :] = value

            @pl.when(jnp.logical_not(stays))
            def _():
                place_copy(which, j).start()

        def finish_place(which):
            for j in range(2):
                stays = (s == 2 * c + j) & (x == c)

                @pl.when(jnp.logical_not(stays))
                def _(j=j):
                    place_copy(which, j).wait_send()

            for m in range(2):
                mine = (s == 2 * m + c) & (y == c)

                @pl.when(jnp.logical_not(mine))
                def _(m=m):
                    remote(
                        R.finished.at[which, 0],
                        (R.out_grad_rows if which else R.out_stream).at[pl.ds(m * Q, Q)],
                        R.fo_send.at[which, 0],
                        R.fo_recv.at[which, m],
                        2 * m + c,
                        2 * zz + y,
                    ).wait_recv()

        def close_forward(phase, m):
            e = phase
            attention = e % 2 == 0
            branch = await_parts(phase, attention, m) + R.small_b[e, 2:3, :D]
            mine = pl.ds(m * Q, Q)
            h = R.hid_rows[e, mine, :].astype(F32)
            position = (2 * c + m) * Q + lax.broadcasted_iota(jnp.int32, (Q, 1), 0)
            valid = (position < length_here).astype(F32)
            square_h = jnp.sum(jnp.sum(h * h * valid, axis=1, keepdims=True), axis=0, keepdims=True)
            square_b = jnp.sum(
                jnp.sum(branch * branch * valid, axis=1, keepdims=True), axis=0, keepdims=True
            )
            spot = (2 * zz + x) * 4 + 2 * y
            R.small_grad[e] += jnp.where((row8 == 6) & (lane8 == spot), square_h, 0.0)
            R.small_grad[e] += jnp.where((row8 == 6) & (lane8 == spot + 1), square_b, 0.0)
            fresh = (h + branch).astype(BF16)
            if e == 3:
                place_rows(0, m, fresh)
                return
            R.hid_rows[e + 1, mine, :] = fresh
            _, _, out = normed_rows(
                fresh.astype(F32), R.small_b[e + 1, 0:1, :D], R.small_b[e + 1, 1:2, :D]
            )
            to_attention = (e + 1) % 2 == 0
            buf = (R.norm_at if to_attention else R.norm_ff).at[(e + 1) // 2]
            send_rows(phase + 1, to_attention, m, buf, out.astype(BF16))

        def close_backward(phase, m):
            e = 7 - phase
            attention = e % 2 == 0
            d_norm = await_parts(phase, attention, m)
            mine = pl.ds(m * Q, Q)
            unit, inverse, _ = normed_rows(R.hid_rows[e, mine, :].astype(F32), 1.0, 0.0)
            flow = R.grad_rows[mine, :].astype(F32)
            note_rows(e, 0, jnp.sum(d_norm * unit, axis=0, keepdims=True))
            note_rows(e, 1, jnp.sum(d_norm, axis=0, keepdims=True))
            note_rows(e, 2, jnp.sum(flow, axis=0, keepdims=True))
            a = d_norm * R.small_b[e, 0:1, :D]
            mean_a = jnp.mean(a, axis=-1, keepdims=True)
            mean_ax = jnp.mean(a * unit, axis=-1, keepdims=True)
            fresh = (flow + (a - mean_a - unit * mean_ax) * inverse).astype(BF16)
            if e == 0:
                place_rows(1, m, fresh)
                return
            R.grad_rows[mine, :] = fresh
            to_attention = (e - 1) % 2 == 0
            buf = R.grad_at if to_attention else R.grad_ff.at[1]
            send_rows(phase + 1, to_attention, m, buf, fresh)

        ga = (R.hidden.at[1], R.slope.at[1])

        def attention_forward(layer):
            bias = R.small_b[2 * layer + c, 3:4, :W]
            xs = R.norm_at.at[layer]
            for t in range(0, W, 256):
                cols = pl.ds(t, 256)
                lin = mm(xs[...], R.wqkv[layer, :, cols]) + bias[:, t : t + 256]
                R.lin_t[layer, cols, :] = lin.T.astype(BF16)

            def head(h):
                q0, k0, v0 = head_rows(h, heads)
                score = mm(
                    R.lin_t[layer, pl.ds(k0, HEAD_DIM), :],
                    R.lin_t[layer, pl.ds(q0, HEAD_DIM), :],
                    TN,
                )
                live = lax.broadcasted_iota(jnp.int32, score.shape, 0) < length_here
                score = jnp.where(live, score * SCALE, MASKED)
                top = jnp.max(score, axis=0, keepdims=True)
                powers = jnp.exp(score - top)
                total = jnp.sum(powers, axis=0, keepdims=True)
                probs = (powers * (1.0 / total)).astype(BF16)
                R.log_total[layer, h] = top + jnp.log(total)
                mixed = mm(R.lin_t[layer, pl.ds(v0, HEAD_DIM), :], probs)
                R.att_t[layer, aligned(h * HEAD_DIM, HEAD_DIM), :] = mixed.astype(BF16)

            loop(heads, head)
            R.parts[pl.ds(0, L), :] = mm(R.att_t[layer], R.wout[layer], TN).astype(BF16)

        def attention_backward(layer):
            stage = 1 - layer
            xs, g = R.norm_at.at[layer], R.grad_at
            R.wide_rows[pl.ds(0, F), :] = mm(R.att_t[layer], g[...])

            def out_rows(k):
                for r in range(ru, ra, 16):
                    top_half = R.wide_rows[aligned(k * ro + r - ru, 8), :]
                    low_half = R.wide_rows[aligned(k * ro + r - ru + 8, 8), :]
                    block = jnp.concatenate([top_half, low_half], axis=0)
                    ga[stage][aligned(r // rp * NO * rp + k * rp + r % rp, 16), 0:D] = block.astype(BF16)

            loop(NO, out_rows)
            R.d_att_t[...] = mm(R.wout[layer], g[...], NT).astype(BF16)

            def head(h):
                q0, k0, v0 = head_rows(h, heads)
                q_t = R.lin_t[layer, pl.ds(q0, HEAD_DIM), :]
                k_t = R.lin_t[layer, pl.ds(k0, HEAD_DIM), :]
                v_t = R.lin_t[layer, pl.ds(v0, HEAD_DIM), :]
                d_a = R.d_att_t[aligned(h * HEAD_DIM, HEAD_DIM), :]
                score = mm(k_t, q_t, TN)
                live = lax.broadcasted_iota(jnp.int32, score.shape, 0) < length_here
                probs = jnp.where(live, jnp.exp(score * SCALE - R.log_total[layer, h]), 0.0)
                d_probs = mm(v_t, d_a, TN)
                product = probs * d_probs
                inner_sum = jnp.sum(product, axis=0, keepdims=True)
                d_score = ((product - probs * inner_sum) * SCALE).astype(BF16)
                R.d_lin_t[pl.ds(q0, HEAD_DIM), :] = mm(k_t, d_score).astype(BF16)
                R.d_lin_t[pl.ds(k0, HEAD_DIM), :] = mm(q_t, d_score, NT).astype(BF16)
                R.d_lin_t[pl.ds(v0, HEAD_DIM), :] = mm(d_a, probs.astype(BF16), NT).astype(BF16)

            loop(heads, head)
            sums = []
            for t in range(0, W, 256):
                cols = pl.ds(t, 256)
                d_lin = R.d_lin_t[cols, :].T
                sums.append(jnp.sum(d_lin.astype(F32), axis=0, keepdims=True))
                d_w = mm(xs[...], d_lin, TN).astype(BF16)
                for k in range(NO):
                    for r in range(0, ru, 16):
                        ga[stage][pl.ds(r // rp * NO * rp + k * rp + r % rp, 16), cols] = d_w[
                            k * ru + r : k * ru + r + 16
                        ]
                part = mm(d_lin, R.wqkv[layer, :, cols], NT)
                if t == 0:
                    R.acc[...] = part
                else:
                    R.acc[...] += part
            R.parts[pl.ds(0, L), :] = R.acc[...].astype(BF16)
            note_rows(2 * layer + c, 3, jnp.concatenate(sums, axis=1))

        def feed_bias(layer):
            block = R.small_b[2 * layer + x]
            return jnp.where(y == 0, block[4:5], block[5:6])[:, :U]

        def feed_forward(layer, m):
            bias = feed_bias(layer)

            def rows_step(r):
                rows = aligned(m * L + r * Q, Q)
                pre = mm(R.norm_ff[layer, rows, :], R.wup[layer]) + bias
                cdf = 0.5 + 0.5 * lax.erf(pre * 0.7071067811865476)
                density = jnp.exp(pre * pre * -0.5) * 0.3989422804014327
                hidden = (pre * cdf).astype(BF16)
                R.hidden[layer, rows, :] = hidden
                R.slope[layer, rows, :] = (cdf + pre * density).astype(BF16)
                R.parts[rows, :] = mm(hidden, R.wdown[layer]).astype(BF16)

            loop(SECTIONS, rows_step)

        def feed_backward(layer, m):
            rows = pl.ds(m * L, L)
            xs = R.norm_ff.at[layer, rows]
            g = R.grad_ff.at[0 if layer == 1 else 1, rows]
            tile = U // 2
            owners = tile // rd
            for j in range(2):
                cols = pl.ds(j * tile, tile)
                d_hidden = mm(g[...], R.wdown[layer, cols, :], NT)
                d_pre = (d_hidden * R.slope[layer, rows, cols].astype(F32)).astype(BF16)
                d_down = mm(R.hidden[layer, rows, cols], g[...], TN)
                d_up = mm(xs[...], d_pre, TN)
                for k in range(owners):
                    owner = j * owners + k
                    place = (owner % 2, pl.ds(owner // 2 * rd, rd), slice(None))
                    block = d_down[k * rd : (k + 1) * rd]
                    if m:
                        block = block + R.sb_down[place].astype(F32)
                    R.sb_down[place] = block.astype(BF16)
                for k in range(NO):
                    place = (k % 2, pl.ds(k // 2 * ru, ru), cols)
                    block = d_up[k * ru : (k + 1) * ru]
                    if m:
                        block = block + R.sb_up[place].astype(F32)
                    R.sb_up[place] = block.astype(BF16)
                total = jnp.sum(d_pre.astype(F32), axis=0, keepdims=True)
                blank = jnp.zeros((1, tile), F32)
                row = jnp.concatenate([total, blank] if j == 0 else [blank, total], axis=1)
                note_rows(2 * layer + x, 4 + y, row)
                part = mm(d_pre, R.wup[layer, :, cols], NT)
                if j == 0:
                    R.acc[...] = part
                else:
                    R.parts[rows, :] = (R.acc[...] + part).astype(BF16)

        z_up, z_down = (R.zb_up, R.wup.at[1]), (R.zb_down, R.wdown.at[1])
        FEED_GRADS = (
            (0, R.sb_up, R.rb_up, R.mb_up, z_up, R.yb_up, R.yr_up, ru),
            (1, R.sb_down, R.rb_down, R.mb_down, z_down, R.yb_down, R.yr_down, rd),
        )

        def mate_grads(stage):
            return [
                remote(sb.at[1 - c], rb, R.r1_send.at[stage, a], R.r1_recv.at[stage, a], s, mate)
                for a, sb, rb, *_ in FEED_GRADS
            ]

        def z_grads(stage, k):
            q = (zz + k) % n
            return [
                remote(
                    mb.at[aligned(q * rows, rows)],
                    zb[stage].at[aligned(zz * rows, rows)],
                    R.r2_send.at[stage, a, q],
                    R.r2_recv.at[stage, a, zz],
                    s,
                    2 * q + c,
                )
                for a, sb, rb, mb, zb, yb, yr, rows in FEED_GRADS
            ]

        def feed_to_mate(stage):
            for copy in mate_grads(stage):
                copy.start()

        def finish_feed_z(stage):
            loop(n, lambda k: [copy.wait_send() for copy in z_grads(stage, k)], 1)

        def feed_along_z(stage):
            for copy in mate_grads(stage):
                copy.wait()
            if stage:
                finish_feed_z(0)
            for a, sb, rb, mb, zb, yb, yr, rows in FEED_GRADS:

                def add(q, sb=sb, rb=rb, mb=mb, rows=rows):
                    part = aligned(q * rows, rows)
                    both = sb[c, part, :].astype(F32) + rb[part, :].astype(F32)
                    mb[part, :] = both.astype(BF16)

                loop(n, add)
            loop(n, lambda k: [copy.start() for copy in z_grads(stage, k)], 1)

        def y_grad(a, yb, yr):
            return remote(yb, yr, R.r4_send.at[a], R.r4_recv.at[a], other_y, o)

        def keep_half(a, h, value):
            if a:
                R.o_down[pl.ds(h * rd, rd), :] = value
                return
            for k in range(NO):
                R.o_up[:, (2 * k + h) * rd : (2 * k + h + 1) * rd] = value[:, k * rd : (k + 1) * rd]

        def feed_owned(stage):
            layer = 1 - stage
            for a, sb, rb, mb, zb, yb, yr, rows in FEED_GRADS:

                def landed(k, a=a, zb=zb, mb=mb, rows=rows):
                    q = (zz + k) % n
                    remote(
                        mb.at[pl.ds(0, rows)],
                        zb[stage].at[aligned(q * rows, rows)],
                        R.r2_send.at[stage, a, q],
                        R.r2_recv.at[stage, a, q],
                        s,
                        2 * q + c,
                    ).wait_recv()

                loop(n, landed, 1)
                total = mb[aligned(zz * rows, rows), :].astype(F32)
                for k in range(1, n):
                    total = total + zb[stage][aligned((zz + k) % n * rows, rows), :].astype(F32)

                @pl.when(y == layer)
                def _(a=a, total=total):
                    keep_half(a, layer, total)

                @pl.when(y != layer)
                def _(a=a, yb=yb, yr=yr, total=total):
                    yb[...] = total.astype(BF16)
                    y_grad(a, yb, yr).start()

        def feed_home():
            for a, sb, rb, mb, zb, yb, yr, rows in FEED_GRADS:
                y_grad(a, yb, yr).wait()
                for h in range(2):

                    @pl.when(y == 1 - h)
                    def _(a=a, h=h, yr=yr):
                        keep_half(a, h, yr[...].astype(F32))

        att_rows = NO * rp

        def plane_grad(stage, k):
            to = (s + k) % SECTIONS
            return remote(
                ga[stage].at[aligned(to * att_rows, att_rows), pl.ds(0, W)],
                R.watt.at[stage, s],
                R.g1_send.at[stage, k],
                R.g1_recv.at[stage, s],
                to,
                o,
            )

        def att_to_plane(stage):
            loop(SECTIONS, lambda k: plane_grad(stage, k).start(), 1)

        def finish_att_plane(stage):
            loop(SECTIONS, lambda k: plane_grad(stage, k).wait_send(), 1)

        def att_z_grad(stage, k):
            q = (zz + k) % n
            return remote(
                R.gs.at[stage, aligned(q * 2 * rp, 2 * rp)],
                R.gz.at[stage, zz],
                R.g2_send.at[stage, q],
                R.g2_recv.at[stage, zz],
                s,
                2 * q + c,
            )

        def finish_att_z(stage):
            loop(n, lambda k: att_z_grad(stage, k).wait_send(), 1)

        def att_along_z(stage):
            def landed(k):
                src = (s + k) % SECTIONS
                remote(
                    ga[stage].at[aligned(src * att_rows, att_rows), pl.ds(0, W)],
                    R.watt.at[stage, src],
                    R.g1_send.at[stage, k],
                    R.g1_recv.at[stage, src],
                    src,
                    o,
                ).wait_recv()

            loop(SECTIONS, landed, 1)

            def add(q):
                part = aligned(q * 2 * rp, 2 * rp)
                own = aligned(s * att_rows + q * 2 * rp, 2 * rp)
                total = ga[stage][own, 0:W].astype(F32)
                for k in range(1, SECTIONS):
                    total = total + R.watt[stage, (s + k) % SECTIONS, part, :].astype(F32)
                R.gs[stage, part, :] = total.astype(BF16)

            loop(n, add)
            loop(n, lambda k: att_z_grad(stage, k).start(), 1)

        def home_copy(stage, core):
            return remote(
                R.gt.at[stage, pl.ds(core * rp, rp)],
                R.att_own.at[aligned(s * rp, rp)],
                R.g3_send.at[stage, core],
                R.g3_recv.at[s],
                2 * (1 - stage) + c,
                2 * zz + core,
            )

        def each_home(stage, act, own):
            for core in range(2):
                stays = (s == 2 * (1 - stage) + c) & (c == core)

                @pl.when(stays)
                def _(core=core):
                    if own:
                        R.att_own[aligned(s * rp, rp), :] = R.gt[stage, pl.ds(core * rp, rp), :]

                @pl.when(jnp.logical_not(stays))
                def _(core=core):
                    act(home_copy(stage, core))

        def att_owned(stage):
            def landed(k):
                q = (zz + k) % n
                remote(
                    R.gs.at[stage, pl.ds(0, 2 * rp)],
                    R.gz.at[stage, q],
                    R.g2_send.at[stage, q],
                    R.g2_recv.at[stage, q],
                    s,
                    2 * q + c,
                ).wait_recv()

            loop(n, landed, 1)
            total = R.gs[stage, aligned(zz * 2 * rp, 2 * rp), :].astype(F32)
            for k in range(1, n):
                total = total + R.gz[stage, (zz + k) % n].astype(F32)
            R.gt[stage] = total.astype(BF16)
            each_home(stage, lambda copy: copy.start(), True)

        def att_home():
            for p in range(SECTIONS):
                mine = (s == p) & (x == c)

                @pl.when(jnp.logical_not(mine))
                def _(p=p):
                    remote(
                        R.gt.at[0, pl.ds(0, rp)],
                        R.att_own.at[pl.ds(p * rp, rp)],
                        R.g3_send.at[0, 0],
                        R.g3_recv.at[p],
                        p,
                        2 * zz + x,
                    ).wait_recv()

            rows = R.att_own[pl.ds(0, ru), :].astype(F32)
            R.o_qkv[...] = from_packed(rows, F, heads)
            rows = R.att_own[pl.ds(ru, ra - ru), :].astype(F32)
            R.o_out[...] = rows[:ro, :D]

        att_collect(0)
        att_onward(1, NEAR)
        attention_forward(0)
        send_parts(0, True, None)
        feed_arrivals(0, NEAR)
        feed_spread(1)
        for m in range(2):
            close_forward(0, m)
        att_onward(1, FAR)
        feed_collect(0)
        finish_send_parts(0, True)
        for m in range(2):
            await_rows(1, False, m, R.norm_ff.at[0])
            feed_forward(0, m)
            send_parts(1, False, m)
        feed_arrivals(1, NEAR)
        for m in range(2):
            close_forward(1, m)
        att_collect(1)
        finish_send_parts(1, False)
        await_rows(2, True, None, R.norm_at.at[1])
        attention_forward(1)
        send_parts(2, True, None)
        for m in range(2):
            close_forward(2, m)
        feed_collect(1)
        finish_send_parts(2, True)
        for m in range(2):
            await_rows(3, False, m, R.norm_ff.at[1])
            feed_forward(1, m)
            send_parts(3, False, m)

        loop(NO, lambda k: small_out(k).wait_send(), 1)
        loop(SECTIONS, lambda k: small_b_copy(k, s).wait_send(), 1)
        len_copy.wait_send()
        each_quarter(lambda copy: copy.wait_send(), False)

        @pl.when(x == c)
        def _():
            seq_copy(False).wait_send()

        for kind in range(2):
            y_copy(kind).wait_send()
        for layer in range(2):
            att_sent(layer)
            feed_sent(layer)
        for m in range(2):
            finish_send_rows(1, False, m, R.norm_ff.at[0])
            finish_send_rows(2, True, m, R.norm_at.at[1])
            finish_send_rows(3, False, m, R.norm_ff.at[1])
            for j in range(2):
                cot_copy(m, j, True).wait()
                cot_copy(m, j, False).wait_send()
                remote(
                    R.cot_in.at[m, pl.ds(0, Q)],
                    R.grad_ff.at[0, aligned(j * L + (2 * m + 1 - c) * Q, Q)],
                    R.cot_send.at[m, j],
                    R.cot_recv.at[m, j],
                    s,
                    mate,
                ).wait_recv()
        for j in range(2):
            R.grad_rows[pl.ds(j * Q, Q), :] = R.grad_ff[0, aligned(j * L + s * Q, Q), :]
        finish_send_parts(3, False)

        for m in range(2):
            feed_backward(1, m)
            send_parts(4, False, m)
        feed_to_mate(0)
        for m in range(2):
            close_forward(3, m)
        for m in range(2):
            close_backward(4, m)
        feed_along_z(0)
        finish_send_parts(4, False)
        await_rows(5, True, None, R.grad_at)
        attention_backward(1)
        send_parts(5, True, None)
        for m in range(2):
            close_backward(5, m)
        finish_send_parts(5, True)
        for m in range(2):
            await_rows(6, False, m, R.grad_ff.at[1])
            feed_backward(0, m)
            send_parts(6, False, m)
        feed_to_mate(1)
        att_to_plane(0)
        for m in range(2):
            finish_send_rows(5, True, m, R.grad_at)
        for m in range(2):
            close_backward(6, m)
        feed_owned(0)
        feed_along_z(1)
        finish_send_parts(6, False)
        await_rows(7, True, None, R.grad_at)
        attention_backward(0)
        send_parts(7, True, None)
        att_to_plane(1)
        att_along_z(0)
        for m in range(2):
            close_backward(7, m)

        def small_grad_copy(k, of):
            to = (s + k) % SECTIONS
            return remote(
                R.small_grad.at[to],
                R.small_sum.at[of],
                R.sga_send.at[k],
                R.sga_recv.at[of],
                to,
                o,
            )

        loop(SECTIONS, lambda k: small_grad_copy(k, s).start(), 1)
        R.small_sum[s] = R.small_grad[s]
        att_along_z(1)
        loop(SECTIONS, lambda k: small_grad_copy(k, (s + k) % SECTIONS).wait_recv(), 1)
        total = R.small_sum[0]
        for k in range(1, SECTIONS):
            total = total + R.small_sum[k]
        R.small_line[...] = total

        def small_line_copy(k, of):
            peer = (o + k) % NO
            return remote(
                R.small_line, R.small_all.at[of], R.sgb_send.at[k], R.sgb_recv.at[of], s, peer
            )

        loop(NO, lambda k: small_line_copy(k, o).start(), 1)
        R.small_all[o] = total
        feed_owned(1)
        att_owned(0)
        att_owned(1)
        loop(NO, lambda k: small_line_copy(k, (o + k) % NO).wait_recv(), 1)
        total = R.small_all[0]
        for k in range(1, NO):
            total = total + R.small_all[k]

        def back(rows, lanes):
            return pltpu.roll(rows, (wide - lanes) % wide, 1)

        norms = back(total, ru * o)
        for k in range(3):
            R.o_norm[k] = norms[k : k + 1, 0:ru]
        units = back(total, rd * o)
        R.o_upb[:, 0:rd] = units[4:5, 0:rd]
        R.o_upb[:, rd : 2 * rd] = units[5:6, 0:rd]
        first, second, third = 3 * low, 3 * low + 2 * rest, 3 * low + 3 * rest
        plain = jnp.where(lane8 < low, total, 0.0)
        plain += back(jnp.where((lane8 >= first) & (lane8 < first + rest), total, 0.0), 2 * low)
        plain += back(jnp.where((lane8 >= 2 * low) & (lane8 < first), total, 0.0), 2 * low - F)
        plain += back(
            jnp.where((lane8 >= second) & (lane8 < third), total, 0.0), 2 * low + 2 * rest - F
        )
        R.o_qvb[...] = back(plain, ru * o)[3:4, 0:ru]
        squares = back(total, 4 * o)
        for m in range(2):
            count = (R.lens[0, m] * D).astype(F32)
            R.o_rms[m : m + 1, :] = jnp.sqrt(squares[6:7, 2 * m : 2 * m + 2] / count)
        feed_home()
        att_home()
        for which in range(2):
            finish_place(which)

        loop(SECTIONS, lambda k: small_grad_copy(k, s).wait_send(), 1)
        loop(NO, lambda k: small_line_copy(k, o).wait_send(), 1)
        for m in range(2):
            finish_send_rows(6, False, m, R.grad_ff.at[1])
            finish_send_rows(7, True, m, R.grad_at)
        finish_send_parts(7, True)
        finish_feed_z(1)
        for stage in range(2):
            finish_att_plane(stage)
            finish_att_z(stage)
            each_home(stage, lambda copy: copy.wait_send(), False)

    return kernel


def one_step(cfg, lens, qkv, qv_b, out, up, up_b, down, norm, stream, cotangent):
    D, L, U, F, W = cfg.width, cfg.length, cfg.units, cfg.features, cfg.packed
    Q = L // SECTIONS
    NO, n = cfg.outer, cfg.outer // 2
    ru, rd, ro, ra = cfg.up_rows, cfg.down_rows, cfg.out_rows, cfg.att_rows
    rp = ra // SECTIONS
    wide = max(U, W)
    lanes = -(-max(ru, rd) // 128) * 128
    dma = pltpu.SemaphoreType.DMA
    inputs = dict(
        lens=lens,
        qkv_w=qkv,
        qv_b=qv_b,
        out_w=out,
        up_w=up,
        up_b=up_b,
        down_w=down,
        norm_v=norm,
        stream_in=stream,
        cot_in=cotangent,
    )
    outputs = dict(
        out_stream=((2 * Q, D), BF16),
        out_grad_rows=((2 * Q, D), BF16),
        o_qkv=((ru, 3 * F), F32),
        o_qvb=((1, ru), F32),
        o_out=((ro, D), F32),
        o_up=((ru, 2 * U), F32),
        o_upb=((1, 2 * rd), F32),
        o_down=((2 * rd, D), F32),
        o_norm=((3, 1, ru), F32),
        o_rms=((2, 2), F32),
    )
    scratch = dict(
        small_in=((8, lanes), F32),
        small_a=((NO, 8, lanes), F32),
        small_own=((8, wide), F32),
        small_b=((SECTIONS, 8, wide), F32),
        small_grad=((SECTIONS, 8, wide), F32),
        small_sum=((SECTIONS, 8, wide), F32),
        small_line=((8, wide), F32),
        small_all=((NO, 8, wide), F32),
        len_own=((8, 128), F32),
        len_mate=((8, 128), F32),
        att_own=((ra, W), BF16),
        watt=((2, SECTIONS, NO * rp, W), BF16),
        wqkv=((2, D, W), BF16),
        wout=((2, F, D), BF16),
        wup=((2, D, U), BF16),
        wdown=((2, U, D), BF16),
        hid_rows=((SECTIONS, 2 * Q, D), BF16),
        grad_rows=((2 * Q, D), BF16),
        norm_at=((2, L, D), BF16),
        norm_ff=((2, 2 * L, D), BF16),
        lin_t=((2, W, L), BF16),
        att_t=((2, F, L), BF16),
        log_total=((2, cfg.heads, 1, L), F32),
        hidden=((2, 2 * L, U), BF16),
        slope=((2, 2 * L, U), BF16),
        grad_ff=((2, 2 * L, D), BF16),
        grad_at=((L, D), BF16),
        seq_rows=((L, D), BF16),
        parts=((2 * L, D), BF16),
        sums=((2, SECTIONS, 2, Q, D), BF16),
        finished=((2, 2, Q, D), BF16),
        acc=((L, D), F32),
        wide_rows=((F + 64, D), F32),
        d_att_t=((F, L), BF16),
        d_lin_t=((W, L), BF16),
        sb_up=((2, n * ru, U), BF16),
        rb_up=((n * ru, U), BF16),
        mb_up=((n * ru, U), BF16),
        zb_up=((n * ru, U), BF16),
        yb_up=((ru, U), BF16),
        yr_up=((ru, U), BF16),
        sb_down=((2, n * rd, D), BF16),
        rb_down=((n * rd, D), BF16),
        mb_down=((n * rd, D), BF16),
        zb_down=((n * rd, D), BF16),
        yb_down=((rd, D), BF16),
        yr_down=((rd, D), BF16),
        gs=((2, NO * rp, W), BF16),
        gz=((2, n, 2 * rp, W), BF16),
        gt=((2, 2 * rp, W), BF16),
    )
    semaphores = dict(
        raw_sem=(4,),
        load_sem=(5,),
        sma_send=(NO,),
        sma_recv=(NO,),
        smb_send=(SECTIONS,),
        smb_recv=(SECTIONS,),
        len_send=(1,),
        len_recv=(1,),
        seq_send=(1,),
        seq_recv=(1,),
        cot_send=(2, 2),
        cot_recv=(2, 2),
        a1_send=(SECTIONS,),
        a1_recv=(2, 2),
        a2_send=(2, n, n),
        a2_recv=(2, n),
        a3_send=(2, n, SECTIONS),
        a3_recv=(2, n, SECTIONS),
        y_send=(2,),
        y_recv=(2,),
        z_send=(4, n, n),
        z_recv=(4, n),
        p_send=(4, n),
        p_recv=(4, n),
        ag_send=(8, 2, SECTIONS),
        ag_recv=(8, 2, SECTIONS),
        rs_send=(8, 2, SECTIONS),
        rs_recv=(8, 2, SECTIONS),
        fo_send=(2, 2),
        fo_recv=(2, 2),
        r1_send=(2, 2),
        r1_recv=(2, 2),
        r2_send=(2, 2, n),
        r2_recv=(2, 2, n),
        r4_send=(2,),
        r4_recv=(2,),
        g1_send=(2, SECTIONS),
        g1_recv=(2, SECTIONS),
        g2_send=(2, n),
        g2_recv=(2, n),
        g3_send=(2, 2),
        g3_recv=(SECTIONS,),
        sga_send=(SECTIONS,),
        sga_recv=(SECTIONS,),
        sgb_send=(NO,),
        sgb_recv=(NO,),
    )
    names = [*inputs, *outputs, *scratch, *semaphores]
    vmem = pl.BlockSpec(memory_space=pltpu.VMEM)
    hbm = pl.BlockSpec(memory_space=pl.ANY)
    smem = pl.BlockSpec(memory_space=pltpu.SMEM)
    shapes = [jax.ShapeDtypeStruct(*spec) for spec in outputs.values()]
    results = pl.pallas_call(
        make_kernel(cfg, names),
        out_shape=shapes,
        in_specs=[smem, hbm, vmem, hbm, hbm, vmem, hbm, vmem, hbm, hbm],
        out_specs=[vmem] * len(outputs),
        scratch_shapes=[pltpu.VMEM(*spec) for spec in scratch.values()]
        + [dma(shape) for shape in semaphores.values()],
        compiler_params=pltpu.CompilerParams(
            collective_id=0, has_side_effects=True, vmem_limit_bytes=63 * 2**20
        ),
        name="layers",
    )(*inputs.values())
    count = len(shapes)

    def hand_over(*refs):
        given, out, held = refs[:count], refs[count : 2 * count], refs[2 * count : 3 * count]
        loads = [pltpu.make_async_copy(given[k], held[k], refs[-2].at[k]) for k in range(count)]
        stores = [pltpu.make_async_copy(held[k], out[k], refs[-1].at[k]) for k in range(count)]
        for copy in loads:
            copy.start()
        for load, store in zip(loads, stores):
            load.wait()
            store.start()
        for copy in stores:
            copy.wait()

    return pl.pallas_call(
        hand_over,
        out_shape=shapes,
        in_specs=[hbm] * count,
        out_specs=[hbm] * count,
        scratch_shapes=[pltpu.VMEM(*spec) for spec in outputs.values()]
        + [dma((count,)), dma((count,))],
        compiler_params=pltpu.CompilerParams(vmem_limit_bytes=63 * 2**20),
        name="outputs",
    )(*results)


def shards(
    layer_input,
    out_cotangent,
    lengths,
    qkv_weight,
    qv_bias,
    out_weight,
    up_weight,
    up_bias,
    down_weight,
    norm_vectors,
):
    section_count = lax.axis_size("section")
    dp_count = lax.axis_size("dp")
    L, D = layer_input.shape[2:]
    sequences = layer_input.shape[0] * layer_input.shape[1]
    assert section_count == SECTIONS and sequences == 2
    F = out_weight.shape[1] * dp_count
    U2 = up_weight.shape[2]
    heads = F // HEAD_DIM
    outer = max(
        k
        for k in range(2, dp_count + 1, 2)
        if dp_count % k == 0 and D % (16 * k) == 0 and U2 % (32 * k) == 0 and F % (8 * k) == 0
    )
    inner = dp_count // outer
    groups = [[g * inner + k for k in range(inner)] for g in range(outer)]

    def joined(block, axis=0):
        if inner == 1:
            return block
        block = block.astype(BF16)
        block = lax.all_gather(block, "dp", axis=axis, tiled=True, axis_index_groups=groups)
        return block.astype(F32)

    def own_share(block, axis=0):
        if inner == 1:
            return block
        return lax.psum_scatter(
            block, "dp", scatter_dimension=axis, tiled=True, axis_index_groups=groups
        )

    shard_rows = D // outer + F // outer
    cfg = types.SimpleNamespace(
        width=D,
        length=L,
        units=U2 // 2,
        features=F,
        packed=-(-3 * F // 256) * 256,
        outer=outer,
        inner=inner,
        heads=heads,
        up_rows=D // outer,
        down_rows=U2 // outer // 2,
        out_rows=F // outer,
        att_rows=-(-shard_rows // (16 * SECTIONS)) * 16 * SECTIONS,
    )
    stream, grad_rows, qkv, qvb, out, up, upb, down, norm, rms = one_step(
        cfg,
        lengths.reshape(1, 2),
        joined(qkv_weight[0]),
        joined(qv_bias, 1),
        joined(out_weight[0]),
        joined(up_weight[0]),
        joined(up_bias, 1),
        joined(down_weight[0]),
        joined(norm_vectors[0], 1)[:, None],
        layer_input.reshape(2, L, D),
        out_cotangent.reshape(2, L, D),
    )
    rows_shape = layer_input.shape[:2] + (L // SECTIONS, D)
    return (
        stream.reshape(rows_shape),
        grad_rows.reshape(rows_shape),
        own_share(qkv)[None],
        own_share(qvb, 1),
        own_share(out)[None],
        own_share(up)[None],
        own_share(upb, 1),
        own_share(down)[None],
        own_share(norm, 2).reshape(1, 3, -1),
        rms.reshape(layer_input.shape[:2] + (1, 2)),
    )


def solution(mesh):
    placed = (
        P(None, "dp", None, None),
        P(None, "dp", None, None),
        P(None, "dp"),
        P("section", "dp", None),
        P("section", "dp"),
        P("section", "dp", None),
        P("section", "dp", None),
        P("section", "dp"),
        P("section", "dp", None),
        P("section", None, "dp"),
    )
    return jax.shard_map(
        shards,
        mesh=mesh,
        in_specs=placed,
        out_specs=(
            P(None, "dp", "section", None),
            P(None, "dp", "section", None),
            P("section", "dp", None),
            P("section", "dp"),
            P("section", "dp", None),
            P("section", "dp", None),
            P("section", "dp"),
            P("section", "dp", None),
            P("section", None, "dp"),
            P(None, "dp", "section", None),
        ),
        check_vma=False,
    )
```

```python
import types

import jax
import jax.numpy as jnp
from jax import lax
from jax.experimental import pallas as pl
from jax.experimental.pallas import tpu as pltpu
from jax.sharding import PartitionSpec as P

F32, BF16 = jnp.float32, jnp.bfloat16
MESH = pl.DeviceIdType.MESH
HEAD_DIM = 32
EPSILON = 1e-05
MASKED = -1e30
SCALE = HEAD_DIM**-0.5
SCALE_2 = SCALE * 1.4426950408889634
SECTIONS = 4
NN = (((1,), (0,)), ((), ()))
NT = (((1,), (1,)), ((), ()))
TN = (((0,), (0,)), ((), ()))


def mm(left, right, dims=NN):
    return lax.dot_general(left, right, dims, preferred_element_type=F32)


def aligned(start, size):
    return pl.ds(pl.multiple_of(start, size), size)


def head_rows(h, heads):
    full = heads // 8 * 8
    low, rest = full * HEAD_DIM, (heads - full) * HEAD_DIM
    high = h // full if rest else 0
    q = h * HEAD_DIM + high * 2 * low
    k = low + h * HEAD_DIM + high * (low + rest)
    v = 2 * low + h * HEAD_DIM + high * 2 * rest
    return tuple(pl.multiple_of(row, HEAD_DIM) for row in (q, k, v))


def to_packed(rows, heads):
    half = rows.shape[-1] // 3
    low = heads // 8 * 8 * HEAD_DIM
    parts = [rows[:, i * half : i * half + low] for i in range(3)]
    parts += [rows[:, i * half + low : (i + 1) * half] for i in range(3)]
    return jnp.concatenate(parts, axis=1)


def from_packed(rows, half, heads):
    low = heads // 8 * 8 * HEAD_DIM
    rest = half - low
    parts = []
    for i in range(3):
        parts.append(rows[:, i * low : (i + 1) * low])
        parts.append(rows[:, 3 * low + i * rest : 3 * low + (i + 1) * rest])
    return jnp.concatenate(parts, axis=1)


def lanes_to(rows, width):
    if rows.shape[1] == width:
        return rows
    return jnp.concatenate([rows, jnp.zeros((rows.shape[0], width - rows.shape[1]), F32)], axis=1)


def normed_rows(h, gain, shift):
    mean = jnp.mean(h, axis=-1, keepdims=True)
    centred = h - mean
    spread = jnp.mean(centred * centred, axis=-1, keepdims=True)
    inverse = lax.rsqrt(spread + EPSILON)
    return centred * inverse, inverse, centred * inverse * gain + shift


def make_kernel(cfg, names):
    c_ = cfg
    D, L, U, F, W = c_.width, c_.length, c_.units, c_.features, c_.packed
    Q = L // SECTIONS
    NO, n, inner, heads = c_.outer, c_.outer // 2, c_.inner, c_.heads
    ru, rd, ro = c_.up_rows, c_.down_rows, c_.out_rows
    ra, rp = c_.att_rows, c_.att_rows // SECTIONS
    wide = max(U, W)
    low = heads // 8 * 8 * HEAD_DIM
    rest = F - low

    def kernel(*refs):
        R = types.SimpleNamespace(**dict(zip(names, refs)))
        s = lax.axis_index("section")
        y, x = s // 2, s % 2
        dp = lax.axis_index("dp")
        o, i = dp // inner, dp % inner
        zz, c = o // 2, o % 2
        other_x, other_y = s + 1 - 2 * x, s + 2 - 4 * y
        mate = o + 1 - 2 * c

        def remote(src, dst, send, recv, section, outer):
            return pltpu.make_async_remote_copy(
                src_ref=src,
                dst_ref=dst,
                send_sem=send,
                recv_sem=recv,
                device_id=(section, outer * inner + i),
                device_id_type=MESH,
            )

        def loop(count, body, first=0):
            def step(k, carry):
                body(k)
                return carry

            lax.fori_loop(first, count, step, 0)

        raw = (R.qkv_w, R.out_w, R.up_w, R.down_w)
        raw_home = (R.o_qkv, R.o_out, R.o_up, R.o_down)
        raw_copies = [
            pltpu.make_async_copy(a, b, R.raw_sem.at[k])
            for k, (a, b) in enumerate(zip(raw, raw_home))
        ]
        for copy in raw_copies:
            copy.start()

        barrier = pltpu.get_barrier_semaphore()

        def greet(section, outer):
            pl.semaphore_signal(
                barrier, inc=1, device_id=(section, outer * inner + i), device_id_type=MESH
            )

        loop(SECTIONS, lambda k: greet((s + k) % SECTIONS, o), 1)
        loop(SECTIONS, lambda k: greet((s + k) % SECTIONS, mate), 1)
        loop(NO, lambda k: greet(s, (o + k) % NO), 1)

        row8 = lax.broadcasted_iota(jnp.int32, (8, wide), 0)
        lane8 = lax.broadcasted_iota(jnp.int32, (8, wide), 1)
        here = row8[:, : R.small_in.shape[1]], lane8[:, : R.small_in.shape[1]]

        def rounded(v):
            return v.astype(BF16).astype(F32)

        R.small_in[...] = jnp.zeros_like(R.small_in)
        for k in range(3):
            R.small_in[k : k + 1, 0:ru] = rounded(R.norm_v[k])
        R.small_in[3:4, 0:ru] = rounded(R.qv_b[...])
        R.small_in[4:5, 0:rd] = rounded(R.up_b[:, 0:rd])
        R.small_in[5:6, 0:rd] = rounded(R.up_b[:, rd : 2 * rd])
        R.len_own[...] = jnp.where(here[1] == 0, R.lens[0, 0], R.lens[0, 1])[:, :128].astype(F32)
        pl.semaphore_wait(barrier, 2 * (SECTIONS - 1) + NO - 1)

        def small_out(k):
            peer = (o + k) % NO
            return remote(
                R.small_in, R.small_a.at[o], R.sma_send.at[k], R.sma_recv.at[o], s, peer
            )

        loop(NO, lambda k: small_out(k).start(), 1)
        R.small_a[o] = R.small_in[...]
        len_copy = remote(R.len_own, R.len_mate, R.len_send.at[0], R.len_recv.at[0], s, mate)
        len_copy.start()

        raw_copies[0].wait()
        raw_copies[1].wait()
        packed = lanes_to(to_packed(R.o_qkv[...], heads), W).astype(BF16)
        R.att_own[pl.ds(0, ru), :] = packed
        bottom = jnp.concatenate([R.o_out[...], jnp.zeros((ra - ru - ro, D), F32)], axis=0)
        R.att_own[pl.ds(ru, ra - ru), :] = lanes_to(bottom, W).astype(BF16)

        def quarter_copy(p):
            return remote(
                R.att_own.at[pl.ds(p * rp, rp)],
                R.watt.at[y, p, aligned(o * rp, rp)],
                R.a1_send.at[p],
                R.a1_recv.at[y, c],
                p,
                2 * zz + x,
            )

        def each_quarter(act, own):
            for p in range(SECTIONS):
                stays = (s == p) & (x == c)

                @pl.when(stays)
                def _(p=p):
                    if own:
                        R.watt[y, p, aligned(o * rp, rp), :] = R.att_own[pl.ds(p * rp, rp), :]

                @pl.when(jnp.logical_not(stays))
                def _(p=p):
                    act(quarter_copy(p))

        each_quarter(lambda copy: copy.start(), True)

        def seq_copy(local):
            if local:
                return pltpu.make_async_copy(R.stream_in.at[y], R.seq_rows, R.load_sem.at[0])
            return remote(
                R.stream_in.at[y], R.seq_rows, R.seq_send.at[0], R.seq_recv.at[0], s, mate
            )

        def cot_copy(m, j, local):
            half = c if local else 1 - c
            src = R.cot_in.at[m, aligned((2 * half + j) * Q, Q)]
            dst = R.grad_ff.at[0, aligned(j * L + (2 * m + c) * Q, Q)]
            if local:
                return pltpu.make_async_copy(src, dst, R.load_sem.at[1 + 2 * m + j])
            return remote(src, dst, R.cot_send.at[m, j], R.cot_recv.at[m, j], s, mate)

        def piece(kind, layer, outer):
            rows = rd if kind else ru
            return (R.wdown if kind else R.wup).at[layer, aligned(outer * rows, rows)]

        def y_copy(kind):
            return remote(
                R.yb_down if kind else R.yb_up,
                piece(kind, y, o),
                R.y_send.at[kind],
                R.y_recv.at[kind],
                other_y,
                o,
            )

        def chips_at(distances, body):
            for distance in distances:
                for sign in (1, -1):
                    q = zz + sign * distance

                    @pl.when((q >= 0) & (q < n))
                    def _(q=q, sign=sign, distance=distance):
                        body(q, sign, distance)

        def relays(distance, sign, body):
            if distance >= 2:
                after = zz - sign

                @pl.when((after >= 0) & (after < n))
                def _():
                    body(after)

        NEAR, FAR = tuple(range(min(2, n - 1), 0, -1)), range(3, n)

        def z_copy(layer, kind, origin, to):
            item = layer * 2 + kind
            part = piece(kind, layer, 2 * origin + c)
            send = R.z_send.at[item, origin, to]
            return remote(part, part, send, R.z_recv.at[item, origin], s, 2 * to + c)

        def mate_copy(layer, kind, q):
            item = layer * 2 + kind
            part = piece(kind, layer, 2 * q + c)
            return remote(part, part, R.p_send.at[item, q], R.p_recv.at[item, q], s, mate)

        def mate_arrival(layer, kind, q):
            item = layer * 2 + kind
            part = piece(kind, layer, 2 * q + 1 - c)
            return remote(part, part, R.p_send.at[item, q], R.p_recv.at[item, q], s, mate)

        def feed_spread(layer):
            for kind in range(2):
                chips_at(NEAR, lambda q, *_: z_copy(layer, kind, zz, q).start())
                mate_copy(layer, kind, zz).start()

        def feed_spread_home(layer):
            @pl.when(y == layer)
            def _():
                feed_spread(layer)

        def feed_spread_away(layer):
            @pl.when(y != layer)
            def _():
                for kind in range(2):
                    src = R.yb_down if kind else R.yb_up
                    remote(
                        src,
                        piece(kind, layer, o),
                        R.y_send.at[kind],
                        R.y_recv.at[kind],
                        other_y,
                        o,
                    ).wait_recv()
                feed_spread(layer)

        def feed_arrivals(layer, distances):
            for kind in range(2):

                def landed(q, sign, distance):
                    z_copy(layer, kind, q, zz).wait_recv()
                    relays(
                        distance, sign, lambda after: z_copy(layer, kind, q, after).start()
                    )
                    mate_copy(layer, kind, q).start()

                chips_at(distances, landed)

        def feed_collect(layer):
            feed_arrivals(layer, FAR)
            for kind in range(2):
                loop(n, lambda q, kind=kind: mate_arrival(layer, kind, q).wait_recv())

        def feed_sent(layer):
            for kind in range(2):
                chips_at(NEAR, lambda q, *_: z_copy(layer, kind, zz, q).wait_send())
                for distances in (NEAR, FAR):
                    chips_at(
                        distances,
                        lambda q, sign, distance: relays(
                            distance,
                            sign,
                            lambda after: z_copy(layer, kind, q, after).wait_send(),
                        ),
                    )
                loop(n, lambda q, kind=kind: mate_copy(layer, kind, q).wait_send())

        def att_block(layer, p, q):
            return R.watt.at[layer, p, aligned(q * 2 * rp, 2 * rp)]

        def att_z_copy(layer, origin, to):
            part = att_block(layer, s, origin)
            send = R.a2_send.at[layer, origin, to]
            return remote(part, part, send, R.a2_recv.at[layer, origin], s, 2 * to + c)

        def att_plane_copy(layer, q, way):
            part = att_block(layer, s, q)
            to = other_y if way else other_x
            return remote(
                part, part, R.a3_send.at[layer, q, way], R.a3_recv.at[layer, q, way], to, o
            )

        def att_plane_half(layer, q, way):
            src, to = (other_y, other_x) if way else (other_x, other_y)
            part = R.watt.at[layer, src, aligned((2 * q + way) * rp, rp)]
            return remote(
                part, part, R.a4_send.at[layer, q, way], R.a4_recv.at[layer, q, way], to, o
            )

        def att_plane_start(layer, q):
            for way in range(2):
                att_plane_copy(layer, q, way).start()

        def att_plane_relay(layer, q):
            for way in range(2):
                src = other_y if way else other_x
                part = att_block(layer, src, q)
                remote(
                    part,
                    part,
                    R.a3_send.at[layer, q, way],
                    R.a3_recv.at[layer, q, way],
                    src,
                    o,
                ).wait_recv()
                att_plane_half(layer, q, way).start()

        def att_spread(layer):
            for core in range(2):
                mine = (s == 2 * layer + c) & (c == core)

                @pl.when(jnp.logical_not(mine))
                def _(core=core):
                    remote(
                        R.att_own.at[pl.ds(0, rp)],
                        R.watt.at[layer, s, aligned((2 * zz + core) * rp, rp)],
                        R.a1_send.at[0],
                        R.a1_recv.at[layer, core],
                        2 * layer + c,
                        2 * zz + core,
                    ).wait_recv()

            chips_at(reach(layer), lambda q, *_: att_z_copy(layer, zz, q).start())
            att_plane_start(layer, zz)

        def reach(layer):
            return NEAR if layer else tuple(range(1, n))

        def att_onward(layer, distances):
            def landed(q, sign, distance):
                att_z_copy(layer, q, zz).wait_recv()
                if layer:
                    relays(distance, sign, lambda after: att_z_copy(layer, q, after).start())
                att_plane_start(layer, q)

            chips_at(distances, landed)

        def att_sent(layer):
            chips_at(reach(layer), lambda q, *_: att_z_copy(layer, zz, q).wait_send())
            if layer:
                for distances in (NEAR, FAR):
                    chips_at(
                        distances,
                        lambda q, sign, distance: relays(
                            distance,
                            sign,
                            lambda after: att_z_copy(layer, q, after).wait_send(),
                        ),
                    )

            def plane_sent(q):
                for way in range(2):
                    att_plane_copy(layer, q, way).wait_send()
                    att_plane_half(layer, q, way).wait_send()

            loop(n, plane_sent)

        def att_plane_onward(layer, distances):
            chips_at(distances, lambda q, *_: att_plane_relay(layer, q))

        def att_collect(layer):
            def block(q):
                for way in range(2):
                    part = R.watt.at[layer, 3 - s, aligned((2 * q + way) * rp, rp)]
                    remote(
                        part,
                        part,
                        R.a4_send.at[layer, q, way],
                        R.a4_recv.at[layer, q, way],
                        other_y,
                        o,
                    ).wait_recv()

            loop(n, block)

            def unpack(k):
                for r in range(0, ru, 16):
                    R.wqkv[layer, aligned(k * ru + r, 16), :] = R.watt[
                        layer, r // rp, aligned(k * rp + r % rp, 16), :
                    ]
                for r in range(0, ro, 16):
                    rows = min(16, ro - r)
                    p, off = (ru + r) // rp, (ru + r) % rp
                    block = R.watt[layer, p, aligned(k * rp + off, 16), :][:, :D].astype(F32)
                    R.wide_rows[aligned(k * ro + r, 8), :] = block[:rows][:8]
                    if rows > 8:
                        R.wide_rows[aligned(k * ro + r + 8, 8), :] = block[8:rows]

            loop(NO, unpack)
            R.wout[layer] = R.wide_rows[pl.ds(0, F), :].astype(BF16)

        att_spread(0)
        att_spread(1)

        raw_copies[2].wait()
        raw_copies[3].wait()
        halves = [
            jnp.concatenate(
                [R.o_up[:, (2 * k + h) * rd : (2 * k + h + 1) * rd] for k in range(NO)], axis=1
            ).astype(BF16)
            for h in range(2)
        ]
        R.wup[y, aligned(o * ru, ru), :] = jnp.where(y == 0, halves[0], halves[1])
        R.yb_up[...] = jnp.where(y == 0, halves[1], halves[0])
        R.wdown[y, aligned(o * rd, rd), :] = R.o_down[aligned(y * rd, rd), :].astype(BF16)
        R.yb_down[...] = R.o_down[aligned((1 - y) * rd, rd), :].astype(BF16)
        for kind in range(2):
            y_copy(kind).start()
        feed_spread_home(0)

        @pl.when(x == c)
        def _():
            seq_copy(True).start()
            seq_copy(False).start()

        for m in range(2):
            for j in range(2):
                cot_copy(m, j, True).start()
                cot_copy(m, j, False).start()

        loop(
            NO,
            lambda k: remote(
                R.small_in,
                R.small_a.at[(o + k) % NO],
                R.sma_send.at[k],
                R.sma_recv.at[(o + k) % NO],
                s,
                (o + k) % NO,
            ).wait_recv(),
            1,
        )
        table = jnp.zeros((8, wide), F32)
        for k in range(NO):
            part = lanes_to(R.small_a[k], wide)
            narrow = pltpu.roll(part, ru * k, 1) if k else part
            broad = pltpu.roll(part, rd * k, 1) if k else part
            table = table + jnp.where(row8 < 4, narrow, broad)
        moved = jnp.where(lane8 < low, table, 0.0)
        moved += pltpu.roll(jnp.where((lane8 >= low) & (lane8 < F), table, 0.0), 2 * low, 1)
        moved += pltpu.roll(
            jnp.where((lane8 >= F) & (lane8 < F + low), table, 0.0), 2 * low - F, 1
        )
        moved += pltpu.roll(
            jnp.where((lane8 >= F + low) & (lane8 < 2 * F), table, 0.0), 2 * low + 2 * rest - F, 1
        )
        table = jnp.where(row8 == 3, moved, table)
        R.small_own[...] = table
        R.small_b[s] = table

        def small_b_copy(k, of):
            return remote(
                R.small_own,
                R.small_b.at[of],
                R.smb_send.at[k],
                R.smb_recv.at[of],
                (s + k) % SECTIONS,
                o,
            )

        loop(SECTIONS, lambda k: small_b_copy(k, s).start(), 1)

        def first_blocks(k):
            q = (zz + k) % n
            att_z_copy(0, q, zz).wait_recv()
            att_plane_start(0, q)
            att_plane_relay(0, (zz + k - 1) % n)

        loop(n, first_blocks, 1)
        feed_spread_away(0)
        att_plane_relay(0, (zz + n - 1) % n)
        loop(SECTIONS, lambda k: small_b_copy(k, (s + k) % SECTIONS).wait_recv(), 1)

        R.small_grad[...] = jnp.zeros_like(R.small_grad)
        def note_rows(block, index, row):
            R.small_grad[block] += jnp.where(row8 == index, lanes_to(row, wide), 0.0)


        @pl.when(x == c)
        def _():
            seq_copy(True).wait()

        @pl.when(x != c)
        def _():
            seq_copy(False).wait_recv()

        gain0 = R.small_b[0, 0:1, :D]
        shift0 = R.small_b[0, 1:2, :D]

        def first_norm(k):
            rows = aligned(k * Q, Q)
            _, _, out = normed_rows(R.seq_rows[rows, :].astype(F32), gain0, shift0)
            R.norm_at[0, rows, :] = out.astype(BF16)

        loop(L // Q, first_norm)
        R.hid_rows[0] = R.seq_rows[aligned(c * 2 * Q, 2 * Q), :]
        len_copy.wait_recv()
        tile = jnp.where(x == c, R.len_own[...], R.len_mate[...])
        tile = jnp.where((row8[:, :128] == 0) & (lane8[:, :128] == y), tile, 0.0)
        length_here = jnp.sum(jnp.sum(tile, axis=1, keepdims=True), axis=0, keepdims=True)
        length_here = length_here.astype(jnp.int32)
        def rows_copy(phase, m, src, dst, slot, to):
            return remote(
                src, dst, R.ag_send.at[phase, m, slot], R.ag_recv.at[phase, m, s], to, o
            )

        def share_all(phase, m, buf):
            part = buf.at[aligned(m * L + s * Q, Q)]
            return lambda k: rows_copy(phase, m, part, part, k, (s + k) % SECTIONS)

        def share_mate(phase, m, buf):
            part = buf.at[aligned((2 * c + m) * Q, Q)]
            return remote(
                part, part, R.ag_send.at[phase, m, 0], R.ag_recv.at[phase, m, c], s, mate
            )

        def arrival(phase, m, buf, base, k):
            src = (s + k) % SECTIONS
            part = buf.at[aligned(base + src * Q, Q)]
            return remote(
                part, part, R.ag_send.at[phase, m, k], R.ag_recv.at[phase, m, src], src, o
            )

        def send_rows(phase, attention, m, buf, value):
            if attention:
                buf[aligned((2 * c + m) * Q, Q), :] = value
                share_mate(phase, m, buf).start()
            else:
                buf[aligned(m * L + s * Q, Q), :] = value
                copies = share_all(phase, m, buf)
                loop(SECTIONS, lambda k: copies(k).start(), 1)

        def finish_send_rows(phase, attention, m, buf):
            if attention:
                share_mate(phase, m, buf).wait_send()
            else:
                copies = share_all(phase, m, buf)
                loop(SECTIONS, lambda k: copies(k).wait_send(), 1)

        def await_rows(phase, attention, m, buf):
            if attention:
                for j in range(2):
                    part = buf.at[aligned((2 * (1 - c) + j) * Q, Q)]
                    remote(
                        part, part, R.ag_send.at[phase, j, 0], R.ag_recv.at[phase, j, 1 - c], s, mate
                    ).wait_recv()
            else:
                loop(SECTIONS, lambda k: arrival(phase, m, buf, m * L, k).wait_recv(), 1)

        def sum_slot(phase):
            return 0 if phase < 4 else 1

        def part_copy(phase, m, base, k):
            to = (s + k) % SECTIONS
            return remote(
                R.parts.at[aligned(base + to * Q, Q)],
                R.sums.at[sum_slot(phase), s, m],
                R.rs_send.at[phase, m, k],
                R.rs_recv.at[phase, m, s],
                to,
                o,
            )

        def mate_part(phase, j):
            return remote(
                R.parts.at[aligned((2 * (1 - c) + j) * Q, Q)],
                R.sums.at[sum_slot(phase), c, j],
                R.rs_send.at[phase, j, 0],
                R.rs_recv.at[phase, j, c],
                s,
                mate,
            )

        def send_parts(phase, attention, m):
            slot = sum_slot(phase)
            if attention:
                for j in range(2):
                    mate_part(phase, j).start()
                    R.sums[slot, c, j] = R.parts[aligned((2 * c + j) * Q, Q), :]
            else:
                loop(SECTIONS, lambda k: part_copy(phase, m, m * L, k).start(), 1)
                R.sums[slot, s, m] = R.parts[aligned(m * L + s * Q, Q), :]

        def finish_send_parts(phase, attention, chunks=(0, 1)):
            for m in chunks:
                if attention:
                    mate_part(phase, m).wait_send()
                else:
                    loop(SECTIONS, lambda k: part_copy(phase, m, m * L, k).wait_send(), 1)

        def part_arrival(phase, m, src):
            return remote(
                R.parts.at[pl.ds(0, Q)],
                R.sums.at[sum_slot(phase), src, m],
                R.rs_send.at[phase, m, 0],
                R.rs_recv.at[phase, m, src],
                s,
                mate,
            )

        def await_parts(phase, attention, m):
            slot = sum_slot(phase)
            if attention:
                part_arrival(phase, m, 1 - c).wait_recv()
                sources = range(2)
            else:
                loop(
                    SECTIONS,
                    lambda k: part_arrival(phase, m, (s + k) % SECTIONS).wait_recv(),
                    1,
                )
                sources = range(SECTIONS)
            total = None
            for src in sources:
                part = R.sums[slot, src, m].astype(F32)
                total = part if total is None else total + part
            return total

        def place_copy(which, j):
            return remote(
                R.finished.at[which, j],
                (R.out_grad_rows if which else R.out_stream).at[aligned(y * Q, Q)],
                R.fo_send.at[which, j],
                R.fo_recv.at[which, y],
                2 * c + j,
                2 * zz + x,
            )

        def place_rows(which, j, value):
            stays = (s == 2 * c + j) & (x == c)
            R.finished[which, j] = value

            @pl.when(stays)
            def _():
                (R.out_grad_rows if which else R.out_stream)[aligned(y * Q, Q), :] = value

            @pl.when(jnp.logical_not(stays))
            def _():
                place_copy(which, j).start()

        def finish_place(which):
            for j in range(2):
                stays = (s == 2 * c + j) & (x == c)

                @pl.when(jnp.logical_not(stays))
                def _(j=j):
                    place_copy(which, j).wait_send()

            for m in range(2):
                mine = (s == 2 * m + c) & (y == c)

                @pl.when(jnp.logical_not(mine))
                def _(m=m):
                    remote(
                        R.finished.at[which, 0],
                        (R.out_grad_rows if which else R.out_stream).at[pl.ds(m * Q, Q)],
                        R.fo_send.at[which, 0],
                        R.fo_recv.at[which, m],
                        2 * m + c,
                        2 * zz + y,
                    ).wait_recv()

        def close_forward(phase, m):
            e = phase
            attention = e % 2 == 0
            branch = await_parts(phase, attention, m) + R.small_b[e, 2:3, :D]
            mine = pl.ds(m * Q, Q)
            h = R.hid_rows[e, mine, :].astype(F32)
            position = (2 * c + m) * Q + lax.broadcasted_iota(jnp.int32, (Q, 1), 0)
            valid = (position < length_here).astype(F32)
            square_h = jnp.sum(jnp.sum(h * h * valid, axis=1, keepdims=True), axis=0, keepdims=True)
            square_b = jnp.sum(
                jnp.sum(branch * branch * valid, axis=1, keepdims=True), axis=0, keepdims=True
            )
            spot = (2 * zz + x) * 4 + 2 * y
            R.small_grad[e] += jnp.where((row8 == 6) & (lane8 == spot), square_h, 0.0)
            R.small_grad[e] += jnp.where((row8 == 6) & (lane8 == spot + 1), square_b, 0.0)
            fresh = (h + branch).astype(BF16)
            if e == 3:
                place_rows(0, m, fresh)
                return
            R.hid_rows[e + 1, mine, :] = fresh
            _, _, out = normed_rows(
                fresh.astype(F32), R.small_b[e + 1, 0:1, :D], R.small_b[e + 1, 1:2, :D]
            )
            to_attention = (e + 1) % 2 == 0
            buf = (R.norm_at if to_attention else R.norm_ff).at[(e + 1) // 2]
            send_rows(phase + 1, to_attention, m, buf, out.astype(BF16))

        grad_at = (R.seq_rows, R.grad_at)

        def close_backward(phase, m):
            e = 7 - phase
            attention = e % 2 == 0
            d_norm = await_parts(phase, attention, m)
            mine = pl.ds(m * Q, Q)
            unit, inverse, _ = normed_rows(R.hid_rows[e, mine, :].astype(F32), 1.0, 0.0)
            flow = R.grad_rows[mine, :].astype(F32)
            note_rows(e, 0, jnp.sum(d_norm * unit, axis=0, keepdims=True))
            note_rows(e, 1, jnp.sum(d_norm, axis=0, keepdims=True))
            note_rows(e, 2, jnp.sum(flow, axis=0, keepdims=True))
            a = d_norm * R.small_b[e, 0:1, :D]
            mean_a = jnp.mean(a, axis=-1, keepdims=True)
            mean_ax = jnp.mean(a * unit, axis=-1, keepdims=True)
            fresh = (flow + (a - mean_a - unit * mean_ax) * inverse).astype(BF16)
            if e == 0:
                place_rows(1, m, fresh)
                return
            R.grad_rows[mine, :] = fresh
            to_attention = (e - 1) % 2 == 0
            buf = grad_at[(e - 1) // 2] if to_attention else R.grad_ff.at[1]
            send_rows(phase + 1, to_attention, m, buf, fresh)

        ga = (R.hidden.at[1], R.slope.at[1])

        def attention_forward(layer):
            bias = R.small_b[2 * layer + c, 3:4, :W]
            xs = R.norm_at.at[layer]
            for t in range(0, W, 256):
                cols = pl.ds(t, 256)
                lin = mm(xs[...], R.wqkv[layer, :, cols]) + bias[:, t : t + 256]
                R.lin_t[layer, cols, :] = lin.T.astype(BF16)

            def head(h):
                q0, k0, v0 = head_rows(h, heads)
                score = mm(
                    R.lin_t[layer, pl.ds(k0, HEAD_DIM), :],
                    R.lin_t[layer, pl.ds(q0, HEAD_DIM), :],
                    TN,
                )
                live = lax.broadcasted_iota(jnp.int32, score.shape, 0) < length_here
                score = jnp.where(live, score, MASKED)
                top = jnp.max(score, axis=0, keepdims=True)
                powers = jnp.exp2((score - top) * SCALE_2)
                total = jnp.sum(powers, axis=0, keepdims=True)
                probs = (powers * (1.0 / total)).astype(BF16)
                R.log_total[layer, h] = top * SCALE_2 + jnp.log2(total)
                mixed = mm(R.lin_t[layer, pl.ds(v0, HEAD_DIM), :], probs)
                R.att_t[layer, aligned(h * HEAD_DIM, HEAD_DIM), :] = mixed.astype(BF16)

            def pair(h):
                head(2 * h)
                head(2 * h + 1)

            loop(heads // 2, pair)
            if heads % 2:
                head(heads - 1)
            R.parts[pl.ds(0, L), :] = mm(R.att_t[layer], R.wout[layer], TN).astype(BF16)

        def attention_back_heads(layer):
            g = grad_at[layer]
            R.d_att_t[...] = mm(R.wout[layer], g[...], NT).astype(BF16)

            def head(h):
                q0, k0, v0 = head_rows(h, heads)
                q_t = R.lin_t[layer, pl.ds(q0, HEAD_DIM), :]
                k_t = R.lin_t[layer, pl.ds(k0, HEAD_DIM), :]
                v_t = R.lin_t[layer, pl.ds(v0, HEAD_DIM), :]
                d_a = R.d_att_t[aligned(h * HEAD_DIM, HEAD_DIM), :]
                score = mm(k_t, q_t, TN)
                live = lax.broadcasted_iota(jnp.int32, score.shape, 0) < length_here
                probs = jnp.where(live, jnp.exp2(score * SCALE_2 - R.log_total[layer, h]), 0.0)
                d_probs = mm(v_t, d_a, TN)
                product = probs * d_probs
                inner_sum = jnp.sum(product, axis=0, keepdims=True)
                d_score = ((product - probs * inner_sum) * SCALE).astype(BF16)
                R.d_lin_t[pl.ds(q0, HEAD_DIM), :] = mm(k_t, d_score).astype(BF16)
                R.d_lin_t[pl.ds(k0, HEAD_DIM), :] = mm(q_t, d_score, NT).astype(BF16)
                R.d_lin_t[pl.ds(v0, HEAD_DIM), :] = mm(d_a, probs.astype(BF16), NT).astype(BF16)

            def pair(h):
                head(2 * h)
                head(2 * h + 1)

            loop(heads // 2, pair)
            if heads % 2:
                head(heads - 1)

        def attention_back_rows(layer):
            for t in range(0, W, 256):
                cols = pl.ds(t, 256)
                part = mm(R.d_lin_t[cols, :], R.wqkv[layer, :, cols], (((0,), (1,)), ((), ())))
                if t == 0:
                    R.acc[...] = part
                else:
                    R.acc[...] += part
            R.parts[pl.ds(0, L), :] = R.acc[...].astype(BF16)

        def attention_back_out(layer):
            stage = 1 - layer
            R.wide_rows[pl.ds(0, F), :] = mm(R.att_t[layer], grad_at[layer][...])

            def out_rows(k):
                for r in range(ru, ra, 16):
                    top_half = R.wide_rows[aligned(k * ro + r - ru, 8), :]
                    low_half = R.wide_rows[aligned(k * ro + r - ru + 8, 8), :]
                    block = jnp.concatenate([top_half, low_half], axis=0)
                    place = aligned(r // rp * NO * rp + k * rp + r % rp, 16)
                    ga[stage][place, 0:D] = block.astype(BF16)

            loop(NO, out_rows)

        def attention_back_weights(layer):
            stage = 1 - layer
            sums = []
            for t in range(0, W, 256):
                cols = pl.ds(t, 256)
                d_lin = R.d_lin_t[cols, :].T
                sums.append(jnp.sum(d_lin.astype(F32), axis=0, keepdims=True))
                d_w = mm(R.norm_at[layer], d_lin, TN).astype(BF16)
                for k in range(NO):
                    for r in range(0, ru, 16):
                        place = pl.ds(r // rp * NO * rp + k * rp + r % rp, 16)
                        ga[stage][place, cols] = d_w[k * ru + r : k * ru + r + 16]
            note_rows(2 * layer + c, 3, jnp.concatenate(sums, axis=1))

        def feed_bias(layer):
            block = R.small_b[2 * layer + x]
            return jnp.where(y == 0, block[4:5], block[5:6])[:, :U]

        def feed_up(layer, m):
            bias = feed_bias(layer)

            def rows_step(r):
                rows = aligned(m * L + r * Q, Q)
                pre = mm(R.norm_ff[layer, rows, :], R.wup[layer]) + bias
                cdf = 0.5 + 0.5 * lax.erf(pre * 0.7071067811865476)
                density = jnp.exp(pre * pre * -0.5) * 0.3989422804014327
                R.hidden[layer, rows, :] = (pre * cdf).astype(BF16)
                R.slope[layer, rows, :] = (cdf + pre * density).astype(BF16)

            loop(SECTIONS, rows_step)

        def feed_down(layer, m):
            rows = pl.ds(m * L, L)
            R.parts[rows, :] = mm(R.hidden[layer, rows, :], R.wdown[layer]).astype(BF16)

        def feed_back_rows(layer, m):
            rows = pl.ds(m * L, L)
            g = R.grad_ff.at[0 if layer == 1 else 1, rows]
            tile = U // 2
            for j in range(2):
                cols = pl.ds(j * tile, tile)
                d_hidden = mm(g[...], R.wdown[layer, cols, :], NT)
                d_pre = (d_hidden * R.slope[layer, rows, cols].astype(F32)).astype(BF16)
                R.slope[layer, rows, cols] = d_pre
                part = mm(d_pre, R.wup[layer, :, cols], NT)
                if j == 0:
                    R.acc[...] = part
                else:
                    R.parts[rows, :] = (R.acc[...] + part).astype(BF16)

        def feed_back_weights(layer):
            xs = R.norm_ff.at[layer]
            g = R.grad_ff.at[0 if layer == 1 else 1]
            tile = U // 2
            owners = tile // rd
            sums = []
            for j in range(2):
                cols = pl.ds(j * tile, tile)
                d_pre = R.slope[layer, :, cols]
                d_down = mm(R.hidden[layer, :, cols], g[...], TN).astype(BF16)
                for k in range(owners):
                    owner = j * owners + k
                    R.sb_down[owner % 2, pl.ds(owner // 2 * rd, rd), :] = d_down[
                        k * rd : (k + 1) * rd
                    ]
                d_up = mm(xs[...], d_pre, TN).astype(BF16)
                for k in range(NO):
                    R.sb_up[k % 2, pl.ds(k // 2 * ru, ru), cols] = d_up[k * ru : (k + 1) * ru]
                sums.append(jnp.sum(d_pre.astype(F32), axis=0, keepdims=True))
            note_rows(2 * layer + x, 4 + y, jnp.concatenate(sums, axis=1))

        z_up, z_down = (R.zb_up, R.wup.at[1]), (R.zb_down, R.norm_ff.at[1])
        FEED_GRADS = (
            (0, R.sb_up, R.rb_up, R.mb_up, z_up, R.yb_up, R.yr_up, ru),
            (1, R.sb_down, R.rb_down, R.mb_down, z_down, R.yb_down, R.yr_down, rd),
        )

        def mate_grads(stage):
            return [
                remote(sb.at[1 - c], rb, R.r1_send.at[stage, a], R.r1_recv.at[stage, a], s, mate)
                for a, sb, rb, *_ in FEED_GRADS
            ]

        def z_grads(stage, k):
            q = (zz + k) % n
            return [
                remote(
                    mb.at[aligned(q * rows, rows)],
                    zb[stage].at[aligned(zz * rows, rows)],
                    R.r2_send.at[stage, a, q],
                    R.r2_recv.at[stage, a, zz],
                    s,
                    2 * q + c,
                )
                for a, sb, rb, mb, zb, yb, yr, rows in FEED_GRADS
            ]

        def feed_to_mate(stage):
            for copy in mate_grads(stage):
                copy.start()

        def finish_feed_z(stage):
            loop(n, lambda k: [copy.wait_send() for copy in z_grads(stage, k)], 1)

        def feed_along_z(stage):
            for copy in mate_grads(stage):
                copy.wait()
            if stage:
                finish_feed_z(0)
            for a, sb, rb, mb, zb, yb, yr, rows in FEED_GRADS:

                def add(q, sb=sb, rb=rb, mb=mb, rows=rows):
                    part = aligned(q * rows, rows)
                    both = sb[c, part, :].astype(F32) + rb[part, :].astype(F32)
                    mb[part, :] = both.astype(BF16)

                loop(n, add)
            loop(n, lambda k: [copy.start() for copy in z_grads(stage, k)], 1)

        def y_grad(a, yb, yr):
            return remote(yb, yr, R.r4_send.at[a], R.r4_recv.at[a], other_y, o)

        def keep_half(a, h, value):
            if a:
                R.o_down[pl.ds(h * rd, rd), :] = value
                return
            for k in range(NO):
                R.o_up[:, (2 * k + h) * rd : (2 * k + h + 1) * rd] = value[:, k * rd : (k + 1) * rd]

        def feed_owned(stage):
            layer = 1 - stage
            for a, sb, rb, mb, zb, yb, yr, rows in FEED_GRADS:

                def landed(k, a=a, zb=zb, mb=mb, rows=rows):
                    q = (zz + k) % n
                    remote(
                        mb.at[pl.ds(0, rows)],
                        zb[stage].at[aligned(q * rows, rows)],
                        R.r2_send.at[stage, a, q],
                        R.r2_recv.at[stage, a, q],
                        s,
                        2 * q + c,
                    ).wait_recv()

                loop(n, landed, 1)
                total = mb[aligned(zz * rows, rows), :].astype(F32)
                for k in range(1, n):
                    total = total + zb[stage][aligned((zz + k) % n * rows, rows), :].astype(F32)

                @pl.when(y == layer)
                def _(a=a, total=total):
                    keep_half(a, layer, total)

                @pl.when(y != layer)
                def _(a=a, yb=yb, yr=yr, total=total):
                    yb[...] = total.astype(BF16)
                    y_grad(a, yb, yr).start()

        def feed_home():
            for a, sb, rb, mb, zb, yb, yr, rows in FEED_GRADS:
                y_grad(a, yb, yr).wait()
                for h in range(2):

                    @pl.when(y == 1 - h)
                    def _(a=a, h=h, yr=yr):
                        keep_half(a, h, yr[...].astype(F32))

        att_rows = NO * rp

        def plane_grad(stage, k, q):
            to = (s + k) % SECTIONS
            return remote(
                ga[stage].at[aligned(to * att_rows + q * 2 * rp, 2 * rp), pl.ds(0, W)],
                R.watt.at[stage, s, aligned(q * 2 * rp, 2 * rp)],
                R.g1_send.at[stage, k, q],
                R.g1_recv.at[stage, s, q],
                to,
                o,
            )

        def each_plane_grad(stage, act):
            def block(j):
                q = (zz + j) % n
                loop(SECTIONS, lambda k: act(plane_grad(stage, k, q)), 1)

            loop(n + 1, block, 1)

        def att_to_plane(stage):
            each_plane_grad(stage, lambda copy: copy.start())

        def finish_att_plane(stage):
            each_plane_grad(stage, lambda copy: copy.wait_send())

        def att_z_grad(stage, k):
            q = (zz + k) % n
            return remote(
                R.gs.at[stage, aligned(q * 2 * rp, 2 * rp)],
                R.gz.at[stage, zz],
                R.g2_send.at[stage, q],
                R.g2_recv.at[stage, zz],
                s,
                2 * q + c,
            )

        def finish_att_z(stage):
            loop(n, lambda k: att_z_grad(stage, k).wait_send(), 1)

        def att_along_z(stage, first=1, last=n):
            def block(j):
                q = (zz + j) % n
                part = aligned(q * 2 * rp, 2 * rp)

                def landed(k):
                    src = (s + k) % SECTIONS
                    remote(
                        ga[stage].at[aligned(q * 2 * rp, 2 * rp), pl.ds(0, W)],
                        R.watt.at[stage, src, part],
                        R.g1_send.at[stage, k, q],
                        R.g1_recv.at[stage, src, q],
                        src,
                        o,
                    ).wait_recv()

                loop(SECTIONS, landed, 1)
                own = aligned(s * att_rows + q * 2 * rp, 2 * rp)
                total = ga[stage][own, 0:W].astype(F32)
                for k in range(1, SECTIONS):
                    total = total + R.watt[stage, (s + k) % SECTIONS, part, :].astype(F32)
                R.gs[stage, part, :] = total.astype(BF16)

                @pl.when(q != zz)
                def _():
                    att_z_grad(stage, j).start()

            loop(last + 1, block, first)

        def home_copy(stage, core):
            return remote(
                R.gt.at[stage, pl.ds(core * rp, rp)],
                R.att_own.at[aligned(s * rp, rp)],
                R.g3_send.at[stage, core],
                R.g3_recv.at[s],
                2 * (1 - stage) + c,
                2 * zz + core,
            )

        def each_home(stage, act, own):
            for core in range(2):
                stays = (s == 2 * (1 - stage) + c) & (c == core)

                @pl.when(stays)
                def _(core=core):
                    if own:
                        R.att_own[aligned(s * rp, rp), :] = R.gt[stage, pl.ds(core * rp, rp), :]

                @pl.when(jnp.logical_not(stays))
                def _(core=core):
                    act(home_copy(stage, core))

        def att_owned(stage):
            def landed(k):
                q = (zz + k) % n
                remote(
                    R.gs.at[stage, pl.ds(0, 2 * rp)],
                    R.gz.at[stage, q],
                    R.g2_send.at[stage, q],
                    R.g2_recv.at[stage, q],
                    s,
                    2 * q + c,
                ).wait_recv()

            loop(n, landed, 1)
            total = R.gs[stage, aligned(zz * 2 * rp, 2 * rp), :].astype(F32)
            for k in range(1, n):
                total = total + R.gz[stage, (zz + k) % n].astype(F32)
            R.gt[stage] = total.astype(BF16)
            each_home(stage, lambda copy: copy.start(), True)

        def att_home():
            for p in range(SECTIONS):
                mine = (s == p) & (x == c)

                @pl.when(jnp.logical_not(mine))
                def _(p=p):
                    remote(
                        R.gt.at[0, pl.ds(0, rp)],
                        R.att_own.at[pl.ds(p * rp, rp)],
                        R.g3_send.at[0, 0],
                        R.g3_recv.at[p],
                        p,
                        2 * zz + x,
                    ).wait_recv()

            rows = R.att_own[pl.ds(0, ru), :].astype(F32)
            R.o_qkv[...] = from_packed(rows, F, heads)
            rows = R.att_own[pl.ds(ru, ra - ru), :].astype(F32)
            R.o_out[...] = rows[:ro, :D]

        att_collect(0)
        att_onward(1, NEAR)
        attention_forward(0)
        send_parts(0, True, None)
        for m in range(2):
            close_forward(0, m)
        feed_arrivals(0, NEAR)
        feed_spread_home(1)
        feed_spread_away(1)
        att_onward(1, FAR)
        feed_collect(0)
        finish_send_parts(0, True)
        await_rows(1, False, 0, R.norm_ff.at[0])
        feed_up(0, 0)
        feed_down(0, 0)
        send_parts(1, False, 0)
        att_plane_relay(1, zz)
        att_plane_onward(1, NEAR)
        await_rows(1, False, 1, R.norm_ff.at[0])
        feed_up(0, 1)
        feed_down(0, 1)
        send_parts(1, False, 1)
        att_plane_onward(1, FAR)
        close_forward(1, 0)
        feed_arrivals(1, NEAR)
        close_forward(1, 1)
        att_collect(1)
        finish_send_parts(1, False)
        await_rows(2, True, None, R.norm_at.at[1])
        attention_forward(1)
        send_parts(2, True, None)
        for m in range(2):
            close_forward(2, m)
        feed_collect(1)
        finish_send_parts(2, True)
        for m in range(2):
            await_rows(3, False, m, R.norm_ff.at[1])
            feed_up(1, m)

        loop(NO, lambda k: small_out(k).wait_send(), 1)
        loop(SECTIONS, lambda k: small_b_copy(k, s).wait_send(), 1)
        len_copy.wait_send()
        each_quarter(lambda copy: copy.wait_send(), False)

        @pl.when(x == c)
        def _():
            seq_copy(False).wait_send()

        for kind in range(2):
            y_copy(kind).wait_send()
        for layer in range(2):
            att_sent(layer)
            feed_sent(layer)
        for m in range(2):
            finish_send_rows(1, False, m, R.norm_ff.at[0])
            finish_send_rows(2, True, m, R.norm_at.at[1])
            finish_send_rows(3, False, m, R.norm_ff.at[1])
            for j in range(2):
                cot_copy(m, j, True).wait()
                cot_copy(m, j, False).wait_send()
                remote(
                    R.cot_in.at[m, pl.ds(0, Q)],
                    R.grad_ff.at[0, aligned(j * L + (2 * m + 1 - c) * Q, Q)],
                    R.cot_send.at[m, j],
                    R.cot_recv.at[m, j],
                    s,
                    mate,
                ).wait_recv()
        for j in range(2):
            R.grad_rows[pl.ds(j * Q, Q), :] = R.grad_ff[0, aligned(j * L + s * Q, Q), :]

        for m in range(2):
            feed_back_rows(1, m)
            send_parts(4, False, m)
        feed_back_weights(1)
        feed_to_mate(0)
        for m in range(2):
            close_backward(4, m)
        feed_along_z(0)
        finish_send_parts(4, False)
        for m in range(2):
            feed_down(1, m)
            send_parts(3, False, m)
        await_rows(5, True, None, grad_at[1])
        attention_back_heads(1)
        finish_send_parts(3, False, (0,))
        attention_back_rows(1)
        send_parts(5, True, None)
        attention_back_out(1)
        attention_back_weights(1)
        for m in range(2):
            close_backward(5, m)
        for m in range(2):
            close_forward(3, m)
        finish_send_parts(3, False, (1,))
        finish_send_parts(5, True)
        for m in range(2):
            await_rows(6, False, m, R.grad_ff.at[1])
            feed_back_rows(0, m)
            send_parts(6, False, m)
        att_to_plane(0)
        feed_back_weights(0)
        feed_to_mate(1)
        for m in range(2):
            finish_send_rows(5, True, m, grad_at[1])
        close_backward(6, 0)
        feed_owned(0)
        feed_along_z(1)
        close_backward(6, 1)
        finish_send_parts(6, False)
        await_rows(7, True, None, grad_at[0])
        attention_back_out(0)
        attention_back_heads(0)
        attention_back_weights(0)
        att_to_plane(1)
        attention_back_rows(0)
        send_parts(7, True, None)
        att_along_z(0)
        for m in range(2):
            close_backward(7, m)

        def small_grad_copy(k, of):
            to = (s + k) % SECTIONS
            return remote(
                R.small_grad.at[to],
                R.small_sum.at[of],
                R.sga_send.at[k],
                R.sga_recv.at[of],
                to,
                o,
            )

        loop(SECTIONS, lambda k: small_grad_copy(k, s).start(), 1)
        R.small_sum[s] = R.small_grad[s]
        att_along_z(1, 1, 2)
        feed_owned(1)
        att_along_z(1, 3, n)
        loop(SECTIONS, lambda k: small_grad_copy(k, (s + k) % SECTIONS).wait_recv(), 1)
        total = R.small_sum[0]
        for k in range(1, SECTIONS):
            total = total + R.small_sum[k]
        R.small_line[...] = total

        def small_line_copy(k, of):
            peer = (o + k) % NO
            return remote(
                R.small_line, R.small_all.at[of], R.sgb_send.at[k], R.sgb_recv.at[of], s, peer
            )

        loop(NO, lambda k: small_line_copy(k, o).start(), 1)
        R.small_all[o] = total
        att_owned(0)
        feed_home()
        att_owned(1)
        loop(NO, lambda k: small_line_copy(k, (o + k) % NO).wait_recv(), 1)
        total = R.small_all[0]
        for k in range(1, NO):
            total = total + R.small_all[k]

        def back(rows, lanes):
            return pltpu.roll(rows, (wide - lanes) % wide, 1)

        norms = back(total, ru * o)
        for k in range(3):
            R.o_norm[k] = norms[k : k + 1, 0:ru]
        units = back(total, rd * o)
        R.o_upb[:, 0:rd] = units[4:5, 0:rd]
        R.o_upb[:, rd : 2 * rd] = units[5:6, 0:rd]
        first, second, third = 3 * low, 3 * low + 2 * rest, 3 * low + 3 * rest
        plain = jnp.where(lane8 < low, total, 0.0)
        plain += back(jnp.where((lane8 >= first) & (lane8 < first + rest), total, 0.0), 2 * low)
        plain += back(jnp.where((lane8 >= 2 * low) & (lane8 < first), total, 0.0), 2 * low - F)
        plain += back(
            jnp.where((lane8 >= second) & (lane8 < third), total, 0.0), 2 * low + 2 * rest - F
        )
        R.o_qvb[...] = back(plain, ru * o)[3:4, 0:ru]
        squares = back(total, 4 * o)
        for m in range(2):
            count = (R.lens[0, m] * D).astype(F32)
            R.o_rms[m : m + 1, :] = jnp.sqrt(squares[6:7, 2 * m : 2 * m + 2] / count)
        att_home()
        for which in range(2):
            finish_place(which)

        loop(SECTIONS, lambda k: small_grad_copy(k, s).wait_send(), 1)
        loop(NO, lambda k: small_line_copy(k, o).wait_send(), 1)
        for m in range(2):
            finish_send_rows(6, False, m, R.grad_ff.at[1])
            finish_send_rows(7, True, m, grad_at[0])
        finish_send_parts(7, True)
        finish_feed_z(1)
        for stage in range(2):
            finish_att_plane(stage)
            finish_att_z(stage)
            each_home(stage, lambda copy: copy.wait_send(), False)

    return kernel


def one_step(cfg, lens, qkv, qv_b, out, up, up_b, down, norm, stream, cotangent):
    D, L, U, F, W = cfg.width, cfg.length, cfg.units, cfg.features, cfg.packed
    Q = L // SECTIONS
    NO, n = cfg.outer, cfg.outer // 2
    ru, rd, ro, ra = cfg.up_rows, cfg.down_rows, cfg.out_rows, cfg.att_rows
    rp = ra // SECTIONS
    wide = max(U, W)
    lanes = -(-max(ru, rd) // 128) * 128
    dma = pltpu.SemaphoreType.DMA
    inputs = dict(
        lens=lens,
        qkv_w=qkv,
        qv_b=qv_b,
        out_w=out,
        up_w=up,
        up_b=up_b,
        down_w=down,
        norm_v=norm,
        stream_in=stream,
        cot_in=cotangent,
    )
    outputs = dict(
        out_stream=((2 * Q, D), BF16),
        out_grad_rows=((2 * Q, D), BF16),
        o_qkv=((ru, 3 * F), F32),
        o_qvb=((1, ru), F32),
        o_out=((ro, D), F32),
        o_up=((ru, 2 * U), F32),
        o_upb=((1, 2 * rd), F32),
        o_down=((2 * rd, D), F32),
        o_norm=((3, 1, ru), F32),
        o_rms=((2, 2), F32),
    )
    scratch = dict(
        small_in=((8, lanes), F32),
        small_a=((NO, 8, lanes), F32),
        small_own=((8, wide), F32),
        small_b=((SECTIONS, 8, wide), F32),
        small_grad=((SECTIONS, 8, wide), F32),
        small_sum=((SECTIONS, 8, wide), F32),
        small_line=((8, wide), F32),
        small_all=((NO, 8, wide), F32),
        len_own=((8, 128), F32),
        len_mate=((8, 128), F32),
        att_own=((ra, W), BF16),
        watt=((2, SECTIONS, NO * rp, W), BF16),
        wqkv=((2, D, W), BF16),
        wout=((2, F, D), BF16),
        wup=((2, D, U), BF16),
        wdown=((2, U, D), BF16),
        hid_rows=((SECTIONS, 2 * Q, D), BF16),
        grad_rows=((2 * Q, D), BF16),
        norm_at=((2, L, D), BF16),
        norm_ff=((2, 2 * L, D), BF16),
        lin_t=((2, W, L), BF16),
        att_t=((2, F, L), BF16),
        log_total=((2, cfg.heads, 1, L), F32),
        hidden=((2, 2 * L, U), BF16),
        slope=((2, 2 * L, U), BF16),
        grad_ff=((2, 2 * L, D), BF16),
        grad_at=((L, D), BF16),
        seq_rows=((L, D), BF16),
        parts=((2 * L, D), BF16),
        sums=((2, SECTIONS, 2, Q, D), BF16),
        finished=((2, 2, Q, D), BF16),
        acc=((L, D), F32),
        wide_rows=((F + 64, D), F32),
        d_att_t=((F, L), BF16),
        d_lin_t=((W, L), BF16),
        sb_up=((2, n * ru, U), BF16),
        rb_up=((n * ru, U), BF16),
        mb_up=((n * ru, U), BF16),
        zb_up=((n * ru, U), BF16),
        yb_up=((ru, U), BF16),
        yr_up=((ru, U), BF16),
        sb_down=((2, n * rd, D), BF16),
        rb_down=((n * rd, D), BF16),
        mb_down=((n * rd, D), BF16),
        zb_down=((n * rd, D), BF16),
        yb_down=((rd, D), BF16),
        yr_down=((rd, D), BF16),
        gs=((2, NO * rp, W), BF16),
        gz=((2, n, 2 * rp, W), BF16),
        gt=((2, 2 * rp, W), BF16),
    )
    semaphores = dict(
        raw_sem=(4,),
        load_sem=(5,),
        sma_send=(NO,),
        sma_recv=(NO,),
        smb_send=(SECTIONS,),
        smb_recv=(SECTIONS,),
        len_send=(1,),
        len_recv=(1,),
        seq_send=(1,),
        seq_recv=(1,),
        cot_send=(2, 2),
        cot_recv=(2, 2),
        a1_send=(SECTIONS,),
        a1_recv=(2, 2),
        a2_send=(2, n, n),
        a2_recv=(2, n),
        a3_send=(2, n, 2),
        a3_recv=(2, n, 2),
        a4_send=(2, n, 2),
        a4_recv=(2, n, 2),
        y_send=(2,),
        y_recv=(2,),
        z_send=(4, n, n),
        z_recv=(4, n),
        p_send=(4, n),
        p_recv=(4, n),
        ag_send=(8, 2, SECTIONS),
        ag_recv=(8, 2, SECTIONS),
        rs_send=(8, 2, SECTIONS),
        rs_recv=(8, 2, SECTIONS),
        fo_send=(2, 2),
        fo_recv=(2, 2),
        r1_send=(2, 2),
        r1_recv=(2, 2),
        r2_send=(2, 2, n),
        r2_recv=(2, 2, n),
        r4_send=(2,),
        r4_recv=(2,),
        g1_send=(2, SECTIONS, n),
        g1_recv=(2, SECTIONS, n),
        g2_send=(2, n),
        g2_recv=(2, n),
        g3_send=(2, 2),
        g3_recv=(SECTIONS,),
        sga_send=(SECTIONS,),
        sga_recv=(SECTIONS,),
        sgb_send=(NO,),
        sgb_recv=(NO,),
    )
    names = [*inputs, *outputs, *scratch, *semaphores]
    vmem = pl.BlockSpec(memory_space=pltpu.VMEM)
    hbm = pl.BlockSpec(memory_space=pl.ANY)
    smem = pl.BlockSpec(memory_space=pltpu.SMEM)
    shapes = [jax.ShapeDtypeStruct(*spec) for spec in outputs.values()]
    results = pl.pallas_call(
        make_kernel(cfg, names),
        out_shape=shapes,
        in_specs=[smem, hbm, vmem, hbm, hbm, vmem, hbm, vmem, hbm, hbm],
        out_specs=[vmem] * len(outputs),
        scratch_shapes=[pltpu.VMEM(*spec) for spec in scratch.values()]
        + [dma(shape) for shape in semaphores.values()],
        compiler_params=pltpu.CompilerParams(
            collective_id=0, has_side_effects=True, vmem_limit_bytes=63 * 2**20
        ),
        name="layers",
    )(*inputs.values())
    count = len(shapes)

    def hand_over(*refs):
        given, out, held = refs[:count], refs[count : 2 * count], refs[2 * count : 3 * count]
        loads = [pltpu.make_async_copy(given[k], held[k], refs[-2].at[k]) for k in range(count)]
        stores = [pltpu.make_async_copy(held[k], out[k], refs[-1].at[k]) for k in range(count)]
        for copy in loads:
            copy.start()
        for load, store in zip(loads, stores):
            load.wait()
            store.start()
        for copy in stores:
            copy.wait()

    return pl.pallas_call(
        hand_over,
        out_shape=shapes,
        in_specs=[hbm] * count,
        out_specs=[hbm] * count,
        scratch_shapes=[pltpu.VMEM(*spec) for spec in outputs.values()]
        + [dma((count,)), dma((count,))],
        compiler_params=pltpu.CompilerParams(vmem_limit_bytes=63 * 2**20),
        name="outputs",
    )(*results)


def shards(
    layer_input,
    out_cotangent,
    lengths,
    qkv_weight,
    qv_bias,
    out_weight,
    up_weight,
    up_bias,
    down_weight,
    norm_vectors,
):
    section_count = lax.axis_size("section")
    dp_count = lax.axis_size("dp")
    L, D = layer_input.shape[2:]
    sequences = layer_input.shape[0] * layer_input.shape[1]
    assert section_count == SECTIONS and sequences == 2
    F = out_weight.shape[1] * dp_count
    U2 = up_weight.shape[2]
    heads = F // HEAD_DIM
    outer = max(
        k
        for k in range(2, dp_count + 1, 2)
        if dp_count % k == 0 and D % (16 * k) == 0 and U2 % (32 * k) == 0 and F % (8 * k) == 0
    )
    inner = dp_count // outer
    groups = [[g * inner + k for k in range(inner)] for g in range(outer)]

    def joined(block, axis=0):
        if inner == 1:
            return block
        block = block.astype(BF16)
        block = lax.all_gather(block, "dp", axis=axis, tiled=True, axis_index_groups=groups)
        return block.astype(F32)

    def own_share(block, axis=0):
        if inner == 1:
            return block
        return lax.psum_scatter(
            block, "dp", scatter_dimension=axis, tiled=True, axis_index_groups=groups
        )

    shard_rows = D // outer + F // outer
    cfg = types.SimpleNamespace(
        width=D,
        length=L,
        units=U2 // 2,
        features=F,
        packed=-(-3 * F // 256) * 256,
        outer=outer,
        inner=inner,
        heads=heads,
        up_rows=D // outer,
        down_rows=U2 // outer // 2,
        out_rows=F // outer,
        att_rows=-(-shard_rows // (16 * SECTIONS)) * 16 * SECTIONS,
    )
    stream, grad_rows, qkv, qvb, out, up, upb, down, norm, rms = one_step(
        cfg,
        lengths.reshape(1, 2),
        joined(qkv_weight[0]),
        joined(qv_bias, 1),
        joined(out_weight[0]),
        joined(up_weight[0]),
        joined(up_bias, 1),
        joined(down_weight[0]),
        joined(norm_vectors[0], 1)[:, None],
        layer_input.reshape(2, L, D),
        out_cotangent.reshape(2, L, D),
    )
    rows_shape = layer_input.shape[:2] + (L // SECTIONS, D)
    return (
        stream.reshape(rows_shape),
        grad_rows.reshape(rows_shape),
        own_share(qkv)[None],
        own_share(qvb, 1),
        own_share(out)[None],
        own_share(up)[None],
        own_share(upb, 1),
        own_share(down)[None],
        own_share(norm, 2).reshape(1, 3, -1),
        rms.reshape(layer_input.shape[:2] + (1, 2)),
    )


def solution(mesh):
    placed = (
        P(None, "dp", None, None),
        P(None, "dp", None, None),
        P(None, "dp"),
        P("section", "dp", None),
        P("section", "dp"),
        P("section", "dp", None),
        P("section", "dp", None),
        P("section", "dp"),
        P("section", "dp", None),
        P("section", None, "dp"),
    )
    return jax.shard_map(
        shards,
        mesh=mesh,
        in_specs=placed,
        out_specs=(
            P(None, "dp", "section", None),
            P(None, "dp", "section", None),
            P("section", "dp", None),
            P("section", "dp"),
            P("section", "dp", None),
            P("section", "dp", None),
            P("section", "dp"),
            P("section", "dp", None),
            P("section", None, "dp"),
            P(None, "dp", "section", None),
        ),
        check_vma=False,
    )
```

```python
import types

import jax
import jax.numpy as jnp
from jax import lax
from jax.experimental import pallas as pl
from jax.experimental.pallas import tpu as pltpu
from jax.sharding import PartitionSpec as P

F32, BF16 = jnp.float32, jnp.bfloat16
MESH = pl.DeviceIdType.MESH
HEAD_DIM = 32
EPSILON = 1e-05
MASKED = -1e30
SCALE = HEAD_DIM**-0.5
SCALE_2 = SCALE * 1.4426950408889634
SECTIONS = 4
NN = (((1,), (0,)), ((), ()))
NT = (((1,), (1,)), ((), ()))
TN = (((0,), (0,)), ((), ()))


def mm(left, right, dims=NN):
    return lax.dot_general(left, right, dims, preferred_element_type=F32)


def aligned(start, size):
    return pl.ds(pl.multiple_of(start, size), size)


def head_rows(h, heads):
    full = heads // 8 * 8
    low, rest = full * HEAD_DIM, (heads - full) * HEAD_DIM
    high = h // full if rest else 0
    q = h * HEAD_DIM + high * 2 * low
    k = low + h * HEAD_DIM + high * (low + rest)
    v = 2 * low + h * HEAD_DIM + high * 2 * rest
    return tuple(pl.multiple_of(row, HEAD_DIM) for row in (q, k, v))


def to_packed(rows, heads):
    half = rows.shape[-1] // 3
    low = heads // 8 * 8 * HEAD_DIM
    parts = [rows[:, i * half : i * half + low] for i in range(3)]
    parts += [rows[:, i * half + low : (i + 1) * half] for i in range(3)]
    return jnp.concatenate(parts, axis=1)


def from_packed(rows, half, heads):
    low = heads // 8 * 8 * HEAD_DIM
    rest = half - low
    parts = []
    for i in range(3):
        parts.append(rows[:, i * low : (i + 1) * low])
        parts.append(rows[:, 3 * low + i * rest : 3 * low + (i + 1) * rest])
    return jnp.concatenate(parts, axis=1)


def lanes_to(rows, width):
    if rows.shape[1] == width:
        return rows
    return jnp.concatenate([rows, jnp.zeros((rows.shape[0], width - rows.shape[1]), F32)], axis=1)


def normed_rows(h, gain, shift):
    mean = jnp.mean(h, axis=-1, keepdims=True)
    centred = h - mean
    spread = jnp.mean(centred * centred, axis=-1, keepdims=True)
    inverse = lax.rsqrt(spread + EPSILON)
    return centred * inverse, inverse, centred * inverse * gain + shift


def make_kernel(cfg, names):
    c_ = cfg
    D, L, U, F, W = c_.width, c_.length, c_.units, c_.features, c_.packed
    Q = L // SECTIONS
    NO, n, inner, heads = c_.outer, c_.outer // 2, c_.inner, c_.heads
    ru, rd, ro = c_.up_rows, c_.down_rows, c_.out_rows
    ra, rp = c_.att_rows, c_.att_rows // SECTIONS
    wide = max(U, W)
    low = heads // 8 * 8 * HEAD_DIM
    rest = F - low

    def kernel(*refs):
        R = types.SimpleNamespace(**dict(zip(names, refs)))
        s = lax.axis_index("section")
        y, x = s // 2, s % 2
        dp = lax.axis_index("dp")
        o, i = dp // inner, dp % inner
        zz, c = o // 2, o % 2
        other_x, other_y = s + 1 - 2 * x, s + 2 - 4 * y
        mate = o + 1 - 2 * c

        def remote(src, dst, send, recv, section, outer):
            return pltpu.make_async_remote_copy(
                src_ref=src,
                dst_ref=dst,
                send_sem=send,
                recv_sem=recv,
                device_id=(section, outer * inner + i),
                device_id_type=MESH,
            )

        def loop(count, body, first=0):
            def step(k, carry):
                body(k)
                return carry

            lax.fori_loop(first, count, step, 0)

        raw = (R.qkv_w, R.out_w, R.up_w, R.down_w)
        raw_home = (R.o_qkv, R.o_out, R.o_up, R.o_down)
        raw_copies = [
            pltpu.make_async_copy(a, b, R.raw_sem.at[k])
            for k, (a, b) in enumerate(zip(raw, raw_home))
        ]
        for copy in raw_copies:
            copy.start()

        barrier = pltpu.get_barrier_semaphore()

        def greet(section, outer):
            pl.semaphore_signal(
                barrier, inc=1, device_id=(section, outer * inner + i), device_id_type=MESH
            )

        loop(SECTIONS, lambda k: greet((s + k) % SECTIONS, o), 1)
        loop(SECTIONS, lambda k: greet((s + k) % SECTIONS, mate), 1)
        loop(NO, lambda k: greet(s, (o + k) % NO), 1)

        row8 = lax.broadcasted_iota(jnp.int32, (8, wide), 0)
        lane8 = lax.broadcasted_iota(jnp.int32, (8, wide), 1)
        here = row8[:, : R.small_in.shape[1]], lane8[:, : R.small_in.shape[1]]

        def rounded(v):
            return v.astype(BF16).astype(F32)

        R.small_in[...] = jnp.zeros_like(R.small_in)
        for k in range(3):
            R.small_in[k : k + 1, 0:ru] = rounded(R.norm_v[k])
        R.small_in[3:4, 0:ru] = rounded(R.qv_b[...])
        R.small_in[4:5, 0:rd] = rounded(R.up_b[:, 0:rd])
        R.small_in[5:6, 0:rd] = rounded(R.up_b[:, rd : 2 * rd])
        R.len_own[...] = jnp.where(here[1] == 0, R.lens[0, 0], R.lens[0, 1])[:, :128].astype(F32)
        pl.semaphore_wait(barrier, 2 * (SECTIONS - 1) + NO - 1)

        def small_out(k):
            peer = (o + k) % NO
            return remote(
                R.small_in, R.small_a.at[o], R.sma_send.at[k], R.sma_recv.at[o], s, peer
            )

        loop(NO, lambda k: small_out(k).start(), 1)
        R.small_a[o] = R.small_in[...]
        len_copy = remote(R.len_own, R.len_mate, R.len_send.at[0], R.len_recv.at[0], s, mate)
        len_copy.start()

        raw_copies[0].wait()
        raw_copies[1].wait()
        packed = lanes_to(to_packed(R.o_qkv[...], heads), W).astype(BF16)
        R.att_own[pl.ds(0, ru), :] = packed
        bottom = jnp.concatenate([R.o_out[...], jnp.zeros((ra - ru - ro, D), F32)], axis=0)
        R.att_own[pl.ds(ru, ra - ru), :] = lanes_to(bottom, W).astype(BF16)

        def quarter_copy(p):
            return remote(
                R.att_own.at[pl.ds(p * rp, rp)],
                R.watt.at[y, p, aligned(o * rp, rp)],
                R.a1_send.at[p],
                R.a1_recv.at[y, c],
                p,
                2 * zz + x,
            )

        def each_quarter(act, own):
            for p in range(SECTIONS):
                stays = (s == p) & (x == c)

                @pl.when(stays)
                def _(p=p):
                    if own:
                        R.watt[y, p, aligned(o * rp, rp), :] = R.att_own[pl.ds(p * rp, rp), :]

                @pl.when(jnp.logical_not(stays))
                def _(p=p):
                    act(quarter_copy(p))

        each_quarter(lambda copy: copy.start(), True)

        def seq_copy(local):
            if local:
                return pltpu.make_async_copy(R.stream_in.at[y], R.seq_rows, R.load_sem.at[0])
            return remote(
                R.stream_in.at[y], R.seq_rows, R.seq_send.at[0], R.seq_recv.at[0], s, mate
            )

        def cot_copy(m, j, local):
            half = c if local else 1 - c
            src = R.cot_in.at[m, aligned((2 * half + j) * Q, Q)]
            dst = R.grad_ff.at[0, aligned(j * L + (2 * m + c) * Q, Q)]
            if local:
                return pltpu.make_async_copy(src, dst, R.load_sem.at[1 + 2 * m + j])
            return remote(src, dst, R.cot_send.at[m, j], R.cot_recv.at[m, j], s, mate)

        def piece(kind, layer, outer):
            rows = rd if kind else ru
            return (R.wdown if kind else R.wup).at[layer, aligned(outer * rows, rows)]

        def y_copy(kind):
            return remote(
                R.yb_down if kind else R.yb_up,
                piece(kind, y, o),
                R.y_send.at[kind],
                R.y_recv.at[kind],
                other_y,
                o,
            )

        def chips_at(distances, body):
            for distance in distances:
                for sign in (1, -1):
                    q = zz + sign * distance

                    @pl.when((q >= 0) & (q < n))
                    def _(q=q, sign=sign, distance=distance):
                        body(q, sign, distance)

        def relays(distance, sign, body):
            if distance >= 2:
                after = zz - sign

                @pl.when((after >= 0) & (after < n))
                def _():
                    body(after)

        NEAR, FAR = tuple(range(min(2, n - 1), 0, -1)), range(3, n)

        def z_copy(layer, kind, origin, to):
            item = layer * 2 + kind
            part = piece(kind, layer, 2 * origin + c)
            send = R.z_send.at[item, origin, to]
            return remote(part, part, send, R.z_recv.at[item, origin], s, 2 * to + c)

        def mate_copy(layer, kind, q):
            item = layer * 2 + kind
            part = piece(kind, layer, 2 * q + c)
            return remote(part, part, R.p_send.at[item, q], R.p_recv.at[item, q], s, mate)

        def mate_arrival(layer, kind, q):
            item = layer * 2 + kind
            part = piece(kind, layer, 2 * q + 1 - c)
            return remote(part, part, R.p_send.at[item, q], R.p_recv.at[item, q], s, mate)

        def feed_spread(layer, kind):
            chips_at(NEAR, lambda q, *_: z_copy(layer, kind, zz, q).start())
            mate_copy(layer, kind, zz).start()

        def feed_spread_home(layer):
            @pl.when(y == layer)
            def _():
                feed_spread(layer, 0)
                feed_spread(layer, 1)

        def feed_spread_away(layer, kind):
            @pl.when(y != layer)
            def _():
                src = R.yb_down if kind else R.yb_up
                remote(
                    src,
                    piece(kind, layer, o),
                    R.y_send.at[kind],
                    R.y_recv.at[kind],
                    other_y,
                    o,
                ).wait_recv()
                feed_spread(layer, kind)

        def feed_arrivals(layer, distances):
            for kind in range(2):

                def landed(q, sign, distance):
                    z_copy(layer, kind, q, zz).wait_recv()
                    relays(
                        distance, sign, lambda after: z_copy(layer, kind, q, after).start()
                    )
                    mate_copy(layer, kind, q).start()

                chips_at(distances, landed)

        def feed_collect(layer):
            feed_arrivals(layer, FAR)
            for kind in range(2):
                loop(n, lambda q, kind=kind: mate_arrival(layer, kind, q).wait_recv())

        def feed_sent(layer):
            for kind in range(2):
                chips_at(NEAR, lambda q, *_: z_copy(layer, kind, zz, q).wait_send())
                for distances in (NEAR, FAR):
                    chips_at(
                        distances,
                        lambda q, sign, distance: relays(
                            distance,
                            sign,
                            lambda after: z_copy(layer, kind, q, after).wait_send(),
                        ),
                    )
                loop(n, lambda q, kind=kind: mate_copy(layer, kind, q).wait_send())

        def att_block(layer, p, q):
            return R.watt.at[layer, p, aligned(q * 2 * rp, 2 * rp)]

        def att_z_copy(layer, origin, to):
            part = att_block(layer, s, origin)
            send = R.a2_send.at[layer, origin, to]
            return remote(part, part, send, R.a2_recv.at[layer, origin], s, 2 * to + c)

        def att_plane_copy(layer, q, way):
            part = att_block(layer, s, q)
            to = other_y if way else other_x
            return remote(
                part, part, R.a3_send.at[layer, q, way], R.a3_recv.at[layer, q, way], to, o
            )

        def plane_half(layer, section, q, way):
            first = rp if layer else rp // 2
            start = q * 2 * rp + (first if way else 0)
            rows = 2 * rp - first if way else first
            return R.watt.at[layer, section, pl.ds(pl.multiple_of(start, 16), rows)]

        def att_plane_half(layer, q, way):
            src, to = (other_y, other_x) if way else (other_x, other_y)
            part = plane_half(layer, src, q, way)
            return remote(
                part, part, R.a4_send.at[layer, q, way], R.a4_recv.at[layer, q, way], to, o
            )

        def att_plane_start(layer, q):
            for way in range(2):
                att_plane_copy(layer, q, way).start()

        def att_plane_relay(layer, q):
            for way in range(2):
                src = other_y if way else other_x
                part = att_block(layer, src, q)
                remote(
                    part,
                    part,
                    R.a3_send.at[layer, q, way],
                    R.a3_recv.at[layer, q, way],
                    src,
                    o,
                ).wait_recv()
                att_plane_half(layer, q, way).start()

        def att_spread(layer):
            for core in range(2):
                mine = (s == 2 * layer + c) & (c == core)

                @pl.when(jnp.logical_not(mine))
                def _(core=core):
                    remote(
                        R.att_own.at[pl.ds(0, rp)],
                        R.watt.at[layer, s, aligned((2 * zz + core) * rp, rp)],
                        R.a1_send.at[0],
                        R.a1_recv.at[layer, core],
                        2 * layer + c,
                        2 * zz + core,
                    ).wait_recv()

            chips_at(reach(layer), lambda q, *_: att_z_copy(layer, zz, q).start())
            att_plane_start(layer, zz)

        def reach(layer):
            return NEAR if layer else tuple(range(1, n))

        def att_onward(layer, distances):
            def landed(q, sign, distance):
                att_z_copy(layer, q, zz).wait_recv()
                if layer:
                    relays(distance, sign, lambda after: att_z_copy(layer, q, after).start())
                att_plane_start(layer, q)

            chips_at(distances, landed)

        def att_sent(layer):
            chips_at(reach(layer), lambda q, *_: att_z_copy(layer, zz, q).wait_send())
            if layer:
                for distances in (NEAR, FAR):
                    chips_at(
                        distances,
                        lambda q, sign, distance: relays(
                            distance,
                            sign,
                            lambda after: att_z_copy(layer, q, after).wait_send(),
                        ),
                    )

            def plane_sent(q):
                for way in range(2):
                    att_plane_copy(layer, q, way).wait_send()
                    att_plane_half(layer, q, way).wait_send()

            loop(n, plane_sent)

        def att_plane_onward(layer, distances):
            chips_at(distances, lambda q, *_: att_plane_relay(layer, q))

        def att_collect(layer):
            def block(q):
                for way in range(2):
                    part = plane_half(layer, 3 - s, q, way)
                    remote(
                        part,
                        part,
                        R.a4_send.at[layer, q, way],
                        R.a4_recv.at[layer, q, way],
                        other_y,
                        o,
                    ).wait_recv()

            loop(n, block)

            def unpack(k):
                for r in range(0, ru, 16):
                    R.wqkv[layer, aligned(k * ru + r, 16), :] = R.watt[
                        layer, r // rp, aligned(k * rp + r % rp, 16), :
                    ]
                for r in range(0, ro, 16):
                    rows = min(16, ro - r)
                    p, off = (ru + r) // rp, (ru + r) % rp
                    block = R.watt[layer, p, aligned(k * rp + off, 16), :][:, :D].astype(F32)
                    R.wide_rows[aligned(k * ro + r, 8), :] = block[:rows][:8]
                    if rows > 8:
                        R.wide_rows[aligned(k * ro + r + 8, 8), :] = block[8:rows]

            loop(NO, unpack)
            R.wout[layer] = R.wide_rows[pl.ds(0, F), :].astype(BF16)

        att_spread(0)
        att_spread(1)

        raw_copies[2].wait()
        raw_copies[3].wait()
        halves = [
            jnp.concatenate(
                [R.o_up[:, (2 * k + h) * rd : (2 * k + h + 1) * rd] for k in range(NO)], axis=1
            ).astype(BF16)
            for h in range(2)
        ]
        R.wup[y, aligned(o * ru, ru), :] = jnp.where(y == 0, halves[0], halves[1])
        R.yb_up[...] = jnp.where(y == 0, halves[1], halves[0])
        R.wdown[y, aligned(o * rd, rd), :] = R.o_down[aligned(y * rd, rd), :].astype(BF16)
        R.yb_down[...] = R.o_down[aligned((1 - y) * rd, rd), :].astype(BF16)
        y_copy(0).start()
        feed_spread_home(0)

        @pl.when(x == c)
        def _():
            seq_copy(True).start()
            seq_copy(False).start()

        for m in range(2):
            for j in range(2):
                cot_copy(m, j, True).start()
                cot_copy(m, j, False).start()

        loop(
            NO,
            lambda k: remote(
                R.small_in,
                R.small_a.at[(o + k) % NO],
                R.sma_send.at[k],
                R.sma_recv.at[(o + k) % NO],
                s,
                (o + k) % NO,
            ).wait_recv(),
            1,
        )
        table = jnp.zeros((8, wide), F32)
        for k in range(NO):
            part = lanes_to(R.small_a[k], wide)
            narrow = pltpu.roll(part, ru * k, 1) if k else part
            broad = pltpu.roll(part, rd * k, 1) if k else part
            table = table + jnp.where(row8 < 4, narrow, broad)
        moved = jnp.where(lane8 < low, table, 0.0)
        moved += pltpu.roll(jnp.where((lane8 >= low) & (lane8 < F), table, 0.0), 2 * low, 1)
        moved += pltpu.roll(
            jnp.where((lane8 >= F) & (lane8 < F + low), table, 0.0), 2 * low - F, 1
        )
        moved += pltpu.roll(
            jnp.where((lane8 >= F + low) & (lane8 < 2 * F), table, 0.0), 2 * low + 2 * rest - F, 1
        )
        table = jnp.where(row8 == 3, moved, table)
        R.small_own[...] = table
        R.small_b[s] = table

        def small_b_copy(k, of):
            return remote(
                R.small_own,
                R.small_b.at[of],
                R.smb_send.at[k],
                R.smb_recv.at[of],
                (s + k) % SECTIONS,
                o,
            )

        loop(SECTIONS, lambda k: small_b_copy(k, s).start(), 1)

        def first_blocks(k):
            q = (zz + k) % n
            att_z_copy(0, q, zz).wait_recv()
            att_plane_start(0, q)
            att_plane_relay(0, (zz + k - 1) % n)

        loop(n, first_blocks, 1)
        y_copy(1).start()
        feed_spread_away(0, 0)
        att_plane_relay(0, (zz + n - 1) % n)
        loop(SECTIONS, lambda k: small_b_copy(k, (s + k) % SECTIONS).wait_recv(), 1)

        R.small_grad[...] = jnp.zeros_like(R.small_grad)
        def note_rows(block, index, row):
            R.small_grad[block] += jnp.where(row8 == index, lanes_to(row, wide), 0.0)


        @pl.when(x == c)
        def _():
            seq_copy(True).wait()

        @pl.when(x != c)
        def _():
            seq_copy(False).wait_recv()

        gain0 = R.small_b[0, 0:1, :D]
        shift0 = R.small_b[0, 1:2, :D]

        def first_norm(k):
            rows = aligned(k * Q, Q)
            _, _, out = normed_rows(R.seq_rows[rows, :].astype(F32), gain0, shift0)
            R.norm_at[0, rows, :] = out.astype(BF16)

        loop(L // Q, first_norm)
        feed_spread_away(0, 1)
        R.hid_rows[0] = R.seq_rows[aligned(c * 2 * Q, 2 * Q), :]
        len_copy.wait_recv()
        tile = jnp.where(x == c, R.len_own[...], R.len_mate[...])
        tile = jnp.where((row8[:, :128] == 0) & (lane8[:, :128] == y), tile, 0.0)
        length_here = jnp.sum(jnp.sum(tile, axis=1, keepdims=True), axis=0, keepdims=True)
        length_here = length_here.astype(jnp.int32)
        def block_copy(phase, m, buf, way):
            part = buf.at[aligned(m * L + s * Q, Q)]
            to = other_y if way else other_x
            return remote(
                part, part, R.ag_send.at[phase, m, way], R.ag_recv.at[phase, m, way], to, o
            )

        def half_copy(phase, m, buf, way):
            src, to = (other_y, other_x) if way else (other_x, other_y)
            part = buf.at[aligned(m * L + src * Q + way * (Q // 2), Q // 2)]
            slot = 2 + way
            return remote(
                part, part, R.ag_send.at[phase, m, slot], R.ag_recv.at[phase, m, slot], to, o
            )

        def share_mate(phase, m, buf):
            part = buf.at[aligned((2 * c + m) * Q, Q)]
            return remote(
                part, part, R.ag_send.at[phase, m, 0], R.ag_recv.at[phase, m, c], s, mate
            )

        def pass_rows(phase, buf):
            for m in range(2):
                for way in range(2):
                    src = other_y if way else other_x
                    part = buf.at[aligned(m * L + src * Q, Q)]
                    remote(
                        part, part, R.ag_send.at[phase, m, way], R.ag_recv.at[phase, m, way], src, o
                    ).wait_recv()
                    half_copy(phase, m, buf, way).start()

        def send_rows(phase, attention, m, buf, value):
            if attention:
                buf[aligned((2 * c + m) * Q, Q), :] = value
                share_mate(phase, m, buf).start()
            else:
                buf[aligned(m * L + s * Q, Q), :] = value
                for way in range(2):
                    block_copy(phase, m, buf, way).start()

        def finish_send_rows(phase, attention, m, buf):
            if attention:
                share_mate(phase, m, buf).wait_send()
            else:
                for way in range(2):
                    block_copy(phase, m, buf, way).wait_send()
                    half_copy(phase, m, buf, way).wait_send()

        def await_rows(phase, attention, m, buf):
            if attention:
                for j in range(2):
                    part = buf.at[aligned((2 * (1 - c) + j) * Q, Q)]
                    remote(
                        part, part, R.ag_send.at[phase, j, 0], R.ag_recv.at[phase, j, 1 - c], s, mate
                    ).wait_recv()
            else:
                for way in range(2):
                    part = buf.at[aligned(m * L + (3 - s) * Q + way * (Q // 2), Q // 2)]
                    slot = 2 + way
                    remote(
                        part,
                        part,
                        R.ag_send.at[phase, m, slot],
                        R.ag_recv.at[phase, m, slot],
                        other_y,
                        o,
                    ).wait_recv()

        def sum_slot(phase):
            return 0 if phase < 4 else 1

        def part_copy(phase, m, base, k):
            to = (s + k) % SECTIONS
            return remote(
                R.parts.at[aligned(base + to * Q, Q)],
                R.sums.at[sum_slot(phase), s, m],
                R.rs_send.at[phase, m, k],
                R.rs_recv.at[phase, m, s],
                to,
                o,
            )

        def mate_part(phase, j):
            return remote(
                R.parts.at[aligned((2 * (1 - c) + j) * Q, Q)],
                R.sums.at[sum_slot(phase), c, j],
                R.rs_send.at[phase, j, 0],
                R.rs_recv.at[phase, j, c],
                s,
                mate,
            )

        def send_parts(phase, attention, m):
            slot = sum_slot(phase)
            if attention:
                for j in range(2):
                    mate_part(phase, j).start()
                    R.sums[slot, c, j] = R.parts[aligned((2 * c + j) * Q, Q), :]
            else:
                loop(SECTIONS, lambda k: part_copy(phase, m, m * L, k).start(), 1)
                R.sums[slot, s, m] = R.parts[aligned(m * L + s * Q, Q), :]

        def finish_send_parts(phase, attention, chunks=(0, 1)):
            for m in chunks:
                if attention:
                    mate_part(phase, m).wait_send()
                else:
                    loop(SECTIONS, lambda k: part_copy(phase, m, m * L, k).wait_send(), 1)

        def part_arrival(phase, m, src):
            return remote(
                R.parts.at[pl.ds(0, Q)],
                R.sums.at[sum_slot(phase), src, m],
                R.rs_send.at[phase, m, 0],
                R.rs_recv.at[phase, m, src],
                s,
                mate,
            )

        def await_parts(phase, attention, m):
            slot = sum_slot(phase)
            if attention:
                part_arrival(phase, m, 1 - c).wait_recv()
                sources = range(2)
            else:
                loop(
                    SECTIONS,
                    lambda k: part_arrival(phase, m, (s + k) % SECTIONS).wait_recv(),
                    1,
                )
                sources = range(SECTIONS)
            total = None
            for src in sources:
                part = R.sums[slot, src, m].astype(F32)
                total = part if total is None else total + part
            return total

        def place_copy(which, j):
            return remote(
                R.finished.at[which, j],
                (R.out_grad_rows if which else R.out_stream).at[aligned(y * Q, Q)],
                R.fo_send.at[which, j],
                R.fo_recv.at[which, y],
                2 * c + j,
                2 * zz + x,
            )

        def place_rows(which, j, value):
            stays = (s == 2 * c + j) & (x == c)
            R.finished[which, j] = value

            @pl.when(stays)
            def _():
                (R.out_grad_rows if which else R.out_stream)[aligned(y * Q, Q), :] = value

            @pl.when(jnp.logical_not(stays))
            def _():
                place_copy(which, j).start()

        def finish_place(which):
            for j in range(2):
                stays = (s == 2 * c + j) & (x == c)

                @pl.when(jnp.logical_not(stays))
                def _(j=j):
                    place_copy(which, j).wait_send()

            for m in range(2):
                mine = (s == 2 * m + c) & (y == c)

                @pl.when(jnp.logical_not(mine))
                def _(m=m):
                    remote(
                        R.finished.at[which, 0],
                        (R.out_grad_rows if which else R.out_stream).at[pl.ds(m * Q, Q)],
                        R.fo_send.at[which, 0],
                        R.fo_recv.at[which, m],
                        2 * m + c,
                        2 * zz + y,
                    ).wait_recv()

        def close_forward(phase, m):
            e = phase
            attention = e % 2 == 0
            branch = await_parts(phase, attention, m) + R.small_b[e, 2:3, :D]
            mine = pl.ds(m * Q, Q)
            h = R.hid_rows[e, mine, :].astype(F32)
            position = (2 * c + m) * Q + lax.broadcasted_iota(jnp.int32, (Q, 1), 0)
            valid = (position < length_here).astype(F32)
            square_h = jnp.sum(jnp.sum(h * h * valid, axis=1, keepdims=True), axis=0, keepdims=True)
            square_b = jnp.sum(
                jnp.sum(branch * branch * valid, axis=1, keepdims=True), axis=0, keepdims=True
            )
            spot = (2 * zz + x) * 4 + 2 * y
            R.small_grad[e] += jnp.where((row8 == 6) & (lane8 == spot), square_h, 0.0)
            R.small_grad[e] += jnp.where((row8 == 6) & (lane8 == spot + 1), square_b, 0.0)
            fresh = (h + branch).astype(BF16)
            if e == 3:
                place_rows(0, m, fresh)
                return
            R.hid_rows[e + 1, mine, :] = fresh
            _, _, out = normed_rows(
                fresh.astype(F32), R.small_b[e + 1, 0:1, :D], R.small_b[e + 1, 1:2, :D]
            )
            to_attention = (e + 1) % 2 == 0
            buf = (R.norm_at if to_attention else R.norm_ff).at[(e + 1) // 2]
            send_rows(phase + 1, to_attention, m, buf, out.astype(BF16))

        grad_at = (R.seq_rows, R.grad_at)

        def close_backward(phase, m):
            e = 7 - phase
            attention = e % 2 == 0
            d_norm = await_parts(phase, attention, m)
            mine = pl.ds(m * Q, Q)
            unit, inverse, _ = normed_rows(R.hid_rows[e, mine, :].astype(F32), 1.0, 0.0)
            flow = R.grad_rows[mine, :].astype(F32)
            note_rows(e, 0, jnp.sum(d_norm * unit, axis=0, keepdims=True))
            note_rows(e, 1, jnp.sum(d_norm, axis=0, keepdims=True))
            note_rows(e, 2, jnp.sum(flow, axis=0, keepdims=True))
            a = d_norm * R.small_b[e, 0:1, :D]
            mean_a = jnp.mean(a, axis=-1, keepdims=True)
            mean_ax = jnp.mean(a * unit, axis=-1, keepdims=True)
            fresh = (flow + (a - mean_a - unit * mean_ax) * inverse).astype(BF16)
            if e == 0:
                place_rows(1, m, fresh)
                return
            R.grad_rows[mine, :] = fresh
            to_attention = (e - 1) % 2 == 0
            buf = grad_at[(e - 1) // 2] if to_attention else R.grad_ff.at[1]
            send_rows(phase + 1, to_attention, m, buf, fresh)

        ga = (R.hidden.at[1], R.slope.at[1])

        def attention_forward(layer):
            bias = R.small_b[2 * layer + c, 3:4, :W]
            xs = R.norm_at.at[layer]
            for t in range(0, W, 256):
                cols = pl.ds(t, 256)
                lin = mm(xs[...], R.wqkv[layer, :, cols]) + bias[:, t : t + 256]
                R.lin_t[layer, cols, :] = lin.T.astype(BF16)

            def head(h):
                q0, k0, v0 = head_rows(h, heads)
                score = mm(
                    R.lin_t[layer, pl.ds(k0, HEAD_DIM), :],
                    R.lin_t[layer, pl.ds(q0, HEAD_DIM), :],
                    TN,
                )
                live = lax.broadcasted_iota(jnp.int32, score.shape, 0) < length_here
                score = jnp.where(live, score, MASKED)
                top = jnp.max(score, axis=0, keepdims=True)
                powers = jnp.exp2((score - top) * SCALE_2)
                total = jnp.sum(powers, axis=0, keepdims=True)
                probs = (powers * (1.0 / total)).astype(BF16)
                R.log_total[layer, h] = top * SCALE_2 + jnp.log2(total)
                mixed = mm(R.lin_t[layer, pl.ds(v0, HEAD_DIM), :], probs)
                R.att_t[layer, aligned(h * HEAD_DIM, HEAD_DIM), :] = mixed.astype(BF16)

            def pair(h):
                head(2 * h)
                head(2 * h + 1)

            loop(heads // 2, pair)
            if heads % 2:
                head(heads - 1)
            R.parts[pl.ds(0, L), :] = mm(R.att_t[layer], R.wout[layer], TN).astype(BF16)

        def attention_back_heads(layer, between):
            g = grad_at[layer]
            R.d_att_t[...] = mm(R.wout[layer], g[...], NT).astype(BF16)

            def head(h):
                q0, k0, v0 = head_rows(h, heads)
                q_t = R.lin_t[layer, pl.ds(q0, HEAD_DIM), :]
                k_t = R.lin_t[layer, pl.ds(k0, HEAD_DIM), :]
                v_t = R.lin_t[layer, pl.ds(v0, HEAD_DIM), :]
                d_a = R.d_att_t[aligned(h * HEAD_DIM, HEAD_DIM), :]
                score = mm(k_t, q_t, TN)
                live = lax.broadcasted_iota(jnp.int32, score.shape, 0) < length_here
                probs = jnp.where(live, jnp.exp2(score * SCALE_2 - R.log_total[layer, h]), 0.0)
                d_probs = mm(v_t, d_a, TN)
                product = probs * d_probs
                inner_sum = jnp.sum(product, axis=0, keepdims=True)
                d_score = ((product - probs * inner_sum) * SCALE).astype(BF16)
                R.d_lin_t[pl.ds(q0, HEAD_DIM), :] = mm(k_t, d_score).astype(BF16)
                R.d_lin_t[pl.ds(k0, HEAD_DIM), :] = mm(q_t, d_score, NT).astype(BF16)
                R.d_lin_t[pl.ds(v0, HEAD_DIM), :] = mm(d_a, probs.astype(BF16), NT).astype(BF16)

            def pair(h):
                head(2 * h)
                head(2 * h + 1)

            loop(heads // 4, pair)
            between()
            loop(heads // 2, pair, heads // 4)
            if heads % 2:
                head(heads - 1)

        def attention_back_rows(layer):
            for t in range(0, W, 256):
                cols = pl.ds(t, 256)
                part = mm(R.d_lin_t[cols, :], R.wqkv[layer, :, cols], (((0,), (1,)), ((), ())))
                if t == 0:
                    R.acc[...] = part
                else:
                    R.acc[...] += part
            R.parts[pl.ds(0, L), :] = R.acc[...].astype(BF16)

        def attention_back_out(layer):
            stage = 1 - layer
            R.wide_rows[pl.ds(0, F), :] = mm(R.att_t[layer], grad_at[layer][...])

            def out_rows(k):
                for r in range(ru, ra, 16):
                    top_half = R.wide_rows[aligned(k * ro + r - ru, 8), :]
                    low_half = R.wide_rows[aligned(k * ro + r - ru + 8, 8), :]
                    block = jnp.concatenate([top_half, low_half], axis=0)
                    place = aligned(r // rp * NO * rp + k * rp + r % rp, 16)
                    ga[stage][place, 0:D] = block.astype(BF16)

            loop(NO, out_rows)

        def attention_back_weights(layer):
            stage = 1 - layer
            sums = []
            for t in range(0, W, 256):
                cols = pl.ds(t, 256)
                d_lin = R.d_lin_t[cols, :].T
                sums.append(jnp.sum(d_lin.astype(F32), axis=0, keepdims=True))
                d_w = mm(R.norm_at[layer], d_lin, TN).astype(BF16)
                for k in range(NO):
                    for r in range(0, ru, 16):
                        place = pl.ds(r // rp * NO * rp + k * rp + r % rp, 16)
                        ga[stage][place, cols] = d_w[k * ru + r : k * ru + r + 16]
            note_rows(2 * layer + c, 3, jnp.concatenate(sums, axis=1))

        def feed_bias(layer):
            block = R.small_b[2 * layer + x]
            return jnp.where(y == 0, block[4:5], block[5:6])[:, :U]

        def feed_up(layer, m):
            bias = feed_bias(layer)

            def rows_step(r):
                rows = aligned(m * L + r * Q, Q)
                pre = mm(R.norm_ff[layer, rows, :], R.wup[layer]) + bias
                cdf = 0.5 + 0.5 * lax.erf(pre * 0.7071067811865476)
                density = jnp.exp(pre * pre * -0.5) * 0.3989422804014327
                R.hidden[layer, rows, :] = (pre * cdf).astype(BF16)
                R.slope[layer, rows, :] = (cdf + pre * density).astype(BF16)

            loop(SECTIONS, rows_step)

        def feed_down(layer, m):
            rows = pl.ds(m * L, L)
            R.parts[rows, :] = mm(R.hidden[layer, rows, :], R.wdown[layer]).astype(BF16)

        def feed_back_rows(layer, m):
            rows = pl.ds(m * L, L)
            g = R.grad_ff.at[0 if layer == 1 else 1, rows]
            tile = U // 2
            for j in range(2):
                cols = pl.ds(j * tile, tile)
                d_hidden = mm(g[...], R.wdown[layer, cols, :], NT)
                d_pre = (d_hidden * R.slope[layer, rows, cols].astype(F32)).astype(BF16)
                R.slope[layer, rows, cols] = d_pre
                part = mm(d_pre, R.wup[layer, :, cols], NT)
                if j == 0:
                    R.acc[...] = part
                else:
                    R.parts[rows, :] = (R.acc[...] + part).astype(BF16)

        def feed_back_weights(layer):
            xs = R.norm_ff.at[layer]
            g = R.grad_ff.at[0 if layer == 1 else 1]
            tile = U // 2
            owners = tile // rd
            sums = []
            for j in range(2):
                cols = pl.ds(j * tile, tile)
                d_pre = R.slope[layer, :, cols]
                d_down = mm(R.hidden[layer, :, cols], g[...], TN).astype(BF16)
                for k in range(owners):
                    owner = j * owners + k
                    R.sb_down[owner % 2, pl.ds(owner // 2 * rd, rd), :] = d_down[
                        k * rd : (k + 1) * rd
                    ]
                d_up = mm(xs[...], d_pre, TN).astype(BF16)
                for k in range(NO):
                    R.sb_up[k % 2, pl.ds(k // 2 * ru, ru), cols] = d_up[k * ru : (k + 1) * ru]
                sums.append(jnp.sum(d_pre.astype(F32), axis=0, keepdims=True))
            note_rows(2 * layer + x, 4 + y, jnp.concatenate(sums, axis=1))

        z_up, z_down = (R.zb_up, R.wup.at[1]), (R.zb_down, R.norm_ff.at[1])
        FEED_GRADS = (
            (0, R.sb_up, R.rb_up, R.mb_up, z_up, R.yb_up, R.yr_up, ru),
            (1, R.sb_down, R.rb_down, R.mb_down, z_down, R.yb_down, R.yr_down, rd),
        )

        def mate_grads(stage):
            return [
                remote(sb.at[1 - c], rb, R.r1_send.at[stage, a], R.r1_recv.at[stage, a], s, mate)
                for a, sb, rb, *_ in FEED_GRADS
            ]

        RELAYED = n == 4

        def z_grad(stage, entry, q, to, slot):
            a, sb, rb, mb, zb, yb, yr, rows = entry
            return remote(
                mb.at[aligned(q * rows, rows)],
                zb[stage].at[aligned(slot * rows, rows)],
                R.r2_send.at[stage, a, q],
                R.r2_recv.at[stage, a, slot],
                s,
                2 * to + c,
            )

        def each_z_grad(stage, act, late):
            def one(entry, q, sign, distance):
                if RELAYED and distance == 3:
                    if not late:
                        act(z_grad(stage, entry, q, zz + sign, zz + sign))
                elif RELAYED and distance == 2:
                    behind = zz - sign
                    waits = (behind >= 0) & (behind < n)

                    @pl.when(waits if late else jnp.logical_not(waits))
                    def _():
                        if late:
                            late_sum(stage, entry, q, act)
                        else:
                            act(z_grad(stage, entry, q, q, zz))
                elif not late:
                    act(z_grad(stage, entry, q, q, zz))

            def each(*where):
                for entry in FEED_GRADS:
                    one(entry, *where)

            chips_at(range(n - 1, 0, -1), each)

        def late_sum(stage, entry, q, act):
            a, sb, rb, mb, zb, yb, yr, rows = entry
            if act is None:
                act = lambda copy: copy.wait_send()
            else:
                hop = aligned(zz * rows, rows)
                remote(
                    mb.at[pl.ds(0, rows)],
                    zb[stage].at[hop],
                    R.r2_send.at[stage, a, zz],
                    R.r2_recv.at[stage, a, zz],
                    s,
                    mate,
                ).wait_recv()
                part = aligned(q * rows, rows)
                both = mb[part, :].astype(F32) + zb[stage][hop, :].astype(F32)
                mb[part, :] = both.astype(BF16)
            act(z_grad(stage, entry, q, q, zz))

        def feed_to_mate(stage):
            for copy in mate_grads(stage):
                copy.start()

        def finish_feed_z(stage):
            each_z_grad(stage, lambda copy: copy.wait_send(), False)
            each_z_grad(stage, None, True)

        def feed_late(stage):
            each_z_grad(stage, lambda copy: copy.start(), True)

        def feed_along_z(stage):
            for copy in mate_grads(stage):
                copy.wait()
            if stage:
                finish_feed_z(0)
            for a, sb, rb, mb, zb, yb, yr, rows in FEED_GRADS:

                def add(q, sb=sb, rb=rb, mb=mb, rows=rows):
                    part = aligned(q * rows, rows)
                    both = sb[c, part, :].astype(F32) + rb[part, :].astype(F32)
                    mb[part, :] = both.astype(BF16)

                loop(n, add)
            each_z_grad(stage, lambda copy: copy.start(), False)

        def y_grad(a, yb, yr):
            return remote(yb, yr, R.r4_send.at[a], R.r4_recv.at[a], other_y, o)

        def keep_half(a, h, value):
            if a:
                R.o_down[pl.ds(h * rd, rd), :] = value
                return
            for k in range(NO):
                R.o_up[:, (2 * k + h) * rd : (2 * k + h + 1) * rd] = value[:, k * rd : (k + 1) * rd]

        def feed_owned(stage):
            layer = 1 - stage
            for a, sb, rb, mb, zb, yb, yr, rows in FEED_GRADS:

                def landed(q, sign, distance, a=a, zb=zb, mb=mb, rows=rows):
                    if not (RELAYED and distance == 3):
                        remote(
                            mb.at[pl.ds(0, rows)],
                            zb[stage].at[aligned(q * rows, rows)],
                            R.r2_send.at[stage, a, q],
                            R.r2_recv.at[stage, a, q],
                            s,
                            2 * q + c,
                        ).wait_recv()

                chips_at(range(1, n), landed)
                total = mb[aligned(zz * rows, rows), :].astype(F32)
                for k in range(1, n):
                    q = (zz + k) % n
                    part = zb[stage][aligned(q * rows, rows), :].astype(F32)
                    if RELAYED:
                        part = jnp.where(jnp.abs(q - zz) == 3, 0.0, part)
                    total = total + part

                @pl.when(y == layer)
                def _(a=a, total=total):
                    keep_half(a, layer, total)

                @pl.when(y != layer)
                def _(a=a, yb=yb, yr=yr, total=total):
                    yb[...] = total.astype(BF16)

        def feed_to_home(stage):
            @pl.when(y == stage)
            def _():
                for a, sb, rb, mb, zb, yb, yr, rows in FEED_GRADS:
                    y_grad(a, yb, yr).start()

        def feed_home():
            for a, sb, rb, mb, zb, yb, yr, rows in FEED_GRADS:
                y_grad(a, yb, yr).wait()
                for h in range(2):

                    @pl.when(y == 1 - h)
                    def _(a=a, h=h, yr=yr):
                        keep_half(a, h, yr[...].astype(F32))

        att_rows = NO * rp

        def plane_grad(stage, k, q):
            to = (s + k) % SECTIONS
            return remote(
                ga[stage].at[aligned(to * att_rows + q * 2 * rp, 2 * rp), pl.ds(0, W)],
                R.watt.at[stage, s, aligned(q * 2 * rp, 2 * rp)],
                R.g1_send.at[stage, k, q],
                R.g1_recv.at[stage, s, q],
                to,
                o,
            )

        def each_plane_grad(stage, act):
            def block(j):
                q = (zz + j) % n
                loop(SECTIONS, lambda k: act(plane_grad(stage, k, q)), 1)

            loop(n + 1, block, 1)

        def att_to_plane(stage):
            each_plane_grad(stage, lambda copy: copy.start())

        def finish_att_plane(stage):
            each_plane_grad(stage, lambda copy: copy.wait_send())

        def att_z_grad(stage, k):
            q = (zz + k) % n
            return remote(
                R.gs.at[stage, aligned(q * 2 * rp, 2 * rp)],
                R.gz.at[stage, zz],
                R.g2_send.at[stage, q],
                R.g2_recv.at[stage, zz],
                s,
                2 * q + c,
            )

        def finish_att_z(stage):
            loop(n, lambda k: att_z_grad(stage, k).wait_send(), 1)

        def att_along_z(stage, first=1, last=n):
            def block(j):
                q = (zz + j) % n
                part = aligned(q * 2 * rp, 2 * rp)

                def landed(k):
                    src = (s + k) % SECTIONS
                    remote(
                        ga[stage].at[aligned(q * 2 * rp, 2 * rp), pl.ds(0, W)],
                        R.watt.at[stage, src, part],
                        R.g1_send.at[stage, k, q],
                        R.g1_recv.at[stage, src, q],
                        src,
                        o,
                    ).wait_recv()

                loop(SECTIONS, landed, 1)
                own = aligned(s * att_rows + q * 2 * rp, 2 * rp)
                total = ga[stage][own, 0:W].astype(F32)
                for k in range(1, SECTIONS):
                    total = total + R.watt[stage, (s + k) % SECTIONS, part, :].astype(F32)
                R.gs[stage, part, :] = total.astype(BF16)

                @pl.when(q != zz)
                def _():
                    att_z_grad(stage, j).start()

            loop(last + 1, block, first)

        def home_copy(stage, core):
            return remote(
                R.gt.at[stage, pl.ds(core * rp, rp)],
                R.att_own.at[aligned(s * rp, rp)],
                R.g3_send.at[stage, core],
                R.g3_recv.at[s],
                2 * (1 - stage) + c,
                2 * zz + core,
            )

        def each_home(stage, act, own):
            for core in range(2):
                stays = (s == 2 * (1 - stage) + c) & (c == core)

                @pl.when(stays)
                def _(core=core):
                    if own:
                        R.att_own[aligned(s * rp, rp), :] = R.gt[stage, pl.ds(core * rp, rp), :]

                @pl.when(jnp.logical_not(stays))
                def _(core=core):
                    act(home_copy(stage, core))

        def att_owned(stage):
            def landed(k):
                q = (zz + k) % n
                remote(
                    R.gs.at[stage, pl.ds(0, 2 * rp)],
                    R.gz.at[stage, q],
                    R.g2_send.at[stage, q],
                    R.g2_recv.at[stage, q],
                    s,
                    2 * q + c,
                ).wait_recv()

            loop(n, landed, 1)
            total = R.gs[stage, aligned(zz * 2 * rp, 2 * rp), :].astype(F32)
            for k in range(1, n):
                total = total + R.gz[stage, (zz + k) % n].astype(F32)
            R.gt[stage] = total.astype(BF16)
            each_home(stage, lambda copy: copy.start(), True)

        def att_home():
            for p in range(SECTIONS):
                mine = (s == p) & (x == c)

                @pl.when(jnp.logical_not(mine))
                def _(p=p):
                    remote(
                        R.gt.at[0, pl.ds(0, rp)],
                        R.att_own.at[pl.ds(p * rp, rp)],
                        R.g3_send.at[0, 0],
                        R.g3_recv.at[p],
                        p,
                        2 * zz + x,
                    ).wait_recv()

            rows = R.att_own[pl.ds(0, ru), :].astype(F32)
            R.o_qkv[...] = from_packed(rows, F, heads)
            rows = R.att_own[pl.ds(ru, ra - ru), :].astype(F32)
            R.o_out[...] = rows[:ro, :D]

        att_collect(0)
        att_onward(1, NEAR)
        attention_forward(0)
        send_parts(0, True, None)
        for m in range(2):
            close_forward(0, m)
        feed_arrivals(0, NEAR)
        feed_spread_home(1)
        feed_spread_away(1, 0)
        feed_spread_away(1, 1)
        pass_rows(1, R.norm_ff.at[0])
        att_onward(1, FAR)
        feed_collect(0)
        finish_send_parts(0, True)
        await_rows(1, False, 0, R.norm_ff.at[0])
        feed_up(0, 0)
        feed_down(0, 0)
        send_parts(1, False, 0)
        att_plane_relay(1, zz)
        att_plane_onward(1, NEAR)
        await_rows(1, False, 1, R.norm_ff.at[0])
        feed_up(0, 1)
        feed_down(0, 1)
        send_parts(1, False, 1)
        att_plane_onward(1, FAR)
        close_forward(1, 0)
        feed_arrivals(1, NEAR)
        close_forward(1, 1)
        att_collect(1)
        finish_send_parts(1, False)
        await_rows(2, True, None, R.norm_at.at[1])
        attention_forward(1)
        send_parts(2, True, None)
        for m in range(2):
            close_forward(2, m)
        feed_collect(1)
        pass_rows(3, R.norm_ff.at[1])
        finish_send_parts(2, True)
        for m in range(2):
            await_rows(3, False, m, R.norm_ff.at[1])
            feed_up(1, m)

        loop(NO, lambda k: small_out(k).wait_send(), 1)
        loop(SECTIONS, lambda k: small_b_copy(k, s).wait_send(), 1)
        len_copy.wait_send()
        each_quarter(lambda copy: copy.wait_send(), False)

        @pl.when(x == c)
        def _():
            seq_copy(False).wait_send()

        for kind in range(2):
            y_copy(kind).wait_send()
        for layer in range(2):
            att_sent(layer)
            feed_sent(layer)
        for m in range(2):
            finish_send_rows(1, False, m, R.norm_ff.at[0])
            finish_send_rows(2, True, m, R.norm_at.at[1])
            finish_send_rows(3, False, m, R.norm_ff.at[1])
            for j in range(2):
                cot_copy(m, j, True).wait()
                cot_copy(m, j, False).wait_send()
                remote(
                    R.cot_in.at[m, pl.ds(0, Q)],
                    R.grad_ff.at[0, aligned(j * L + (2 * m + 1 - c) * Q, Q)],
                    R.cot_send.at[m, j],
                    R.cot_recv.at[m, j],
                    s,
                    mate,
                ).wait_recv()
        for j in range(2):
            R.grad_rows[pl.ds(j * Q, Q), :] = R.grad_ff[0, aligned(j * L + s * Q, Q), :]

        for m in range(2):
            feed_back_rows(1, m)
            send_parts(4, False, m)
        feed_back_weights(1)
        feed_to_mate(0)
        feed_along_z(0)
        for m in range(2):
            close_backward(4, m)
        finish_send_parts(4, False)
        for m in range(2):
            feed_down(1, m)
            send_parts(3, False, m)
        await_rows(5, True, None, grad_at[1])
        attention_back_heads(1, lambda: feed_late(0))
        finish_send_parts(3, False, (0,))
        attention_back_rows(1)
        send_parts(5, True, None)
        attention_back_out(1)
        attention_back_weights(1)
        for m in range(2):
            close_backward(5, m)
        for m in range(2):
            close_forward(3, m)
        finish_send_parts(3, False, (1,))
        finish_send_parts(5, True)
        pass_rows(6, R.grad_ff.at[1])
        for m in range(2):
            await_rows(6, False, m, R.grad_ff.at[1])
            feed_back_rows(0, m)
            send_parts(6, False, m)
        att_to_plane(0)
        feed_back_weights(0)
        feed_to_mate(1)
        for m in range(2):
            finish_send_rows(5, True, m, grad_at[1])
        feed_owned(0)
        feed_along_z(1)
        for m in range(2):
            close_backward(6, m)
        finish_send_parts(6, False)
        await_rows(7, True, None, grad_at[0])
        attention_back_out(0)
        attention_back_heads(0, lambda: feed_late(1))
        attention_back_weights(0)
        att_to_plane(1)
        feed_to_home(0)
        attention_back_rows(0)
        send_parts(7, True, None)
        att_along_z(0)
        for m in range(2):
            close_backward(7, m)

        def small_grad_copy(k, of):
            to = (s + k) % SECTIONS
            return remote(
                R.small_grad.at[to],
                R.small_sum.at[of],
                R.sga_send.at[k],
                R.sga_recv.at[of],
                to,
                o,
            )

        loop(SECTIONS, lambda k: small_grad_copy(k, s).start(), 1)
        R.small_sum[s] = R.small_grad[s]
        att_along_z(1, 1, 2)
        feed_owned(1)
        feed_to_home(1)
        att_along_z(1, 3, n)
        loop(SECTIONS, lambda k: small_grad_copy(k, (s + k) % SECTIONS).wait_recv(), 1)
        total = R.small_sum[0]
        for k in range(1, SECTIONS):
            total = total + R.small_sum[k]
        R.small_line[...] = total

        def small_line_copy(k, of):
            peer = (o + k) % NO
            return remote(
                R.small_line, R.small_all.at[of], R.sgb_send.at[k], R.sgb_recv.at[of], s, peer
            )

        loop(NO, lambda k: small_line_copy(k, o).start(), 1)
        R.small_all[o] = total
        att_owned(0)
        feed_home()
        att_owned(1)
        loop(NO, lambda k: small_line_copy(k, (o + k) % NO).wait_recv(), 1)
        total = R.small_all[0]
        for k in range(1, NO):
            total = total + R.small_all[k]

        def back(rows, lanes):
            return pltpu.roll(rows, (wide - lanes) % wide, 1)

        norms = back(total, ru * o)
        for k in range(3):
            R.o_norm[k] = norms[k : k + 1, 0:ru]
        units = back(total, rd * o)
        R.o_upb[:, 0:rd] = units[4:5, 0:rd]
        R.o_upb[:, rd : 2 * rd] = units[5:6, 0:rd]
        first, second, third = 3 * low, 3 * low + 2 * rest, 3 * low + 3 * rest
        plain = jnp.where(lane8 < low, total, 0.0)
        plain += back(jnp.where((lane8 >= first) & (lane8 < first + rest), total, 0.0), 2 * low)
        plain += back(jnp.where((lane8 >= 2 * low) & (lane8 < first), total, 0.0), 2 * low - F)
        plain += back(
            jnp.where((lane8 >= second) & (lane8 < third), total, 0.0), 2 * low + 2 * rest - F
        )
        R.o_qvb[...] = back(plain, ru * o)[3:4, 0:ru]
        squares = back(total, 4 * o)
        for m in range(2):
            count = (R.lens[0, m] * D).astype(F32)
            R.o_rms[m : m + 1, :] = jnp.sqrt(squares[6:7, 2 * m : 2 * m + 2] / count)
        att_home()
        for which in range(2):
            finish_place(which)

        loop(SECTIONS, lambda k: small_grad_copy(k, s).wait_send(), 1)
        loop(NO, lambda k: small_line_copy(k, o).wait_send(), 1)
        for m in range(2):
            finish_send_rows(6, False, m, R.grad_ff.at[1])
            finish_send_rows(7, True, m, grad_at[0])
        finish_send_parts(7, True)
        finish_feed_z(1)
        for stage in range(2):
            finish_att_plane(stage)
            finish_att_z(stage)
            each_home(stage, lambda copy: copy.wait_send(), False)

    return kernel


def one_step(cfg, lens, qkv, qv_b, out, up, up_b, down, norm, stream, cotangent):
    D, L, U, F, W = cfg.width, cfg.length, cfg.units, cfg.features, cfg.packed
    Q = L // SECTIONS
    NO, n = cfg.outer, cfg.outer // 2
    ru, rd, ro, ra = cfg.up_rows, cfg.down_rows, cfg.out_rows, cfg.att_rows
    rp = ra // SECTIONS
    wide = max(U, W)
    lanes = -(-max(ru, rd) // 128) * 128
    dma = pltpu.SemaphoreType.DMA
    inputs = dict(
        lens=lens,
        qkv_w=qkv,
        qv_b=qv_b,
        out_w=out,
        up_w=up,
        up_b=up_b,
        down_w=down,
        norm_v=norm,
        stream_in=stream,
        cot_in=cotangent,
    )
    outputs = dict(
        out_stream=((2 * Q, D), BF16),
        out_grad_rows=((2 * Q, D), BF16),
        o_qkv=((ru, 3 * F), F32),
        o_qvb=((1, ru), F32),
        o_out=((ro, D), F32),
        o_up=((ru, 2 * U), F32),
        o_upb=((1, 2 * rd), F32),
        o_down=((2 * rd, D), F32),
        o_norm=((3, 1, ru), F32),
        o_rms=((2, 2), F32),
    )
    scratch = dict(
        small_in=((8, lanes), F32),
        small_a=((NO, 8, lanes), F32),
        small_own=((8, wide), F32),
        small_b=((SECTIONS, 8, wide), F32),
        small_grad=((SECTIONS, 8, wide), F32),
        small_sum=((SECTIONS, 8, wide), F32),
        small_line=((8, wide), F32),
        small_all=((NO, 8, wide), F32),
        len_own=((8, 128), F32),
        len_mate=((8, 128), F32),
        att_own=((ra, W), BF16),
        watt=((2, SECTIONS, NO * rp, W), BF16),
        wqkv=((2, D, W), BF16),
        wout=((2, F, D), BF16),
        wup=((2, D, U), BF16),
        wdown=((2, U, D), BF16),
        hid_rows=((SECTIONS, 2 * Q, D), BF16),
        grad_rows=((2 * Q, D), BF16),
        norm_at=((2, L, D), BF16),
        norm_ff=((2, 2 * L, D), BF16),
        lin_t=((2, W, L), BF16),
        att_t=((2, F, L), BF16),
        log_total=((2, cfg.heads, 1, L), F32),
        hidden=((2, 2 * L, U), BF16),
        slope=((2, 2 * L, U), BF16),
        grad_ff=((2, 2 * L, D), BF16),
        grad_at=((L, D), BF16),
        seq_rows=((L, D), BF16),
        parts=((2 * L, D), BF16),
        sums=((2, SECTIONS, 2, Q, D), BF16),
        finished=((2, 2, Q, D), BF16),
        acc=((L, D), F32),
        wide_rows=((F + 64, D), F32),
        d_att_t=((F, L), BF16),
        d_lin_t=((W, L), BF16),
        sb_up=((2, n * ru, U), BF16),
        rb_up=((n * ru, U), BF16),
        mb_up=((n * ru, U), BF16),
        zb_up=((n * ru, U), BF16),
        yb_up=((ru, U), BF16),
        yr_up=((ru, U), BF16),
        sb_down=((2, n * rd, D), BF16),
        rb_down=((n * rd, D), BF16),
        mb_down=((n * rd, D), BF16),
        zb_down=((n * rd, D), BF16),
        yb_down=((rd, D), BF16),
        yr_down=((rd, D), BF16),
        gs=((2, NO * rp, W), BF16),
        gz=((2, n, 2 * rp, W), BF16),
        gt=((2, 2 * rp, W), BF16),
    )
    semaphores = dict(
        raw_sem=(4,),
        load_sem=(5,),
        sma_send=(NO,),
        sma_recv=(NO,),
        smb_send=(SECTIONS,),
        smb_recv=(SECTIONS,),
        len_send=(1,),
        len_recv=(1,),
        seq_send=(1,),
        seq_recv=(1,),
        cot_send=(2, 2),
        cot_recv=(2, 2),
        a1_send=(SECTIONS,),
        a1_recv=(2, 2),
        a2_send=(2, n, n),
        a2_recv=(2, n),
        a3_send=(2, n, 2),
        a3_recv=(2, n, 2),
        a4_send=(2, n, 2),
        a4_recv=(2, n, 2),
        y_send=(2,),
        y_recv=(2,),
        z_send=(4, n, n),
        z_recv=(4, n),
        p_send=(4, n),
        p_recv=(4, n),
        ag_send=(8, 2, SECTIONS),
        ag_recv=(8, 2, SECTIONS),
        rs_send=(8, 2, SECTIONS),
        rs_recv=(8, 2, SECTIONS),
        fo_send=(2, 2),
        fo_recv=(2, 2),
        r1_send=(2, 2),
        r1_recv=(2, 2),
        r2_send=(2, 2, n),
        r2_recv=(2, 2, n),
        r4_send=(2,),
        r4_recv=(2,),
        g1_send=(2, SECTIONS, n),
        g1_recv=(2, SECTIONS, n),
        g2_send=(2, n),
        g2_recv=(2, n),
        g3_send=(2, 2),
        g3_recv=(SECTIONS,),
        sga_send=(SECTIONS,),
        sga_recv=(SECTIONS,),
        sgb_send=(NO,),
        sgb_recv=(NO,),
    )
    names = [*inputs, *outputs, *scratch, *semaphores]
    vmem = pl.BlockSpec(memory_space=pltpu.VMEM)
    hbm = pl.BlockSpec(memory_space=pl.ANY)
    smem = pl.BlockSpec(memory_space=pltpu.SMEM)
    shapes = [jax.ShapeDtypeStruct(*spec) for spec in outputs.values()]
    results = pl.pallas_call(
        make_kernel(cfg, names),
        out_shape=shapes,
        in_specs=[smem, hbm, vmem, hbm, hbm, vmem, hbm, vmem, hbm, hbm],
        out_specs=[vmem] * len(outputs),
        scratch_shapes=[pltpu.VMEM(*spec) for spec in scratch.values()]
        + [dma(shape) for shape in semaphores.values()],
        compiler_params=pltpu.CompilerParams(
            collective_id=0, has_side_effects=True, vmem_limit_bytes=63 * 2**20
        ),
        name="layers",
    )(*inputs.values())
    count = len(shapes)

    def hand_over(*refs):
        given, out, held = refs[:count], refs[count : 2 * count], refs[2 * count : 3 * count]
        loads = [pltpu.make_async_copy(given[k], held[k], refs[-2].at[k]) for k in range(count)]
        stores = [pltpu.make_async_copy(held[k], out[k], refs[-1].at[k]) for k in range(count)]
        for copy in loads:
            copy.start()
        for load, store in zip(loads, stores):
            load.wait()
            store.start()
        for copy in stores:
            copy.wait()

    return pl.pallas_call(
        hand_over,
        out_shape=shapes,
        in_specs=[hbm] * count,
        out_specs=[hbm] * count,
        scratch_shapes=[pltpu.VMEM(*spec) for spec in outputs.values()]
        + [dma((count,)), dma((count,))],
        compiler_params=pltpu.CompilerParams(vmem_limit_bytes=63 * 2**20),
        name="outputs",
    )(*results)


def shards(
    layer_input,
    out_cotangent,
    lengths,
    qkv_weight,
    qv_bias,
    out_weight,
    up_weight,
    up_bias,
    down_weight,
    norm_vectors,
):
    section_count = lax.axis_size("section")
    dp_count = lax.axis_size("dp")
    L, D = layer_input.shape[2:]
    sequences = layer_input.shape[0] * layer_input.shape[1]
    assert section_count == SECTIONS and sequences == 2
    F = out_weight.shape[1] * dp_count
    U2 = up_weight.shape[2]
    heads = F // HEAD_DIM
    outer = max(
        k
        for k in range(2, dp_count + 1, 2)
        if dp_count % k == 0 and D % (16 * k) == 0 and U2 % (32 * k) == 0 and F % (8 * k) == 0
    )
    inner = dp_count // outer
    groups = [[g * inner + k for k in range(inner)] for g in range(outer)]

    def joined(block, axis=0):
        if inner == 1:
            return block
        block = block.astype(BF16)
        block = lax.all_gather(block, "dp", axis=axis, tiled=True, axis_index_groups=groups)
        return block.astype(F32)

    def own_share(block, axis=0):
        if inner == 1:
            return block
        return lax.psum_scatter(
            block, "dp", scatter_dimension=axis, tiled=True, axis_index_groups=groups
        )

    shard_rows = D // outer + F // outer
    cfg = types.SimpleNamespace(
        width=D,
        length=L,
        units=U2 // 2,
        features=F,
        packed=-(-3 * F // 256) * 256,
        outer=outer,
        inner=inner,
        heads=heads,
        up_rows=D // outer,
        down_rows=U2 // outer // 2,
        out_rows=F // outer,
        att_rows=-(-shard_rows // (16 * SECTIONS)) * 16 * SECTIONS,
    )
    stream, grad_rows, qkv, qvb, out, up, upb, down, norm, rms = one_step(
        cfg,
        lengths.reshape(1, 2),
        joined(qkv_weight[0]),
        joined(qv_bias, 1),
        joined(out_weight[0]),
        joined(up_weight[0]),
        joined(up_bias, 1),
        joined(down_weight[0]),
        joined(norm_vectors[0], 1)[:, None],
        layer_input.reshape(2, L, D),
        out_cotangent.reshape(2, L, D),
    )
    rows_shape = layer_input.shape[:2] + (L // SECTIONS, D)
    return (
        stream.reshape(rows_shape),
        grad_rows.reshape(rows_shape),
        own_share(qkv)[None],
        own_share(qvb, 1),
        own_share(out)[None],
        own_share(up)[None],
        own_share(upb, 1),
        own_share(down)[None],
        own_share(norm, 2).reshape(1, 3, -1),
        rms.reshape(layer_input.shape[:2] + (1, 2)),
    )


def solution(mesh):
    placed = (
        P(None, "dp", None, None),
        P(None, "dp", None, None),
        P(None, "dp"),
        P("section", "dp", None),
        P("section", "dp"),
        P("section", "dp", None),
        P("section", "dp", None),
        P("section", "dp"),
        P("section", "dp", None),
        P("section", None, "dp"),
    )
    return jax.shard_map(
        shards,
        mesh=mesh,
        in_specs=placed,
        out_specs=(
            P(None, "dp", "section", None),
            P(None, "dp", "section", None),
            P("section", "dp", None),
            P("section", "dp"),
            P("section", "dp", None),
            P("section", "dp", None),
            P("section", "dp"),
            P("section", "dp", None),
            P("section", None, "dp"),
            P(None, "dp", "section", None),
        ),
        check_vma=False,
    )
```

```python
import types

import jax
import jax.numpy as jnp
from jax import lax
from jax.experimental import pallas as pl
from jax.experimental.pallas import tpu as pltpu
from jax.sharding import PartitionSpec as P

F32, BF16 = jnp.float32, jnp.bfloat16
MESH = pl.DeviceIdType.MESH
HEAD_DIM = 32
EPSILON = 1e-05
MASKED = -1e30
SCALE = HEAD_DIM**-0.5
SCALE_2 = SCALE * 1.4426950408889634
SECTIONS = 4
NN = (((1,), (0,)), ((), ()))
NT = (((1,), (1,)), ((), ()))
TN = (((0,), (0,)), ((), ()))


def mm(left, right, dims=NN):
    return lax.dot_general(left, right, dims, preferred_element_type=F32)


def aligned(start, size):
    return pl.ds(pl.multiple_of(start, size), size)


def head_rows(h, heads):
    full = heads // 8 * 8
    low, rest = full * HEAD_DIM, (heads - full) * HEAD_DIM
    high = h // full if rest else 0
    q = h * HEAD_DIM + high * 2 * low
    k = low + h * HEAD_DIM + high * (low + rest)
    v = 2 * low + h * HEAD_DIM + high * 2 * rest
    return tuple(pl.multiple_of(row, HEAD_DIM) for row in (q, k, v))


def to_packed(rows, heads):
    half = rows.shape[-1] // 3
    low = heads // 8 * 8 * HEAD_DIM
    parts = [rows[:, i * half : i * half + low] for i in range(3)]
    parts += [rows[:, i * half + low : (i + 1) * half] for i in range(3)]
    return jnp.concatenate(parts, axis=1)


def from_packed(rows, half, heads):
    low = heads // 8 * 8 * HEAD_DIM
    rest = half - low
    parts = []
    for i in range(3):
        parts.append(rows[:, i * low : (i + 1) * low])
        parts.append(rows[:, 3 * low + i * rest : 3 * low + (i + 1) * rest])
    return jnp.concatenate(parts, axis=1)


def lanes_to(rows, width):
    if rows.shape[1] == width:
        return rows
    return jnp.concatenate([rows, jnp.zeros((rows.shape[0], width - rows.shape[1]), F32)], axis=1)


def normed_rows(h, gain, shift):
    mean = jnp.mean(h, axis=-1, keepdims=True)
    centred = h - mean
    spread = jnp.mean(centred * centred, axis=-1, keepdims=True)
    inverse = lax.rsqrt(spread + EPSILON)
    return centred * inverse, inverse, centred * inverse * gain + shift


def make_kernel(cfg, names):
    c_ = cfg
    D, L, U, F, W = c_.width, c_.length, c_.units, c_.features, c_.packed
    Q = L // SECTIONS
    NO, n, inner, heads = c_.outer, c_.outer // 2, c_.inner, c_.heads
    ru, rd, ro = c_.up_rows, c_.down_rows, c_.out_rows
    ra, rp = c_.att_rows, c_.att_rows // SECTIONS
    wide = max(U, W)
    low = heads // 8 * 8 * HEAD_DIM
    rest = F - low

    def kernel(*refs):
        R = types.SimpleNamespace(**dict(zip(names, refs)))
        s = lax.axis_index("section")
        y, x = s // 2, s % 2
        dp = lax.axis_index("dp")
        o, i = dp // inner, dp % inner
        zz, c = o // 2, o % 2
        other_x, other_y = s + 1 - 2 * x, s + 2 - 4 * y
        mate = o + 1 - 2 * c

        def remote(src, dst, send, recv, section, outer):
            return pltpu.make_async_remote_copy(
                src_ref=src,
                dst_ref=dst,
                send_sem=send,
                recv_sem=recv,
                device_id=(section, outer * inner + i),
                device_id_type=MESH,
            )

        def loop(count, body, first=0):
            def step(k, carry):
                body(k)
                return carry

            lax.fori_loop(first, count, step, 0)

        raw = (R.qkv_w, R.out_w, R.up_w, R.down_w)
        raw_home = (R.o_qkv, R.o_out, R.o_up, R.o_down)
        raw_copies = [
            pltpu.make_async_copy(a, b, R.raw_sem.at[k])
            for k, (a, b) in enumerate(zip(raw, raw_home))
        ]
        for copy in raw_copies:
            copy.start()

        barrier = pltpu.get_barrier_semaphore()

        def greet(section, outer):
            pl.semaphore_signal(
                barrier, inc=1, device_id=(section, outer * inner + i), device_id_type=MESH
            )

        loop(SECTIONS, lambda k: greet((s + k) % SECTIONS, o), 1)
        loop(SECTIONS, lambda k: greet((s + k) % SECTIONS, mate), 1)
        loop(NO, lambda k: greet(s, (o + k) % NO), 1)

        row8 = lax.broadcasted_iota(jnp.int32, (8, wide), 0)
        lane8 = lax.broadcasted_iota(jnp.int32, (8, wide), 1)
        here = row8[:, : R.small_in.shape[1]], lane8[:, : R.small_in.shape[1]]

        def rounded(v):
            return v.astype(BF16).astype(F32)

        R.small_in[...] = jnp.zeros_like(R.small_in)
        for k in range(3):
            R.small_in[k : k + 1, 0:ru] = rounded(R.norm_v[k])
        R.small_in[3:4, 0:ru] = rounded(R.qv_b[...])
        R.small_in[4:5, 0:rd] = rounded(R.up_b[:, 0:rd])
        R.small_in[5:6, 0:rd] = rounded(R.up_b[:, rd : 2 * rd])
        R.len_own[...] = jnp.where(here[1] == 0, R.lens[0, 0], R.lens[0, 1])[:, :128].astype(F32)
        pl.semaphore_wait(barrier, 2 * (SECTIONS - 1) + NO - 1)

        def small_out(k):
            peer = (o + k) % NO
            return remote(
                R.small_in, R.small_a.at[o], R.sma_send.at[k], R.sma_recv.at[o], s, peer
            )

        loop(NO, lambda k: small_out(k).start(), 1)
        R.small_a[o] = R.small_in[...]
        len_copy = remote(R.len_own, R.len_mate, R.len_send.at[0], R.len_recv.at[0], s, mate)
        len_copy.start()

        raw_copies[0].wait()
        raw_copies[1].wait()
        packed = lanes_to(to_packed(R.o_qkv[...], heads), W).astype(BF16)
        R.att_own[pl.ds(0, ru), :] = packed
        bottom = jnp.concatenate([R.o_out[...], jnp.zeros((ra - ru - ro, D), F32)], axis=0)
        R.att_own[pl.ds(ru, ra - ru), :] = lanes_to(bottom, W).astype(BF16)

        def quarter_copy(p):
            return remote(
                R.att_own.at[pl.ds(p * rp, rp)],
                R.watt.at[y, p, aligned(o * rp, rp)],
                R.a1_send.at[p],
                R.a1_recv.at[y, c],
                p,
                2 * zz + x,
            )

        def each_quarter(act, own):
            for p in range(SECTIONS):
                stays = (s == p) & (x == c)

                @pl.when(stays)
                def _(p=p):
                    if own:
                        R.watt[y, p, aligned(o * rp, rp), :] = R.att_own[pl.ds(p * rp, rp), :]

                @pl.when(jnp.logical_not(stays))
                def _(p=p):
                    act(quarter_copy(p))

        each_quarter(lambda copy: copy.start(), True)

        def seq_copy(local):
            if local:
                return pltpu.make_async_copy(R.stream_in.at[y], R.seq_rows, R.load_sem.at[0])
            return remote(
                R.stream_in.at[y], R.seq_rows, R.seq_send.at[0], R.seq_recv.at[0], s, mate
            )

        def cot_copy(m, j, local):
            half = c if local else 1 - c
            src = R.cot_in.at[m, aligned((2 * half + j) * Q, Q)]
            dst = R.grad_ff.at[0, aligned(j * L + (2 * m + c) * Q, Q)]
            if local:
                return pltpu.make_async_copy(src, dst, R.load_sem.at[1 + 2 * m + j])
            return remote(src, dst, R.cot_send.at[m, j], R.cot_recv.at[m, j], s, mate)

        def piece(kind, layer, outer):
            rows = rd if kind else ru
            return (R.wdown if kind else R.wup).at[layer, aligned(outer * rows, rows)]

        def y_copy(kind):
            return remote(
                R.yb_down if kind else R.yb_up,
                piece(kind, y, o),
                R.y_send.at[kind],
                R.y_recv.at[kind],
                other_y,
                o,
            )

        def chips_at(distances, body):
            for distance in distances:
                for sign in (1, -1):
                    q = zz + sign * distance

                    @pl.when((q >= 0) & (q < n))
                    def _(q=q, sign=sign, distance=distance):
                        body(q, sign, distance)

        def relays(distance, sign, body):
            if distance >= 2:
                after = zz - sign

                @pl.when((after >= 0) & (after < n))
                def _():
                    body(after)

        NEAR, FAR = tuple(range(min(2, n - 1), 0, -1)), range(3, n)

        def z_copy(layer, kind, origin, to):
            item = layer * 2 + kind
            part = piece(kind, layer, 2 * origin + c)
            send = R.z_send.at[item, origin, to]
            return remote(part, part, send, R.z_recv.at[item, origin], s, 2 * to + c)

        def mate_copy(layer, kind, q):
            item = layer * 2 + kind
            part = piece(kind, layer, 2 * q + c)
            return remote(part, part, R.p_send.at[item, q], R.p_recv.at[item, q], s, mate)

        def mate_arrival(layer, kind, q):
            item = layer * 2 + kind
            part = piece(kind, layer, 2 * q + 1 - c)
            return remote(part, part, R.p_send.at[item, q], R.p_recv.at[item, q], s, mate)

        def feed_spread(layer, kind):
            chips_at(NEAR, lambda q, *_: z_copy(layer, kind, zz, q).start())
            mate_copy(layer, kind, zz).start()

        def feed_spread_home(layer):
            @pl.when(y == layer)
            def _():
                feed_spread(layer, 0)
                feed_spread(layer, 1)

        def feed_spread_away(layer, kind):
            @pl.when(y != layer)
            def _():
                src = R.yb_down if kind else R.yb_up
                remote(
                    src,
                    piece(kind, layer, o),
                    R.y_send.at[kind],
                    R.y_recv.at[kind],
                    other_y,
                    o,
                ).wait_recv()
                feed_spread(layer, kind)

        def feed_arrivals(layer, distances):
            for kind in range(2):

                def landed(q, sign, distance):
                    z_copy(layer, kind, q, zz).wait_recv()
                    relays(
                        distance, sign, lambda after: z_copy(layer, kind, q, after).start()
                    )
                    mate_copy(layer, kind, q).start()

                chips_at(distances, landed)

        def feed_collect(layer):
            feed_arrivals(layer, FAR)
            for kind in range(2):
                loop(n, lambda q, kind=kind: mate_arrival(layer, kind, q).wait_recv())

        def feed_sent(layer):
            for kind in range(2):
                chips_at(NEAR, lambda q, *_: z_copy(layer, kind, zz, q).wait_send())
                for distances in (NEAR, FAR):
                    chips_at(
                        distances,
                        lambda q, sign, distance: relays(
                            distance,
                            sign,
                            lambda after: z_copy(layer, kind, q, after).wait_send(),
                        ),
                    )
                loop(n, lambda q, kind=kind: mate_copy(layer, kind, q).wait_send())

        def att_block(layer, p, q):
            return R.watt.at[layer, p, aligned(q * 2 * rp, 2 * rp)]

        def att_z_copy(layer, origin, to):
            part = att_block(layer, s, origin)
            send = R.a2_send.at[layer, origin, to]
            return remote(part, part, send, R.a2_recv.at[layer, origin], s, 2 * to + c)

        def att_plane_copy(layer, q, way):
            part = att_block(layer, s, q)
            to = other_y if way else other_x
            return remote(
                part, part, R.a3_send.at[layer, q, way], R.a3_recv.at[layer, q, way], to, o
            )

        def plane_half(layer, section, q, way):
            first = rp if layer else rp // 2
            start = q * 2 * rp + (first if way else 0)
            rows = 2 * rp - first if way else first
            return R.watt.at[layer, section, pl.ds(pl.multiple_of(start, 16), rows)]

        def att_plane_half(layer, q, way):
            src, to = (other_y, other_x) if way else (other_x, other_y)
            part = plane_half(layer, src, q, way)
            return remote(
                part, part, R.a4_send.at[layer, q, way], R.a4_recv.at[layer, q, way], to, o
            )

        def att_plane_start(layer, q):
            for way in range(2):
                att_plane_copy(layer, q, way).start()

        def att_plane_relay(layer, q):
            for way in range(2):
                src = other_y if way else other_x
                part = att_block(layer, src, q)
                remote(
                    part,
                    part,
                    R.a3_send.at[layer, q, way],
                    R.a3_recv.at[layer, q, way],
                    src,
                    o,
                ).wait_recv()
                att_plane_half(layer, q, way).start()

        def att_spread(layer):
            for core in range(2):
                mine = (s == 2 * layer + c) & (c == core)

                @pl.when(jnp.logical_not(mine))
                def _(core=core):
                    remote(
                        R.att_own.at[pl.ds(0, rp)],
                        R.watt.at[layer, s, aligned((2 * zz + core) * rp, rp)],
                        R.a1_send.at[0],
                        R.a1_recv.at[layer, core],
                        2 * layer + c,
                        2 * zz + core,
                    ).wait_recv()

            chips_at(reach(layer), lambda q, *_: att_z_copy(layer, zz, q).start())
            att_plane_start(layer, zz)

        def reach(layer):
            return NEAR if layer else tuple(range(1, n))

        def att_onward(layer, distances):
            def landed(q, sign, distance):
                att_z_copy(layer, q, zz).wait_recv()
                if layer:
                    relays(distance, sign, lambda after: att_z_copy(layer, q, after).start())
                att_plane_start(layer, q)

            chips_at(distances, landed)

        def att_sent(layer):
            chips_at(reach(layer), lambda q, *_: att_z_copy(layer, zz, q).wait_send())
            if layer:
                for distances in (NEAR, FAR):
                    chips_at(
                        distances,
                        lambda q, sign, distance: relays(
                            distance,
                            sign,
                            lambda after: att_z_copy(layer, q, after).wait_send(),
                        ),
                    )

            def plane_sent(q):
                for way in range(2):
                    att_plane_copy(layer, q, way).wait_send()
                    att_plane_half(layer, q, way).wait_send()

            loop(n, plane_sent)

        def att_plane_onward(layer, distances):
            chips_at(distances, lambda q, *_: att_plane_relay(layer, q))

        def att_collect(layer):
            def block(q):
                for way in range(2):
                    part = plane_half(layer, 3 - s, q, way)
                    remote(
                        part,
                        part,
                        R.a4_send.at[layer, q, way],
                        R.a4_recv.at[layer, q, way],
                        other_y,
                        o,
                    ).wait_recv()

            loop(n, block)

            def unpack(k):
                for r in range(0, ru, 16):
                    R.wqkv[layer, aligned(k * ru + r, 16), :] = R.watt[
                        layer, r // rp, aligned(k * rp + r % rp, 16), :
                    ]
                for r in range(0, ro, 16):
                    rows = min(16, ro - r)
                    p, off = (ru + r) // rp, (ru + r) % rp
                    block = R.watt[layer, p, aligned(k * rp + off, 16), :][:, :D].astype(F32)
                    R.wide_rows[aligned(k * ro + r, 8), :] = block[:rows][:8]
                    if rows > 8:
                        R.wide_rows[aligned(k * ro + r + 8, 8), :] = block[8:rows]

            loop(NO, unpack)
            R.wout[layer] = R.wide_rows[pl.ds(0, F), :].astype(BF16)

        att_spread(0)
        att_spread(1)

        raw_copies[2].wait()
        raw_copies[3].wait()
        halves = [
            jnp.concatenate(
                [R.o_up[:, (2 * k + h) * rd : (2 * k + h + 1) * rd] for k in range(NO)], axis=1
            ).astype(BF16)
            for h in range(2)
        ]
        R.wup[y, aligned(o * ru, ru), :] = jnp.where(y == 0, halves[0], halves[1])
        R.yb_up[...] = jnp.where(y == 0, halves[1], halves[0])
        R.wdown[y, aligned(o * rd, rd), :] = R.o_down[aligned(y * rd, rd), :].astype(BF16)
        R.yb_down[...] = R.o_down[aligned((1 - y) * rd, rd), :].astype(BF16)
        y_copy(0).start()
        feed_spread_home(0)

        @pl.when(x == c)
        def _():
            seq_copy(True).start()
            seq_copy(False).start()

        for m in range(2):
            for j in range(2):
                cot_copy(m, j, True).start()
                cot_copy(m, j, False).start()

        loop(
            NO,
            lambda k: remote(
                R.small_in,
                R.small_a.at[(o + k) % NO],
                R.sma_send.at[k],
                R.sma_recv.at[(o + k) % NO],
                s,
                (o + k) % NO,
            ).wait_recv(),
            1,
        )
        table = jnp.zeros((8, wide), F32)
        for k in range(NO):
            part = lanes_to(R.small_a[k], wide)
            narrow = pltpu.roll(part, ru * k, 1) if k else part
            broad = pltpu.roll(part, rd * k, 1) if k else part
            table = table + jnp.where(row8 < 4, narrow, broad)
        moved = jnp.where(lane8 < low, table, 0.0)
        moved += pltpu.roll(jnp.where((lane8 >= low) & (lane8 < F), table, 0.0), 2 * low, 1)
        moved += pltpu.roll(
            jnp.where((lane8 >= F) & (lane8 < F + low), table, 0.0), 2 * low - F, 1
        )
        moved += pltpu.roll(
            jnp.where((lane8 >= F + low) & (lane8 < 2 * F), table, 0.0), 2 * low + 2 * rest - F, 1
        )
        table = jnp.where(row8 == 3, moved, table)
        R.small_own[...] = table
        R.small_b[s] = table

        def small_b_copy(k, of):
            return remote(
                R.small_own,
                R.small_b.at[of],
                R.smb_send.at[k],
                R.smb_recv.at[of],
                (s + k) % SECTIONS,
                o,
            )

        loop(SECTIONS, lambda k: small_b_copy(k, s).start(), 1)

        def first_blocks(k):
            q = (zz + k) % n
            att_z_copy(0, q, zz).wait_recv()
            att_plane_start(0, q)
            att_plane_relay(0, (zz + k - 1) % n)

        loop(n, first_blocks, 1)
        y_copy(1).start()
        feed_spread_away(0, 0)
        att_plane_relay(0, (zz + n - 1) % n)
        loop(SECTIONS, lambda k: small_b_copy(k, (s + k) % SECTIONS).wait_recv(), 1)

        R.small_grad[...] = jnp.zeros_like(R.small_grad)
        def note_rows(block, index, row):
            R.small_grad[block] += jnp.where(row8 == index, lanes_to(row, wide), 0.0)


        @pl.when(x == c)
        def _():
            seq_copy(True).wait()

        @pl.when(x != c)
        def _():
            seq_copy(False).wait_recv()

        gain0 = R.small_b[0, 0:1, :D]
        shift0 = R.small_b[0, 1:2, :D]

        def first_norm(k):
            rows = aligned(k * Q, Q)
            _, _, out = normed_rows(R.seq_rows[rows, :].astype(F32), gain0, shift0)
            R.norm_at[0, rows, :] = out.astype(BF16)

        loop(L // Q, first_norm)
        feed_spread_away(0, 1)
        R.hid_rows[0] = R.seq_rows[aligned(c * 2 * Q, 2 * Q), :]
        len_copy.wait_recv()
        tile = jnp.where(x == c, R.len_own[...], R.len_mate[...])
        tile = jnp.where((row8[:, :128] == 0) & (lane8[:, :128] == y), tile, 0.0)
        length_here = jnp.sum(jnp.sum(tile, axis=1, keepdims=True), axis=0, keepdims=True)
        length_here = length_here.astype(jnp.int32)
        def block_copy(phase, m, buf, way):
            part = buf.at[aligned(m * L + s * Q, Q)]
            to = other_y if way else other_x
            return remote(
                part, part, R.ag_send.at[phase, m, way], R.ag_recv.at[phase, m, way], to, o
            )

        def half_copy(phase, m, buf, way):
            src, to = (other_y, other_x) if way else (other_x, other_y)
            part = buf.at[aligned(m * L + src * Q + way * (Q // 2), Q // 2)]
            slot = 2 + way
            return remote(
                part, part, R.ag_send.at[phase, m, slot], R.ag_recv.at[phase, m, slot], to, o
            )

        def share_mate(phase, m, buf):
            part = buf.at[aligned((2 * c + m) * Q, Q)]
            return remote(
                part, part, R.ag_send.at[phase, m, 0], R.ag_recv.at[phase, m, c], s, mate
            )

        def pass_rows(phase, buf):
            for m in range(2):
                for way in range(2):
                    src = other_y if way else other_x
                    part = buf.at[aligned(m * L + src * Q, Q)]
                    remote(
                        part, part, R.ag_send.at[phase, m, way], R.ag_recv.at[phase, m, way], src, o
                    ).wait_recv()
                    half_copy(phase, m, buf, way).start()

        def send_rows(phase, attention, m, buf, value):
            if attention:
                buf[aligned((2 * c + m) * Q, Q), :] = value
                share_mate(phase, m, buf).start()
            else:
                buf[aligned(m * L + s * Q, Q), :] = value
                for way in range(2):
                    block_copy(phase, m, buf, way).start()

        def finish_send_rows(phase, attention, m, buf):
            if attention:
                share_mate(phase, m, buf).wait_send()
            else:
                for way in range(2):
                    block_copy(phase, m, buf, way).wait_send()
                    half_copy(phase, m, buf, way).wait_send()

        def await_rows(phase, attention, m, buf):
            if attention:
                for j in range(2):
                    part = buf.at[aligned((2 * (1 - c) + j) * Q, Q)]
                    remote(
                        part, part, R.ag_send.at[phase, j, 0], R.ag_recv.at[phase, j, 1 - c], s, mate
                    ).wait_recv()
            else:
                for way in range(2):
                    part = buf.at[aligned(m * L + (3 - s) * Q + way * (Q // 2), Q // 2)]
                    slot = 2 + way
                    remote(
                        part,
                        part,
                        R.ag_send.at[phase, m, slot],
                        R.ag_recv.at[phase, m, slot],
                        other_y,
                        o,
                    ).wait_recv()

        def sum_slot(phase):
            return 0 if phase < 4 else 1

        HOP, STRAIGHT, LATE = 0, 2, 4

        def half_rows(m, section, way):
            return aligned(m * L + section * Q + way * (Q // 2), Q // 2)

        def half_sum(phase, src, m, way):
            return R.sums.at[sum_slot(phase), src, m, pl.ds(way * (Q // 2), Q // 2)]

        def part_copy(phase, m, step, way):
            near, far = (other_y, other_x) if way else (other_x, other_y)
            if step == HOP:
                to, rows, dst = near, half_rows(m, 3 - s, way), half_sum(phase, far, m, way)
            elif step == STRAIGHT:
                to, rows, dst = near, half_rows(m, near, way), half_sum(phase, s, m, way)
            else:
                to, rows, dst = far, half_rows(m, far, way), half_sum(phase, s, m, way)
            slot = step + way
            return remote(
                R.parts.at[rows],
                dst,
                R.rs_send.at[phase, m, slot],
                R.rs_recv.at[phase, m, slot],
                to,
                o,
            )

        def part_landed(phase, m, step, way):
            near, far = (other_y, other_x) if way else (other_x, other_y)
            src = 3 - s if step == HOP else (near if step == STRAIGHT else far)
            slot = step + way
            remote(
                R.parts.at[pl.ds(0, Q // 2)],
                half_sum(phase, src, m, way),
                R.rs_send.at[phase, m, slot],
                R.rs_recv.at[phase, m, slot],
                near,
                o,
            ).wait_recv()

        def late_parts(phase, m):
            for way in range(2):
                part_landed(phase, m, HOP, way)
                rows = half_rows(m, other_x if way else other_y, way)
                hop = R.sums[sum_slot(phase), 3 - s, m, pl.ds(way * (Q // 2), Q // 2), :]
                both = R.parts[rows, :].astype(F32) + hop.astype(F32)
                R.parts[rows, :] = both.astype(BF16)
                part_copy(phase, m, LATE, way).start()

        def mate_part(phase, j):
            return remote(
                R.parts.at[aligned((2 * (1 - c) + j) * Q, Q)],
                R.sums.at[sum_slot(phase), c, j],
                R.rs_send.at[phase, j, 0],
                R.rs_recv.at[phase, j, c],
                s,
                mate,
            )

        def send_parts(phase, attention, m):
            slot = sum_slot(phase)
            if attention:
                for j in range(2):
                    mate_part(phase, j).start()
                    R.sums[slot, c, j] = R.parts[aligned((2 * c + j) * Q, Q), :]
            else:
                for step in (HOP, STRAIGHT):
                    for way in range(2):
                        part_copy(phase, m, step, way).start()
                R.sums[slot, s, m] = R.parts[aligned(m * L + s * Q, Q), :]

        def finish_send_parts(phase, attention, chunks=(0, 1)):
            for m in chunks:
                if attention:
                    mate_part(phase, m).wait_send()
                else:
                    for step in (HOP, STRAIGHT, LATE):
                        for way in range(2):
                            part_copy(phase, m, step, way).wait_send()

        def part_arrival(phase, m, src):
            return remote(
                R.parts.at[pl.ds(0, Q)],
                R.sums.at[sum_slot(phase), src, m],
                R.rs_send.at[phase, m, 0],
                R.rs_recv.at[phase, m, src],
                s,
                mate,
            )

        def await_parts(phase, attention, m):
            slot = sum_slot(phase)
            if attention:
                part_arrival(phase, m, 1 - c).wait_recv()
                sources = range(2)
            else:
                for step in (STRAIGHT, LATE):
                    for way in range(2):
                        part_landed(phase, m, step, way)
                sources = (s, other_x, other_y)
            total = None
            for src in sources:
                part = R.sums[slot, src, m].astype(F32)
                total = part if total is None else total + part
            return total

        def place_copy(which, j):
            return remote(
                R.finished.at[which, j],
                (R.out_grad_rows if which else R.out_stream).at[aligned(y * Q, Q)],
                R.fo_send.at[which, j],
                R.fo_recv.at[which, y],
                2 * c + j,
                2 * zz + x,
            )

        def place_rows(which, j, value):
            stays = (s == 2 * c + j) & (x == c)
            R.finished[which, j] = value

            @pl.when(stays)
            def _():
                (R.out_grad_rows if which else R.out_stream)[aligned(y * Q, Q), :] = value

            @pl.when(jnp.logical_not(stays))
            def _():
                place_copy(which, j).start()

        def finish_place(which):
            for j in range(2):
                stays = (s == 2 * c + j) & (x == c)

                @pl.when(jnp.logical_not(stays))
                def _(j=j):
                    place_copy(which, j).wait_send()

            for m in range(2):
                mine = (s == 2 * m + c) & (y == c)

                @pl.when(jnp.logical_not(mine))
                def _(m=m):
                    remote(
                        R.finished.at[which, 0],
                        (R.out_grad_rows if which else R.out_stream).at[pl.ds(m * Q, Q)],
                        R.fo_send.at[which, 0],
                        R.fo_recv.at[which, m],
                        2 * m + c,
                        2 * zz + y,
                    ).wait_recv()

        def close_forward(phase, m):
            e = phase
            attention = e % 2 == 0
            branch = await_parts(phase, attention, m) + R.small_b[e, 2:3, :D]
            mine = pl.ds(m * Q, Q)
            h = R.hid_rows[e, mine, :].astype(F32)
            position = (2 * c + m) * Q + lax.broadcasted_iota(jnp.int32, (Q, 1), 0)
            valid = (position < length_here).astype(F32)
            square_h = jnp.sum(jnp.sum(h * h * valid, axis=1, keepdims=True), axis=0, keepdims=True)
            square_b = jnp.sum(
                jnp.sum(branch * branch * valid, axis=1, keepdims=True), axis=0, keepdims=True
            )
            spot = (2 * zz + x) * 4 + 2 * y
            R.small_grad[e] += jnp.where((row8 == 6) & (lane8 == spot), square_h, 0.0)
            R.small_grad[e] += jnp.where((row8 == 6) & (lane8 == spot + 1), square_b, 0.0)
            fresh = (h + branch).astype(BF16)
            if e == 3:
                place_rows(0, m, fresh)
                return
            R.hid_rows[e + 1, mine, :] = fresh
            _, _, out = normed_rows(
                fresh.astype(F32), R.small_b[e + 1, 0:1, :D], R.small_b[e + 1, 1:2, :D]
            )
            to_attention = (e + 1) % 2 == 0
            buf = (R.norm_at if to_attention else R.norm_ff).at[(e + 1) // 2]
            send_rows(phase + 1, to_attention, m, buf, out.astype(BF16))

        grad_at = (R.seq_rows, R.grad_at)

        def close_backward(phase, m):
            e = 7 - phase
            attention = e % 2 == 0
            d_norm = await_parts(phase, attention, m)
            mine = pl.ds(m * Q, Q)
            unit, inverse, _ = normed_rows(R.hid_rows[e, mine, :].astype(F32), 1.0, 0.0)
            flow = R.grad_rows[mine, :].astype(F32)
            note_rows(e, 0, jnp.sum(d_norm * unit, axis=0, keepdims=True))
            note_rows(e, 1, jnp.sum(d_norm, axis=0, keepdims=True))
            note_rows(e, 2, jnp.sum(flow, axis=0, keepdims=True))
            a = d_norm * R.small_b[e, 0:1, :D]
            mean_a = jnp.mean(a, axis=-1, keepdims=True)
            mean_ax = jnp.mean(a * unit, axis=-1, keepdims=True)
            fresh = (flow + (a - mean_a - unit * mean_ax) * inverse).astype(BF16)
            if e == 0:
                place_rows(1, m, fresh)
                return
            R.grad_rows[mine, :] = fresh
            to_attention = (e - 1) % 2 == 0
            buf = grad_at[(e - 1) // 2] if to_attention else R.grad_ff.at[1]
            send_rows(phase + 1, to_attention, m, buf, fresh)

        ga = (R.hidden.at[1], R.slope.at[1])

        def attention_forward(layer):
            bias = R.small_b[2 * layer + c, 3:4, :W]
            xs = R.norm_at.at[layer]
            for t in range(0, W, 256):
                cols = pl.ds(t, 256)
                lin = mm(xs[...], R.wqkv[layer, :, cols]) + bias[:, t : t + 256]
                R.lin_t[layer, cols, :] = lin.T.astype(BF16)

            def head(h):
                q0, k0, v0 = head_rows(h, heads)
                score = mm(
                    R.lin_t[layer, pl.ds(k0, HEAD_DIM), :],
                    R.lin_t[layer, pl.ds(q0, HEAD_DIM), :],
                    TN,
                )
                live = lax.broadcasted_iota(jnp.int32, score.shape, 0) < length_here
                score = jnp.where(live, score, MASKED)
                top = jnp.max(score, axis=0, keepdims=True)
                powers = jnp.exp2((score - top) * SCALE_2)
                total = jnp.sum(powers, axis=0, keepdims=True)
                probs = (powers * (1.0 / total)).astype(BF16)
                R.log_total[layer, h] = top * SCALE_2 + jnp.log2(total)
                mixed = mm(R.lin_t[layer, pl.ds(v0, HEAD_DIM), :], probs)
                R.att_t[layer, aligned(h * HEAD_DIM, HEAD_DIM), :] = mixed.astype(BF16)

            def pair(h):
                head(2 * h)
                head(2 * h + 1)

            loop(heads // 2, pair)
            if heads % 2:
                head(heads - 1)
            R.parts[pl.ds(0, L), :] = mm(R.att_t[layer], R.wout[layer], TN).astype(BF16)

        def attention_back_heads(layer, between):
            g = grad_at[layer]
            R.d_att_t[...] = mm(R.wout[layer], g[...], NT).astype(BF16)

            def head(h):
                q0, k0, v0 = head_rows(h, heads)
                q_t = R.lin_t[layer, pl.ds(q0, HEAD_DIM), :]
                k_t = R.lin_t[layer, pl.ds(k0, HEAD_DIM), :]
                v_t = R.lin_t[layer, pl.ds(v0, HEAD_DIM), :]
                d_a = R.d_att_t[aligned(h * HEAD_DIM, HEAD_DIM), :]
                score = mm(k_t, q_t, TN)
                live = lax.broadcasted_iota(jnp.int32, score.shape, 0) < length_here
                probs = jnp.where(live, jnp.exp2(score * SCALE_2 - R.log_total[layer, h]), 0.0)
                d_probs = mm(v_t, d_a, TN)
                product = probs * d_probs
                inner_sum = jnp.sum(product, axis=0, keepdims=True)
                d_score = ((product - probs * inner_sum) * SCALE).astype(BF16)
                R.d_lin_t[pl.ds(q0, HEAD_DIM), :] = mm(k_t, d_score).astype(BF16)
                R.d_lin_t[pl.ds(k0, HEAD_DIM), :] = mm(q_t, d_score, NT).astype(BF16)
                R.d_lin_t[pl.ds(v0, HEAD_DIM), :] = mm(d_a, probs.astype(BF16), NT).astype(BF16)

            def pair(h):
                head(2 * h)
                head(2 * h + 1)

            loop(heads // 4, pair)
            between()
            loop(heads // 2, pair, heads // 4)
            if heads % 2:
                head(heads - 1)

        def attention_back_rows(layer):
            for t in range(0, W, 256):
                cols = pl.ds(t, 256)
                part = mm(R.d_lin_t[cols, :], R.wqkv[layer, :, cols], (((0,), (1,)), ((), ())))
                if t == 0:
                    R.acc[...] = part
                else:
                    R.acc[...] += part
            R.parts[pl.ds(0, L), :] = R.acc[...].astype(BF16)

        def attention_back_out(layer):
            stage = 1 - layer
            R.wide_rows[pl.ds(0, F), :] = mm(R.att_t[layer], grad_at[layer][...])

            def out_rows(k):
                for r in range(ru, ra, 16):
                    top_half = R.wide_rows[aligned(k * ro + r - ru, 8), :]
                    low_half = R.wide_rows[aligned(k * ro + r - ru + 8, 8), :]
                    block = jnp.concatenate([top_half, low_half], axis=0)
                    place = aligned(r // rp * NO * rp + k * rp + r % rp, 16)
                    ga[stage][place, 0:D] = block.astype(BF16)

            loop(NO, out_rows)

        def attention_back_weights(layer):
            stage = 1 - layer
            sums = []
            for t in range(0, W, 256):
                cols = pl.ds(t, 256)
                d_lin = R.d_lin_t[cols, :].T
                sums.append(jnp.sum(d_lin.astype(F32), axis=0, keepdims=True))
                d_w = mm(R.norm_at[layer], d_lin, TN).astype(BF16)
                for k in range(NO):
                    for r in range(0, ru, 16):
                        place = pl.ds(r // rp * NO * rp + k * rp + r % rp, 16)
                        ga[stage][place, cols] = d_w[k * ru + r : k * ru + r + 16]
            note_rows(2 * layer + c, 3, jnp.concatenate(sums, axis=1))

        def feed_bias(layer):
            block = R.small_b[2 * layer + x]
            return jnp.where(y == 0, block[4:5], block[5:6])[:, :U]

        def feed_up(layer, m):
            bias = feed_bias(layer)

            def rows_step(r):
                rows = aligned(m * L + r * Q, Q)
                pre = mm(R.norm_ff[layer, rows, :], R.wup[layer]) + bias
                cdf = 0.5 + 0.5 * lax.erf(pre * 0.7071067811865476)
                density = jnp.exp(pre * pre * -0.5) * 0.3989422804014327
                R.hidden[layer, rows, :] = (pre * cdf).astype(BF16)
                R.slope[layer, rows, :] = (cdf + pre * density).astype(BF16)

            loop(SECTIONS, rows_step)

        def feed_down(layer, m):
            rows = pl.ds(m * L, L)
            R.parts[rows, :] = mm(R.hidden[layer, rows, :], R.wdown[layer]).astype(BF16)

        def feed_back_rows(layer, m):
            rows = pl.ds(m * L, L)
            g = R.grad_ff.at[0 if layer == 1 else 1, rows]
            tile = U // 2
            for j in range(2):
                cols = pl.ds(j * tile, tile)
                d_hidden = mm(g[...], R.wdown[layer, cols, :], NT)
                d_pre = (d_hidden * R.slope[layer, rows, cols].astype(F32)).astype(BF16)
                R.slope[layer, rows, cols] = d_pre
                part = mm(d_pre, R.wup[layer, :, cols], NT)
                if j == 0:
                    R.acc[...] = part
                else:
                    R.parts[rows, :] = (R.acc[...] + part).astype(BF16)

        def feed_back_weights(layer):
            xs = R.norm_ff.at[layer]
            g = R.grad_ff.at[0 if layer == 1 else 1]
            tile = U // 2
            owners = tile // rd
            sums = []
            for j in range(2):
                cols = pl.ds(j * tile, tile)
                d_pre = R.slope[layer, :, cols]
                d_down = mm(R.hidden[layer, :, cols], g[...], TN).astype(BF16)
                for k in range(owners):
                    owner = j * owners + k
                    R.sb_down[owner % 2, pl.ds(owner // 2 * rd, rd), :] = d_down[
                        k * rd : (k + 1) * rd
                    ]
                d_up = mm(xs[...], d_pre, TN).astype(BF16)
                for k in range(NO):
                    R.sb_up[k % 2, pl.ds(k // 2 * ru, ru), cols] = d_up[k * ru : (k + 1) * ru]
                sums.append(jnp.sum(d_pre.astype(F32), axis=0, keepdims=True))
            note_rows(2 * layer + x, 4 + y, jnp.concatenate(sums, axis=1))

        z_up, z_down = (R.zb_up, R.wup.at[1]), (R.zb_down, R.norm_ff.at[1])
        FEED_GRADS = (
            (0, R.sb_up, R.rb_up, R.mb_up, z_up, R.yb_up, R.yr_up, ru),
            (1, R.sb_down, R.rb_down, R.mb_down, z_down, R.yb_down, R.yr_down, rd),
        )

        def mate_grads(stage):
            return [
                remote(sb.at[1 - c], rb, R.r1_send.at[stage, a], R.r1_recv.at[stage, a], s, mate)
                for a, sb, rb, *_ in FEED_GRADS
            ]

        RELAYED = n == 4

        def z_grad(stage, entry, q, to, slot):
            a, sb, rb, mb, zb, yb, yr, rows = entry
            return remote(
                mb.at[aligned(q * rows, rows)],
                zb[stage].at[aligned(slot * rows, rows)],
                R.r2_send.at[stage, a, q],
                R.r2_recv.at[stage, a, slot],
                s,
                2 * to + c,
            )

        def each_z_grad(stage, act, late):
            def one(entry, q, sign, distance):
                if RELAYED and distance == 3:
                    if not late:
                        act(z_grad(stage, entry, q, zz + sign, zz + sign))
                elif RELAYED and distance == 2:
                    behind = zz - sign
                    waits = (behind >= 0) & (behind < n)

                    @pl.when(waits if late else jnp.logical_not(waits))
                    def _():
                        if late:
                            late_sum(stage, entry, q, act)
                        else:
                            act(z_grad(stage, entry, q, q, zz))
                elif not late:
                    act(z_grad(stage, entry, q, q, zz))

            def each(*where):
                for entry in FEED_GRADS:
                    one(entry, *where)

            chips_at(range(n - 1, 0, -1), each)

        def late_sum(stage, entry, q, act):
            a, sb, rb, mb, zb, yb, yr, rows = entry
            if act is None:
                act = lambda copy: copy.wait_send()
            else:
                hop = aligned(zz * rows, rows)
                remote(
                    mb.at[pl.ds(0, rows)],
                    zb[stage].at[hop],
                    R.r2_send.at[stage, a, zz],
                    R.r2_recv.at[stage, a, zz],
                    s,
                    mate,
                ).wait_recv()
                part = aligned(q * rows, rows)
                both = mb[part, :].astype(F32) + zb[stage][hop, :].astype(F32)
                mb[part, :] = both.astype(BF16)
            act(z_grad(stage, entry, q, q, zz))

        def feed_to_mate(stage):
            for copy in mate_grads(stage):
                copy.start()

        def finish_feed_z(stage):
            each_z_grad(stage, lambda copy: copy.wait_send(), False)
            each_z_grad(stage, None, True)

        def feed_late(stage):
            each_z_grad(stage, lambda copy: copy.start(), True)

        def feed_along_z(stage):
            for copy in mate_grads(stage):
                copy.wait()
            if stage:
                finish_feed_z(0)
            for a, sb, rb, mb, zb, yb, yr, rows in FEED_GRADS:

                def add(q, sb=sb, rb=rb, mb=mb, rows=rows):
                    part = aligned(q * rows, rows)
                    both = sb[c, part, :].astype(F32) + rb[part, :].astype(F32)
                    mb[part, :] = both.astype(BF16)

                loop(n, add)
            each_z_grad(stage, lambda copy: copy.start(), False)

        def y_grad(a, yb, yr):
            return remote(yb, yr, R.r4_send.at[a], R.r4_recv.at[a], other_y, o)

        def keep_half(a, h, value):
            if a:
                R.o_down[pl.ds(h * rd, rd), :] = value
                return
            for k in range(NO):
                R.o_up[:, (2 * k + h) * rd : (2 * k + h + 1) * rd] = value[:, k * rd : (k + 1) * rd]

        def feed_owned(stage):
            layer = 1 - stage
            for a, sb, rb, mb, zb, yb, yr, rows in FEED_GRADS:

                def landed(q, sign, distance, a=a, zb=zb, mb=mb, rows=rows):
                    if not (RELAYED and distance == 3):
                        remote(
                            mb.at[pl.ds(0, rows)],
                            zb[stage].at[aligned(q * rows, rows)],
                            R.r2_send.at[stage, a, q],
                            R.r2_recv.at[stage, a, q],
                            s,
                            2 * q + c,
                        ).wait_recv()

                chips_at(range(1, n), landed)
                total = mb[aligned(zz * rows, rows), :].astype(F32)
                for k in range(1, n):
                    q = (zz + k) % n
                    part = zb[stage][aligned(q * rows, rows), :].astype(F32)
                    if RELAYED:
                        part = jnp.where(jnp.abs(q - zz) == 3, 0.0, part)
                    total = total + part

                @pl.when(y == layer)
                def _(a=a, total=total):
                    keep_half(a, layer, total)

                @pl.when(y != layer)
                def _(a=a, yb=yb, yr=yr, total=total):
                    yb[...] = total.astype(BF16)

        def feed_to_home(stage):
            @pl.when(y == stage)
            def _():
                for a, sb, rb, mb, zb, yb, yr, rows in FEED_GRADS:
                    y_grad(a, yb, yr).start()

        def feed_home():
            for a, sb, rb, mb, zb, yb, yr, rows in FEED_GRADS:
                y_grad(a, yb, yr).wait()
                for h in range(2):

                    @pl.when(y == 1 - h)
                    def _(a=a, h=h, yr=yr):
                        keep_half(a, h, yr[...].astype(F32))

        att_rows = NO * rp

        def plane_grad(stage, k, q):
            to = (s + k) % SECTIONS
            return remote(
                ga[stage].at[aligned(to * att_rows + q * 2 * rp, 2 * rp), pl.ds(0, W)],
                R.watt.at[stage, s, aligned(q * 2 * rp, 2 * rp)],
                R.g1_send.at[stage, k, q],
                R.g1_recv.at[stage, s, q],
                to,
                o,
            )

        def each_plane_grad(stage, act):
            def block(j):
                q = (zz + j) % n
                loop(SECTIONS, lambda k: act(plane_grad(stage, k, q)), 1)

            loop(n + 1, block, 1)

        def att_to_plane(stage):
            each_plane_grad(stage, lambda copy: copy.start())

        def finish_att_plane(stage):
            each_plane_grad(stage, lambda copy: copy.wait_send())

        def att_z_grad(stage, k):
            q = (zz + k) % n
            return remote(
                R.gs.at[stage, aligned(q * 2 * rp, 2 * rp)],
                R.gz.at[stage, zz],
                R.g2_send.at[stage, q],
                R.g2_recv.at[stage, zz],
                s,
                2 * q + c,
            )

        def finish_att_z(stage):
            loop(n, lambda k: att_z_grad(stage, k).wait_send(), 1)

        def att_along_z(stage, first=1, last=n):
            def block(j):
                q = (zz + j) % n
                part = aligned(q * 2 * rp, 2 * rp)

                def landed(k):
                    src = (s + k) % SECTIONS
                    remote(
                        ga[stage].at[aligned(q * 2 * rp, 2 * rp), pl.ds(0, W)],
                        R.watt.at[stage, src, part],
                        R.g1_send.at[stage, k, q],
                        R.g1_recv.at[stage, src, q],
                        src,
                        o,
                    ).wait_recv()

                loop(SECTIONS, landed, 1)
                own = aligned(s * att_rows + q * 2 * rp, 2 * rp)
                total = ga[stage][own, 0:W].astype(F32)
                for k in range(1, SECTIONS):
                    total = total + R.watt[stage, (s + k) % SECTIONS, part, :].astype(F32)
                R.gs[stage, part, :] = total.astype(BF16)

                @pl.when(q != zz)
                def _():
                    att_z_grad(stage, j).start()

            loop(last + 1, block, first)

        def home_copy(stage, core):
            return remote(
                R.gt.at[stage, pl.ds(core * rp, rp)],
                R.att_own.at[aligned(s * rp, rp)],
                R.g3_send.at[stage, core],
                R.g3_recv.at[s],
                2 * (1 - stage) + c,
                2 * zz + core,
            )

        def each_home(stage, act, own):
            for core in range(2):
                stays = (s == 2 * (1 - stage) + c) & (c == core)

                @pl.when(stays)
                def _(core=core):
                    if own:
                        R.att_own[aligned(s * rp, rp), :] = R.gt[stage, pl.ds(core * rp, rp), :]

                @pl.when(jnp.logical_not(stays))
                def _(core=core):
                    act(home_copy(stage, core))

        def att_owned(stage):
            def landed(k):
                q = (zz + k) % n
                remote(
                    R.gs.at[stage, pl.ds(0, 2 * rp)],
                    R.gz.at[stage, q],
                    R.g2_send.at[stage, q],
                    R.g2_recv.at[stage, q],
                    s,
                    2 * q + c,
                ).wait_recv()

            loop(n, landed, 1)
            total = R.gs[stage, aligned(zz * 2 * rp, 2 * rp), :].astype(F32)
            for k in range(1, n):
                total = total + R.gz[stage, (zz + k) % n].astype(F32)
            R.gt[stage] = total.astype(BF16)
            each_home(stage, lambda copy: copy.start(), True)

        def att_home():
            for p in range(SECTIONS):
                mine = (s == p) & (x == c)

                @pl.when(jnp.logical_not(mine))
                def _(p=p):
                    remote(
                        R.gt.at[0, pl.ds(0, rp)],
                        R.att_own.at[pl.ds(p * rp, rp)],
                        R.g3_send.at[0, 0],
                        R.g3_recv.at[p],
                        p,
                        2 * zz + x,
                    ).wait_recv()

            rows = R.att_own[pl.ds(0, ru), :].astype(F32)
            R.o_qkv[...] = from_packed(rows, F, heads)
            rows = R.att_own[pl.ds(ru, ra - ru), :].astype(F32)
            R.o_out[...] = rows[:ro, :D]

        att_collect(0)
        att_onward(1, NEAR)
        attention_forward(0)
        send_parts(0, True, None)
        for m in range(2):
            close_forward(0, m)
        feed_arrivals(0, NEAR)
        feed_spread_home(1)
        feed_spread_away(1, 0)
        feed_spread_away(1, 1)
        pass_rows(1, R.norm_ff.at[0])
        att_onward(1, FAR)
        feed_collect(0)
        finish_send_parts(0, True)
        await_rows(1, False, 0, R.norm_ff.at[0])
        feed_up(0, 0)
        feed_down(0, 0)
        send_parts(1, False, 0)
        att_plane_relay(1, zz)
        att_plane_onward(1, NEAR)
        await_rows(1, False, 1, R.norm_ff.at[0])
        feed_up(0, 1)
        feed_down(0, 1)
        send_parts(1, False, 1)
        late_parts(1, 0)
        att_plane_onward(1, FAR)
        late_parts(1, 1)
        close_forward(1, 0)
        feed_arrivals(1, NEAR)
        close_forward(1, 1)
        att_collect(1)
        finish_send_parts(1, False)
        await_rows(2, True, None, R.norm_at.at[1])
        attention_forward(1)
        send_parts(2, True, None)
        for m in range(2):
            close_forward(2, m)
        feed_collect(1)
        pass_rows(3, R.norm_ff.at[1])
        finish_send_parts(2, True)
        for m in range(2):
            await_rows(3, False, m, R.norm_ff.at[1])
            feed_up(1, m)

        loop(NO, lambda k: small_out(k).wait_send(), 1)
        loop(SECTIONS, lambda k: small_b_copy(k, s).wait_send(), 1)
        len_copy.wait_send()
        each_quarter(lambda copy: copy.wait_send(), False)

        @pl.when(x == c)
        def _():
            seq_copy(False).wait_send()

        for kind in range(2):
            y_copy(kind).wait_send()
        for layer in range(2):
            att_sent(layer)
            feed_sent(layer)
        for m in range(2):
            finish_send_rows(1, False, m, R.norm_ff.at[0])
            finish_send_rows(2, True, m, R.norm_at.at[1])
            finish_send_rows(3, False, m, R.norm_ff.at[1])
            for j in range(2):
                cot_copy(m, j, True).wait()
                cot_copy(m, j, False).wait_send()
                remote(
                    R.cot_in.at[m, pl.ds(0, Q)],
                    R.grad_ff.at[0, aligned(j * L + (2 * m + 1 - c) * Q, Q)],
                    R.cot_send.at[m, j],
                    R.cot_recv.at[m, j],
                    s,
                    mate,
                ).wait_recv()
        for j in range(2):
            R.grad_rows[pl.ds(j * Q, Q), :] = R.grad_ff[0, aligned(j * L + s * Q, Q), :]

        for m in range(2):
            feed_back_rows(1, m)
            send_parts(4, False, m)
        feed_back_weights(1)
        feed_to_mate(0)
        for m in range(2):
            late_parts(4, m)
        feed_along_z(0)
        for m in range(2):
            close_backward(4, m)
        finish_send_parts(4, False)
        for m in range(2):
            feed_down(1, m)
            send_parts(3, False, m)
        await_rows(5, True, None, grad_at[1])
        attention_back_heads(
            1, lambda: (feed_late(0), late_parts(3, 0), late_parts(3, 1))
        )
        finish_send_parts(3, False, (0,))
        attention_back_rows(1)
        send_parts(5, True, None)
        attention_back_out(1)
        attention_back_weights(1)
        for m in range(2):
            close_backward(5, m)
        for m in range(2):
            close_forward(3, m)
        finish_send_parts(3, False, (1,))
        finish_send_parts(5, True)
        pass_rows(6, R.grad_ff.at[1])
        for m in range(2):
            await_rows(6, False, m, R.grad_ff.at[1])
            feed_back_rows(0, m)
            send_parts(6, False, m)
        feed_back_weights(0)
        feed_to_mate(1)
        for m in range(2):
            late_parts(6, m)
        att_to_plane(0)
        for m in range(2):
            finish_send_rows(5, True, m, grad_at[1])
        feed_owned(0)
        feed_along_z(1)
        for m in range(2):
            close_backward(6, m)
        finish_send_parts(6, False)
        await_rows(7, True, None, grad_at[0])
        attention_back_out(0)
        attention_back_heads(0, lambda: feed_late(1))
        attention_back_weights(0)
        att_to_plane(1)
        feed_to_home(0)
        attention_back_rows(0)
        send_parts(7, True, None)
        att_along_z(0)
        for m in range(2):
            close_backward(7, m)

        def small_grad_copy(k, of):
            to = (s + k) % SECTIONS
            return remote(
                R.small_grad.at[to],
                R.small_sum.at[of],
                R.sga_send.at[k],
                R.sga_recv.at[of],
                to,
                o,
            )

        loop(SECTIONS, lambda k: small_grad_copy(k, s).start(), 1)
        R.small_sum[s] = R.small_grad[s]
        att_along_z(1, 1, 2)
        feed_owned(1)
        feed_to_home(1)
        att_along_z(1, 3, n)
        loop(SECTIONS, lambda k: small_grad_copy(k, (s + k) % SECTIONS).wait_recv(), 1)
        total = R.small_sum[0]
        for k in range(1, SECTIONS):
            total = total + R.small_sum[k]
        R.small_line[...] = total

        def small_line_copy(k, of):
            peer = (o + k) % NO
            return remote(
                R.small_line, R.small_all.at[of], R.sgb_send.at[k], R.sgb_recv.at[of], s, peer
            )

        loop(NO, lambda k: small_line_copy(k, o).start(), 1)
        R.small_all[o] = total
        att_owned(0)
        feed_home()
        att_owned(1)
        loop(NO, lambda k: small_line_copy(k, (o + k) % NO).wait_recv(), 1)
        total = R.small_all[0]
        for k in range(1, NO):
            total = total + R.small_all[k]

        def back(rows, lanes):
            return pltpu.roll(rows, (wide - lanes) % wide, 1)

        norms = back(total, ru * o)
        for k in range(3):
            R.o_norm[k] = norms[k : k + 1, 0:ru]
        units = back(total, rd * o)
        R.o_upb[:, 0:rd] = units[4:5, 0:rd]
        R.o_upb[:, rd : 2 * rd] = units[5:6, 0:rd]
        first, second, third = 3 * low, 3 * low + 2 * rest, 3 * low + 3 * rest
        plain = jnp.where(lane8 < low, total, 0.0)
        plain += back(jnp.where((lane8 >= first) & (lane8 < first + rest), total, 0.0), 2 * low)
        plain += back(jnp.where((lane8 >= 2 * low) & (lane8 < first), total, 0.0), 2 * low - F)
        plain += back(
            jnp.where((lane8 >= second) & (lane8 < third), total, 0.0), 2 * low + 2 * rest - F
        )
        R.o_qvb[...] = back(plain, ru * o)[3:4, 0:ru]
        squares = back(total, 4 * o)
        for m in range(2):
            count = (R.lens[0, m] * D).astype(F32)
            R.o_rms[m : m + 1, :] = jnp.sqrt(squares[6:7, 2 * m : 2 * m + 2] / count)
        att_home()
        for which in range(2):
            finish_place(which)

        loop(SECTIONS, lambda k: small_grad_copy(k, s).wait_send(), 1)
        loop(NO, lambda k: small_line_copy(k, o).wait_send(), 1)
        for m in range(2):
            finish_send_rows(6, False, m, R.grad_ff.at[1])
            finish_send_rows(7, True, m, grad_at[0])
        finish_send_parts(7, True)
        finish_feed_z(1)
        for stage in range(2):
            finish_att_plane(stage)
            finish_att_z(stage)
            each_home(stage, lambda copy: copy.wait_send(), False)

    return kernel


def one_step(cfg, lens, qkv, qv_b, out, up, up_b, down, norm, stream, cotangent):
    D, L, U, F, W = cfg.width, cfg.length, cfg.units, cfg.features, cfg.packed
    Q = L // SECTIONS
    NO, n = cfg.outer, cfg.outer // 2
    ru, rd, ro, ra = cfg.up_rows, cfg.down_rows, cfg.out_rows, cfg.att_rows
    rp = ra // SECTIONS
    wide = max(U, W)
    lanes = -(-max(ru, rd) // 128) * 128
    dma = pltpu.SemaphoreType.DMA
    inputs = dict(
        lens=lens,
        qkv_w=qkv,
        qv_b=qv_b,
        out_w=out,
        up_w=up,
        up_b=up_b,
        down_w=down,
        norm_v=norm,
        stream_in=stream,
        cot_in=cotangent,
    )
    outputs = dict(
        out_stream=((2 * Q, D), BF16),
        out_grad_rows=((2 * Q, D), BF16),
        o_qkv=((ru, 3 * F), F32),
        o_qvb=((1, ru), F32),
        o_out=((ro, D), F32),
        o_up=((ru, 2 * U), F32),
        o_upb=((1, 2 * rd), F32),
        o_down=((2 * rd, D), F32),
        o_norm=((3, 1, ru), F32),
        o_rms=((2, 2), F32),
    )
    scratch = dict(
        small_in=((8, lanes), F32),
        small_a=((NO, 8, lanes), F32),
        small_own=((8, wide), F32),
        small_b=((SECTIONS, 8, wide), F32),
        small_grad=((SECTIONS, 8, wide), F32),
        small_sum=((SECTIONS, 8, wide), F32),
        small_line=((8, wide), F32),
        small_all=((NO, 8, wide), F32),
        len_own=((8, 128), F32),
        len_mate=((8, 128), F32),
        att_own=((ra, W), BF16),
        watt=((2, SECTIONS, NO * rp, W), BF16),
        wqkv=((2, D, W), BF16),
        wout=((2, F, D), BF16),
        wup=((2, D, U), BF16),
        wdown=((2, U, D), BF16),
        hid_rows=((SECTIONS, 2 * Q, D), BF16),
        grad_rows=((2 * Q, D), BF16),
        norm_at=((2, L, D), BF16),
        norm_ff=((2, 2 * L, D), BF16),
        lin_t=((2, W, L), BF16),
        att_t=((2, F, L), BF16),
        log_total=((2, cfg.heads, 1, L), F32),
        hidden=((2, 2 * L, U), BF16),
        slope=((2, 2 * L, U), BF16),
        grad_ff=((2, 2 * L, D), BF16),
        grad_at=((L, D), BF16),
        seq_rows=((L, D), BF16),
        parts=((2 * L, D), BF16),
        sums=((2, SECTIONS, 2, Q, D), BF16),
        finished=((2, 2, Q, D), BF16),
        acc=((L, D), F32),
        wide_rows=((F + 64, D), F32),
        d_att_t=((F, L), BF16),
        d_lin_t=((W, L), BF16),
        sb_up=((2, n * ru, U), BF16),
        rb_up=((n * ru, U), BF16),
        mb_up=((n * ru, U), BF16),
        zb_up=((n * ru, U), BF16),
        yb_up=((ru, U), BF16),
        yr_up=((ru, U), BF16),
        sb_down=((2, n * rd, D), BF16),
        rb_down=((n * rd, D), BF16),
        mb_down=((n * rd, D), BF16),
        zb_down=((n * rd, D), BF16),
        yb_down=((rd, D), BF16),
        yr_down=((rd, D), BF16),
        gs=((2, NO * rp, W), BF16),
        gz=((2, n, 2 * rp, W), BF16),
        gt=((2, 2 * rp, W), BF16),
    )
    semaphores = dict(
        raw_sem=(4,),
        load_sem=(5,),
        sma_send=(NO,),
        sma_recv=(NO,),
        smb_send=(SECTIONS,),
        smb_recv=(SECTIONS,),
        len_send=(1,),
        len_recv=(1,),
        seq_send=(1,),
        seq_recv=(1,),
        cot_send=(2, 2),
        cot_recv=(2, 2),
        a1_send=(SECTIONS,),
        a1_recv=(2, 2),
        a2_send=(2, n, n),
        a2_recv=(2, n),
        a3_send=(2, n, 2),
        a3_recv=(2, n, 2),
        a4_send=(2, n, 2),
        a4_recv=(2, n, 2),
        y_send=(2,),
        y_recv=(2,),
        z_send=(4, n, n),
        z_recv=(4, n),
        p_send=(4, n),
        p_recv=(4, n),
        ag_send=(8, 2, SECTIONS),
        ag_recv=(8, 2, SECTIONS),
        rs_send=(8, 2, 6),
        rs_recv=(8, 2, 6),
        fo_send=(2, 2),
        fo_recv=(2, 2),
        r1_send=(2, 2),
        r1_recv=(2, 2),
        r2_send=(2, 2, n),
        r2_recv=(2, 2, n),
        r4_send=(2,),
        r4_recv=(2,),
        g1_send=(2, SECTIONS, n),
        g1_recv=(2, SECTIONS, n),
        g2_send=(2, n),
        g2_recv=(2, n),
        g3_send=(2, 2),
        g3_recv=(SECTIONS,),
        sga_send=(SECTIONS,),
        sga_recv=(SECTIONS,),
        sgb_send=(NO,),
        sgb_recv=(NO,),
    )
    names = [*inputs, *outputs, *scratch, *semaphores]
    vmem = pl.BlockSpec(memory_space=pltpu.VMEM)
    hbm = pl.BlockSpec(memory_space=pl.ANY)
    smem = pl.BlockSpec(memory_space=pltpu.SMEM)
    shapes = [jax.ShapeDtypeStruct(*spec) for spec in outputs.values()]
    results = pl.pallas_call(
        make_kernel(cfg, names),
        out_shape=shapes,
        in_specs=[smem, hbm, vmem, hbm, hbm, vmem, hbm, vmem, hbm, hbm],
        out_specs=[vmem] * len(outputs),
        scratch_shapes=[pltpu.VMEM(*spec) for spec in scratch.values()]
        + [dma(shape) for shape in semaphores.values()],
        compiler_params=pltpu.CompilerParams(
            collective_id=0, has_side_effects=True, vmem_limit_bytes=63 * 2**20
        ),
        name="layers",
    )(*inputs.values())
    count = len(shapes)

    def hand_over(*refs):
        given, out, held = refs[:count], refs[count : 2 * count], refs[2 * count : 3 * count]
        loads = [pltpu.make_async_copy(given[k], held[k], refs[-2].at[k]) for k in range(count)]
        stores = [pltpu.make_async_copy(held[k], out[k], refs[-1].at[k]) for k in range(count)]
        for copy in loads:
            copy.start()
        for load, store in zip(loads, stores):
            load.wait()
            store.start()
        for copy in stores:
            copy.wait()

    return pl.pallas_call(
        hand_over,
        out_shape=shapes,
        in_specs=[hbm] * count,
        out_specs=[hbm] * count,
        scratch_shapes=[pltpu.VMEM(*spec) for spec in outputs.values()]
        + [dma((count,)), dma((count,))],
        compiler_params=pltpu.CompilerParams(vmem_limit_bytes=63 * 2**20),
        name="outputs",
    )(*results)


def shards(
    layer_input,
    out_cotangent,
    lengths,
    qkv_weight,
    qv_bias,
    out_weight,
    up_weight,
    up_bias,
    down_weight,
    norm_vectors,
):
    section_count = lax.axis_size("section")
    dp_count = lax.axis_size("dp")
    L, D = layer_input.shape[2:]
    sequences = layer_input.shape[0] * layer_input.shape[1]
    assert section_count == SECTIONS and sequences == 2
    F = out_weight.shape[1] * dp_count
    U2 = up_weight.shape[2]
    heads = F // HEAD_DIM
    outer = max(
        k
        for k in range(2, dp_count + 1, 2)
        if dp_count % k == 0 and D % (16 * k) == 0 and U2 % (32 * k) == 0 and F % (8 * k) == 0
    )
    inner = dp_count // outer
    groups = [[g * inner + k for k in range(inner)] for g in range(outer)]

    def joined(block, axis=0):
        if inner == 1:
            return block
        block = block.astype(BF16)
        block = lax.all_gather(block, "dp", axis=axis, tiled=True, axis_index_groups=groups)
        return block.astype(F32)

    def own_share(block, axis=0):
        if inner == 1:
            return block
        return lax.psum_scatter(
            block, "dp", scatter_dimension=axis, tiled=True, axis_index_groups=groups
        )

    shard_rows = D // outer + F // outer
    cfg = types.SimpleNamespace(
        width=D,
        length=L,
        units=U2 // 2,
        features=F,
        packed=-(-3 * F // 256) * 256,
        outer=outer,
        inner=inner,
        heads=heads,
        up_rows=D // outer,
        down_rows=U2 // outer // 2,
        out_rows=F // outer,
        att_rows=-(-shard_rows // (16 * SECTIONS)) * 16 * SECTIONS,
    )
    stream, grad_rows, qkv, qvb, out, up, upb, down, norm, rms = one_step(
        cfg,
        lengths.reshape(1, 2),
        joined(qkv_weight[0]),
        joined(qv_bias, 1),
        joined(out_weight[0]),
        joined(up_weight[0]),
        joined(up_bias, 1),
        joined(down_weight[0]),
        joined(norm_vectors[0], 1)[:, None],
        layer_input.reshape(2, L, D),
        out_cotangent.reshape(2, L, D),
    )
    rows_shape = layer_input.shape[:2] + (L // SECTIONS, D)
    return (
        stream.reshape(rows_shape),
        grad_rows.reshape(rows_shape),
        own_share(qkv)[None],
        own_share(qvb, 1),
        own_share(out)[None],
        own_share(up)[None],
        own_share(upb, 1),
        own_share(down)[None],
        own_share(norm, 2).reshape(1, 3, -1),
        rms.reshape(layer_input.shape[:2] + (1, 2)),
    )


def solution(mesh):
    placed = (
        P(None, "dp", None, None),
        P(None, "dp", None, None),
        P(None, "dp"),
        P("section", "dp", None),
        P("section", "dp"),
        P("section", "dp", None),
        P("section", "dp", None),
        P("section", "dp"),
        P("section", "dp", None),
        P("section", None, "dp"),
    )
    return jax.shard_map(
        shards,
        mesh=mesh,
        in_specs=placed,
        out_specs=(
            P(None, "dp", "section", None),
            P(None, "dp", "section", None),
            P("section", "dp", None),
            P("section", "dp"),
            P("section", "dp", None),
            P("section", "dp", None),
            P("section", "dp"),
            P("section", "dp", None),
            P("section", None, "dp"),
            P(None, "dp", "section", None),
        ),
        check_vma=False,
    )
```

```python
import types

import jax
import jax.numpy as jnp
from jax import lax
from jax.experimental import pallas as pl
from jax.experimental.pallas import tpu as pltpu
from jax.sharding import PartitionSpec as P

F32, BF16 = jnp.float32, jnp.bfloat16
MESH = pl.DeviceIdType.MESH
HEAD_DIM = 32
EPSILON = 1e-05
MASKED = -1e30
SCALE = HEAD_DIM**-0.5
SCALE_2 = SCALE * 1.4426950408889634
SECTIONS = 4
NN = (((1,), (0,)), ((), ()))
NT = (((1,), (1,)), ((), ()))
TN = (((0,), (0,)), ((), ()))


def mm(left, right, dims=NN):
    return lax.dot_general(left, right, dims, preferred_element_type=F32)


def aligned(start, size):
    return pl.ds(pl.multiple_of(start, size), size)


def head_rows(h, heads):
    full = heads // 8 * 8
    low, rest = full * HEAD_DIM, (heads - full) * HEAD_DIM
    high = h // full if rest else 0
    q = h * HEAD_DIM + high * 2 * low
    k = low + h * HEAD_DIM + high * (low + rest)
    v = 2 * low + h * HEAD_DIM + high * 2 * rest
    return tuple(pl.multiple_of(row, HEAD_DIM) for row in (q, k, v))


def to_packed(rows, heads):
    half = rows.shape[-1] // 3
    low = heads // 8 * 8 * HEAD_DIM
    parts = [rows[:, i * half : i * half + low] for i in range(3)]
    parts += [rows[:, i * half + low : (i + 1) * half] for i in range(3)]
    return jnp.concatenate(parts, axis=1)


def from_packed(rows, half, heads):
    low = heads // 8 * 8 * HEAD_DIM
    rest = half - low
    parts = []
    for i in range(3):
        parts.append(rows[:, i * low : (i + 1) * low])
        parts.append(rows[:, 3 * low + i * rest : 3 * low + (i + 1) * rest])
    return jnp.concatenate(parts, axis=1)


def lanes_to(rows, width):
    if rows.shape[1] == width:
        return rows
    return jnp.concatenate([rows, jnp.zeros((rows.shape[0], width - rows.shape[1]), F32)], axis=1)


def normed_rows(h, gain, shift):
    mean = jnp.mean(h, axis=-1, keepdims=True)
    centred = h - mean
    spread = jnp.mean(centred * centred, axis=-1, keepdims=True)
    inverse = lax.rsqrt(spread + EPSILON)
    return centred * inverse, inverse, centred * inverse * gain + shift


def make_kernel(cfg, names):
    c_ = cfg
    D, L, U, F, W = c_.width, c_.length, c_.units, c_.features, c_.packed
    Q = L // SECTIONS
    NO, n, inner, heads = c_.outer, c_.outer // 2, c_.inner, c_.heads
    ru, rd, ro = c_.up_rows, c_.down_rows, c_.out_rows
    ra, rp = c_.att_rows, c_.att_rows // SECTIONS
    wide = max(U, W)
    low = heads // 8 * 8 * HEAD_DIM
    rest = F - low

    def kernel(*refs):
        R = types.SimpleNamespace(**dict(zip(names, refs)))
        s = lax.axis_index("section")
        y, x = s // 2, s % 2
        dp = lax.axis_index("dp")
        o, i = dp // inner, dp % inner
        zz, c = o // 2, o % 2
        other_x, other_y = s + 1 - 2 * x, s + 2 - 4 * y
        mate = o + 1 - 2 * c

        def remote(src, dst, send, recv, section, outer):
            return pltpu.make_async_remote_copy(
                src_ref=src,
                dst_ref=dst,
                send_sem=send,
                recv_sem=recv,
                device_id=(section, outer * inner + i),
                device_id_type=MESH,
            )

        def loop(count, body, first=0):
            def step(k, carry):
                body(k)
                return carry

            lax.fori_loop(first, count, step, 0)

        raw = (R.qkv_w, R.out_w, R.up_w, R.down_w)
        raw_home = (R.o_qkv, R.o_out, R.o_up, R.o_down)
        raw_copies = [
            pltpu.make_async_copy(a, b, R.raw_sem.at[k])
            for k, (a, b) in enumerate(zip(raw, raw_home))
        ]
        for copy in raw_copies:
            copy.start()

        barrier = pltpu.get_barrier_semaphore()

        def greet(section, outer):
            pl.semaphore_signal(
                barrier, inc=1, device_id=(section, outer * inner + i), device_id_type=MESH
            )

        loop(SECTIONS, lambda k: greet((s + k) % SECTIONS, o), 1)
        loop(SECTIONS, lambda k: greet((s + k) % SECTIONS, mate), 1)
        loop(NO, lambda k: greet(s, (o + k) % NO), 1)

        row8 = lax.broadcasted_iota(jnp.int32, (8, wide), 0)
        lane8 = lax.broadcasted_iota(jnp.int32, (8, wide), 1)
        here = row8[:, : R.small_in.shape[1]], lane8[:, : R.small_in.shape[1]]

        def rounded(v):
            return v.astype(BF16).astype(F32)

        R.small_in[...] = jnp.zeros_like(R.small_in)
        for k in range(3):
            R.small_in[k : k + 1, 0:ru] = rounded(R.norm_v[k])
        R.small_in[3:4, 0:ru] = rounded(R.qv_b[...])
        R.small_in[4:5, 0:rd] = rounded(R.up_b[:, 0:rd])
        R.small_in[5:6, 0:rd] = rounded(R.up_b[:, rd : 2 * rd])
        R.len_own[...] = jnp.where(here[1] == 0, R.lens[0, 0], R.lens[0, 1])[:, :128].astype(F32)
        pl.semaphore_wait(barrier, 2 * (SECTIONS - 1) + NO - 1)

        def small_out(k):
            peer = (o + k) % NO
            return remote(
                R.small_in, R.small_a.at[o], R.sma_send.at[k], R.sma_recv.at[o], s, peer
            )

        loop(NO, lambda k: small_out(k).start(), 1)
        R.small_a[o] = R.small_in[...]
        len_copy = remote(R.len_own, R.len_mate, R.len_send.at[0], R.len_recv.at[0], s, mate)
        len_copy.start()

        raw_copies[0].wait()
        raw_copies[1].wait()
        packed = lanes_to(to_packed(R.o_qkv[...], heads), W).astype(BF16)
        R.att_own[pl.ds(0, ru), :] = packed
        bottom = jnp.concatenate([R.o_out[...], jnp.zeros((ra - ru - ro, D), F32)], axis=0)
        R.att_own[pl.ds(ru, ra - ru), :] = lanes_to(bottom, W).astype(BF16)

        def quarter_copy(p):
            return remote(
                R.att_own.at[pl.ds(p * rp, rp)],
                R.watt.at[y, p, aligned(o * rp, rp)],
                R.a1_send.at[p],
                R.a1_recv.at[y, c],
                p,
                2 * zz + x,
            )

        def each_quarter(act, own):
            for p in range(SECTIONS):
                stays = (s == p) & (x == c)

                @pl.when(stays)
                def _(p=p):
                    if own:
                        R.watt[y, p, aligned(o * rp, rp), :] = R.att_own[pl.ds(p * rp, rp), :]

                @pl.when(jnp.logical_not(stays))
                def _(p=p):
                    act(quarter_copy(p))

        each_quarter(lambda copy: copy.start(), True)

        def seq_copy(local):
            if local:
                return pltpu.make_async_copy(R.stream_in.at[y], R.seq_rows, R.load_sem.at[0])
            return remote(
                R.stream_in.at[y], R.seq_rows, R.seq_send.at[0], R.seq_recv.at[0], s, mate
            )

        def cot_copy(m, j, local):
            half = c if local else 1 - c
            src = R.cot_in.at[m, aligned((2 * half + j) * Q, Q)]
            dst = R.grad_ff.at[0, aligned(j * L + (2 * m + c) * Q, Q)]
            if local:
                return pltpu.make_async_copy(src, dst, R.load_sem.at[1 + 2 * m + j])
            return remote(src, dst, R.cot_send.at[m, j], R.cot_recv.at[m, j], s, mate)

        def piece(kind, layer, outer):
            rows = rd if kind else ru
            return (R.wdown if kind else R.wup).at[layer, aligned(outer * rows, rows)]

        def y_copy(kind):
            return remote(
                R.yb_down if kind else R.yb_up,
                piece(kind, y, o),
                R.y_send.at[kind],
                R.y_recv.at[kind],
                other_y,
                o,
            )

        def chips_at(distances, body):
            for distance in distances:
                for sign in (1, -1):
                    q = zz + sign * distance

                    @pl.when((q >= 0) & (q < n))
                    def _(q=q, sign=sign, distance=distance):
                        body(q, sign, distance)

        def relays(distance, sign, body):
            if distance >= 2:
                after = zz - sign

                @pl.when((after >= 0) & (after < n))
                def _():
                    body(after)

        NEAR, FAR = tuple(range(min(2, n - 1), 0, -1)), range(3, n)

        def z_copy(layer, kind, origin, to):
            item = layer * 2 + kind
            part = piece(kind, layer, 2 * origin + c)
            send = R.z_send.at[item, origin, to]
            return remote(part, part, send, R.z_recv.at[item, origin], s, 2 * to + c)

        def mate_copy(layer, kind, q):
            item = layer * 2 + kind
            part = piece(kind, layer, 2 * q + c)
            return remote(part, part, R.p_send.at[item, q], R.p_recv.at[item, q], s, mate)

        def mate_arrival(layer, kind, q):
            item = layer * 2 + kind
            part = piece(kind, layer, 2 * q + 1 - c)
            return remote(part, part, R.p_send.at[item, q], R.p_recv.at[item, q], s, mate)

        def feed_spread(layer, kind):
            chips_at(NEAR, lambda q, *_: z_copy(layer, kind, zz, q).start())
            mate_copy(layer, kind, zz).start()

        def feed_spread_home(layer):
            @pl.when(y == layer)
            def _():
                feed_spread(layer, 0)
                feed_spread(layer, 1)

        def feed_spread_away(layer, kind):
            @pl.when(y != layer)
            def _():
                src = R.yb_down if kind else R.yb_up
                remote(
                    src,
                    piece(kind, layer, o),
                    R.y_send.at[kind],
                    R.y_recv.at[kind],
                    other_y,
                    o,
                ).wait_recv()
                feed_spread(layer, kind)

        def feed_arrivals(layer, distances, kinds=(0, 1)):
            for kind in kinds:

                def landed(q, sign, distance):
                    z_copy(layer, kind, q, zz).wait_recv()
                    relays(
                        distance, sign, lambda after: z_copy(layer, kind, q, after).start()
                    )
                    mate_copy(layer, kind, q).start()

                chips_at(distances, landed)

        def feed_collect(layer, kinds=(0, 1)):
            feed_arrivals(layer, FAR, kinds)
            for kind in kinds:
                loop(n, lambda q, kind=kind: mate_arrival(layer, kind, q).wait_recv())

        def feed_sent(layer):
            for kind in range(2):
                chips_at(NEAR, lambda q, *_: z_copy(layer, kind, zz, q).wait_send())
                for distances in (NEAR, FAR):
                    chips_at(
                        distances,
                        lambda q, sign, distance: relays(
                            distance,
                            sign,
                            lambda after: z_copy(layer, kind, q, after).wait_send(),
                        ),
                    )
                loop(n, lambda q, kind=kind: mate_copy(layer, kind, q).wait_send())

        def att_block(layer, p, q):
            return R.watt.at[layer, p, aligned(q * 2 * rp, 2 * rp)]

        def att_z_copy(layer, origin, to):
            part = att_block(layer, s, origin)
            send = R.a2_send.at[layer, origin, to]
            return remote(part, part, send, R.a2_recv.at[layer, origin], s, 2 * to + c)

        def att_plane_copy(layer, q, way):
            part = att_block(layer, s, q)
            to = other_y if way else other_x
            return remote(
                part, part, R.a3_send.at[layer, q, way], R.a3_recv.at[layer, q, way], to, o
            )

        def plane_half(layer, section, q, way):
            first = rp if layer else rp // 2
            start = q * 2 * rp + (first if way else 0)
            rows = 2 * rp - first if way else first
            return R.watt.at[layer, section, pl.ds(pl.multiple_of(start, 16), rows)]

        def att_plane_half(layer, q, way):
            src, to = (other_y, other_x) if way else (other_x, other_y)
            part = plane_half(layer, src, q, way)
            return remote(
                part, part, R.a4_send.at[layer, q, way], R.a4_recv.at[layer, q, way], to, o
            )

        def att_plane_start(layer, q):
            for way in range(2):
                att_plane_copy(layer, q, way).start()

        def att_plane_relay(layer, q):
            for way in range(2):
                src = other_y if way else other_x
                part = att_block(layer, src, q)
                remote(
                    part,
                    part,
                    R.a3_send.at[layer, q, way],
                    R.a3_recv.at[layer, q, way],
                    src,
                    o,
                ).wait_recv()
                att_plane_half(layer, q, way).start()

        def att_spread(layer):
            for core in range(2):
                mine = (s == 2 * layer + c) & (c == core)

                @pl.when(jnp.logical_not(mine))
                def _(core=core):
                    remote(
                        R.att_own.at[pl.ds(0, rp)],
                        R.watt.at[layer, s, aligned((2 * zz + core) * rp, rp)],
                        R.a1_send.at[0],
                        R.a1_recv.at[layer, core],
                        2 * layer + c,
                        2 * zz + core,
                    ).wait_recv()

            chips_at(reach(layer), lambda q, *_: att_z_copy(layer, zz, q).start())
            att_plane_start(layer, zz)

        def reach(layer):
            return NEAR if layer else tuple(range(1, n))

        def att_onward(layer, distances):
            def landed(q, sign, distance):
                att_z_copy(layer, q, zz).wait_recv()
                if layer:
                    relays(distance, sign, lambda after: att_z_copy(layer, q, after).start())
                att_plane_start(layer, q)

            chips_at(distances, landed)

        def att_sent(layer):
            chips_at(reach(layer), lambda q, *_: att_z_copy(layer, zz, q).wait_send())
            if layer:
                for distances in (NEAR, FAR):
                    chips_at(
                        distances,
                        lambda q, sign, distance: relays(
                            distance,
                            sign,
                            lambda after: att_z_copy(layer, q, after).wait_send(),
                        ),
                    )

            def plane_sent(q):
                for way in range(2):
                    att_plane_copy(layer, q, way).wait_send()
                    att_plane_half(layer, q, way).wait_send()

            loop(n, plane_sent)

        def att_plane_onward(layer, distances):
            chips_at(distances, lambda q, *_: att_plane_relay(layer, q))

        def att_collect(layer):
            def block(q):
                for way in range(2):
                    part = plane_half(layer, 3 - s, q, way)
                    remote(
                        part,
                        part,
                        R.a4_send.at[layer, q, way],
                        R.a4_recv.at[layer, q, way],
                        other_y,
                        o,
                    ).wait_recv()

            loop(n, block)

            def unpack(k):
                for r in range(0, ru, 16):
                    R.wqkv[layer, aligned(k * ru + r, 16), :] = R.watt[
                        layer, r // rp, aligned(k * rp + r % rp, 16), :
                    ]
                for r in range(0, ro, 16):
                    rows = min(16, ro - r)
                    p, off = (ru + r) // rp, (ru + r) % rp
                    block = R.watt[layer, p, aligned(k * rp + off, 16), :][:, :D].astype(F32)
                    R.wide_rows[aligned(k * ro + r, 8), :] = block[:rows][:8]
                    if rows > 8:
                        R.wide_rows[aligned(k * ro + r + 8, 8), :] = block[8:rows]

            loop(NO, unpack)
            R.wout[layer] = R.wide_rows[pl.ds(0, F), :].astype(BF16)

        att_spread(0)
        att_spread(1)

        raw_copies[2].wait()
        raw_copies[3].wait()
        halves = [
            jnp.concatenate(
                [R.o_up[:, (2 * k + h) * rd : (2 * k + h + 1) * rd] for k in range(NO)], axis=1
            ).astype(BF16)
            for h in range(2)
        ]
        R.wup[y, aligned(o * ru, ru), :] = jnp.where(y == 0, halves[0], halves[1])
        R.yb_up[...] = jnp.where(y == 0, halves[1], halves[0])
        R.wdown[y, aligned(o * rd, rd), :] = R.o_down[aligned(y * rd, rd), :].astype(BF16)
        R.yb_down[...] = R.o_down[aligned((1 - y) * rd, rd), :].astype(BF16)
        y_copy(0).start()
        feed_spread_home(0)

        @pl.when(x == c)
        def _():
            seq_copy(True).start()
            seq_copy(False).start()

        for m in range(2):
            for j in range(2):
                cot_copy(m, j, True).start()
                cot_copy(m, j, False).start()

        loop(
            NO,
            lambda k: remote(
                R.small_in,
                R.small_a.at[(o + k) % NO],
                R.sma_send.at[k],
                R.sma_recv.at[(o + k) % NO],
                s,
                (o + k) % NO,
            ).wait_recv(),
            1,
        )
        table = jnp.zeros((8, wide), F32)
        for k in range(NO):
            part = lanes_to(R.small_a[k], wide)
            narrow = pltpu.roll(part, ru * k, 1) if k else part
            broad = pltpu.roll(part, rd * k, 1) if k else part
            table = table + jnp.where(row8 < 4, narrow, broad)
        moved = jnp.where(lane8 < low, table, 0.0)
        moved += pltpu.roll(jnp.where((lane8 >= low) & (lane8 < F), table, 0.0), 2 * low, 1)
        moved += pltpu.roll(
            jnp.where((lane8 >= F) & (lane8 < F + low), table, 0.0), 2 * low - F, 1
        )
        moved += pltpu.roll(
            jnp.where((lane8 >= F + low) & (lane8 < 2 * F), table, 0.0), 2 * low + 2 * rest - F, 1
        )
        table = jnp.where(row8 == 3, moved, table)
        R.small_own[...] = table
        R.small_b[s] = table

        def small_b_copy(k, of):
            return remote(
                R.small_own,
                R.small_b.at[of],
                R.smb_send.at[k],
                R.smb_recv.at[of],
                (s + k) % SECTIONS,
                o,
            )

        loop(SECTIONS, lambda k: small_b_copy(k, s).start(), 1)

        def first_blocks(k):
            q = (zz + k) % n
            att_z_copy(0, q, zz).wait_recv()
            att_plane_start(0, q)
            att_plane_relay(0, (zz + k - 1) % n)

        loop(n, first_blocks, 1)
        y_copy(1).start()
        feed_spread_away(0, 0)
        att_plane_relay(0, (zz + n - 1) % n)
        loop(SECTIONS, lambda k: small_b_copy(k, (s + k) % SECTIONS).wait_recv(), 1)

        R.small_grad[...] = jnp.zeros_like(R.small_grad)
        def note_rows(block, index, row):
            R.small_grad[block] += jnp.where(row8 == index, lanes_to(row, wide), 0.0)


        @pl.when(x == c)
        def _():
            seq_copy(True).wait()

        @pl.when(x != c)
        def _():
            seq_copy(False).wait_recv()

        gain0 = R.small_b[0, 0:1, :D]
        shift0 = R.small_b[0, 1:2, :D]

        def first_norm(k):
            rows = aligned(k * Q, Q)
            _, _, out = normed_rows(R.seq_rows[rows, :].astype(F32), gain0, shift0)
            R.norm_at[0, rows, :] = out.astype(BF16)

        loop(L // Q, first_norm)
        feed_spread_away(0, 1)
        R.hid_rows[0] = R.seq_rows[aligned(c * 2 * Q, 2 * Q), :]
        len_copy.wait_recv()
        tile = jnp.where(x == c, R.len_own[...], R.len_mate[...])
        tile = jnp.where((row8[:, :128] == 0) & (lane8[:, :128] == y), tile, 0.0)
        length_here = jnp.sum(jnp.sum(tile, axis=1, keepdims=True), axis=0, keepdims=True)
        length_here = length_here.astype(jnp.int32)
        def block_copy(phase, m, buf, way):
            part = buf.at[aligned(m * L + s * Q, Q)]
            to = other_y if way else other_x
            return remote(
                part, part, R.ag_send.at[phase, m, way], R.ag_recv.at[phase, m, way], to, o
            )

        def half_copy(phase, m, buf, way):
            src, to = (other_y, other_x) if way else (other_x, other_y)
            part = buf.at[aligned(m * L + src * Q + way * (Q // 2), Q // 2)]
            slot = 2 + way
            return remote(
                part, part, R.ag_send.at[phase, m, slot], R.ag_recv.at[phase, m, slot], to, o
            )

        def share_mate(phase, m, buf):
            part = buf.at[aligned((2 * c + m) * Q, Q)]
            return remote(
                part, part, R.ag_send.at[phase, m, 0], R.ag_recv.at[phase, m, c], s, mate
            )

        def pass_rows(phase, buf):
            for m in range(2):
                for way in range(2):
                    src = other_y if way else other_x
                    part = buf.at[aligned(m * L + src * Q, Q)]
                    remote(
                        part, part, R.ag_send.at[phase, m, way], R.ag_recv.at[phase, m, way], src, o
                    ).wait_recv()
                    half_copy(phase, m, buf, way).start()

        def send_rows(phase, attention, m, buf, value):
            if attention:
                buf[aligned((2 * c + m) * Q, Q), :] = value
                share_mate(phase, m, buf).start()
            else:
                buf[aligned(m * L + s * Q, Q), :] = value
                for way in range(2):
                    block_copy(phase, m, buf, way).start()

        def finish_send_rows(phase, attention, m, buf):
            if attention:
                share_mate(phase, m, buf).wait_send()
            else:
                for way in range(2):
                    block_copy(phase, m, buf, way).wait_send()
                    half_copy(phase, m, buf, way).wait_send()

        def await_rows(phase, attention, m, buf):
            if attention:
                for j in range(2):
                    part = buf.at[aligned((2 * (1 - c) + j) * Q, Q)]
                    remote(
                        part, part, R.ag_send.at[phase, j, 0], R.ag_recv.at[phase, j, 1 - c], s, mate
                    ).wait_recv()
            else:
                for way in range(2):
                    part = buf.at[aligned(m * L + (3 - s) * Q + way * (Q // 2), Q // 2)]
                    slot = 2 + way
                    remote(
                        part,
                        part,
                        R.ag_send.at[phase, m, slot],
                        R.ag_recv.at[phase, m, slot],
                        other_y,
                        o,
                    ).wait_recv()

        def sum_slot(phase):
            return 0 if phase < 4 else 1

        HOP, STRAIGHT, LATE = 0, 2, 4

        def half_rows(m, section, way):
            return aligned(m * L + section * Q + way * (Q // 2), Q // 2)

        def half_sum(phase, src, m, way):
            return R.sums.at[sum_slot(phase), src, m, pl.ds(way * (Q // 2), Q // 2)]

        def part_copy(phase, m, step, way):
            near, far = (other_y, other_x) if way else (other_x, other_y)
            if step == HOP:
                to, rows, dst = near, half_rows(m, 3 - s, way), half_sum(phase, far, m, way)
            elif step == STRAIGHT:
                to, rows, dst = near, half_rows(m, near, way), half_sum(phase, s, m, way)
            else:
                to, rows, dst = far, half_rows(m, far, way), half_sum(phase, s, m, way)
            slot = step + way
            return remote(
                R.parts.at[rows],
                dst,
                R.rs_send.at[phase, m, slot],
                R.rs_recv.at[phase, m, slot],
                to,
                o,
            )

        def part_landed(phase, m, step, way):
            near, far = (other_y, other_x) if way else (other_x, other_y)
            src = 3 - s if step == HOP else (near if step == STRAIGHT else far)
            slot = step + way
            remote(
                R.parts.at[pl.ds(0, Q // 2)],
                half_sum(phase, src, m, way),
                R.rs_send.at[phase, m, slot],
                R.rs_recv.at[phase, m, slot],
                near,
                o,
            ).wait_recv()

        def late_parts(phase, m):
            for way in range(2):
                part_landed(phase, m, HOP, way)
                rows = half_rows(m, other_x if way else other_y, way)
                hop = R.sums[sum_slot(phase), 3 - s, m, pl.ds(way * (Q // 2), Q // 2), :]
                both = R.parts[rows, :].astype(F32) + hop.astype(F32)
                R.parts[rows, :] = both.astype(BF16)
                part_copy(phase, m, LATE, way).start()

        def mate_part(phase, j):
            return remote(
                R.parts.at[aligned((2 * (1 - c) + j) * Q, Q)],
                R.sums.at[sum_slot(phase), c, j],
                R.rs_send.at[phase, j, 0],
                R.rs_recv.at[phase, j, c],
                s,
                mate,
            )

        def send_parts(phase, attention, m):
            slot = sum_slot(phase)
            if attention:
                for j in range(2):
                    mate_part(phase, j).start()
                    R.sums[slot, c, j] = R.parts[aligned((2 * c + j) * Q, Q), :]
            else:
                for step in (HOP, STRAIGHT):
                    for way in range(2):
                        part_copy(phase, m, step, way).start()
                R.sums[slot, s, m] = R.parts[aligned(m * L + s * Q, Q), :]

        def finish_send_parts(phase, attention, chunks=(0, 1)):
            for m in chunks:
                if attention:
                    mate_part(phase, m).wait_send()
                else:
                    for step in (HOP, STRAIGHT, LATE):
                        for way in range(2):
                            part_copy(phase, m, step, way).wait_send()

        def part_arrival(phase, m, src):
            return remote(
                R.parts.at[pl.ds(0, Q)],
                R.sums.at[sum_slot(phase), src, m],
                R.rs_send.at[phase, m, 0],
                R.rs_recv.at[phase, m, src],
                s,
                mate,
            )

        def await_parts(phase, attention, m):
            slot = sum_slot(phase)
            if attention:
                part_arrival(phase, m, 1 - c).wait_recv()
                sources = range(2)
            else:
                for step in (STRAIGHT, LATE):
                    for way in range(2):
                        part_landed(phase, m, step, way)
                sources = (s, other_x, other_y)
            total = None
            for src in sources:
                part = R.sums[slot, src, m].astype(F32)
                total = part if total is None else total + part
            return total

        def place_copy(which, j):
            return remote(
                R.finished.at[which, j],
                (R.out_grad_rows if which else R.out_stream).at[aligned(y * Q, Q)],
                R.fo_send.at[which, j],
                R.fo_recv.at[which, y],
                2 * c + j,
                2 * zz + x,
            )

        def place_rows(which, j, value):
            stays = (s == 2 * c + j) & (x == c)
            R.finished[which, j] = value

            @pl.when(stays)
            def _():
                (R.out_grad_rows if which else R.out_stream)[aligned(y * Q, Q), :] = value

            @pl.when(jnp.logical_not(stays))
            def _():
                place_copy(which, j).start()

        def finish_place(which):
            for j in range(2):
                stays = (s == 2 * c + j) & (x == c)

                @pl.when(jnp.logical_not(stays))
                def _(j=j):
                    place_copy(which, j).wait_send()

            for m in range(2):
                mine = (s == 2 * m + c) & (y == c)

                @pl.when(jnp.logical_not(mine))
                def _(m=m):
                    remote(
                        R.finished.at[which, 0],
                        (R.out_grad_rows if which else R.out_stream).at[pl.ds(m * Q, Q)],
                        R.fo_send.at[which, 0],
                        R.fo_recv.at[which, m],
                        2 * m + c,
                        2 * zz + y,
                    ).wait_recv()

        def close_forward(phase, m):
            e = phase
            attention = e % 2 == 0
            branch = await_parts(phase, attention, m) + R.small_b[e, 2:3, :D]
            mine = pl.ds(m * Q, Q)
            h = R.hid_rows[e, mine, :].astype(F32)
            position = (2 * c + m) * Q + lax.broadcasted_iota(jnp.int32, (Q, 1), 0)
            valid = (position < length_here).astype(F32)
            square_h = jnp.sum(jnp.sum(h * h * valid, axis=1, keepdims=True), axis=0, keepdims=True)
            square_b = jnp.sum(
                jnp.sum(branch * branch * valid, axis=1, keepdims=True), axis=0, keepdims=True
            )
            spot = (2 * zz + x) * 4 + 2 * y
            R.small_grad[e] += jnp.where((row8 == 6) & (lane8 == spot), square_h, 0.0)
            R.small_grad[e] += jnp.where((row8 == 6) & (lane8 == spot + 1), square_b, 0.0)
            fresh = (h + branch).astype(BF16)
            if e == 3:
                place_rows(0, m, fresh)
                return
            R.hid_rows[e + 1, mine, :] = fresh
            _, _, out = normed_rows(
                fresh.astype(F32), R.small_b[e + 1, 0:1, :D], R.small_b[e + 1, 1:2, :D]
            )
            to_attention = (e + 1) % 2 == 0
            buf = (R.norm_at if to_attention else R.norm_ff).at[(e + 1) // 2]
            send_rows(phase + 1, to_attention, m, buf, out.astype(BF16))

        grad_at = (R.seq_rows, R.grad_at)

        def close_backward(phase, m):
            e = 7 - phase
            attention = e % 2 == 0
            d_norm = await_parts(phase, attention, m)
            mine = pl.ds(m * Q, Q)
            unit, inverse, _ = normed_rows(R.hid_rows[e, mine, :].astype(F32), 1.0, 0.0)
            flow = R.grad_rows[mine, :].astype(F32)
            note_rows(e, 0, jnp.sum(d_norm * unit, axis=0, keepdims=True))
            note_rows(e, 1, jnp.sum(d_norm, axis=0, keepdims=True))
            note_rows(e, 2, jnp.sum(flow, axis=0, keepdims=True))
            a = d_norm * R.small_b[e, 0:1, :D]
            mean_a = jnp.mean(a, axis=-1, keepdims=True)
            mean_ax = jnp.mean(a * unit, axis=-1, keepdims=True)
            fresh = (flow + (a - mean_a - unit * mean_ax) * inverse).astype(BF16)
            if e == 0:
                place_rows(1, m, fresh)
                return
            R.grad_rows[mine, :] = fresh
            to_attention = (e - 1) % 2 == 0
            buf = grad_at[(e - 1) // 2] if to_attention else R.grad_ff.at[1]
            send_rows(phase + 1, to_attention, m, buf, fresh)

        ga = (R.hidden.at[1], R.slope.at[1])

        def attention_forward(layer):
            bias = R.small_b[2 * layer + c, 3:4, :W]
            xs = R.norm_at.at[layer]
            for t in range(0, W, 256):
                cols = pl.ds(t, 256)
                lin = mm(xs[...], R.wqkv[layer, :, cols]) + bias[:, t : t + 256]
                R.lin_t[layer, cols, :] = lin.T.astype(BF16)

            def head(h):
                q0, k0, v0 = head_rows(h, heads)
                score = mm(
                    R.lin_t[layer, pl.ds(k0, HEAD_DIM), :],
                    R.lin_t[layer, pl.ds(q0, HEAD_DIM), :],
                    TN,
                )
                live = lax.broadcasted_iota(jnp.int32, score.shape, 0) < length_here
                score = jnp.where(live, score, MASKED)
                top = jnp.max(score, axis=0, keepdims=True)
                powers = jnp.exp2((score - top) * SCALE_2)
                total = jnp.sum(powers, axis=0, keepdims=True)
                probs = (powers * (1.0 / total)).astype(BF16)
                R.log_total[layer, h] = top * SCALE_2 + jnp.log2(total)
                mixed = mm(R.lin_t[layer, pl.ds(v0, HEAD_DIM), :], probs)
                R.att_t[layer, aligned(h * HEAD_DIM, HEAD_DIM), :] = mixed.astype(BF16)

            def pair(h):
                head(2 * h)
                head(2 * h + 1)

            loop(heads // 2, pair)
            if heads % 2:
                head(heads - 1)
            R.parts[pl.ds(0, L), :] = mm(R.att_t[layer], R.wout[layer], TN).astype(BF16)

        def attention_back_heads(layer, between):
            g = grad_at[layer]
            R.d_att_t[...] = mm(R.wout[layer], g[...], NT).astype(BF16)

            def head(h):
                q0, k0, v0 = head_rows(h, heads)
                q_t = R.lin_t[layer, pl.ds(q0, HEAD_DIM), :]
                k_t = R.lin_t[layer, pl.ds(k0, HEAD_DIM), :]
                v_t = R.lin_t[layer, pl.ds(v0, HEAD_DIM), :]
                d_a = R.d_att_t[aligned(h * HEAD_DIM, HEAD_DIM), :]
                score = mm(k_t, q_t, TN)
                live = lax.broadcasted_iota(jnp.int32, score.shape, 0) < length_here
                probs = jnp.where(live, jnp.exp2(score * SCALE_2 - R.log_total[layer, h]), 0.0)
                d_probs = mm(v_t, d_a, TN)
                product = probs * d_probs
                inner_sum = jnp.sum(product, axis=0, keepdims=True)
                d_score = ((product - probs * inner_sum) * SCALE).astype(BF16)
                R.d_lin_t[pl.ds(q0, HEAD_DIM), :] = mm(k_t, d_score).astype(BF16)
                R.d_lin_t[pl.ds(k0, HEAD_DIM), :] = mm(q_t, d_score, NT).astype(BF16)
                R.d_lin_t[pl.ds(v0, HEAD_DIM), :] = mm(d_a, probs.astype(BF16), NT).astype(BF16)

            def pair(h):
                head(2 * h)
                head(2 * h + 1)

            loop(heads // 4, pair)
            between()
            loop(heads // 2, pair, heads // 4)
            if heads % 2:
                head(heads - 1)

        def attention_back_rows(layer):
            for t in range(0, W, 256):
                cols = pl.ds(t, 256)
                part = mm(R.d_lin_t[cols, :], R.wqkv[layer, :, cols], (((0,), (1,)), ((), ())))
                if t == 0:
                    R.acc[...] = part
                else:
                    R.acc[...] += part
            R.parts[pl.ds(0, L), :] = R.acc[...].astype(BF16)

        def attention_back_out(layer):
            stage = 1 - layer
            R.wide_rows[pl.ds(0, F), :] = mm(R.att_t[layer], grad_at[layer][...])

            def out_rows(k):
                for r in range(ru, ra, 16):
                    top_half = R.wide_rows[aligned(k * ro + r - ru, 8), :]
                    low_half = R.wide_rows[aligned(k * ro + r - ru + 8, 8), :]
                    block = jnp.concatenate([top_half, low_half], axis=0)
                    place = aligned(r // rp * NO * rp + k * rp + r % rp, 16)
                    ga[stage][place, 0:D] = block.astype(BF16)

            loop(NO, out_rows)

        def attention_back_weights(layer):
            stage = 1 - layer
            sums = []
            for t in range(0, W, 256):
                cols = pl.ds(t, 256)
                d_lin = R.d_lin_t[cols, :].T
                sums.append(jnp.sum(d_lin.astype(F32), axis=0, keepdims=True))
                d_w = mm(R.norm_at[layer], d_lin, TN).astype(BF16)
                for k in range(NO):
                    for r in range(0, ru, 16):
                        place = pl.ds(r // rp * NO * rp + k * rp + r % rp, 16)
                        ga[stage][place, cols] = d_w[k * ru + r : k * ru + r + 16]
            note_rows(2 * layer + c, 3, jnp.concatenate(sums, axis=1))

        def feed_bias(layer):
            block = R.small_b[2 * layer + x]
            return jnp.where(y == 0, block[4:5], block[5:6])[:, :U]

        def feed_up(layer, m):
            bias = feed_bias(layer)

            def rows_step(r):
                rows = aligned(m * L + r * Q, Q)
                pre = mm(R.norm_ff[layer, rows, :], R.wup[layer]) + bias
                cdf = 0.5 + 0.5 * lax.erf(pre * 0.7071067811865476)
                density = jnp.exp(pre * pre * -0.5) * 0.3989422804014327
                R.hidden[layer, rows, :] = (pre * cdf).astype(BF16)
                R.slope[layer, rows, :] = (cdf + pre * density).astype(BF16)

            loop(SECTIONS, rows_step)

        def feed_down(layer, m):
            rows = pl.ds(m * L, L)
            R.parts[rows, :] = mm(R.hidden[layer, rows, :], R.wdown[layer]).astype(BF16)

        def feed_back_rows(layer, m):
            rows = pl.ds(m * L, L)
            g = R.grad_ff.at[0 if layer == 1 else 1, rows]
            tile = U // 2
            for j in range(2):
                cols = pl.ds(j * tile, tile)
                d_hidden = mm(g[...], R.wdown[layer, cols, :], NT)
                d_pre = (d_hidden * R.slope[layer, rows, cols].astype(F32)).astype(BF16)
                R.slope[layer, rows, cols] = d_pre
                part = mm(d_pre, R.wup[layer, :, cols], NT)
                if j == 0:
                    R.acc[...] = part
                else:
                    R.parts[rows, :] = (R.acc[...] + part).astype(BF16)

        def feed_back_down(layer):
            g = R.grad_ff.at[0 if layer == 1 else 1]
            tile = U // 2
            owners = tile // rd
            for j in range(2):
                cols = pl.ds(j * tile, tile)
                d_down = mm(R.hidden[layer, :, cols], g[...], TN).astype(BF16)
                for k in range(owners):
                    owner = j * owners + k
                    R.sb_down[owner % 2, pl.ds(owner // 2 * rd, rd), :] = d_down[
                        k * rd : (k + 1) * rd
                    ]

        def feed_back_up(layer):
            tile = U // 2
            sums = []
            for j in range(2):
                cols = pl.ds(j * tile, tile)
                d_pre = R.slope[layer, :, cols]
                d_up = mm(R.norm_ff[layer], d_pre, TN).astype(BF16)
                for k in range(NO):
                    R.sb_up[k % 2, pl.ds(k // 2 * ru, ru), cols] = d_up[k * ru : (k + 1) * ru]
                sums.append(jnp.sum(d_pre.astype(F32), axis=0, keepdims=True))
            note_rows(2 * layer + x, 4 + y, jnp.concatenate(sums, axis=1))

        z_up, z_down = (R.zb_up, R.wup.at[1]), (R.zb_down, R.norm_ff.at[1])
        UP, DOWN = (0,), (1,)
        FEED_GRADS = (
            (0, R.sb_up, R.rb_up, R.mb_up, z_up, R.yb_up, R.yr_up, ru),
            (1, R.sb_down, R.rb_down, R.mb_down, z_down, R.yb_down, R.yr_down, rd),
        )

        def mate_grads(stage, which):
            return [
                remote(sb.at[1 - c], rb, R.r1_send.at[stage, a], R.r1_recv.at[stage, a], s, mate)
                for a, sb, rb, *_ in [FEED_GRADS[k] for k in which]
            ]

        RELAYED = n == 4

        def z_grad(stage, entry, q, to, slot):
            a, sb, rb, mb, zb, yb, yr, rows = entry
            return remote(
                mb.at[aligned(q * rows, rows)],
                zb[stage].at[aligned(slot * rows, rows)],
                R.r2_send.at[stage, a, q],
                R.r2_recv.at[stage, a, slot],
                s,
                2 * to + c,
            )

        def each_z_grad(stage, act, late, which=(0, 1)):
            def one(entry, q, sign, distance):
                if RELAYED and distance == 3:
                    if not late:
                        act(z_grad(stage, entry, q, zz + sign, zz + sign))
                elif RELAYED and distance == 2:
                    behind = zz - sign
                    waits = (behind >= 0) & (behind < n)

                    @pl.when(waits if late else jnp.logical_not(waits))
                    def _():
                        if late:
                            late_sum(stage, entry, q, act)
                        else:
                            act(z_grad(stage, entry, q, q, zz))
                elif not late:
                    act(z_grad(stage, entry, q, q, zz))

            def each(*where):
                for k in which:
                    one(FEED_GRADS[k], *where)

            chips_at(range(n - 1, 0, -1), each)

        def late_sum(stage, entry, q, act):
            a, sb, rb, mb, zb, yb, yr, rows = entry
            if act is None:
                act = lambda copy: copy.wait_send()
            else:
                hop = aligned(zz * rows, rows)
                remote(
                    mb.at[pl.ds(0, rows)],
                    zb[stage].at[hop],
                    R.r2_send.at[stage, a, zz],
                    R.r2_recv.at[stage, a, zz],
                    s,
                    mate,
                ).wait_recv()
                part = aligned(q * rows, rows)
                both = mb[part, :].astype(F32) + zb[stage][hop, :].astype(F32)
                mb[part, :] = both.astype(BF16)
            act(z_grad(stage, entry, q, q, zz))

        def feed_to_mate(stage, which):
            for copy in mate_grads(stage, which):
                copy.start()

        def finish_feed_z(stage):
            each_z_grad(stage, lambda copy: copy.wait_send(), False)
            each_z_grad(stage, None, True)

        def feed_late(stage, which):
            each_z_grad(stage, lambda copy: copy.start(), True, which)

        def feed_along_z(stage, which):
            for copy in mate_grads(stage, which):
                copy.wait()
            for a, sb, rb, mb, zb, yb, yr, rows in [FEED_GRADS[k] for k in which]:

                def add(q, sb=sb, rb=rb, mb=mb, rows=rows):
                    part = aligned(q * rows, rows)
                    both = sb[c, part, :].astype(F32) + rb[part, :].astype(F32)
                    mb[part, :] = both.astype(BF16)

                loop(n, add)
            each_z_grad(stage, lambda copy: copy.start(), False, which)

        def y_grad(a, yb, yr):
            return remote(yb, yr, R.r4_send.at[a], R.r4_recv.at[a], other_y, o)

        def keep_half(a, h, value):
            if a:
                R.o_down[pl.ds(h * rd, rd), :] = value
                return
            for k in range(NO):
                R.o_up[:, (2 * k + h) * rd : (2 * k + h + 1) * rd] = value[:, k * rd : (k + 1) * rd]

        def feed_owned(stage):
            layer = 1 - stage
            for a, sb, rb, mb, zb, yb, yr, rows in FEED_GRADS:

                def landed(q, sign, distance, a=a, zb=zb, mb=mb, rows=rows):
                    if not (RELAYED and distance == 3):
                        remote(
                            mb.at[pl.ds(0, rows)],
                            zb[stage].at[aligned(q * rows, rows)],
                            R.r2_send.at[stage, a, q],
                            R.r2_recv.at[stage, a, q],
                            s,
                            2 * q + c,
                        ).wait_recv()

                chips_at(range(1, n), landed)
                total = mb[aligned(zz * rows, rows), :].astype(F32)
                for k in range(1, n):
                    q = (zz + k) % n
                    part = zb[stage][aligned(q * rows, rows), :].astype(F32)
                    if RELAYED:
                        part = jnp.where(jnp.abs(q - zz) == 3, 0.0, part)
                    total = total + part

                @pl.when(y == layer)
                def _(a=a, total=total):
                    keep_half(a, layer, total)

                @pl.when(y != layer)
                def _(a=a, yb=yb, yr=yr, total=total):
                    yb[...] = total.astype(BF16)

        def feed_to_home(stage):
            @pl.when(y == stage)
            def _():
                for a, sb, rb, mb, zb, yb, yr, rows in FEED_GRADS:
                    y_grad(a, yb, yr).start()

        def feed_home():
            for a, sb, rb, mb, zb, yb, yr, rows in FEED_GRADS:
                y_grad(a, yb, yr).wait()
                for h in range(2):

                    @pl.when(y == 1 - h)
                    def _(a=a, h=h, yr=yr):
                        keep_half(a, h, yr[...].astype(F32))

        att_rows = NO * rp

        def grad_half(stage, section, q, way):
            return aligned(section * att_rows + (2 * q + way) * rp, rp)

        def plane_half_at(stage, section, q, way):
            return R.watt.at[stage, section, aligned((2 * q + way) * rp, rp)]

        def plane_grad(stage, q, step, way):
            near, far = (other_y, other_x) if way else (other_x, other_y)
            part, to = ((3 - s, near), (near, near), (far, far))[step // 2]
            slot = step + way
            return remote(
                ga[stage].at[grad_half(stage, part, q, way), pl.ds(0, W)],
                plane_half_at(stage, far if step == HOP else s, q, way),
                R.g1_send.at[stage, q, slot],
                R.g1_recv.at[stage, q, slot],
                to,
                o,
            )

        def plane_landed(stage, q, step, way):
            near, far = (other_y, other_x) if way else (other_x, other_y)
            src = (3 - s, near, far)[step // 2]
            slot = step + way
            remote(
                ga[stage].at[grad_half(stage, s, q, way), pl.ds(0, W)],
                plane_half_at(stage, src, q, way),
                R.g1_send.at[stage, q, slot],
                R.g1_recv.at[stage, q, slot],
                near,
                o,
            ).wait_recv()

        def each_chip(distances, body):
            for distance in distances:
                if distance:
                    chips_at((distance,), lambda q, sign, distance: body(q, sign, distance))
                else:
                    body(zz, 0, 0)

        FIRST, SECOND = tuple(range(n - 1, 1, -1)), (1, 0)

        def each_plane_grad(stage, steps, act):
            def block(q, *_):
                for step in steps:
                    for way in range(2):
                        act(plane_grad(stage, q, step, way))

            each_chip(FIRST + SECOND, block)

        def att_to_plane(stage):
            each_plane_grad(stage, (HOP, STRAIGHT), lambda copy: copy.start())

        def att_plane_late(stage, distances):
            def block(q, *_):
                for way in range(2):
                    plane_landed(stage, q, HOP, way)
                    part = grad_half(stage, other_x if way else other_y, q, way)
                    hop = R.watt[stage, 3 - s, aligned((2 * q + way) * rp, rp), :]
                    both = ga[stage][part, 0:W].astype(F32) + hop.astype(F32)
                    ga[stage][part, 0:W] = both.astype(BF16)
                    plane_grad(stage, q, LATE, way).start()

            each_chip(distances, block)

        def finish_att_plane(stage):
            each_plane_grad(stage, (HOP, STRAIGHT, LATE), lambda copy: copy.wait_send())

        def att_z_grad(stage, q, to, slot):
            return remote(
                R.gs.at[stage, aligned(q * 2 * rp, 2 * rp)],
                R.gz.at[stage, slot],
                R.g2_send.at[stage, q],
                R.g2_recv.at[stage, slot],
                s,
                2 * to + c,
            )

        def waits_behind(sign, distance):
            behind = zz - sign
            return (behind >= 0) & (behind < n) if RELAYED and distance == 2 else False

        def att_z_straight(stage, q, sign, distance, act):
            if RELAYED and distance == 3:
                act(att_z_grad(stage, q, zz + sign, zz + sign))
            elif RELAYED and distance == 2:

                @pl.when(jnp.logical_not(waits_behind(sign, distance)))
                def _():
                    act(att_z_grad(stage, q, q, zz))
            elif distance:
                act(att_z_grad(stage, q, q, zz))

        def att_z_late(stage, act, add):
            def one(q, sign, distance):
                @pl.when(waits_behind(sign, distance))
                def _():
                    if add:
                        remote(
                            R.gs.at[stage, pl.ds(0, 2 * rp)],
                            R.gz.at[stage, zz],
                            R.g2_send.at[stage, q],
                            R.g2_recv.at[stage, zz],
                            s,
                            mate,
                        ).wait_recv()
                        part = aligned(q * 2 * rp, 2 * rp)
                        both = R.gs[stage, part, :].astype(F32) + R.gz[stage, zz].astype(F32)
                        R.gs[stage, part, :] = both.astype(BF16)
                    act(att_z_grad(stage, q, q, zz))

            if RELAYED:
                chips_at((2,), one)

        def att_late(stage):
            att_z_late(stage, lambda copy: copy.start(), True)

        def finish_att_z(stage):
            each_chip(
                FIRST + SECOND,
                lambda q, sign, distance: att_z_straight(
                    stage, q, sign, distance, lambda copy: copy.wait_send()
                ),
            )
            att_z_late(stage, lambda copy: copy.wait_send(), False)

        def att_along_z(stage, distances):
            def block(q, sign, distance):
                part = aligned(q * 2 * rp, 2 * rp)

                for step in (STRAIGHT, LATE):
                    for way in range(2):
                        plane_landed(stage, q, step, way)
                own = aligned(s * att_rows + q * 2 * rp, 2 * rp)
                total = ga[stage][own, 0:W].astype(F32)
                for src in (other_x, other_y):
                    total = total + R.watt[stage, src, part, :].astype(F32)
                R.gs[stage, part, :] = total.astype(BF16)
                att_z_straight(stage, q, sign, distance, lambda copy: copy.start())

            each_chip(distances, block)

        def home_copy(stage, core):
            return remote(
                R.gt.at[stage, pl.ds(core * rp, rp)],
                R.att_own.at[aligned(s * rp, rp)],
                R.g3_send.at[stage, core],
                R.g3_recv.at[s],
                2 * (1 - stage) + c,
                2 * zz + core,
            )

        def each_home(stage, act, own):
            for core in range(2):
                stays = (s == 2 * (1 - stage) + c) & (c == core)

                @pl.when(stays)
                def _(core=core):
                    if own:
                        R.att_own[aligned(s * rp, rp), :] = R.gt[stage, pl.ds(core * rp, rp), :]

                @pl.when(jnp.logical_not(stays))
                def _(core=core):
                    act(home_copy(stage, core))

        def att_owned(stage):
            def landed(q, sign, distance):
                if not (RELAYED and distance == 3):
                    remote(
                        R.gs.at[stage, pl.ds(0, 2 * rp)],
                        R.gz.at[stage, q],
                        R.g2_send.at[stage, q],
                        R.g2_recv.at[stage, q],
                        s,
                        2 * q + c,
                    ).wait_recv()

            chips_at(range(1, n), landed)
            total = R.gs[stage, aligned(zz * 2 * rp, 2 * rp), :].astype(F32)
            for k in range(1, n):
                q = (zz + k) % n
                part = R.gz[stage, q].astype(F32)
                if RELAYED:
                    part = jnp.where(jnp.abs(q - zz) == 3, 0.0, part)
                total = total + part
            R.gt[stage] = total.astype(BF16)
            each_home(stage, lambda copy: copy.start(), True)

        def att_home():
            for p in range(SECTIONS):
                mine = (s == p) & (x == c)

                @pl.when(jnp.logical_not(mine))
                def _(p=p):
                    remote(
                        R.gt.at[0, pl.ds(0, rp)],
                        R.att_own.at[pl.ds(p * rp, rp)],
                        R.g3_send.at[0, 0],
                        R.g3_recv.at[p],
                        p,
                        2 * zz + x,
                    ).wait_recv()

            rows = R.att_own[pl.ds(0, ru), :].astype(F32)
            R.o_qkv[...] = from_packed(rows, F, heads)
            rows = R.att_own[pl.ds(ru, ra - ru), :].astype(F32)
            R.o_out[...] = rows[:ro, :D]

        att_collect(0)
        att_onward(1, NEAR)
        attention_forward(0)
        send_parts(0, True, None)
        for m in range(2):
            close_forward(0, m)
        feed_arrivals(0, NEAR, (0,))
        pass_rows(1, R.norm_ff.at[0])
        feed_arrivals(0, NEAR, (1,))
        feed_spread_home(1)
        feed_spread_away(1, 0)
        feed_spread_away(1, 1)
        att_onward(1, FAR)
        feed_collect(0, (0,))
        finish_send_parts(0, True)
        for m in range(2):
            await_rows(1, False, m, R.norm_ff.at[0])
            feed_up(0, m)
        att_plane_relay(1, zz)
        att_plane_onward(1, NEAR)
        feed_collect(0, (1,))
        for m in range(2):
            feed_down(0, m)
            send_parts(1, False, m)
        late_parts(1, 0)
        att_plane_onward(1, FAR)
        late_parts(1, 1)
        close_forward(1, 0)
        feed_arrivals(1, NEAR)
        close_forward(1, 1)
        att_collect(1)
        finish_send_parts(1, False)
        await_rows(2, True, None, R.norm_at.at[1])
        attention_forward(1)
        send_parts(2, True, None)
        for m in range(2):
            close_forward(2, m)
        feed_collect(1)
        pass_rows(3, R.norm_ff.at[1])
        finish_send_parts(2, True)
        for m in range(2):
            await_rows(3, False, m, R.norm_ff.at[1])
            feed_up(1, m)

        loop(NO, lambda k: small_out(k).wait_send(), 1)
        loop(SECTIONS, lambda k: small_b_copy(k, s).wait_send(), 1)
        len_copy.wait_send()
        each_quarter(lambda copy: copy.wait_send(), False)

        @pl.when(x == c)
        def _():
            seq_copy(False).wait_send()

        for kind in range(2):
            y_copy(kind).wait_send()
        for layer in range(2):
            att_sent(layer)
            feed_sent(layer)
        for m in range(2):
            finish_send_rows(1, False, m, R.norm_ff.at[0])
            finish_send_rows(2, True, m, R.norm_at.at[1])
            finish_send_rows(3, False, m, R.norm_ff.at[1])
            for j in range(2):
                cot_copy(m, j, True).wait()
                cot_copy(m, j, False).wait_send()
                remote(
                    R.cot_in.at[m, pl.ds(0, Q)],
                    R.grad_ff.at[0, aligned(j * L + (2 * m + 1 - c) * Q, Q)],
                    R.cot_send.at[m, j],
                    R.cot_recv.at[m, j],
                    s,
                    mate,
                ).wait_recv()
        for j in range(2):
            R.grad_rows[pl.ds(j * Q, Q), :] = R.grad_ff[0, aligned(j * L + s * Q, Q), :]

        for m in range(2):
            feed_back_rows(1, m)
            send_parts(4, False, m)
        feed_back_down(1)
        feed_to_mate(0, DOWN)
        feed_back_up(1)
        feed_to_mate(0, UP)
        for m in range(2):
            late_parts(4, m)
        feed_along_z(0, DOWN)
        feed_along_z(0, UP)
        for m in range(2):
            close_backward(4, m)
        finish_send_parts(4, False)
        for m in range(2):
            feed_down(1, m)
            send_parts(3, False, m)
        await_rows(5, True, None, grad_at[1])
        attention_back_heads(
            1, lambda: (feed_late(0, DOWN), late_parts(3, 0), late_parts(3, 1))
        )
        feed_late(0, UP)
        finish_send_parts(3, False, (0,))
        attention_back_rows(1)
        send_parts(5, True, None)
        attention_back_out(1)
        attention_back_weights(1)
        for m in range(2):
            close_backward(5, m)
        for m in range(2):
            close_forward(3, m)
        finish_send_parts(3, False, (1,))
        finish_send_parts(5, True)
        pass_rows(6, R.grad_ff.at[1])
        for m in range(2):
            await_rows(6, False, m, R.grad_ff.at[1])
            feed_back_rows(0, m)
            send_parts(6, False, m)
        feed_back_down(0)
        feed_to_mate(1, DOWN)
        late_parts(6, 0)
        feed_back_up(0)
        feed_to_mate(1, UP)
        late_parts(6, 1)
        att_to_plane(0)
        for m in range(2):
            finish_send_rows(5, True, m, grad_at[1])
        feed_owned(0)
        finish_feed_z(0)
        feed_along_z(1, DOWN)
        feed_along_z(1, UP)
        for m in range(2):
            close_backward(6, m)
        finish_send_parts(6, False)
        await_rows(7, True, None, grad_at[0])
        attention_back_out(0)
        attention_back_heads(0, lambda: feed_late(1, DOWN))
        att_plane_late(0, FIRST + SECOND)
        feed_late(1, UP)
        attention_back_weights(0)
        att_to_plane(1)
        attention_back_rows(0)
        send_parts(7, True, None)
        att_along_z(0, FIRST + SECOND)
        for m in range(2):
            close_backward(7, m)

        emitted = []

        def emit(*pairs):
            for held, out in pairs:
                copy = pltpu.make_async_copy(held, out, R.out_sem.at[len(emitted)])
                copy.start()
                emitted.append(copy)

        def small_grad_copy(k, of):
            to = (s + k) % SECTIONS
            return remote(
                R.small_grad.at[to],
                R.small_sum.at[of],
                R.sga_send.at[k],
                R.sga_recv.at[of],
                to,
                o,
            )

        def small_mate_copy(of):
            return remote(
                R.small_line, R.small_all.at[of], R.sgb_send.at[0], R.sgb_recv.at[of], s, mate
            )

        def small_z_copy(k, of):
            to = 2 * ((zz + k) % n) + c
            return remote(
                R.small_own, R.small_all.at[of], R.sgb_send.at[k], R.sgb_recv.at[of], s, to
            )

        def small_to_mate():
            loop(SECTIONS, lambda k: small_grad_copy(k, (s + k) % SECTIONS).wait_recv(), 1)
            total = R.small_sum[0]
            for k in range(1, SECTIONS):
                total = total + R.small_sum[k]
            R.small_line[...] = total
            small_mate_copy(o).start()

        def small_along_z():
            small_mate_copy(mate).wait_recv()
            R.small_own[...] = R.small_line[...] + R.small_all[mate]
            loop(n, lambda k: small_z_copy(k, o).start(), 1)

        loop(SECTIONS, lambda k: small_grad_copy(k, s).start(), 1)
        R.small_sum[s] = R.small_grad[s]
        att_plane_late(1, FIRST)
        att_late(0)
        small_to_mate()
        att_plane_late(1, SECOND)
        feed_to_home(0)
        small_along_z()
        att_along_z(1, FIRST)
        feed_owned(1)
        feed_to_home(1)
        att_along_z(1, SECOND)
        att_late(1)
        att_owned(0)
        feed_home()
        att_owned(1)
        loop(n, lambda k: small_z_copy(k, 2 * ((zz + k) % n) + c).wait_recv(), 1)
        total = R.small_own[...]
        for k in range(1, n):
            total = total + R.small_all[2 * ((zz + k) % n) + c]

        def back(rows, lanes):
            return pltpu.roll(rows, (wide - lanes) % wide, 1)

        norms = back(total, ru * o)
        for k in range(3):
            R.o_norm[k] = norms[k : k + 1, 0:ru]
        units = back(total, rd * o)
        R.o_upb[:, 0:rd] = units[4:5, 0:rd]
        R.o_upb[:, rd : 2 * rd] = units[5:6, 0:rd]
        first, second, third = 3 * low, 3 * low + 2 * rest, 3 * low + 3 * rest
        plain = jnp.where(lane8 < low, total, 0.0)
        plain += back(jnp.where((lane8 >= first) & (lane8 < first + rest), total, 0.0), 2 * low)
        plain += back(jnp.where((lane8 >= 2 * low) & (lane8 < first), total, 0.0), 2 * low - F)
        plain += back(
            jnp.where((lane8 >= second) & (lane8 < third), total, 0.0), 2 * low + 2 * rest - F
        )
        R.o_qvb[...] = back(plain, ru * o)[3:4, 0:ru]
        squares = back(total, 4 * o)
        for m in range(2):
            count = (R.lens[0, m] * D).astype(F32)
            R.o_rms[m : m + 1, :] = jnp.sqrt(squares[6:7, 2 * m : 2 * m + 2] / count)
        emit(
            (R.o_up, R.h_o_up),
            (R.o_down, R.h_o_down),
            (R.o_norm, R.h_o_norm),
            (R.o_qvb, R.h_o_qvb),
            (R.o_upb, R.h_o_upb),
            (R.o_rms, R.h_o_rms),
        )
        for which in range(2):
            finish_place(which)
        emit((R.out_stream, R.h_out_stream), (R.out_grad_rows, R.h_out_grad_rows))
        att_home()
        emit((R.o_qkv, R.h_o_qkv), (R.o_out, R.h_o_out))

        loop(SECTIONS, lambda k: small_grad_copy(k, s).wait_send(), 1)
        small_mate_copy(o).wait_send()
        loop(n, lambda k: small_z_copy(k, o).wait_send(), 1)
        for m in range(2):
            finish_send_rows(6, False, m, R.grad_ff.at[1])
            finish_send_rows(7, True, m, grad_at[0])
        finish_send_parts(7, True)
        finish_feed_z(1)
        for stage in range(2):
            finish_att_plane(stage)
            finish_att_z(stage)
            each_home(stage, lambda copy: copy.wait_send(), False)

        for copy in emitted:
            copy.wait()

    return kernel


def one_step(cfg, lens, qkv, qv_b, out, up, up_b, down, norm, stream, cotangent):
    D, L, U, F, W = cfg.width, cfg.length, cfg.units, cfg.features, cfg.packed
    Q = L // SECTIONS
    NO, n = cfg.outer, cfg.outer // 2
    ru, rd, ro, ra = cfg.up_rows, cfg.down_rows, cfg.out_rows, cfg.att_rows
    rp = ra // SECTIONS
    wide = max(U, W)
    lanes = -(-max(ru, rd) // 128) * 128
    dma = pltpu.SemaphoreType.DMA
    inputs = dict(
        lens=lens,
        qkv_w=qkv,
        qv_b=qv_b,
        out_w=out,
        up_w=up,
        up_b=up_b,
        down_w=down,
        norm_v=norm,
        stream_in=stream,
        cot_in=cotangent,
    )
    outputs = dict(
        out_stream=((2 * Q, D), BF16),
        out_grad_rows=((2 * Q, D), BF16),
        o_qkv=((ru, 3 * F), F32),
        o_qvb=((1, ru), F32),
        o_out=((ro, D), F32),
        o_up=((ru, 2 * U), F32),
        o_upb=((1, 2 * rd), F32),
        o_down=((2 * rd, D), F32),
        o_norm=((3, 1, ru), F32),
        o_rms=((2, 2), F32),
    )
    scratch = dict(
        small_in=((8, lanes), F32),
        small_a=((NO, 8, lanes), F32),
        small_own=((8, wide), F32),
        small_b=((SECTIONS, 8, wide), F32),
        small_grad=((SECTIONS, 8, wide), F32),
        small_sum=((SECTIONS, 8, wide), F32),
        small_line=((8, wide), F32),
        small_all=((NO, 8, wide), F32),
        len_own=((8, 128), F32),
        len_mate=((8, 128), F32),
        att_own=((ra, W), BF16),
        watt=((2, SECTIONS, NO * rp, W), BF16),
        wqkv=((2, D, W), BF16),
        wout=((2, F, D), BF16),
        wup=((2, D, U), BF16),
        wdown=((2, U, D), BF16),
        hid_rows=((SECTIONS, 2 * Q, D), BF16),
        grad_rows=((2 * Q, D), BF16),
        norm_at=((2, L, D), BF16),
        norm_ff=((2, 2 * L, D), BF16),
        lin_t=((2, W, L), BF16),
        att_t=((2, F, L), BF16),
        log_total=((2, cfg.heads, 1, L), F32),
        hidden=((2, 2 * L, U), BF16),
        slope=((2, 2 * L, U), BF16),
        grad_ff=((2, 2 * L, D), BF16),
        grad_at=((L, D), BF16),
        seq_rows=((L, D), BF16),
        parts=((2 * L, D), BF16),
        sums=((2, SECTIONS, 2, Q, D), BF16),
        finished=((2, 2, Q, D), BF16),
        acc=((L, D), F32),
        wide_rows=((F + 64, D), F32),
        d_att_t=((F, L), BF16),
        d_lin_t=((W, L), BF16),
        sb_up=((2, n * ru, U), BF16),
        rb_up=((n * ru, U), BF16),
        mb_up=((n * ru, U), BF16),
        zb_up=((n * ru, U), BF16),
        yb_up=((ru, U), BF16),
        yr_up=((ru, U), BF16),
        sb_down=((2, n * rd, D), BF16),
        rb_down=((n * rd, D), BF16),
        mb_down=((n * rd, D), BF16),
        zb_down=((n * rd, D), BF16),
        yb_down=((rd, D), BF16),
        yr_down=((rd, D), BF16),
        gs=((2, NO * rp, W), BF16),
        gz=((2, n, 2 * rp, W), BF16),
        gt=((2, 2 * rp, W), BF16),
    )
    semaphores = dict(
        raw_sem=(4,),
        load_sem=(5,),
        sma_send=(NO,),
        sma_recv=(NO,),
        smb_send=(SECTIONS,),
        smb_recv=(SECTIONS,),
        len_send=(1,),
        len_recv=(1,),
        seq_send=(1,),
        seq_recv=(1,),
        cot_send=(2, 2),
        cot_recv=(2, 2),
        a1_send=(SECTIONS,),
        a1_recv=(2, 2),
        a2_send=(2, n, n),
        a2_recv=(2, n),
        a3_send=(2, n, 2),
        a3_recv=(2, n, 2),
        a4_send=(2, n, 2),
        a4_recv=(2, n, 2),
        y_send=(2,),
        y_recv=(2,),
        z_send=(4, n, n),
        z_recv=(4, n),
        p_send=(4, n),
        p_recv=(4, n),
        ag_send=(8, 2, SECTIONS),
        ag_recv=(8, 2, SECTIONS),
        rs_send=(8, 2, 6),
        rs_recv=(8, 2, 6),
        fo_send=(2, 2),
        fo_recv=(2, 2),
        r1_send=(2, 2),
        r1_recv=(2, 2),
        r2_send=(2, 2, n),
        r2_recv=(2, 2, n),
        r4_send=(2,),
        r4_recv=(2,),
        g1_send=(2, n, 6),
        g1_recv=(2, n, 6),
        g2_send=(2, n),
        g2_recv=(2, n),
        g3_send=(2, 2),
        g3_recv=(SECTIONS,),
        sga_send=(SECTIONS,),
        sga_recv=(SECTIONS,),
        sgb_send=(NO,),
        sgb_recv=(NO,),
        out_sem=(len(outputs),),
    )
    placed = ["h_" + key for key in outputs]
    names = [*inputs, *placed, *outputs, *scratch, *semaphores]
    vmem = pl.BlockSpec(memory_space=pltpu.VMEM)
    hbm = pl.BlockSpec(memory_space=pl.ANY)
    smem = pl.BlockSpec(memory_space=pltpu.SMEM)
    shapes = [jax.ShapeDtypeStruct(*spec) for spec in outputs.values()]
    results = pl.pallas_call(
        make_kernel(cfg, names),
        out_shape=shapes,
        in_specs=[smem, hbm, vmem, hbm, hbm, vmem, hbm, vmem, hbm, hbm],
        out_specs=[hbm] * len(outputs),
        scratch_shapes=[pltpu.VMEM(*spec) for spec in (outputs | scratch).values()]
        + [dma(shape) for shape in semaphores.values()],
        compiler_params=pltpu.CompilerParams(
            collective_id=0, has_side_effects=True, vmem_limit_bytes=63 * 2**20
        ),
        name="layers",
    )(*inputs.values())
    count = len(shapes)

    def hand_over(*refs):
        given, out, held = refs[:count], refs[count : 2 * count], refs[2 * count : 3 * count]
        loads = [pltpu.make_async_copy(given[k], held[k], refs[-2].at[k]) for k in range(count)]
        stores = [pltpu.make_async_copy(held[k], out[k], refs[-1].at[k]) for k in range(count)]
        for copy in loads:
            copy.start()
        for load, store in zip(loads, stores):
            load.wait()
            store.start()
        for copy in stores:
            copy.wait()

    return pl.pallas_call(
        hand_over,
        out_shape=shapes,
        in_specs=[hbm] * count,
        out_specs=[hbm] * count,
        scratch_shapes=[pltpu.VMEM(*spec) for spec in outputs.values()]
        + [dma((count,)), dma((count,))],
        compiler_params=pltpu.CompilerParams(vmem_limit_bytes=63 * 2**20),
        name="outputs",
    )(*results)


def shards(
    layer_input,
    out_cotangent,
    lengths,
    qkv_weight,
    qv_bias,
    out_weight,
    up_weight,
    up_bias,
    down_weight,
    norm_vectors,
):
    section_count = lax.axis_size("section")
    dp_count = lax.axis_size("dp")
    L, D = layer_input.shape[2:]
    sequences = layer_input.shape[0] * layer_input.shape[1]
    assert section_count == SECTIONS and sequences == 2
    F = out_weight.shape[1] * dp_count
    U2 = up_weight.shape[2]
    heads = F // HEAD_DIM
    outer = max(
        k
        for k in range(2, dp_count + 1, 2)
        if dp_count % k == 0 and D % (16 * k) == 0 and U2 % (32 * k) == 0 and F % (8 * k) == 0
    )
    inner = dp_count // outer
    groups = [[g * inner + k for k in range(inner)] for g in range(outer)]

    def joined(block, axis=0):
        if inner == 1:
            return block
        block = block.astype(BF16)
        block = lax.all_gather(block, "dp", axis=axis, tiled=True, axis_index_groups=groups)
        return block.astype(F32)

    def own_share(block, axis=0):
        if inner == 1:
            return block
        return lax.psum_scatter(
            block, "dp", scatter_dimension=axis, tiled=True, axis_index_groups=groups
        )

    shard_rows = D // outer + F // outer
    cfg = types.SimpleNamespace(
        width=D,
        length=L,
        units=U2 // 2,
        features=F,
        packed=-(-3 * F // 256) * 256,
        outer=outer,
        inner=inner,
        heads=heads,
        up_rows=D // outer,
        down_rows=U2 // outer // 2,
        out_rows=F // outer,
        att_rows=-(-shard_rows // (16 * SECTIONS)) * 16 * SECTIONS,
    )
    stream, grad_rows, qkv, qvb, out, up, upb, down, norm, rms = one_step(
        cfg,
        lengths.reshape(1, 2),
        joined(qkv_weight[0]),
        joined(qv_bias, 1),
        joined(out_weight[0]),
        joined(up_weight[0]),
        joined(up_bias, 1),
        joined(down_weight[0]),
        joined(norm_vectors[0], 1)[:, None],
        layer_input.reshape(2, L, D),
        out_cotangent.reshape(2, L, D),
    )
    rows_shape = layer_input.shape[:2] + (L // SECTIONS, D)
    return (
        stream.reshape(rows_shape),
        grad_rows.reshape(rows_shape),
        own_share(qkv)[None],
        own_share(qvb, 1),
        own_share(out)[None],
        own_share(up)[None],
        own_share(upb, 1),
        own_share(down)[None],
        own_share(norm, 2).reshape(1, 3, -1),
        rms.reshape(layer_input.shape[:2] + (1, 2)),
    )


def solution(mesh):
    placed = (
        P(None, "dp", None, None),
        P(None, "dp", None, None),
        P(None, "dp"),
        P("section", "dp", None),
        P("section", "dp"),
        P("section", "dp", None),
        P("section", "dp", None),
        P("section", "dp"),
        P("section", "dp", None),
        P("section", None, "dp"),
    )
    return jax.shard_map(
        shards,
        mesh=mesh,
        in_specs=placed,
        out_specs=(
            P(None, "dp", "section", None),
            P(None, "dp", "section", None),
            P("section", "dp", None),
            P("section", "dp"),
            P("section", "dp", None),
            P("section", "dp", None),
            P("section", "dp"),
            P("section", "dp", None),
            P("section", None, "dp"),
            P(None, "dp", "section", None),
        ),
        check_vma=False,
    )
```

```python
import types

import jax
import jax.numpy as jnp
from jax import lax
from jax.experimental import pallas as pl
from jax.experimental.pallas import tpu as pltpu
from jax.sharding import PartitionSpec as P

F32, BF16 = jnp.float32, jnp.bfloat16
MESH = pl.DeviceIdType.MESH
HEAD_DIM = 32
EPSILON = 1e-05
MASKED = -1e30
SCALE = HEAD_DIM**-0.5
SCALE_2 = SCALE * 1.4426950408889634
SECTIONS = 4
NN = (((1,), (0,)), ((), ()))
NT = (((1,), (1,)), ((), ()))
TN = (((0,), (0,)), ((), ()))


def mm(left, right, dims=NN):
    return lax.dot_general(left, right, dims, preferred_element_type=F32)


def aligned(start, size):
    return pl.ds(pl.multiple_of(start, size), size)


def head_rows(h, heads):
    full = heads // 8 * 8
    low, rest = full * HEAD_DIM, (heads - full) * HEAD_DIM
    high = h // full if rest else 0
    q = h * HEAD_DIM + high * 2 * low
    k = low + h * HEAD_DIM + high * (low + rest)
    v = 2 * low + h * HEAD_DIM + high * 2 * rest
    return tuple(pl.multiple_of(row, HEAD_DIM) for row in (q, k, v))


def to_packed(rows, heads):
    half = rows.shape[-1] // 3
    low = heads // 8 * 8 * HEAD_DIM
    parts = [rows[:, i * half : i * half + low] for i in range(3)]
    parts += [rows[:, i * half + low : (i + 1) * half] for i in range(3)]
    return jnp.concatenate(parts, axis=1)


def from_packed(rows, half, heads):
    low = heads // 8 * 8 * HEAD_DIM
    rest = half - low
    parts = []
    for i in range(3):
        parts.append(rows[:, i * low : (i + 1) * low])
        parts.append(rows[:, 3 * low + i * rest : 3 * low + (i + 1) * rest])
    return jnp.concatenate(parts, axis=1)


def lanes_to(rows, width):
    if rows.shape[1] == width:
        return rows
    return jnp.concatenate([rows, jnp.zeros((rows.shape[0], width - rows.shape[1]), F32)], axis=1)


def normed_rows(h, gain, shift):
    mean = jnp.mean(h, axis=-1, keepdims=True)
    centred = h - mean
    spread = jnp.mean(centred * centred, axis=-1, keepdims=True)
    inverse = lax.rsqrt(spread + EPSILON)
    return centred * inverse, inverse, centred * inverse * gain + shift


def make_kernel(cfg, names):
    c_ = cfg
    D, L, U, F, W = c_.width, c_.length, c_.units, c_.features, c_.packed
    Q = L // SECTIONS
    NO, n, inner, heads = c_.outer, c_.outer // 2, c_.inner, c_.heads
    ru, rd, ro = c_.up_rows, c_.down_rows, c_.out_rows
    ra, rp = c_.att_rows, c_.att_rows // SECTIONS
    wide = max(U, W)
    low = heads // 8 * 8 * HEAD_DIM
    rest = F - low

    def kernel(*refs):
        R = types.SimpleNamespace(**dict(zip(names, refs)))
        s = lax.axis_index("section")
        y, x = s // 2, s % 2
        dp = lax.axis_index("dp")
        o, i = dp // inner, dp % inner
        zz, c = o // 2, o % 2
        other_x, other_y = s + 1 - 2 * x, s + 2 - 4 * y
        mate = o + 1 - 2 * c

        def remote(src, dst, send, recv, section, outer):
            return pltpu.make_async_remote_copy(
                src_ref=src,
                dst_ref=dst,
                send_sem=send,
                recv_sem=recv,
                device_id=(section, outer * inner + i),
                device_id_type=MESH,
            )

        def loop(count, body, first=0):
            def step(k, carry):
                body(k)
                return carry

            lax.fori_loop(first, count, step, 0)

        raw = (R.qkv_w, R.out_w, R.up_w, R.down_w)
        raw_home = (R.o_qkv, R.o_out, R.o_up, R.o_down)
        raw_copies = [
            pltpu.make_async_copy(a, b, R.raw_sem.at[k])
            for k, (a, b) in enumerate(zip(raw, raw_home))
        ]
        for copy in raw_copies:
            copy.start()

        barrier = pltpu.get_barrier_semaphore()

        def greet(section, outer):
            pl.semaphore_signal(
                barrier, inc=1, device_id=(section, outer * inner + i), device_id_type=MESH
            )

        loop(SECTIONS, lambda k: greet((s + k) % SECTIONS, o), 1)
        loop(SECTIONS, lambda k: greet((s + k) % SECTIONS, mate), 1)
        loop(NO, lambda k: greet(s, (o + k) % NO), 1)

        row8 = lax.broadcasted_iota(jnp.int32, (8, wide), 0)
        lane8 = lax.broadcasted_iota(jnp.int32, (8, wide), 1)
        here = row8[:, : R.small_in.shape[1]], lane8[:, : R.small_in.shape[1]]

        def rounded(v):
            return v.astype(BF16).astype(F32)

        R.small_in[...] = jnp.zeros_like(R.small_in)
        for k in range(3):
            R.small_in[k : k + 1, 0:ru] = rounded(R.norm_v[k])
        R.small_in[3:4, 0:ru] = rounded(R.qv_b[...])
        R.small_in[4:5, 0:rd] = rounded(R.up_b[:, 0:rd])
        R.small_in[5:6, 0:rd] = rounded(R.up_b[:, rd : 2 * rd])
        R.len_own[...] = jnp.where(here[1] == 0, R.lens[0, 0], R.lens[0, 1])[:, :128].astype(F32)
        pl.semaphore_wait(barrier, 2 * (SECTIONS - 1) + NO - 1)

        def small_out(k):
            peer = (o + k) % NO
            return remote(
                R.small_in, R.small_a.at[o], R.sma_send.at[k], R.sma_recv.at[o], s, peer
            )

        loop(NO, lambda k: small_out(k).start(), 1)
        R.small_a[o] = R.small_in[...]
        len_copy = remote(R.len_own, R.len_mate, R.len_send.at[0], R.len_recv.at[0], s, mate)
        len_copy.start()

        raw_copies[0].wait()
        raw_copies[1].wait()
        packed = lanes_to(to_packed(R.o_qkv[...], heads), W).astype(BF16)
        R.att_own[pl.ds(0, ru), :] = packed
        bottom = jnp.concatenate([R.o_out[...], jnp.zeros((ra - ru - ro, D), F32)], axis=0)
        R.att_own[pl.ds(ru, ra - ru), :] = lanes_to(bottom, W).astype(BF16)

        def quarter_copy(p):
            return remote(
                R.att_own.at[pl.ds(p * rp, rp)],
                R.watt.at[y, p, aligned(o * rp, rp)],
                R.a1_send.at[p],
                R.a1_recv.at[y, c],
                p,
                2 * zz + x,
            )

        def each_quarter(act, own):
            for p in range(SECTIONS):
                stays = (s == p) & (x == c)

                @pl.when(stays)
                def _(p=p):
                    if own:
                        R.watt[y, p, aligned(o * rp, rp), :] = R.att_own[pl.ds(p * rp, rp), :]

                @pl.when(jnp.logical_not(stays))
                def _(p=p):
                    act(quarter_copy(p))

        each_quarter(lambda copy: copy.start(), True)

        def seq_copy(local):
            if local:
                return pltpu.make_async_copy(R.stream_in.at[y], R.seq_rows, R.load_sem.at[0])
            return remote(
                R.stream_in.at[y], R.seq_rows, R.seq_send.at[0], R.seq_recv.at[0], s, mate
            )

        def cot_copy(m, j, local):
            half = c if local else 1 - c
            src = R.cot_in.at[m, aligned((2 * half + j) * Q, Q)]
            dst = R.grad_ff.at[0, aligned(j * L + (2 * m + c) * Q, Q)]
            if local:
                return pltpu.make_async_copy(src, dst, R.load_sem.at[1 + 2 * m + j])
            return remote(src, dst, R.cot_send.at[m, j], R.cot_recv.at[m, j], s, mate)

        def piece(kind, layer, outer):
            rows = rd if kind else ru
            return (R.wdown if kind else R.wup).at[layer, aligned(outer * rows, rows)]

        def y_copy(kind):
            return remote(
                R.yb_down if kind else R.yb_up,
                piece(kind, y, o),
                R.y_send.at[kind],
                R.y_recv.at[kind],
                other_y,
                o,
            )

        def chips_at(distances, body):
            for distance in distances:
                for sign in (1, -1):
                    q = zz + sign * distance

                    @pl.when((q >= 0) & (q < n))
                    def _(q=q, sign=sign, distance=distance):
                        body(q, sign, distance)

        def relays(distance, sign, body):
            if distance >= 2:
                after = zz - sign

                @pl.when((after >= 0) & (after < n))
                def _():
                    body(after)

        NEAR, FAR = tuple(range(min(2, n - 1), 0, -1)), range(3, n)

        def z_copy(layer, kind, origin, to):
            item = layer * 2 + kind
            part = piece(kind, layer, 2 * origin + c)
            send = R.z_send.at[item, origin, to]
            return remote(part, part, send, R.z_recv.at[item, origin], s, 2 * to + c)

        def mate_copy(layer, kind, q):
            item = layer * 2 + kind
            part = piece(kind, layer, 2 * q + c)
            return remote(part, part, R.p_send.at[item, q], R.p_recv.at[item, q], s, mate)

        def mate_arrival(layer, kind, q):
            item = layer * 2 + kind
            part = piece(kind, layer, 2 * q + 1 - c)
            return remote(part, part, R.p_send.at[item, q], R.p_recv.at[item, q], s, mate)

        def feed_spread(layer, kind):
            chips_at(NEAR, lambda q, *_: z_copy(layer, kind, zz, q).start())
            mate_copy(layer, kind, zz).start()

        def feed_spread_home(layer):
            @pl.when(y == layer)
            def _():
                feed_spread(layer, 0)
                feed_spread(layer, 1)

        def feed_spread_away(layer, kind):
            @pl.when(y != layer)
            def _():
                src = R.yb_down if kind else R.yb_up
                remote(
                    src,
                    piece(kind, layer, o),
                    R.y_send.at[kind],
                    R.y_recv.at[kind],
                    other_y,
                    o,
                ).wait_recv()
                feed_spread(layer, kind)

        def feed_arrivals(layer, distances, kinds=(0, 1)):
            for kind in kinds:

                def landed(q, sign, distance):
                    z_copy(layer, kind, q, zz).wait_recv()
                    relays(
                        distance, sign, lambda after: z_copy(layer, kind, q, after).start()
                    )
                    mate_copy(layer, kind, q).start()

                chips_at(distances, landed)

        def feed_collect(layer, kinds=(0, 1)):
            feed_arrivals(layer, FAR, kinds)
            for kind in kinds:
                loop(n, lambda q, kind=kind: mate_arrival(layer, kind, q).wait_recv())

        def feed_sent(layer):
            for kind in range(2):
                chips_at(NEAR, lambda q, *_: z_copy(layer, kind, zz, q).wait_send())
                for distances in (NEAR, FAR):
                    chips_at(
                        distances,
                        lambda q, sign, distance: relays(
                            distance,
                            sign,
                            lambda after: z_copy(layer, kind, q, after).wait_send(),
                        ),
                    )
                loop(n, lambda q, kind=kind: mate_copy(layer, kind, q).wait_send())

        def att_block(layer, p, q):
            return R.watt.at[layer, p, aligned(q * 2 * rp, 2 * rp)]

        def att_z_copy(layer, origin, to):
            part = att_block(layer, s, origin)
            send = R.a2_send.at[layer, origin, to]
            return remote(part, part, send, R.a2_recv.at[layer, origin], s, 2 * to + c)

        def att_plane_copy(layer, q, way):
            part = att_block(layer, s, q)
            to = other_y if way else other_x
            return remote(
                part, part, R.a3_send.at[layer, q, way], R.a3_recv.at[layer, q, way], to, o
            )

        def plane_half(layer, section, q, way):
            first = rp if layer else rp // 2
            start = q * 2 * rp + (first if way else 0)
            rows = 2 * rp - first if way else first
            return R.watt.at[layer, section, pl.ds(pl.multiple_of(start, 16), rows)]

        def att_plane_half(layer, q, way):
            src, to = (other_y, other_x) if way else (other_x, other_y)
            part = plane_half(layer, src, q, way)
            return remote(
                part, part, R.a4_send.at[layer, q, way], R.a4_recv.at[layer, q, way], to, o
            )

        def att_plane_start(layer, q):
            for way in range(2):
                att_plane_copy(layer, q, way).start()

        def att_plane_relay(layer, q):
            for way in range(2):
                src = other_y if way else other_x
                part = att_block(layer, src, q)
                remote(
                    part,
                    part,
                    R.a3_send.at[layer, q, way],
                    R.a3_recv.at[layer, q, way],
                    src,
                    o,
                ).wait_recv()
                att_plane_half(layer, q, way).start()

        def att_spread(layer):
            for core in range(2):
                mine = (s == 2 * layer + c) & (c == core)

                @pl.when(jnp.logical_not(mine))
                def _(core=core):
                    remote(
                        R.att_own.at[pl.ds(0, rp)],
                        R.watt.at[layer, s, aligned((2 * zz + core) * rp, rp)],
                        R.a1_send.at[0],
                        R.a1_recv.at[layer, core],
                        2 * layer + c,
                        2 * zz + core,
                    ).wait_recv()

            chips_at(reach(layer), lambda q, *_: att_z_copy(layer, zz, q).start())
            att_plane_start(layer, zz)

        def reach(layer):
            return NEAR if layer else tuple(range(1, n))

        def att_onward(layer, distances):
            def landed(q, sign, distance):
                att_z_copy(layer, q, zz).wait_recv()
                if layer:
                    relays(distance, sign, lambda after: att_z_copy(layer, q, after).start())
                att_plane_start(layer, q)

            chips_at(distances, landed)

        def att_sent(layer):
            chips_at(reach(layer), lambda q, *_: att_z_copy(layer, zz, q).wait_send())
            if layer:
                for distances in (NEAR, FAR):
                    chips_at(
                        distances,
                        lambda q, sign, distance: relays(
                            distance,
                            sign,
                            lambda after: att_z_copy(layer, q, after).wait_send(),
                        ),
                    )

            def plane_sent(q):
                for way in range(2):
                    att_plane_copy(layer, q, way).wait_send()
                    att_plane_half(layer, q, way).wait_send()

            loop(n, plane_sent)

        def att_plane_onward(layer, distances):
            chips_at(distances, lambda q, *_: att_plane_relay(layer, q))

        def att_collect(layer):
            def block(q):
                for way in range(2):
                    part = plane_half(layer, 3 - s, q, way)
                    remote(
                        part,
                        part,
                        R.a4_send.at[layer, q, way],
                        R.a4_recv.at[layer, q, way],
                        other_y,
                        o,
                    ).wait_recv()

            loop(n, block)

            def unpack(k):
                for r in range(0, ru, 16):
                    R.wqkv[layer, aligned(k * ru + r, 16), :] = R.watt[
                        layer, r // rp, aligned(k * rp + r % rp, 16), :
                    ]
                for r in range(0, ro, 16):
                    rows = min(16, ro - r)
                    p, off = (ru + r) // rp, (ru + r) % rp
                    block = R.watt[layer, p, aligned(k * rp + off, 16), :][:, :D].astype(F32)
                    R.wide_rows[aligned(k * ro + r, 8), :] = block[:rows][:8]
                    if rows > 8:
                        R.wide_rows[aligned(k * ro + r + 8, 8), :] = block[8:rows]

            loop(NO, unpack)
            R.wout[layer] = R.wide_rows[pl.ds(0, F), :].astype(BF16)

        att_spread(0)
        att_spread(1)

        raw_copies[2].wait()
        raw_copies[3].wait()
        halves = [
            jnp.concatenate(
                [R.o_up[:, (2 * k + h) * rd : (2 * k + h + 1) * rd] for k in range(NO)], axis=1
            ).astype(BF16)
            for h in range(2)
        ]
        R.wup[y, aligned(o * ru, ru), :] = jnp.where(y == 0, halves[0], halves[1])
        R.yb_up[...] = jnp.where(y == 0, halves[1], halves[0])
        R.wdown[y, aligned(o * rd, rd), :] = R.o_down[aligned(y * rd, rd), :].astype(BF16)
        R.yb_down[...] = R.o_down[aligned((1 - y) * rd, rd), :].astype(BF16)
        y_copy(0).start()
        feed_spread_home(0)

        @pl.when(x == c)
        def _():
            seq_copy(True).start()
            seq_copy(False).start()

        for m in range(2):
            for j in range(2):
                cot_copy(m, j, True).start()
                cot_copy(m, j, False).start()

        loop(
            NO,
            lambda k: remote(
                R.small_in,
                R.small_a.at[(o + k) % NO],
                R.sma_send.at[k],
                R.sma_recv.at[(o + k) % NO],
                s,
                (o + k) % NO,
            ).wait_recv(),
            1,
        )
        table = jnp.zeros((8, wide), F32)
        for k in range(NO):
            part = lanes_to(R.small_a[k], wide)
            narrow = pltpu.roll(part, ru * k, 1) if k else part
            broad = pltpu.roll(part, rd * k, 1) if k else part
            table = table + jnp.where(row8 < 4, narrow, broad)
        moved = jnp.where(lane8 < low, table, 0.0)
        moved += pltpu.roll(jnp.where((lane8 >= low) & (lane8 < F), table, 0.0), 2 * low, 1)
        moved += pltpu.roll(
            jnp.where((lane8 >= F) & (lane8 < F + low), table, 0.0), 2 * low - F, 1
        )
        moved += pltpu.roll(
            jnp.where((lane8 >= F + low) & (lane8 < 2 * F), table, 0.0), 2 * low + 2 * rest - F, 1
        )
        table = jnp.where(row8 == 3, moved, table)
        R.small_own[...] = table
        R.small_b[s] = table

        def small_b_copy(k, of):
            return remote(
                R.small_own,
                R.small_b.at[of],
                R.smb_send.at[k],
                R.smb_recv.at[of],
                (s + k) % SECTIONS,
                o,
            )

        loop(SECTIONS, lambda k: small_b_copy(k, s).start(), 1)

        def first_blocks(k):
            q = (zz + k) % n
            att_z_copy(0, q, zz).wait_recv()
            att_plane_start(0, q)
            att_plane_relay(0, (zz + k - 1) % n)

        loop(n, first_blocks, 1)
        y_copy(1).start()
        feed_spread_away(0, 0)
        att_plane_relay(0, (zz + n - 1) % n)
        loop(SECTIONS, lambda k: small_b_copy(k, (s + k) % SECTIONS).wait_recv(), 1)

        R.small_grad[...] = jnp.zeros_like(R.small_grad)
        def note_rows(block, index, row):
            R.small_grad[block] += jnp.where(row8 == index, lanes_to(row, wide), 0.0)


        @pl.when(x == c)
        def _():
            seq_copy(True).wait()

        @pl.when(x != c)
        def _():
            seq_copy(False).wait_recv()

        gain0 = R.small_b[0, 0:1, :D]
        shift0 = R.small_b[0, 1:2, :D]

        def first_norm(k):
            rows = aligned(k * Q, Q)
            _, _, out = normed_rows(R.seq_rows[rows, :].astype(F32), gain0, shift0)
            R.norm_at[0, rows, :] = out.astype(BF16)

        loop(L // Q, first_norm)
        feed_spread_away(0, 1)
        R.hid_rows[0] = R.seq_rows[aligned(c * 2 * Q, 2 * Q), :]
        len_copy.wait_recv()
        tile = jnp.where(x == c, R.len_own[...], R.len_mate[...])
        tile = jnp.where((row8[:, :128] == 0) & (lane8[:, :128] == y), tile, 0.0)
        length_here = jnp.sum(jnp.sum(tile, axis=1, keepdims=True), axis=0, keepdims=True)
        length_here = length_here.astype(jnp.int32)
        def block_copy(phase, m, buf, way):
            part = buf.at[aligned(m * L + s * Q, Q)]
            to = other_y if way else other_x
            return remote(
                part, part, R.ag_send.at[phase, m, way], R.ag_recv.at[phase, m, way], to, o
            )

        def half_copy(phase, m, buf, way):
            src, to = (other_y, other_x) if way else (other_x, other_y)
            part = buf.at[aligned(m * L + src * Q + way * (Q // 2), Q // 2)]
            slot = 2 + way
            return remote(
                part, part, R.ag_send.at[phase, m, slot], R.ag_recv.at[phase, m, slot], to, o
            )

        def share_mate(phase, m, buf):
            part = buf.at[aligned((2 * c + m) * Q, Q)]
            return remote(
                part, part, R.ag_send.at[phase, m, 0], R.ag_recv.at[phase, m, c], s, mate
            )

        def pass_rows(phase, buf):
            for m in range(2):
                for way in range(2):
                    src = other_y if way else other_x
                    part = buf.at[aligned(m * L + src * Q, Q)]
                    remote(
                        part, part, R.ag_send.at[phase, m, way], R.ag_recv.at[phase, m, way], src, o
                    ).wait_recv()
                    half_copy(phase, m, buf, way).start()

        def send_rows(phase, attention, m, buf, value):
            if attention:
                buf[aligned((2 * c + m) * Q, Q), :] = value
                share_mate(phase, m, buf).start()
            else:
                buf[aligned(m * L + s * Q, Q), :] = value
                for way in range(2):
                    block_copy(phase, m, buf, way).start()

        def finish_send_rows(phase, attention, m, buf):
            if attention:
                share_mate(phase, m, buf).wait_send()
            else:
                for way in range(2):
                    block_copy(phase, m, buf, way).wait_send()
                    half_copy(phase, m, buf, way).wait_send()

        def await_rows(phase, attention, m, buf):
            if attention:
                for j in range(2):
                    part = buf.at[aligned((2 * (1 - c) + j) * Q, Q)]
                    remote(
                        part, part, R.ag_send.at[phase, j, 0], R.ag_recv.at[phase, j, 1 - c], s, mate
                    ).wait_recv()
            else:
                for way in range(2):
                    part = buf.at[aligned(m * L + (3 - s) * Q + way * (Q // 2), Q // 2)]
                    slot = 2 + way
                    remote(
                        part,
                        part,
                        R.ag_send.at[phase, m, slot],
                        R.ag_recv.at[phase, m, slot],
                        other_y,
                        o,
                    ).wait_recv()

        def sum_slot(phase):
            return 0 if phase < 4 else 1

        HOP, STRAIGHT, LATE = 0, 2, 4

        def half_rows(m, section, way):
            return aligned(m * L + section * Q + way * (Q // 2), Q // 2)

        def half_sum(phase, src, m, way):
            return R.sums.at[sum_slot(phase), src, m, pl.ds(way * (Q // 2), Q // 2)]

        def part_copy(phase, m, step, way):
            near, far = (other_y, other_x) if way else (other_x, other_y)
            if step == HOP:
                to, rows, dst = near, half_rows(m, 3 - s, way), half_sum(phase, far, m, way)
            elif step == STRAIGHT:
                to, rows, dst = near, half_rows(m, near, way), half_sum(phase, s, m, way)
            else:
                to, rows, dst = far, half_rows(m, far, way), half_sum(phase, s, m, way)
            slot = step + way
            return remote(
                R.parts.at[rows],
                dst,
                R.rs_send.at[phase, m, slot],
                R.rs_recv.at[phase, m, slot],
                to,
                o,
            )

        def part_landed(phase, m, step, way):
            near, far = (other_y, other_x) if way else (other_x, other_y)
            src = 3 - s if step == HOP else (near if step == STRAIGHT else far)
            slot = step + way
            remote(
                R.parts.at[pl.ds(0, Q // 2)],
                half_sum(phase, src, m, way),
                R.rs_send.at[phase, m, slot],
                R.rs_recv.at[phase, m, slot],
                near,
                o,
            ).wait_recv()

        def late_parts(phase, m):
            for way in range(2):
                part_landed(phase, m, HOP, way)
                rows = half_rows(m, other_x if way else other_y, way)
                hop = R.sums[sum_slot(phase), 3 - s, m, pl.ds(way * (Q // 2), Q // 2), :]
                both = R.parts[rows, :].astype(F32) + hop.astype(F32)
                R.parts[rows, :] = both.astype(BF16)
                part_copy(phase, m, LATE, way).start()

        def mate_part(phase, j):
            return remote(
                R.parts.at[aligned((2 * (1 - c) + j) * Q, Q)],
                R.sums.at[sum_slot(phase), c, j],
                R.rs_send.at[phase, j, 0],
                R.rs_recv.at[phase, j, c],
                s,
                mate,
            )

        def send_parts(phase, attention, m):
            slot = sum_slot(phase)
            if attention:
                for j in range(2):
                    mate_part(phase, j).start()
                    R.sums[slot, c, j] = R.parts[aligned((2 * c + j) * Q, Q), :]
            else:
                for step in (HOP, STRAIGHT):
                    for way in range(2):
                        part_copy(phase, m, step, way).start()
                R.sums[slot, s, m] = R.parts[aligned(m * L + s * Q, Q), :]

        def finish_send_parts(phase, attention, chunks=(0, 1)):
            for m in chunks:
                if attention:
                    mate_part(phase, m).wait_send()
                else:
                    for step in (HOP, STRAIGHT, LATE):
                        for way in range(2):
                            part_copy(phase, m, step, way).wait_send()

        def part_arrival(phase, m, src):
            return remote(
                R.parts.at[pl.ds(0, Q)],
                R.sums.at[sum_slot(phase), src, m],
                R.rs_send.at[phase, m, 0],
                R.rs_recv.at[phase, m, src],
                s,
                mate,
            )

        def await_parts(phase, attention, m):
            slot = sum_slot(phase)
            if attention:
                part_arrival(phase, m, 1 - c).wait_recv()
                sources = range(2)
            else:
                for step in (STRAIGHT, LATE):
                    for way in range(2):
                        part_landed(phase, m, step, way)
                sources = (s, other_x, other_y)
            total = None
            for src in sources:
                part = R.sums[slot, src, m].astype(F32)
                total = part if total is None else total + part
            return total

        def place_copy(which, j):
            return remote(
                R.finished.at[which, j],
                (R.out_grad_rows if which else R.out_stream).at[aligned(y * Q, Q)],
                R.fo_send.at[which, j],
                R.fo_recv.at[which, y],
                2 * c + j,
                2 * zz + x,
            )

        def place_rows(which, j):
            stays = (s == 2 * c + j) & (x == c)

            @pl.when(stays)
            def _():
                held = R.out_grad_rows if which else R.out_stream
                held[aligned(y * Q, Q), :] = R.finished[which, j]

            @pl.when(jnp.logical_not(stays))
            def _():
                place_copy(which, j).start()

        def finish_place(which):
            for j in range(2):
                stays = (s == 2 * c + j) & (x == c)

                @pl.when(jnp.logical_not(stays))
                def _(j=j):
                    place_copy(which, j).wait_send()

            for m in range(2):
                mine = (s == 2 * m + c) & (y == c)

                @pl.when(jnp.logical_not(mine))
                def _(m=m):
                    remote(
                        R.finished.at[which, 0],
                        (R.out_grad_rows if which else R.out_stream).at[pl.ds(m * Q, Q)],
                        R.fo_send.at[which, 0],
                        R.fo_recv.at[which, m],
                        2 * m + c,
                        2 * zz + y,
                    ).wait_recv()

        def close_forward(phase, m):
            e = phase
            attention = e % 2 == 0
            branch = await_parts(phase, attention, m) + R.small_b[e, 2:3, :D]
            mine = pl.ds(m * Q, Q)
            h = R.hid_rows[e, mine, :].astype(F32)
            position = (2 * c + m) * Q + lax.broadcasted_iota(jnp.int32, (Q, 1), 0)
            valid = (position < length_here).astype(F32)
            square_h = jnp.sum(jnp.sum(h * h * valid, axis=1, keepdims=True), axis=0, keepdims=True)
            square_b = jnp.sum(
                jnp.sum(branch * branch * valid, axis=1, keepdims=True), axis=0, keepdims=True
            )
            spot = (2 * zz + x) * 4 + 2 * y
            R.small_grad[e] += jnp.where((row8 == 6) & (lane8 == spot), square_h, 0.0)
            R.small_grad[e] += jnp.where((row8 == 6) & (lane8 == spot + 1), square_b, 0.0)
            fresh = (h + branch).astype(BF16)
            if e == 3:
                R.finished[0, m] = fresh
                place_rows(0, m)
                return
            R.hid_rows[e + 1, mine, :] = fresh
            _, _, out = normed_rows(
                fresh.astype(F32), R.small_b[e + 1, 0:1, :D], R.small_b[e + 1, 1:2, :D]
            )
            to_attention = (e + 1) % 2 == 0
            buf = (R.norm_at if to_attention else R.norm_ff).at[(e + 1) // 2]
            send_rows(phase + 1, to_attention, m, buf, out.astype(BF16))

        grad_at = (R.seq_rows, R.grad_at)

        def close_backward(phase, m):
            e = 7 - phase
            attention = e % 2 == 0
            d_norm = await_parts(phase, attention, m)
            mine = pl.ds(m * Q, Q)
            unit, inverse, _ = normed_rows(R.hid_rows[e, mine, :].astype(F32), 1.0, 0.0)
            flow = R.grad_rows[mine, :].astype(F32)
            note_rows(e, 0, jnp.sum(d_norm * unit, axis=0, keepdims=True))
            note_rows(e, 1, jnp.sum(d_norm, axis=0, keepdims=True))
            note_rows(e, 2, jnp.sum(flow, axis=0, keepdims=True))
            a = d_norm * R.small_b[e, 0:1, :D]
            mean_a = jnp.mean(a, axis=-1, keepdims=True)
            mean_ax = jnp.mean(a * unit, axis=-1, keepdims=True)
            fresh = (flow + (a - mean_a - unit * mean_ax) * inverse).astype(BF16)
            if e == 0:
                R.finished[1, m] = fresh
                return
            R.grad_rows[mine, :] = fresh
            to_attention = (e - 1) % 2 == 0
            buf = grad_at[(e - 1) // 2] if to_attention else R.grad_ff.at[1]
            send_rows(phase + 1, to_attention, m, buf, fresh)

        ga = (R.hidden.at[1], R.slope.at[1])

        def attention_forward(layer):
            bias = R.small_b[2 * layer + c, 3:4, :W]
            xs = R.norm_at.at[layer]
            for t in range(0, W, 256):
                cols = pl.ds(t, 256)
                lin = mm(xs[...], R.wqkv[layer, :, cols]) + bias[:, t : t + 256]
                R.lin_t[layer, cols, :] = lin.T.astype(BF16)

            def head(h):
                q0, k0, v0 = head_rows(h, heads)
                score = mm(
                    R.lin_t[layer, pl.ds(k0, HEAD_DIM), :],
                    R.lin_t[layer, pl.ds(q0, HEAD_DIM), :],
                    TN,
                )
                live = lax.broadcasted_iota(jnp.int32, score.shape, 0) < length_here
                score = jnp.where(live, score, MASKED)
                top = jnp.max(score, axis=0, keepdims=True)
                powers = jnp.exp2((score - top) * SCALE_2)
                total = jnp.sum(powers, axis=0, keepdims=True)
                probs = (powers * (1.0 / total)).astype(BF16)
                R.log_total[layer, h] = top * SCALE_2 + jnp.log2(total)
                mixed = mm(R.lin_t[layer, pl.ds(v0, HEAD_DIM), :], probs)
                R.att_t[layer, aligned(h * HEAD_DIM, HEAD_DIM), :] = mixed.astype(BF16)

            def pair(h):
                head(2 * h)
                head(2 * h + 1)

            loop(heads // 2, pair)
            if heads % 2:
                head(heads - 1)
            R.parts[pl.ds(0, L), :] = mm(R.att_t[layer], R.wout[layer], TN).astype(BF16)

        def attention_back_heads(layer, between):
            g = grad_at[layer]
            R.d_att_t[...] = mm(R.wout[layer], g[...], NT).astype(BF16)

            def head(h):
                q0, k0, v0 = head_rows(h, heads)
                q_t = R.lin_t[layer, pl.ds(q0, HEAD_DIM), :]
                k_t = R.lin_t[layer, pl.ds(k0, HEAD_DIM), :]
                v_t = R.lin_t[layer, pl.ds(v0, HEAD_DIM), :]
                d_a = R.d_att_t[aligned(h * HEAD_DIM, HEAD_DIM), :]
                score = mm(k_t, q_t, TN)
                live = lax.broadcasted_iota(jnp.int32, score.shape, 0) < length_here
                probs = jnp.where(live, jnp.exp2(score * SCALE_2 - R.log_total[layer, h]), 0.0)
                d_probs = mm(v_t, d_a, TN)
                product = probs * d_probs
                inner_sum = jnp.sum(product, axis=0, keepdims=True)
                d_score = ((product - probs * inner_sum) * SCALE).astype(BF16)
                R.d_lin_t[pl.ds(q0, HEAD_DIM), :] = mm(k_t, d_score).astype(BF16)
                R.d_lin_t[pl.ds(k0, HEAD_DIM), :] = mm(q_t, d_score, NT).astype(BF16)
                R.d_lin_t[pl.ds(v0, HEAD_DIM), :] = mm(d_a, probs.astype(BF16), NT).astype(BF16)

            def pair(h):
                head(2 * h)
                head(2 * h + 1)

            loop(heads // 4, pair)
            between()
            loop(heads // 2, pair, heads // 4)
            if heads % 2:
                head(heads - 1)

        def attention_back_rows(layer):
            for t in range(0, W, 256):
                cols = pl.ds(t, 256)
                part = mm(R.d_lin_t[cols, :], R.wqkv[layer, :, cols], (((0,), (1,)), ((), ())))
                if t == 0:
                    R.acc[...] = part
                else:
                    R.acc[...] += part
            R.parts[pl.ds(0, L), :] = R.acc[...].astype(BF16)

        def attention_back_out(layer):
            stage = 1 - layer
            R.wide_rows[pl.ds(0, F), :] = mm(R.att_t[layer], grad_at[layer][...])

            def out_rows(k):
                for r in range(ru, ra, 16):
                    top_half = R.wide_rows[aligned(k * ro + r - ru, 8), :]
                    low_half = R.wide_rows[aligned(k * ro + r - ru + 8, 8), :]
                    block = jnp.concatenate([top_half, low_half], axis=0)
                    place = aligned(r // rp * NO * rp + k * rp + r % rp, 16)
                    ga[stage][place, 0:D] = block.astype(BF16)

            loop(NO, out_rows)

        def attention_back_weights(layer):
            stage = 1 - layer
            sums = []
            for t in range(0, W, 256):
                cols = pl.ds(t, 256)
                d_lin = R.d_lin_t[cols, :].T
                sums.append(jnp.sum(d_lin.astype(F32), axis=0, keepdims=True))
                d_w = mm(R.norm_at[layer], d_lin, TN).astype(BF16)
                for k in range(NO):
                    for r in range(0, ru, 16):
                        place = pl.ds(r // rp * NO * rp + k * rp + r % rp, 16)
                        ga[stage][place, cols] = d_w[k * ru + r : k * ru + r + 16]
            note_rows(2 * layer + c, 3, jnp.concatenate(sums, axis=1))

        def feed_bias(layer):
            block = R.small_b[2 * layer + x]
            return jnp.where(y == 0, block[4:5], block[5:6])[:, :U]

        def feed_up(layer, m):
            bias = feed_bias(layer)

            def rows_step(r):
                rows = aligned(m * L + r * Q, Q)
                pre = mm(R.norm_ff[layer, rows, :], R.wup[layer]) + bias
                cdf = 0.5 + 0.5 * lax.erf(pre * 0.7071067811865476)
                density = jnp.exp(pre * pre * -0.5) * 0.3989422804014327
                R.hidden[layer, rows, :] = (pre * cdf).astype(BF16)
                R.slope[layer, rows, :] = (cdf + pre * density).astype(BF16)

            loop(SECTIONS, rows_step)

        def feed_down(layer, m):
            rows = pl.ds(m * L, L)
            R.parts[rows, :] = mm(R.hidden[layer, rows, :], R.wdown[layer]).astype(BF16)

        def feed_back_rows(layer, m):
            rows = pl.ds(m * L, L)
            g = R.grad_ff.at[0 if layer == 1 else 1, rows]
            tile = U // 2
            for j in range(2):
                cols = pl.ds(j * tile, tile)
                d_hidden = mm(g[...], R.wdown[layer, cols, :], NT)
                d_pre = (d_hidden * R.slope[layer, rows, cols].astype(F32)).astype(BF16)
                R.slope[layer, rows, cols] = d_pre
                part = mm(d_pre, R.wup[layer, :, cols], NT)
                if j == 0:
                    R.acc[...] = part
                else:
                    R.parts[rows, :] = (R.acc[...] + part).astype(BF16)

        def feed_back_down(layer):
            g = R.grad_ff.at[0 if layer == 1 else 1]
            tile = U // 2
            owners = tile // rd
            for j in range(2):
                cols = pl.ds(j * tile, tile)
                d_down = mm(R.hidden[layer, :, cols], g[...], TN).astype(BF16)
                for k in range(owners):
                    owner = j * owners + k
                    R.sb_down[owner % 2, pl.ds(owner // 2 * rd, rd), :] = d_down[
                        k * rd : (k + 1) * rd
                    ]

        def feed_back_up(layer):
            tile = U // 2
            sums = []
            for j in range(2):
                cols = pl.ds(j * tile, tile)
                d_pre = R.slope[layer, :, cols]
                d_up = mm(R.norm_ff[layer], d_pre, TN).astype(BF16)
                for k in range(NO):
                    R.sb_up[k % 2, pl.ds(k // 2 * ru, ru), cols] = d_up[k * ru : (k + 1) * ru]
                sums.append(jnp.sum(d_pre.astype(F32), axis=0, keepdims=True))
            note_rows(2 * layer + x, 4 + y, jnp.concatenate(sums, axis=1))

        z_up, z_down = (R.zb_up, R.wup.at[1]), (R.zb_down, R.norm_ff.at[1])
        UP, DOWN = (0,), (1,)
        FEED_GRADS = (
            (0, R.sb_up, R.rb_up, R.mb_up, z_up, R.yb_up, R.yr_up, ru),
            (1, R.sb_down, R.rb_down, R.mb_down, z_down, R.yb_down, R.yr_down, rd),
        )

        def mate_grads(stage, which):
            return [
                remote(sb.at[1 - c], rb, R.r1_send.at[stage, a], R.r1_recv.at[stage, a], s, mate)
                for a, sb, rb, *_ in [FEED_GRADS[k] for k in which]
            ]

        RELAYED = n == 4

        def z_grad(stage, entry, q, to, slot):
            a, sb, rb, mb, zb, yb, yr, rows = entry
            return remote(
                mb.at[aligned(q * rows, rows)],
                zb[stage].at[aligned(slot * rows, rows)],
                R.r2_send.at[stage, a, q],
                R.r2_recv.at[stage, a, slot],
                s,
                2 * to + c,
            )

        def each_z_grad(stage, act, late, which=(0, 1)):
            def one(entry, q, sign, distance):
                if RELAYED and distance == 3:
                    if not late:
                        act(z_grad(stage, entry, q, zz + sign, zz + sign))
                elif RELAYED and distance == 2:
                    behind = zz - sign
                    waits = (behind >= 0) & (behind < n)

                    @pl.when(waits if late else jnp.logical_not(waits))
                    def _():
                        if late:
                            late_sum(stage, entry, q, act)
                        else:
                            act(z_grad(stage, entry, q, q, zz))
                elif not late:
                    act(z_grad(stage, entry, q, q, zz))

            def each(*where):
                for k in which:
                    one(FEED_GRADS[k], *where)

            chips_at(range(n - 1, 0, -1), each)

        def late_sum(stage, entry, q, act):
            a, sb, rb, mb, zb, yb, yr, rows = entry
            if act is None:
                act = lambda copy: copy.wait_send()
            else:
                hop = aligned(zz * rows, rows)
                remote(
                    mb.at[pl.ds(0, rows)],
                    zb[stage].at[hop],
                    R.r2_send.at[stage, a, zz],
                    R.r2_recv.at[stage, a, zz],
                    s,
                    mate,
                ).wait_recv()
                part = aligned(q * rows, rows)
                both = mb[part, :].astype(F32) + zb[stage][hop, :].astype(F32)
                mb[part, :] = both.astype(BF16)
            act(z_grad(stage, entry, q, q, zz))

        def feed_to_mate(stage, which):
            for copy in mate_grads(stage, which):
                copy.start()

        def finish_feed_z(stage):
            each_z_grad(stage, lambda copy: copy.wait_send(), False)
            each_z_grad(stage, None, True)

        def feed_late(stage, which):
            each_z_grad(stage, lambda copy: copy.start(), True, which)

        def feed_along_z(stage, which):
            for copy in mate_grads(stage, which):
                copy.wait()
            for a, sb, rb, mb, zb, yb, yr, rows in [FEED_GRADS[k] for k in which]:

                def add(q, sb=sb, rb=rb, mb=mb, rows=rows):
                    part = aligned(q * rows, rows)
                    both = sb[c, part, :].astype(F32) + rb[part, :].astype(F32)
                    mb[part, :] = both.astype(BF16)

                loop(n, add)
            each_z_grad(stage, lambda copy: copy.start(), False, which)

        def y_grad(a, yb, yr):
            return remote(yb, yr, R.r4_send.at[a], R.r4_recv.at[a], other_y, o)

        def keep_half(a, h, value):
            if a:
                R.o_down[pl.ds(h * rd, rd), :] = value
                return
            for k in range(NO):
                R.o_up[:, (2 * k + h) * rd : (2 * k + h + 1) * rd] = value[:, k * rd : (k + 1) * rd]

        def feed_owned(stage):
            layer = 1 - stage
            for a, sb, rb, mb, zb, yb, yr, rows in FEED_GRADS:

                def landed(q, sign, distance, a=a, zb=zb, mb=mb, rows=rows):
                    if not (RELAYED and distance == 3):
                        remote(
                            mb.at[pl.ds(0, rows)],
                            zb[stage].at[aligned(q * rows, rows)],
                            R.r2_send.at[stage, a, q],
                            R.r2_recv.at[stage, a, q],
                            s,
                            2 * q + c,
                        ).wait_recv()

                chips_at(range(1, n), landed)
                total = mb[aligned(zz * rows, rows), :].astype(F32)
                for k in range(1, n):
                    q = (zz + k) % n
                    part = zb[stage][aligned(q * rows, rows), :].astype(F32)
                    if RELAYED:
                        part = jnp.where(jnp.abs(q - zz) == 3, 0.0, part)
                    total = total + part

                @pl.when(y == layer)
                def _(a=a, total=total):
                    keep_half(a, layer, total)

                @pl.when(y != layer)
                def _(a=a, yb=yb, yr=yr, total=total):
                    yb[...] = total.astype(BF16)

        def feed_to_home(stage):
            @pl.when(y == stage)
            def _():
                for a, sb, rb, mb, zb, yb, yr, rows in FEED_GRADS:
                    y_grad(a, yb, yr).start()

        def feed_home():
            for a, sb, rb, mb, zb, yb, yr, rows in FEED_GRADS:
                y_grad(a, yb, yr).wait()
                for h in range(2):

                    @pl.when(y == 1 - h)
                    def _(a=a, h=h, yr=yr):
                        keep_half(a, h, yr[...].astype(F32))

        att_rows = NO * rp

        def grad_half(stage, section, q, way):
            return aligned(section * att_rows + (2 * q + way) * rp, rp)

        def plane_half_at(stage, section, q, way):
            return R.watt.at[stage, section, aligned((2 * q + way) * rp, rp)]

        def plane_grad(stage, q, step, way):
            near, far = (other_y, other_x) if way else (other_x, other_y)
            part, to = ((3 - s, near), (near, near), (far, far))[step // 2]
            slot = step + way
            return remote(
                ga[stage].at[grad_half(stage, part, q, way), pl.ds(0, W)],
                plane_half_at(stage, far if step == HOP else s, q, way),
                R.g1_send.at[stage, q, slot],
                R.g1_recv.at[stage, q, slot],
                to,
                o,
            )

        def plane_landed(stage, q, step, way):
            near, far = (other_y, other_x) if way else (other_x, other_y)
            src = (3 - s, near, far)[step // 2]
            slot = step + way
            remote(
                ga[stage].at[grad_half(stage, s, q, way), pl.ds(0, W)],
                plane_half_at(stage, src, q, way),
                R.g1_send.at[stage, q, slot],
                R.g1_recv.at[stage, q, slot],
                near,
                o,
            ).wait_recv()

        def each_chip(distances, body):
            for distance in distances:
                if distance:
                    chips_at((distance,), lambda q, sign, distance: body(q, sign, distance))
                else:
                    body(zz, 0, 0)

        FIRST, SECOND = tuple(range(n - 1, 1, -1)), (1, 0)

        def each_plane_grad(stage, steps, act):
            def block(q, *_):
                for step in steps:
                    for way in range(2):
                        act(plane_grad(stage, q, step, way))

            each_chip(FIRST + SECOND, block)

        def att_to_plane(stage):
            each_plane_grad(stage, (HOP, STRAIGHT), lambda copy: copy.start())

        def att_plane_late(stage, distances):
            def block(q, *_):
                for way in range(2):
                    plane_landed(stage, q, HOP, way)
                    part = grad_half(stage, other_x if way else other_y, q, way)
                    hop = R.watt[stage, 3 - s, aligned((2 * q + way) * rp, rp), :]
                    both = ga[stage][part, 0:W].astype(F32) + hop.astype(F32)
                    ga[stage][part, 0:W] = both.astype(BF16)
                    plane_grad(stage, q, LATE, way).start()

            each_chip(distances, block)

        def finish_att_plane(stage):
            each_plane_grad(stage, (HOP, STRAIGHT, LATE), lambda copy: copy.wait_send())

        def att_z_grad(stage, q, to, slot):
            return remote(
                R.gs.at[stage, aligned(q * 2 * rp, 2 * rp)],
                R.gz.at[stage, slot],
                R.g2_send.at[stage, q],
                R.g2_recv.at[stage, slot],
                s,
                2 * to + c,
            )

        def waits_behind(sign, distance):
            behind = zz - sign
            return (behind >= 0) & (behind < n) if RELAYED and distance == 2 else False

        def att_z_straight(stage, q, sign, distance, act):
            if RELAYED and distance == 3:
                act(att_z_grad(stage, q, zz + sign, zz + sign))
            elif RELAYED and distance == 2:

                @pl.when(jnp.logical_not(waits_behind(sign, distance)))
                def _():
                    act(att_z_grad(stage, q, q, zz))
            elif distance:
                act(att_z_grad(stage, q, q, zz))

        def att_z_late(stage, act, add):
            def one(q, sign, distance):
                @pl.when(waits_behind(sign, distance))
                def _():
                    if add:
                        remote(
                            R.gs.at[stage, pl.ds(0, 2 * rp)],
                            R.gz.at[stage, zz],
                            R.g2_send.at[stage, q],
                            R.g2_recv.at[stage, zz],
                            s,
                            mate,
                        ).wait_recv()
                        part = aligned(q * 2 * rp, 2 * rp)
                        both = R.gs[stage, part, :].astype(F32) + R.gz[stage, zz].astype(F32)
                        R.gs[stage, part, :] = both.astype(BF16)
                    act(att_z_grad(stage, q, q, zz))

            if RELAYED:
                chips_at((2,), one)

        def att_late(stage):
            att_z_late(stage, lambda copy: copy.start(), True)

        def finish_att_z(stage):
            each_chip(
                FIRST + SECOND,
                lambda q, sign, distance: att_z_straight(
                    stage, q, sign, distance, lambda copy: copy.wait_send()
                ),
            )
            att_z_late(stage, lambda copy: copy.wait_send(), False)

        def att_along_z(stage, distances):
            def block(q, sign, distance):
                part = aligned(q * 2 * rp, 2 * rp)

                for step in (STRAIGHT, LATE):
                    for way in range(2):
                        plane_landed(stage, q, step, way)
                own = aligned(s * att_rows + q * 2 * rp, 2 * rp)
                total = ga[stage][own, 0:W].astype(F32)
                for src in (other_x, other_y):
                    total = total + R.watt[stage, src, part, :].astype(F32)
                R.gs[stage, part, :] = total.astype(BF16)
                att_z_straight(stage, q, sign, distance, lambda copy: copy.start())

            each_chip(distances, block)

        def home_copy(stage, core):
            return remote(
                R.gt.at[stage, pl.ds(core * rp, rp)],
                R.att_own.at[aligned(s * rp, rp)],
                R.g3_send.at[stage, core],
                R.g3_recv.at[s],
                2 * (1 - stage) + c,
                2 * zz + core,
            )

        def each_home(stage, act, own):
            for core in range(2):
                stays = (s == 2 * (1 - stage) + c) & (c == core)

                @pl.when(stays)
                def _(core=core):
                    if own:
                        R.att_own[aligned(s * rp, rp), :] = R.gt[stage, pl.ds(core * rp, rp), :]

                @pl.when(jnp.logical_not(stays))
                def _(core=core):
                    act(home_copy(stage, core))

        def att_owned(stage):
            def landed(q, sign, distance):
                if not (RELAYED and distance == 3):
                    remote(
                        R.gs.at[stage, pl.ds(0, 2 * rp)],
                        R.gz.at[stage, q],
                        R.g2_send.at[stage, q],
                        R.g2_recv.at[stage, q],
                        s,
                        2 * q + c,
                    ).wait_recv()

            chips_at(range(1, n), landed)
            total = R.gs[stage, aligned(zz * 2 * rp, 2 * rp), :].astype(F32)
            for k in range(1, n):
                q = (zz + k) % n
                part = R.gz[stage, q].astype(F32)
                if RELAYED:
                    part = jnp.where(jnp.abs(q - zz) == 3, 0.0, part)
                total = total + part
            R.gt[stage] = total.astype(BF16)
            each_home(stage, lambda copy: copy.start(), True)

        def att_home():
            for p in range(SECTIONS):
                mine = (s == p) & (x == c)

                @pl.when(jnp.logical_not(mine))
                def _(p=p):
                    remote(
                        R.gt.at[0, pl.ds(0, rp)],
                        R.att_own.at[pl.ds(p * rp, rp)],
                        R.g3_send.at[0, 0],
                        R.g3_recv.at[p],
                        p,
                        2 * zz + x,
                    ).wait_recv()

            rows = R.att_own[pl.ds(0, ru), :].astype(F32)
            R.o_qkv[...] = from_packed(rows, F, heads)
            rows = R.att_own[pl.ds(ru, ra - ru), :].astype(F32)
            R.o_out[...] = rows[:ro, :D]

        att_collect(0)
        att_onward(1, NEAR)
        attention_forward(0)
        send_parts(0, True, None)
        for m in range(2):
            close_forward(0, m)
        feed_arrivals(0, NEAR, (0,))
        pass_rows(1, R.norm_ff.at[0])
        feed_arrivals(0, NEAR, (1,))
        feed_spread_home(1)
        feed_spread_away(1, 0)
        feed_spread_away(1, 1)
        att_onward(1, FAR)
        feed_collect(0, (0,))
        finish_send_parts(0, True)
        for m in range(2):
            await_rows(1, False, m, R.norm_ff.at[0])
            feed_up(0, m)
        att_plane_relay(1, zz)
        att_plane_onward(1, NEAR)
        feed_collect(0, (1,))
        for m in range(2):
            feed_down(0, m)
            send_parts(1, False, m)
        late_parts(1, 0)
        att_plane_onward(1, FAR)
        late_parts(1, 1)
        close_forward(1, 0)
        feed_arrivals(1, NEAR)
        close_forward(1, 1)
        att_collect(1)
        finish_send_parts(1, False)
        await_rows(2, True, None, R.norm_at.at[1])
        attention_forward(1)
        send_parts(2, True, None)
        for m in range(2):
            close_forward(2, m)
        feed_collect(1)
        pass_rows(3, R.norm_ff.at[1])
        finish_send_parts(2, True)
        for m in range(2):
            await_rows(3, False, m, R.norm_ff.at[1])
            feed_up(1, m)

        loop(NO, lambda k: small_out(k).wait_send(), 1)
        loop(SECTIONS, lambda k: small_b_copy(k, s).wait_send(), 1)
        len_copy.wait_send()
        each_quarter(lambda copy: copy.wait_send(), False)

        @pl.when(x == c)
        def _():
            seq_copy(False).wait_send()

        for kind in range(2):
            y_copy(kind).wait_send()
        for layer in range(2):
            att_sent(layer)
            feed_sent(layer)
        for m in range(2):
            finish_send_rows(1, False, m, R.norm_ff.at[0])
            finish_send_rows(2, True, m, R.norm_at.at[1])
            finish_send_rows(3, False, m, R.norm_ff.at[1])
            for j in range(2):
                cot_copy(m, j, True).wait()
                cot_copy(m, j, False).wait_send()
                remote(
                    R.cot_in.at[m, pl.ds(0, Q)],
                    R.grad_ff.at[0, aligned(j * L + (2 * m + 1 - c) * Q, Q)],
                    R.cot_send.at[m, j],
                    R.cot_recv.at[m, j],
                    s,
                    mate,
                ).wait_recv()
        for j in range(2):
            R.grad_rows[pl.ds(j * Q, Q), :] = R.grad_ff[0, aligned(j * L + s * Q, Q), :]

        for m in range(2):
            feed_back_rows(1, m)
            send_parts(4, False, m)
        feed_back_down(1)
        feed_to_mate(0, DOWN)
        feed_back_up(1)
        feed_to_mate(0, UP)
        for m in range(2):
            late_parts(4, m)
        feed_along_z(0, DOWN)
        feed_along_z(0, UP)
        for m in range(2):
            close_backward(4, m)
        finish_send_parts(4, False)
        for m in range(2):
            feed_down(1, m)
            send_parts(3, False, m)
        await_rows(5, True, None, grad_at[1])
        attention_back_heads(
            1, lambda: (feed_late(0, DOWN), late_parts(3, 0), late_parts(3, 1))
        )
        feed_late(0, UP)
        finish_send_parts(3, False, (0,))
        attention_back_rows(1)
        send_parts(5, True, None)
        attention_back_out(1)
        attention_back_weights(1)
        for m in range(2):
            close_backward(5, m)
        for m in range(2):
            close_forward(3, m)
        finish_send_parts(3, False, (1,))
        finish_send_parts(5, True)
        pass_rows(6, R.grad_ff.at[1])
        for m in range(2):
            await_rows(6, False, m, R.grad_ff.at[1])
            feed_back_rows(0, m)
            send_parts(6, False, m)
        feed_back_down(0)
        feed_to_mate(1, DOWN)
        late_parts(6, 0)
        feed_back_up(0)
        feed_to_mate(1, UP)
        late_parts(6, 1)
        att_to_plane(0)
        for m in range(2):
            finish_send_rows(5, True, m, grad_at[1])
        feed_owned(0)
        finish_feed_z(0)
        feed_along_z(1, DOWN)
        feed_along_z(1, UP)
        for m in range(2):
            close_backward(6, m)
        finish_send_parts(6, False)
        await_rows(7, True, None, grad_at[0])
        attention_back_out(0)
        attention_back_heads(0, lambda: feed_late(1, DOWN))
        att_plane_late(0, FIRST + SECOND)
        feed_late(1, UP)
        attention_back_weights(0)
        att_to_plane(1)
        attention_back_rows(0)
        send_parts(7, True, None)
        att_along_z(0, FIRST + SECOND)
        for m in range(2):
            close_backward(7, m)

        emitted = []

        def emit(*pairs):
            for held, out in pairs:
                copy = pltpu.make_async_copy(held, out, R.out_sem.at[len(emitted)])
                copy.start()
                emitted.append(copy)

        def small_grad_copy(k, of):
            to = (s + k) % SECTIONS
            return remote(
                R.small_grad.at[to],
                R.small_sum.at[of],
                R.sga_send.at[k],
                R.sga_recv.at[of],
                to,
                o,
            )

        def small_mate_copy(of):
            return remote(
                R.small_line, R.small_all.at[of], R.sgb_send.at[0], R.sgb_recv.at[of], s, mate
            )

        def small_z_copy(k, of):
            to = 2 * ((zz + k) % n) + c
            return remote(
                R.small_own, R.small_all.at[of], R.sgb_send.at[k], R.sgb_recv.at[of], s, to
            )

        def small_to_mate():
            loop(SECTIONS, lambda k: small_grad_copy(k, (s + k) % SECTIONS).wait_recv(), 1)
            total = R.small_sum[0]
            for k in range(1, SECTIONS):
                total = total + R.small_sum[k]
            R.small_line[...] = total
            small_mate_copy(o).start()

        def small_along_z():
            small_mate_copy(mate).wait_recv()
            R.small_own[...] = R.small_line[...] + R.small_all[mate]
            loop(n, lambda k: small_z_copy(k, o).start(), 1)

        R.small_sum[s] = R.small_grad[s]
        att_plane_late(1, FIRST)
        att_late(0)
        att_plane_late(1, SECOND)
        loop(SECTIONS, lambda k: small_grad_copy(k, s).start(), 1)
        for m in range(2):
            place_rows(1, m)
        feed_to_home(0)
        feed_owned(1)
        feed_to_home(1)
        att_along_z(1, FIRST)
        att_along_z(1, SECOND)
        att_owned(0)
        att_late(1)
        small_to_mate()
        small_along_z()
        att_owned(1)
        feed_home()
        loop(n, lambda k: small_z_copy(k, 2 * ((zz + k) % n) + c).wait_recv(), 1)
        total = R.small_own[...]
        for k in range(1, n):
            total = total + R.small_all[2 * ((zz + k) % n) + c]

        def back(rows, lanes):
            return pltpu.roll(rows, (wide - lanes) % wide, 1)

        norms = back(total, ru * o)
        for k in range(3):
            R.o_norm[k] = norms[k : k + 1, 0:ru]
        units = back(total, rd * o)
        R.o_upb[:, 0:rd] = units[4:5, 0:rd]
        R.o_upb[:, rd : 2 * rd] = units[5:6, 0:rd]
        first, second, third = 3 * low, 3 * low + 2 * rest, 3 * low + 3 * rest
        plain = jnp.where(lane8 < low, total, 0.0)
        plain += back(jnp.where((lane8 >= first) & (lane8 < first + rest), total, 0.0), 2 * low)
        plain += back(jnp.where((lane8 >= 2 * low) & (lane8 < first), total, 0.0), 2 * low - F)
        plain += back(
            jnp.where((lane8 >= second) & (lane8 < third), total, 0.0), 2 * low + 2 * rest - F
        )
        R.o_qvb[...] = back(plain, ru * o)[3:4, 0:ru]
        squares = back(total, 4 * o)
        for m in range(2):
            count = (R.lens[0, m] * D).astype(F32)
            R.o_rms[m : m + 1, :] = jnp.sqrt(squares[6:7, 2 * m : 2 * m + 2] / count)
        emit(
            (R.o_up, R.h_o_up),
            (R.o_down, R.h_o_down),
            (R.o_norm, R.h_o_norm),
            (R.o_qvb, R.h_o_qvb),
            (R.o_upb, R.h_o_upb),
            (R.o_rms, R.h_o_rms),
        )
        for which in range(2):
            finish_place(which)
        emit((R.out_stream, R.h_out_stream), (R.out_grad_rows, R.h_out_grad_rows))
        att_home()
        emit((R.o_qkv, R.h_o_qkv), (R.o_out, R.h_o_out))

        loop(SECTIONS, lambda k: small_grad_copy(k, s).wait_send(), 1)
        small_mate_copy(o).wait_send()
        loop(n, lambda k: small_z_copy(k, o).wait_send(), 1)
        for m in range(2):
            finish_send_rows(6, False, m, R.grad_ff.at[1])
            finish_send_rows(7, True, m, grad_at[0])
        finish_send_parts(7, True)
        finish_feed_z(1)
        for stage in range(2):
            finish_att_plane(stage)
            finish_att_z(stage)
            each_home(stage, lambda copy: copy.wait_send(), False)

        for copy in emitted:
            copy.wait()

    return kernel


def one_step(cfg, lens, qkv, qv_b, out, up, up_b, down, norm, stream, cotangent):
    D, L, U, F, W = cfg.width, cfg.length, cfg.units, cfg.features, cfg.packed
    Q = L // SECTIONS
    NO, n = cfg.outer, cfg.outer // 2
    ru, rd, ro, ra = cfg.up_rows, cfg.down_rows, cfg.out_rows, cfg.att_rows
    rp = ra // SECTIONS
    wide = max(U, W)
    lanes = -(-max(ru, rd) // 128) * 128
    dma = pltpu.SemaphoreType.DMA
    inputs = dict(
        lens=lens,
        qkv_w=qkv,
        qv_b=qv_b,
        out_w=out,
        up_w=up,
        up_b=up_b,
        down_w=down,
        norm_v=norm,
        stream_in=stream,
        cot_in=cotangent,
    )
    outputs = dict(
        out_stream=((2 * Q, D), BF16),
        out_grad_rows=((2 * Q, D), BF16),
        o_qkv=((ru, 3 * F), F32),
        o_qvb=((1, ru), F32),
        o_out=((ro, D), F32),
        o_up=((ru, 2 * U), F32),
        o_upb=((1, 2 * rd), F32),
        o_down=((2 * rd, D), F32),
        o_norm=((3, 1, ru), F32),
        o_rms=((2, 2), F32),
    )
    scratch = dict(
        small_in=((8, lanes), F32),
        small_a=((NO, 8, lanes), F32),
        small_own=((8, wide), F32),
        small_b=((SECTIONS, 8, wide), F32),
        small_grad=((SECTIONS, 8, wide), F32),
        small_sum=((SECTIONS, 8, wide), F32),
        small_line=((8, wide), F32),
        small_all=((NO, 8, wide), F32),
        len_own=((8, 128), F32),
        len_mate=((8, 128), F32),
        att_own=((ra, W), BF16),
        watt=((2, SECTIONS, NO * rp, W), BF16),
        wqkv=((2, D, W), BF16),
        wout=((2, F, D), BF16),
        wup=((2, D, U), BF16),
        wdown=((2, U, D), BF16),
        hid_rows=((SECTIONS, 2 * Q, D), BF16),
        grad_rows=((2 * Q, D), BF16),
        norm_at=((2, L, D), BF16),
        norm_ff=((2, 2 * L, D), BF16),
        lin_t=((2, W, L), BF16),
        att_t=((2, F, L), BF16),
        log_total=((2, cfg.heads, 1, L), F32),
        hidden=((2, 2 * L, U), BF16),
        slope=((2, 2 * L, U), BF16),
        grad_ff=((2, 2 * L, D), BF16),
        grad_at=((L, D), BF16),
        seq_rows=((L, D), BF16),
        parts=((2 * L, D), BF16),
        sums=((2, SECTIONS, 2, Q, D), BF16),
        finished=((2, 2, Q, D), BF16),
        acc=((L, D), F32),
        wide_rows=((F + 64, D), F32),
        d_att_t=((F, L), BF16),
        d_lin_t=((W, L), BF16),
        sb_up=((2, n * ru, U), BF16),
        rb_up=((n * ru, U), BF16),
        mb_up=((n * ru, U), BF16),
        zb_up=((n * ru, U), BF16),
        yb_up=((ru, U), BF16),
        yr_up=((ru, U), BF16),
        sb_down=((2, n * rd, D), BF16),
        rb_down=((n * rd, D), BF16),
        mb_down=((n * rd, D), BF16),
        zb_down=((n * rd, D), BF16),
        yb_down=((rd, D), BF16),
        yr_down=((rd, D), BF16),
        gs=((2, NO * rp, W), BF16),
        gz=((2, n, 2 * rp, W), BF16),
        gt=((2, 2 * rp, W), BF16),
    )
    semaphores = dict(
        raw_sem=(4,),
        load_sem=(5,),
        sma_send=(NO,),
        sma_recv=(NO,),
        smb_send=(SECTIONS,),
        smb_recv=(SECTIONS,),
        len_send=(1,),
        len_recv=(1,),
        seq_send=(1,),
        seq_recv=(1,),
        cot_send=(2, 2),
        cot_recv=(2, 2),
        a1_send=(SECTIONS,),
        a1_recv=(2, 2),
        a2_send=(2, n, n),
        a2_recv=(2, n),
        a3_send=(2, n, 2),
        a3_recv=(2, n, 2),
        a4_send=(2, n, 2),
        a4_recv=(2, n, 2),
        y_send=(2,),
        y_recv=(2,),
        z_send=(4, n, n),
        z_recv=(4, n),
        p_send=(4, n),
        p_recv=(4, n),
        ag_send=(8, 2, SECTIONS),
        ag_recv=(8, 2, SECTIONS),
        rs_send=(8, 2, 6),
        rs_recv=(8, 2, 6),
        fo_send=(2, 2),
        fo_recv=(2, 2),
        r1_send=(2, 2),
        r1_recv=(2, 2),
        r2_send=(2, 2, n),
        r2_recv=(2, 2, n),
        r4_send=(2,),
        r4_recv=(2,),
        g1_send=(2, n, 6),
        g1_recv=(2, n, 6),
        g2_send=(2, n),
        g2_recv=(2, n),
        g3_send=(2, 2),
        g3_recv=(SECTIONS,),
        sga_send=(SECTIONS,),
        sga_recv=(SECTIONS,),
        sgb_send=(NO,),
        sgb_recv=(NO,),
        out_sem=(len(outputs),),
    )
    placed = ["h_" + key for key in outputs]
    names = [*inputs, *placed, *outputs, *scratch, *semaphores]
    vmem = pl.BlockSpec(memory_space=pltpu.VMEM)
    hbm = pl.BlockSpec(memory_space=pl.ANY)
    smem = pl.BlockSpec(memory_space=pltpu.SMEM)
    shapes = [jax.ShapeDtypeStruct(*spec) for spec in outputs.values()]
    results = pl.pallas_call(
        make_kernel(cfg, names),
        out_shape=shapes,
        in_specs=[smem, hbm, vmem, hbm, hbm, vmem, hbm, vmem, hbm, hbm],
        out_specs=[hbm] * len(outputs),
        scratch_shapes=[pltpu.VMEM(*spec) for spec in (outputs | scratch).values()]
        + [dma(shape) for shape in semaphores.values()],
        compiler_params=pltpu.CompilerParams(
            collective_id=0, has_side_effects=True, vmem_limit_bytes=63 * 2**20
        ),
        name="layers",
    )(*inputs.values())
    count = len(shapes)

    def hand_over(*refs):
        given, out, held = refs[:count], refs[count : 2 * count], refs[2 * count : 3 * count]
        loads = [pltpu.make_async_copy(given[k], held[k], refs[-2].at[k]) for k in range(count)]
        stores = [pltpu.make_async_copy(held[k], out[k], refs[-1].at[k]) for k in range(count)]
        for copy in loads:
            copy.start()
        for load, store in zip(loads, stores):
            load.wait()
            store.start()
        for copy in stores:
            copy.wait()

    return pl.pallas_call(
        hand_over,
        out_shape=shapes,
        in_specs=[hbm] * count,
        out_specs=[hbm] * count,
        scratch_shapes=[pltpu.VMEM(*spec) for spec in outputs.values()]
        + [dma((count,)), dma((count,))],
        compiler_params=pltpu.CompilerParams(vmem_limit_bytes=63 * 2**20),
        name="outputs",
    )(*results)


def shards(
    layer_input,
    out_cotangent,
    lengths,
    qkv_weight,
    qv_bias,
    out_weight,
    up_weight,
    up_bias,
    down_weight,
    norm_vectors,
):
    section_count = lax.axis_size("section")
    dp_count = lax.axis_size("dp")
    L, D = layer_input.shape[2:]
    sequences = layer_input.shape[0] * layer_input.shape[1]
    assert section_count == SECTIONS and sequences == 2
    F = out_weight.shape[1] * dp_count
    U2 = up_weight.shape[2]
    heads = F // HEAD_DIM
    outer = max(
        k
        for k in range(2, dp_count + 1, 2)
        if dp_count % k == 0 and D % (16 * k) == 0 and U2 % (32 * k) == 0 and F % (8 * k) == 0
    )
    inner = dp_count // outer
    groups = [[g * inner + k for k in range(inner)] for g in range(outer)]

    def joined(block, axis=0):
        if inner == 1:
            return block
        block = block.astype(BF16)
        block = lax.all_gather(block, "dp", axis=axis, tiled=True, axis_index_groups=groups)
        return block.astype(F32)

    def own_share(block, axis=0):
        if inner == 1:
            return block
        return lax.psum_scatter(
            block, "dp", scatter_dimension=axis, tiled=True, axis_index_groups=groups
        )

    shard_rows = D // outer + F // outer
    cfg = types.SimpleNamespace(
        width=D,
        length=L,
        units=U2 // 2,
        features=F,
        packed=-(-3 * F // 256) * 256,
        outer=outer,
        inner=inner,
        heads=heads,
        up_rows=D // outer,
        down_rows=U2 // outer // 2,
        out_rows=F // outer,
        att_rows=-(-shard_rows // (16 * SECTIONS)) * 16 * SECTIONS,
    )
    stream, grad_rows, qkv, qvb, out, up, upb, down, norm, rms = one_step(
        cfg,
        lengths.reshape(1, 2),
        joined(qkv_weight[0]),
        joined(qv_bias, 1),
        joined(out_weight[0]),
        joined(up_weight[0]),
        joined(up_bias, 1),
        joined(down_weight[0]),
        joined(norm_vectors[0], 1)[:, None],
        layer_input.reshape(2, L, D),
        out_cotangent.reshape(2, L, D),
    )
    rows_shape = layer_input.shape[:2] + (L // SECTIONS, D)
    return (
        stream.reshape(rows_shape),
        grad_rows.reshape(rows_shape),
        own_share(qkv)[None],
        own_share(qvb, 1),
        own_share(out)[None],
        own_share(up)[None],
        own_share(upb, 1),
        own_share(down)[None],
        own_share(norm, 2).reshape(1, 3, -1),
        rms.reshape(layer_input.shape[:2] + (1, 2)),
    )


def solution(mesh):
    placed = (
        P(None, "dp", None, None),
        P(None, "dp", None, None),
        P(None, "dp"),
        P("section", "dp", None),
        P("section", "dp"),
        P("section", "dp", None),
        P("section", "dp", None),
        P("section", "dp"),
        P("section", "dp", None),
        P("section", None, "dp"),
    )
    return jax.shard_map(
        shards,
        mesh=mesh,
        in_specs=placed,
        out_specs=(
            P(None, "dp", "section", None),
            P(None, "dp", "section", None),
            P("section", "dp", None),
            P("section", "dp"),
            P("section", "dp", None),
            P("section", "dp", None),
            P("section", "dp"),
            P("section", "dp", None),
            P("section", None, "dp"),
            P(None, "dp", "section", None),
        ),
        check_vma=False,
    )
```
